32 devices in a mesh: dp: 4 (over y, x), ctx: 8 (over z, core).
Axes of the slice: x: 2, y: 2, z: 4, core: 2. Of those that a mesh axis runs over, the one named last changes fastest.
Arguments:
- hidden_in: bfloat16 [4, 1536, 16384], P('dp', 'ctx'), may hold values from -8 to 8
- queries: bfloat16 [4, 1536, 1024], P('dp', 'ctx'), may hold values from -14 to 14
- grad_out: bfloat16 [4, 1536, 1024], P('dp', 'ctx'), may hold values from -6 to 6
- w_key: bfloat16 [16384, 128], P('dp'), may hold values from -1 to 1
- w_value: bfloat16 [16384, 128], P('dp'), may hold values from -0.046875 to 0.046875
- stretch_order: int32 [16], replicated, may hold values from 0 to 15, each once
- doc_lengths: int32 [4, 8], P('dp'), may hold values from 1 to 768, 1536 in all within a row
Outputs:
- query_grad: bfloat16 [4, 1536, 1024], P('dp', 'ctx')
- key_weight_grad: float32 [16384, 128], P('dp')
- value_weight_grad: float32 [16384, 128], P('dp')
The draws below stay inside these ranges and needn't reach their ends.
Inputs may be any that keep to these rules, and one draw needn't show every extreme that they name: `stretch_order`: every block number appears exactly once. `doc_lengths`: each sequence's lengths sum to 1536, and one of them is 768.
All inputs are finite; a program needn't handle non-finite values.
Results may differ from the reference program's by a relative error of at most 0.03.
Values may be sent and summed in bfloat16 or wider, within the bound.
No kernel may reach another device: no remote copies, remote signals or barrier semaphores. Data moves between devices by JAX's collectives and lax.ppermute only.
A program may use at most 128 MiB of HBM per device.

```python
import math
import jax
import jax.numpy as jnp
import numpy as np
from jax import lax

D = 16384
HEADS = 8
HD = 128
TOK_DEV = 192
DOCS = 8
SEQ = 1536
SEQS = 4
STRETCHES = 16


def draw_hidden_in(key, part):
    key = jax.random.fold_in(key, 11)
    base = jnp.clip(jax.random.normal(key, (SEQS, SEQ, D), jnp.float32), -6.0, 6.0)
    return base.astype(jnp.bfloat16)


def draw_w_key(key, part):
    key = jax.random.fold_in(key, 12)
    base = jnp.clip(jax.random.normal(key, (D, HD), jnp.float32), -6.0, 6.0) * D ** (-0.5)
    return base.astype(jnp.bfloat16)


def draw_queries(key, part):
    key = jax.random.fold_in(key, 13)
    base = jnp.clip(jax.random.normal(key, (SEQS, SEQ, HEADS, HD), jnp.float32), -6.0, 6.0)
    return base.reshape(SEQS, SEQ, HEADS * HD).astype(jnp.bfloat16)


def block_levels(own_key, extent, pieces, least, largest):
    gain, own = 1.0, jax.random.fold_in(own_key, 6)
    for axis_at, shards_of in pieces:
        draws = jnp.exp(jax.random.uniform(jax.random.fold_in(own, axis_at), (shards_of,), jnp.float32, least / len(pieces), largest / len(pieces)))
        gain = gain * jnp.repeat(draws, extent[axis_at] // shards_of).reshape([-1 if axis == axis_at else 1 for axis in range(len(extent))])
    return gain


def split_up(count, total, bound, skew):
    loads = [(1 << 20) // math.isqrt(rank ** skew) + 1 for rank in range(2, count + 1)]
    surplus, holding = total - bound - (count - 1), [1] * (count - 1)
    while surplus > 0:
        movable = [i for i in range(count - 1) if holding[i] < bound]
        whole, budget = sum([loads[i] for i in movable]), surplus
        for i in movable:
            extra = min(bound - holding[i], max(1, budget * loads[i] // whole), surplus)
            holding[i] = holding[i] + extra
            surplus = surplus - extra
    return np.array([bound] + holding)


def uneven(own_key, amount, total, bound, slope):
    if amount == 2:
        one = jax.random.randint(own_key, (), max(1, total - bound), min(bound, total - 1) + 1)
        return jnp.stack([one, total - one])
    sizes = jnp.asarray(split_up(amount, total, bound, slope), jnp.int32)
    couples = (amount - 1) // 2
    donor, taker = sizes[1:1 + 2 * couples:2], sizes[2:2 + 2 * couples:2]
    margin = jnp.minimum(donor - 1, bound - taker)
    moved = jax.random.randint(jax.random.fold_in(own_key, 1), (couples,), 0, 1 << 20) % (margin + 1)
    sizes = sizes.at[1:1 + 2 * couples:2].set(donor - moved).at[2:2 + 2 * couples:2].set(taker + moved)
    return sizes[jax.random.permutation(jax.random.fold_in(own_key, 2), amount)]


def normal_values(own_key, shape, width, limit, split=(), kind=jnp.bfloat16):
    array = jax.random.normal(own_key, shape, jnp.float32) * width
    if len(split) > 0:
        array = block_levels(own_key, shape, split, -0.22, 0.18) * array
    return jnp.clip(array, min=-limit, max=limit).astype(kind)


def setup_inputs(seed: int = 0) -> dict:
    keys = jax.random.split(jax.random.key(seed), 8)
    return {
        "hidden_in": draw_hidden_in(jax.random.fold_in(keys[7], 71), 0),
        "queries": draw_queries(jax.random.fold_in(keys[7], 71), 0),
        "grad_out": normal_values(keys[2], (SEQS, SEQ, HEADS * HD), 1.0, 6.0, ((0, 4), (1, 8))),
        "w_key": draw_w_key(jax.random.fold_in(keys[7], 71), 0),
        "w_value": normal_values(keys[4], (D, HD), D ** -0.5, 0.046875, ((0, 4),)),
        "stretch_order": jax.random.permutation(keys[5], STRETCHES).astype(jnp.int32),
        "doc_lengths": jax.vmap(lambda own: uneven(own, DOCS, SEQ, SEQ // 2, 2))(jax.random.split(keys[6], SEQS)).reshape((SEQS, DOCS)).astype(jnp.int32),
    }


def positions(stretch_order, row_count, stretch_rows):
    stored = jnp.arange(row_count, dtype=jnp.int32)
    return stretch_order[stored // stretch_rows] * stretch_rows + stored % stretch_rows

def doc_numbers(place, lengths):
    doc_ends = jnp.cumsum(lengths)
    return lax.optimization_barrier(jnp.sum((place[:, None] >= doc_ends[None, :]).astype(jnp.int32), axis=1))

def attention_grads(query_rows, key_rows, value_rows, cotangent, allowed):
    row_count = query_rows.shape[0]
    score_scale = 1.0 / math.sqrt(HD)
    query_three = query_rows.reshape(row_count, HEADS, HD).astype(jnp.float32)
    cot_three = cotangent.reshape(row_count, HEADS, HD).astype(jnp.float32)
    keys_float = key_rows.astype(jnp.float32)
    values_float = value_rows.astype(jnp.float32)
    scores = jnp.einsum('thd,kd->htk', query_three, keys_float) * score_scale
    masked = jnp.where(allowed[None], scores, -jnp.inf)
    row_max = lax.optimization_barrier(jnp.max(masked, axis=-1, keepdims=True))
    expsum = jnp.where(allowed[None], jnp.exp(masked - row_max), 0.0)
    probabilities = expsum / lax.optimization_barrier(jnp.sum(expsum, axis=-1, keepdims=True))
    probs_low = probabilities.astype(jnp.bfloat16)
    probs_back = probs_low.astype(jnp.float32)
    attended = jnp.einsum('htk,kd->thd', probs_back, values_float)
    delta_rows = lax.optimization_barrier(jnp.sum(cot_three * attended, axis=-1))
    dprob = jnp.einsum('thd,kd->htk', cot_three, values_float)
    dscore = (probabilities * (dprob - jnp.transpose(delta_rows)[:, :, None])).astype(jnp.bfloat16)
    dscore_back = dscore.astype(jnp.float32)
    query_grad = (jnp.einsum('htk,kd->thd', dscore_back, keys_float) * score_scale).astype(jnp.bfloat16)
    key_grad = jnp.einsum('htk,thd->kd', dscore_back, query_three) * score_scale
    value_grad = jnp.einsum('htk,thd->kd', probs_back, cot_three)
    return (query_grad.reshape(row_count, HEADS * HD), jnp.concatenate([key_grad, value_grad], axis=1))

def reference(hidden_in, queries, grad_out, w_key, w_value, stretch_order, doc_lengths):
    stacked = jnp.concatenate([w_key, w_value], axis=1)
    stretch_rows = TOK_DEV // 2
    place = positions(stretch_order, SEQ, stretch_rows)
    causal = place[None, :] <= place[:, None]

    def per_sequence(running, items):
        inputs, query_rows, cotangent, lengths = items
        documents = doc_numbers(place, lengths)
        allowed = causal & (documents[:, None] == documents[None, :])
        projected = jnp.dot(inputs, stacked, preferred_element_type=jnp.float32).astype(jnp.bfloat16)
        query_grad, kv_grads = attention_grads(query_rows, projected[:, :HD], projected[:, HD:], cotangent, allowed)
        kv_low = kv_grads.astype(jnp.bfloat16)
        running = running + jnp.dot(jnp.transpose(inputs), kv_low, preferred_element_type=jnp.float32)
        return (running, query_grad)
    start_sum = jnp.zeros((D, 2 * HD), jnp.float32)
    weight_grads, query_grad = lax.scan(per_sequence, start_sum, (hidden_in, queries, grad_out, doc_lengths))
    return (query_grad, weight_grads[:, :HD], weight_grads[:, HD:])
```

```python
import functools
import math

import jax
import jax.numpy as jnp
from jax import lax
from jax.experimental import pallas as pl
from jax.experimental.pallas import tpu as pltpu
from jax.sharding import PartitionSpec as P

VMEM_LIMIT = 48 * 1024 * 1024


def swap(array, axis, distance):
    count = lax.axis_size(axis)
    return lax.ppermute(array, axis, [(i, i ^ distance) for i in range(count)])


def after(arrays, *earlier):
    tied = lax.optimization_barrier((tuple(arrays), tuple(earlier)))
    return list(tied[0]), list(tied[1])


def attention_kernel(
    shape, ids, order, lengths, q_ref, g_ref, *refs
):
    ctx_count, stretch_rows, head_count, head_dim, window, chunk = shape
    kv_refs = refs[:ctx_count]
    qgrad_ref, keep_ref, send_ref, keys, values, total, qs, gs, dqs = refs[ctx_count:]
    me = ids[0]
    row_count = 2 * stretch_rows
    stretch_count = 2 * ctx_count
    score_scale = 1.0 / math.sqrt(head_dim)

    def place(device, half):
        return pl.multiple_of(order[2 * device + half] * stretch_rows, stretch_rows)

    for index in range(ctx_count):
        for half in range(2):
            rows = pl.ds(place(me ^ index, half), stretch_rows)
            block = kv_refs[index][half * stretch_rows : (half + 1) * stretch_rows, :]
            keys[rows, :] = block[:, :head_dim]
            values[rows, :] = block[:, head_dim:]
    total[...] = jnp.zeros_like(total)
    for half in range(2):
        for head in range(head_count):
            to = slice((half * head_count + head) * stretch_rows, (half * head_count + head + 1) * stretch_rows)
            rows = slice(half * stretch_rows, (half + 1) * stretch_rows)
            columns = slice(head * head_dim, (head + 1) * head_dim)
            qs[to, :] = q_ref[rows, columns]
            gs[to, :] = g_ref[rows, columns]
    ends = []
    running = 0
    for at in range(lengths.shape[0]):
        running = running + lengths[at]
        ends.append(running)
    chunks_half = head_count * stretch_rows // chunk

    def step(at, carry):
        half = at // chunks_half
        block = order[2 * me + half]
        first = jnp.maximum(block - stretch_count // 2, 0) * stretch_rows
        first = pl.multiple_of(first, stretch_rows)
        part = pl.ds(pl.multiple_of(at * chunk, chunk), chunk)
        inside = (at - half * chunks_half) * chunk + lax.broadcasted_iota(jnp.int32, (1, chunk), 1)
        at_query = block * stretch_rows + lax.rem(inside, stretch_rows)
        begin = jnp.zeros_like(at_query)
        for end in ends:
            begin = jnp.where(at_query >= end, end, begin)
        at_key = first + lax.broadcasted_iota(jnp.int32, (window, chunk), 0)
        allowed = (at_key >= begin) & (at_key <= at_query)
        k = keys[pl.ds(first, window), :]
        v = values[pl.ds(first, window), :]
        q = qs[part, :]
        g = gs[part, :]
        last = (((1,), (1,)), ((), ()))
        scores = lax.dot_general(k, q, last, preferred_element_type=jnp.float32) * score_scale
        masked = jnp.where(allowed, scores, -jnp.inf)
        expsum = jnp.exp(masked - jnp.max(masked, axis=0, keepdims=True))
        probs = expsum * (1.0 / jnp.sum(expsum, axis=0, keepdims=True))
        probs_low = probs.astype(jnp.bfloat16)
        dprob = lax.dot_general(v, g, last, preferred_element_type=jnp.float32)
        delta = jnp.sum(probs_low.astype(jnp.float32) * dprob, axis=0, keepdims=True)
        dscore = (probs * (dprob - delta)).astype(jnp.bfloat16)
        dq = lax.dot_general(
            k, dscore, (((0,), (0,)), ((), ())), preferred_element_type=jnp.float32
        )
        dqs[part, :] = (jnp.transpose(dq) * score_scale).astype(jnp.bfloat16)
        dk = jnp.dot(dscore, q, preferred_element_type=jnp.float32) * score_scale
        dv = jnp.dot(probs_low, g, preferred_element_type=jnp.float32)
        total[pl.ds(first, window), :head_dim] += dk
        total[pl.ds(first, window), head_dim:] += dv
        return carry

    lax.fori_loop(0, 2 * chunks_half, step, 0)
    for half in range(2):
        for head in range(head_count):
            origin = slice((half * head_count + head) * stretch_rows, (half * head_count + head + 1) * stretch_rows)
            rows = slice(half * stretch_rows, (half + 1) * stretch_rows)
            columns = slice(head * head_dim, (head + 1) * head_dim)
            qgrad_ref[rows, columns] = dqs[origin, :]
    for index in range(ctx_count):
        for half in range(2):
            rows = pl.ds(place(me ^ index, half), stretch_rows)
            start = (index // 2) * row_count + half * stretch_rows
            if index % 2:
                send_ref[start : start + stretch_rows, :] = total[rows, :].astype(jnp.bfloat16)
            else:
                keep_ref[start : start + stretch_rows, :] = total[rows, :]


def attention(me, order, lengths, queries, cotangent, kv_blocks, head_dim):
    row_count, width = queries.shape
    ctx_count = len(kv_blocks)
    stretch_rows = row_count // 2
    head_count = width // head_dim
    seq_rows = row_count * ctx_count
    window = seq_rows // 2 + stretch_rows
    stacked = head_count * stretch_rows
    chunk = 256 if stacked % 256 == 0 else 128
    shape = (ctx_count, stretch_rows, head_count, head_dim, window, chunk)
    smem = pl.BlockSpec(memory_space=pltpu.SMEM)
    vmem = pl.BlockSpec(memory_space=pltpu.VMEM)
    half_rows = seq_rows // 2
    return pl.pallas_call(
        functools.partial(attention_kernel, shape),
        out_shape=(
            jax.ShapeDtypeStruct((row_count, width), jnp.bfloat16),
            jax.ShapeDtypeStruct((half_rows, 2 * head_dim), jnp.float32),
            jax.ShapeDtypeStruct((half_rows, 2 * head_dim), jnp.bfloat16),
        ),
        in_specs=[smem] * 3 + [vmem] * (2 + ctx_count),
        out_specs=(vmem,) * 3,
        scratch_shapes=[
            pltpu.VMEM((seq_rows, head_dim), jnp.bfloat16),
            pltpu.VMEM((seq_rows, head_dim), jnp.bfloat16),
            pltpu.VMEM((seq_rows, 2 * head_dim), jnp.float32),
            pltpu.VMEM((2 * stacked, head_dim), jnp.bfloat16),
            pltpu.VMEM((2 * stacked, head_dim), jnp.bfloat16),
            pltpu.VMEM((2 * stacked, head_dim), jnp.bfloat16),
        ],
        compiler_params=pltpu.CompilerParams(vmem_limit_bytes=VMEM_LIMIT),
        cost_estimate=pl.CostEstimate(
            flops=10 * window * 2 * stacked * head_dim,
            bytes_accessed=8 * row_count * width + 10 * seq_rows * head_dim,
            transcendentals=window * 2 * stacked,
        ),
        name="attention",
    )(me, order, lengths, queries, cotangent, *kv_blocks)


def weight_kernel(dp_count, z_count, z, *refs):
    hidden, grads, out_ref = refs[:dp_count], refs[dp_count : 2 * dp_count], refs[-1]
    columns = hidden[0].shape[1]
    share = columns // z_count
    tile = max(share, 128)
    for start in range(0, columns, tile):
        product = None
        for one, grad in zip(hidden, grads):
            term = lax.dot_general(
                one[:, start : start + tile],
                grad[...],
                (((0,), (0,)), ((), ())),
                preferred_element_type=jnp.float32,
            )
            product = term if product is None else product + term
        for inner in range(0, tile, share):
            to = pl.multiple_of((z[0] ^ ((start + inner) // share)) * share, share)
            out_ref[pl.ds(to, share), :] = product[inner : inner + share, :].astype(out_ref.dtype)


def weight_rows(z, hidden, grads, z_count, kind):
    columns, width = hidden[0].shape[1], grads[0].shape[1]
    rows = sum(one.shape[0] for one in hidden)
    smem = pl.BlockSpec(memory_space=pltpu.SMEM)
    vmem = pl.BlockSpec(memory_space=pltpu.VMEM)
    return pl.pallas_call(
        functools.partial(weight_kernel, len(hidden), z_count),
        out_shape=jax.ShapeDtypeStruct((columns, width), kind),
        in_specs=[smem] + [vmem] * (2 * len(hidden)),
        out_specs=vmem,
        compiler_params=pltpu.CompilerParams(vmem_limit_bytes=VMEM_LIMIT),
        cost_estimate=pl.CostEstimate(
            flops=2 * rows * columns * width,
            bytes_accessed=2 * rows * (columns + width) + 4 * columns * width,
            transcendentals=0,
        ),
        name="weight_rows",
    )(z, *hidden, *grads)


def assemble_kernel(z_count, ids, *refs):
    blocks, key_ref, value_ref = refs[:-2], refs[-2], refs[-1]
    share, width = blocks[0].shape
    for side in range(2):
        for m in range(z_count):
            to = ((ids[1] ^ side) * z_count + (ids[0] ^ m)) * share
            to = pl.multiple_of(to, share)
            block = blocks[side * z_count + m][...].astype(jnp.float32)
            key_ref[pl.ds(to, share), :] = block[:, : width // 2]
            value_ref[pl.ds(to, share), :] = block[:, width // 2 :]


def assemble(ids, blocks, z_count):
    share, width = blocks[0].shape
    shape = jax.ShapeDtypeStruct((2 * z_count * share, width // 2), jnp.float32)
    smem = pl.BlockSpec(memory_space=pltpu.SMEM)
    vmem = pl.BlockSpec(memory_space=pltpu.VMEM)
    return pl.pallas_call(
        functools.partial(assemble_kernel, z_count),
        out_shape=(shape, shape),
        in_specs=[smem] + [vmem] * len(blocks),
        out_specs=(vmem, vmem),
        compiler_params=pltpu.CompilerParams(vmem_limit_bytes=VMEM_LIMIT),
        name="assemble",
    )(ids, *blocks)


def dot32(left, right):
    return jnp.dot(left, right, preferred_element_type=jnp.float32)


def on_device(hidden_in, queries, grad_out, w_key, w_value, stretch_order, doc_lengths):
    inputs = hidden_in[0]
    row_count = inputs.shape[0]
    head_dim = w_key.shape[1]
    dp_count = lax.axis_size("dp")
    ctx_count = lax.axis_size("ctx")
    z_count = ctx_count // 2
    dp, ctx = lax.axis_index("dp"), lax.axis_index("ctx")
    z, core = ctx // 2, ctx % 2
    block_rows = w_key.shape[0]
    half_rows = block_rows // 2

    bits = [1 << at for at in range(dp_count.bit_length() - 1)]

    def gather(weight, order):
        mine = {0: lax.dynamic_slice_in_dim(weight, core * half_rows, half_rows, 0)}
        for bit in order:
            mine.update({j | bit: swap(piece, "dp", bit) for j, piece in list(mine.items())})
        other = {0: lax.dynamic_slice_in_dim(weight, (1 - core) * half_rows, half_rows, 0)}
        other.update({j: swap(mine[j], "ctx", 1) for j in mine if j})
        return mine, other

    key_pieces = gather(w_key, bits)
    value_pieces = gather(w_value, bits[::-1])

    def columns(j, side):
        start = (dp ^ j) * block_rows + (core ^ side) * half_rows
        return lax.dynamic_slice_in_dim(inputs, start, half_rows, 1)

    hidden = {(j, side): columns(j, side) for j in range(dp_count) for side in range(2)}

    landed = [pieces[0][j] for pieces in (key_pieces, value_pieces) for j in range(1, dp_count)]
    names = [name for name in hidden if name[0]]
    sent, landed = after([hidden[name] for name in names], *landed)
    landed = iter(landed)
    for pieces in (key_pieces, value_pieces):
        for j in range(1, dp_count):
            pieces[0][j] = next(landed)
    swapped = {name: swap(one, "dp", name[0]) for name, one in zip(names, sent)}
    for side in range(2):
        swapped[0, side] = hidden[0, side]

    keys = sum(dot32(hidden[j, side], key_pieces[side][j]) for j in range(dp_count) for side in range(2))
    values = sum(dot32(hidden[j, side], value_pieces[side][j]) for j in range(dp_count) for side in range(2))
    own = jnp.concatenate([keys.astype(jnp.bfloat16), values.astype(jnp.bfloat16)], axis=1)

    along = [own] + [swap(own, "ctx", 2 * m) for m in range(1, z_count)]
    kv_blocks = []
    for one in along:
        kv_blocks += [one, swap(one, "ctx", 1)]

    me = jnp.reshape(ctx, (1,)).astype(jnp.int32)
    query_grad, keep, send = attention(
        me, stretch_order, doc_lengths[0], queries[0], grad_out[0], kv_blocks, head_dim
    )

    chip = keep + swap(send, "ctx", 1).astype(jnp.float32)
    chip = chip.reshape(z_count, row_count, 2 * head_dim)
    kv_grad = chip[0]
    for m in range(1, z_count):
        kv_grad = kv_grad + swap(chip[m].astype(jnp.bfloat16), "ctx", 2 * m).astype(jnp.float32)
    kv_grad = kv_grad.astype(jnp.bfloat16)
    grads = [kv_grad] + [swap(kv_grad, "dp", j) for j in range(1, dp_count)]

    z_id = jnp.reshape(z, (1,)).astype(jnp.int32)
    theirs = weight_rows(
        z_id, [swapped[j, 1] for j in range(dp_count)], grads, z_count, jnp.bfloat16
    )
    from_core = swap(theirs, "ctx", 1)
    ours = weight_rows(
        z_id, [swapped[j, 0] for j in range(dp_count)], grads, z_count, jnp.float32
    )
    share = half_rows // z_count
    partial = (ours + from_core.astype(jnp.float32)).reshape(z_count, share, 2 * head_dim)
    final = partial[0]
    for m in range(1, z_count):
        final = final + swap(partial[m].astype(jnp.bfloat16), "ctx", 2 * m).astype(jnp.float32)
    final = final.astype(jnp.bfloat16)
    rows = [final] + [swap(final, "ctx", 2 * m) for m in range(1, z_count)]
    blocks = rows + [swap(one, "ctx", 1) for one in rows]
    ids = jnp.stack([z, core]).astype(jnp.int32)
    key_rows, value_rows = assemble(ids, blocks, z_count)
    return query_grad[None], key_rows, value_rows


def solution(mesh):
    return jax.shard_map(
        on_device,
        mesh=mesh,
        in_specs=(
            P("dp", "ctx", None),
            P("dp", "ctx", None),
            P("dp", "ctx", None),
            P("dp", None),
            P("dp", None),
            P(),
            P("dp", None),
        ),
        out_specs=(P("dp", "ctx", None), P("dp", None), P("dp", None)),
        check_vma=False,
    )
```

```python
import functools
import math

import jax
import jax.numpy as jnp
from jax import lax
from jax.experimental import pallas as pl
from jax.experimental.pallas import tpu as pltpu
from jax.sharding import PartitionSpec as P

VMEM_LIMIT = 48 * 1024 * 1024
NO_COST = pl.CostEstimate(flops=0, bytes_accessed=0, transcendentals=0)


def moved_rows(block_rows):
    return block_rows * 4 // 8 // 256 * 256


def swap(array, axis, distance):
    count = lax.axis_size(axis)
    return lax.ppermute(array, axis, [(i, i ^ distance) for i in range(count)])


def after(arrays, *earlier):
    tied = lax.optimization_barrier((tuple(arrays), tuple(earlier)))
    return list(tied[0]), list(tied[1])


def attention_kernel(
    shape, ids, order, lengths, q_ref, g_ref, *refs
):
    ctx_count, stretch_rows, head_count, head_dim, window, chunk = shape
    kv_refs = refs[:ctx_count]
    qgrad_ref, keep_ref, send_ref, keys, values, total, qs, gs, dqs = refs[ctx_count:]
    me = ids[0]
    row_count = 2 * stretch_rows
    stretch_count = 2 * ctx_count
    score_scale = 1.0 / math.sqrt(head_dim)

    def place(device, half):
        return pl.multiple_of(order[2 * device + half] * stretch_rows, stretch_rows)

    for index in range(ctx_count):
        for half in range(2):
            rows = pl.ds(place(me ^ index, half), stretch_rows)
            block = kv_refs[index][half * stretch_rows : (half + 1) * stretch_rows, :]
            keys[rows, :] = block[:, :head_dim]
            values[rows, :] = block[:, head_dim:]
    total[...] = jnp.zeros_like(total)
    for half in range(2):
        for head in range(head_count):
            to = slice((half * head_count + head) * stretch_rows, (half * head_count + head + 1) * stretch_rows)
            rows = slice(half * stretch_rows, (half + 1) * stretch_rows)
            columns = slice(head * head_dim, (head + 1) * head_dim)
            qs[to, :] = q_ref[rows, columns]
            gs[to, :] = g_ref[rows, columns]
    ends = []
    running = 0
    for at in range(lengths.shape[0]):
        running = running + lengths[at]
        ends.append(running)
    chunks_half = head_count * stretch_rows // chunk

    def step(at, carry):
        half = at // chunks_half
        block = order[2 * me + half]
        first = jnp.maximum(block - stretch_count // 2, 0) * stretch_rows
        first = pl.multiple_of(first, stretch_rows)
        part = pl.ds(pl.multiple_of(at * chunk, chunk), chunk)
        inside = (at - half * chunks_half) * chunk + lax.broadcasted_iota(jnp.int32, (1, chunk), 1)
        at_query = block * stretch_rows + lax.rem(inside, stretch_rows)
        begin = jnp.zeros_like(at_query)
        for end in ends:
            begin = jnp.where(at_query >= end, end, begin)
        at_key = first + lax.broadcasted_iota(jnp.int32, (window, chunk), 0)
        allowed = (at_key >= begin) & (at_key <= at_query)
        k = keys[pl.ds(first, window), :]
        v = values[pl.ds(first, window), :]
        q = qs[part, :]
        g = gs[part, :]
        last = (((1,), (1,)), ((), ()))
        scores = lax.dot_general(k, q, last, preferred_element_type=jnp.float32) * score_scale
        masked = jnp.where(allowed, scores, -jnp.inf)
        expsum = jnp.exp(masked - jnp.max(masked, axis=0, keepdims=True))
        probs = expsum * (1.0 / jnp.sum(expsum, axis=0, keepdims=True))
        probs_low = probs.astype(jnp.bfloat16)
        dprob = lax.dot_general(v, g, last, preferred_element_type=jnp.float32)
        delta = jnp.sum(probs_low.astype(jnp.float32) * dprob, axis=0, keepdims=True)
        dscore = (probs * (dprob - delta)).astype(jnp.bfloat16)
        dq = lax.dot_general(
            k, dscore, (((0,), (0,)), ((), ())), preferred_element_type=jnp.float32
        )
        dqs[part, :] = (jnp.transpose(dq) * score_scale).astype(jnp.bfloat16)
        dk = jnp.dot(dscore, q, preferred_element_type=jnp.float32) * score_scale
        dv = jnp.dot(probs_low, g, preferred_element_type=jnp.float32)
        total[pl.ds(first, window), :head_dim] += dk
        total[pl.ds(first, window), head_dim:] += dv
        return carry

    lax.fori_loop(0, 2 * chunks_half, step, 0)
    for half in range(2):
        for head in range(head_count):
            origin = slice((half * head_count + head) * stretch_rows, (half * head_count + head + 1) * stretch_rows)
            rows = slice(half * stretch_rows, (half + 1) * stretch_rows)
            columns = slice(head * head_dim, (head + 1) * head_dim)
            qgrad_ref[rows, columns] = dqs[origin, :]
    for index in range(ctx_count):
        for half in range(2):
            rows = pl.ds(place(me ^ index, half), stretch_rows)
            start = (index // 2) * row_count + half * stretch_rows
            if index % 2:
                send_ref[start : start + stretch_rows, :] = total[rows, :].astype(jnp.bfloat16)
            else:
                keep_ref[start : start + stretch_rows, :] = total[rows, :]


def attention(me, order, lengths, queries, cotangent, kv_blocks, head_dim):
    row_count, width = queries.shape
    ctx_count = len(kv_blocks)
    stretch_rows = row_count // 2
    head_count = width // head_dim
    seq_rows = row_count * ctx_count
    window = seq_rows // 2 + stretch_rows
    stacked = head_count * stretch_rows
    chunk = 256 if stacked % 256 == 0 else 128
    shape = (ctx_count, stretch_rows, head_count, head_dim, window, chunk)
    smem = pl.BlockSpec(memory_space=pltpu.SMEM)
    vmem = pl.BlockSpec(memory_space=pltpu.VMEM)
    half_rows = seq_rows // 2
    return pl.pallas_call(
        functools.partial(attention_kernel, shape),
        out_shape=(
            jax.ShapeDtypeStruct((row_count, width), jnp.bfloat16),
            jax.ShapeDtypeStruct((half_rows, 2 * head_dim), jnp.float32),
            jax.ShapeDtypeStruct((half_rows, 2 * head_dim), jnp.bfloat16),
        ),
        in_specs=[smem] * 3 + [vmem] * (2 + ctx_count),
        out_specs=(vmem,) * 3,
        scratch_shapes=[
            pltpu.VMEM((seq_rows, head_dim), jnp.bfloat16),
            pltpu.VMEM((seq_rows, head_dim), jnp.bfloat16),
            pltpu.VMEM((seq_rows, 2 * head_dim), jnp.float32),
            pltpu.VMEM((2 * stacked, head_dim), jnp.bfloat16),
            pltpu.VMEM((2 * stacked, head_dim), jnp.bfloat16),
            pltpu.VMEM((2 * stacked, head_dim), jnp.bfloat16),
        ],
        compiler_params=pltpu.CompilerParams(vmem_limit_bytes=VMEM_LIMIT),
        cost_estimate=NO_COST,
        name="attention",
    )(me, order, lengths, queries, cotangent, *kv_blocks)


def project_kernel(plan, side_rows, core, *refs):
    start_ref, out_ref = refs[0], refs[-1]
    hidden = refs[1 : 1 + plan.hidden]
    weights = refs[1 + plan.hidden : -1]
    width = weights[0].shape[1]
    total = [start_ref[:, :width], start_ref[:, width:]] if plan.start else [None, None]
    for (which, block, side), weight in zip(plan.terms, weights):
        from_column = pl.multiple_of((core[0] ^ side) * side_rows, side_rows)
        left = hidden[block][:, pl.ds(from_column, side_rows)]
        term = jnp.dot(left, weight[...], preferred_element_type=jnp.float32)
        total[which] = term if total[which] is None else total[which] + term
    out_ref[:, :width] = total[0].astype(out_ref.dtype)
    out_ref[:, width:] = total[1].astype(out_ref.dtype)


class Plan:
    def __init__(self, **fields):
        self.__dict__.update(fields)


def project(core, start, hidden, terms, kind):
    row_count = hidden[0].shape[0]
    side_rows, width = terms[0][3].shape
    plan = Plan(hidden=len(hidden), terms=[term[:3] for term in terms], start=start is not None)
    if start is None:
        start = core
    smem = pl.BlockSpec(memory_space=pltpu.SMEM)
    vmem = pl.BlockSpec(memory_space=pltpu.VMEM)
    return pl.pallas_call(
        functools.partial(project_kernel, plan, side_rows),
        out_shape=jax.ShapeDtypeStruct((row_count, 2 * width), kind),
        in_specs=[smem, vmem if plan.start else smem] + [vmem] * (len(hidden) + len(terms)),
        out_specs=vmem,
        compiler_params=pltpu.CompilerParams(vmem_limit_bytes=VMEM_LIMIT),
        cost_estimate=NO_COST,
        name="project",
    )(core, start, *hidden, *[term[3] for term in terms])


def weight_kernel(plan, ids, *refs):
    hidden = refs[: plan.hidden]
    grads = refs[plan.hidden : plan.hidden + plan.grads]
    theirs_ref, key_ref, value_ref = refs[plan.hidden + plan.grads :]
    z, core = ids[0] % plan.sub_count, ids[1]
    rows, width = plan.rows, grads[0].shape[1] // 2
    share = rows // plan.sub_count
    tile = next(size for size in (512, 256, 128) if rows % size == 0)
    step = math.gcd(share, tile)
    for side in (1, 0):
        origin = plan.origin + (core ^ side) * rows
        for at, group in enumerate(plan.groups):
            for start in range(0, rows, tile):
                product = None
                for block, grad in group:
                    columns = pl.ds(pl.multiple_of(origin + start, 128), tile)
                    term = lax.dot_general(
                        hidden[block][:, columns],
                        grads[grad][...],
                        (((0,), (0,)), ((), ())),
                        preferred_element_type=jnp.float32,
                    )
                    product = term if product is None else product + term
                for inner in range(0, tile, step):
                    part, offset = divmod(start + inner, share)
                    to = pl.multiple_of(at * rows + (z ^ part) * share + offset, step)
                    piece = product[inner : inner + step, :]
                    if side:
                        theirs_ref[pl.ds(to, step), :] = piece.astype(theirs_ref.dtype)
                    else:
                        key_ref[pl.ds(to, step), :] = piece[:, :width]
                        value_ref[pl.ds(to, step), :] = piece[:, width:]


def weight_rows(ids, hidden, grads, groups, origin, rows, sub_count):
    width = grads[0].shape[1]
    total_rows = rows * len(groups)
    smem = pl.BlockSpec(memory_space=pltpu.SMEM)
    vmem = pl.BlockSpec(memory_space=pltpu.VMEM)
    plan = Plan(
        hidden=len(hidden),
        grads=len(grads),
        groups=groups,
        origin=origin,
        rows=rows,
        sub_count=sub_count,
    )
    half = jax.ShapeDtypeStruct((total_rows, width // 2), jnp.float32)
    return pl.pallas_call(
        functools.partial(weight_kernel, plan),
        out_shape=(jax.ShapeDtypeStruct((total_rows, width), jnp.bfloat16), half, half),
        in_specs=[smem] + [vmem] * (len(hidden) + len(grads)),
        out_specs=(vmem, vmem, vmem),
        compiler_params=pltpu.CompilerParams(vmem_limit_bytes=VMEM_LIMIT),
        cost_estimate=NO_COST,
        name="weight_rows",
    )(ids, *hidden, *grads)


def assemble_kernel(sub_count, regions, ids, *refs):
    blocks, key_ref, value_ref = refs[:-2], refs[-2], refs[-1]
    z, core = ids[0] % sub_count, ids[1]
    blocks = iter(blocks)
    for origin, rows in regions:
        share = rows // sub_count
        for side in range(2):
            for m in range(sub_count):
                to = origin + (core ^ side) * rows + (z ^ m) * share
                to = pl.multiple_of(to, share)
                block_ref = next(blocks)
                width = block_ref.shape[1] // 2
                key_ref[pl.ds(to, share), :] = block_ref[:, :width].astype(jnp.float32)
                value_ref[pl.ds(to, share), :] = block_ref[:, width:].astype(jnp.float32)


def assemble(ids, blocks, sub_count, regions):
    rows = sum(block.shape[0] for block in blocks)
    shape = jax.ShapeDtypeStruct((rows, blocks[0].shape[1] // 2), jnp.float32)
    smem = pl.BlockSpec(memory_space=pltpu.SMEM)
    vmem = pl.BlockSpec(memory_space=pltpu.VMEM)
    return pl.pallas_call(
        functools.partial(assemble_kernel, sub_count, regions),
        out_shape=(shape, shape),
        in_specs=[smem] + [vmem] * len(blocks),
        out_specs=(vmem, vmem),
        compiler_params=pltpu.CompilerParams(vmem_limit_bytes=VMEM_LIMIT),
        cost_estimate=NO_COST,
        name="assemble",
    )(ids, *blocks)


def add_cores(theirs, keys, values):
    width = keys.shape[1]
    came = swap(theirs, "ctx", 1).astype(jnp.float32)
    return keys + came[:, :width], values + came[:, width:]


def sum_over_dp(array, order):
    count = lax.axis_size("dp")
    rows = array.shape[0] // count
    parts = {j: array[j * rows : (j + 1) * rows] for j in range(count)}
    for bit in order:
        leaving = [j for j in parts if j & bit]
        stacked = jnp.concatenate([parts.pop(j).astype(jnp.bfloat16) for j in leaving], axis=0)
        came = swap(stacked, "dp", bit).astype(jnp.float32)
        for at, j in enumerate(leaving):
            parts[j ^ bit] = parts[j ^ bit] + came[at * rows : (at + 1) * rows]
    return parts[0]


def sum_along_z(full, sub_count):
    share = full.shape[0] // sub_count
    parts = {m: full[m * share : (m + 1) * share] for m in range(sub_count)}
    bits = [1 << at for at in range(sub_count.bit_length() - 1)]
    for bit in bits:
        for m in list(parts):
            if m & bit:
                came = swap(parts.pop(m).astype(jnp.bfloat16), "ctx", 2 * bit)
                parts[m ^ bit] = parts[m ^ bit] + came.astype(jnp.float32)
    low = parts[0].astype(jnp.bfloat16)
    final = (parts[0] + swap(low, "ctx", 2 * sub_count).astype(jnp.float32)).astype(jnp.bfloat16)
    rows = {0: final}
    for bit in bits[::-1]:
        rows.update({m | bit: swap(one, "ctx", 2 * bit) for m, one in list(rows.items())})
    own = [rows[m] for m in range(sub_count)]
    return own + [swap(one, "ctx", 1) for one in own]


def on_device(hidden_in, queries, grad_out, w_key, w_value, stretch_order, doc_lengths):
    inputs = hidden_in[0]
    row_count = inputs.shape[0]
    head_dim = w_key.shape[1]
    dp_count = lax.axis_size("dp")
    ctx_count = lax.axis_size("ctx")
    z_count = ctx_count // 2
    dp, ctx = lax.axis_index("dp"), lax.axis_index("ctx")
    z, core = ctx // 2, ctx % 2
    block_rows = w_key.shape[0]
    half_rows = block_rows // 2

    bits = [1 << at for at in range(dp_count.bit_length() - 1)]

    def gather(weight, order):
        mine = {0: lax.dynamic_slice_in_dim(weight, core * half_rows, half_rows, 0)}
        for bit in order:
            mine.update({j | bit: swap(piece, "dp", bit) for j, piece in list(mine.items())})
        other = {0: lax.dynamic_slice_in_dim(weight, (1 - core) * half_rows, half_rows, 0)}
        other.update({j: swap(mine[j], "ctx", 1) for j in mine if j})
        return mine, other

    key_pieces = gather(w_key, bits)
    value_pieces = gather(w_value, bits[::-1])

    hidden = [
        lax.dynamic_slice_in_dim(inputs, (dp ^ j) * block_rows, block_rows, 1)
        for j in range(dp_count)
    ]

    landed = [pieces[0][j] for pieces in (key_pieces, value_pieces) for j in range(1, dp_count)]
    first_rows = moved_rows(block_rows)
    sent, landed = after([one[:, :first_rows] for one in hidden[1:]], *landed)
    landed = iter(landed)
    for pieces in (key_pieces, value_pieces):
        for j in range(1, dp_count):
            pieces[0][j] = next(landed)
    near = [j for j in range(1, dp_count) if j in bits]
    far = [j for j in range(1, dp_count) if j not in bits]
    swapped = {0: hidden[0][:, :first_rows]}
    swapped.update({j: swap(sent[j - 1], "dp", j) for j in near})

    core_id = jnp.reshape(core, (1,)).astype(jnp.int32)
    early, late = [], []
    for which, (pieces, first) in enumerate(((key_pieces, bits[0]), (value_pieces, bits[-1]))):
        for j in range(dp_count):
            for side in range(2):
                (early if j in (0, first) else late).append((which, j, side, pieces[side][j]))
    partial = project(core_id, None, hidden, early, jnp.float32)
    own = project(core_id, partial, hidden, late, jnp.bfloat16)

    along = [own] + [swap(own, "ctx", 2 * m) for m in range(1, z_count)]
    kv_blocks = []
    for one in along:
        kv_blocks += [one, swap(one, "ctx", 1)]

    ready = kv_blocks + [sent[j - 1] for j in far]
    ready, ended = after(ready, *[swapped[j] for j in near])
    kv_blocks = ready[:ctx_count]
    swapped.update(zip(near, ended))
    swapped.update({j: swap(one, "dp", j) for j, one in zip(far, ready[ctx_count:])})

    me = jnp.reshape(ctx, (1,)).astype(jnp.int32)
    query_grad, keep, send = attention(
        me, stretch_order, doc_lengths[0], queries[0], grad_out[0], kv_blocks, head_dim
    )

    chip = keep + swap(send, "ctx", 1).astype(jnp.float32)
    chip = chip.reshape(z_count, row_count, 2 * head_dim)
    kv_grad = chip[0]
    for m in range(1, z_count):
        kv_grad = kv_grad + swap(chip[m].astype(jnp.bfloat16), "ctx", 2 * m).astype(jnp.float32)
    kv_grad = kv_grad.astype(jnp.bfloat16)
    (kv_grad,), ended = after([kv_grad], *[swapped[j] for j in far])
    swapped.update(zip(far, ended))
    grads = [kv_grad] + [swap(kv_grad, "dp", j) for j in range(1, dp_count)]

    ids = jnp.stack([z, core]).astype(jnp.int32)
    sub_count = z_count // 2
    first_half, last_half = first_rows // 2, (block_rows - first_rows) // 2
    regions = ((0, first_half), (first_rows, last_half))

    groups = [[(j, 0)] for j in range(dp_count)]
    parts = weight_rows(ids, hidden, [kv_grad], groups, first_rows, last_half, sub_count)
    key_part, value_part = add_cores(*parts)
    last = [sum_over_dp(key_part, bits), sum_over_dp(value_part, bits[::-1])]

    moved = [swapped[j] for j in range(dp_count)]

    groups = [[(j, j) for j in range(dp_count)]]
    first = add_cores(*weight_rows(ids, moved, grads, groups, 0, first_half, sub_count))
    blocks = sum_along_z(jnp.concatenate(first, axis=1), sub_count)
    blocks += sum_along_z(jnp.concatenate(last, axis=1), sub_count)
    key_rows, value_rows = assemble(ids, blocks, sub_count, regions)
    return query_grad[None], key_rows, value_rows


def solution(mesh):
    return jax.shard_map(
        on_device,
        mesh=mesh,
        in_specs=(
            P("dp", "ctx", None),
            P("dp", "ctx", None),
            P("dp", "ctx", None),
            P("dp", None),
            P("dp", None),
            P(),
            P("dp", None),
        ),
        out_specs=(P("dp", "ctx", None), P("dp", None), P("dp", None)),
        check_vma=False,
    )
```

```python
import functools
import math

import jax
import jax.numpy as jnp
from jax import lax
from jax.experimental import pallas as pl
from jax.experimental.pallas import tpu as pltpu
from jax.sharding import PartitionSpec as P

VMEM_LIMIT = 28 * 1024 * 1024
NO_COST = pl.CostEstimate(flops=0, bytes_accessed=0, transcendentals=0)


def moved_rows(block_rows):
    return block_rows * 4 // 8 // 256 * 256


class Plan:
    def __init__(self, **fields):
        self.__dict__.update(fields)


def swap(array, axis, distance):
    count = lax.axis_size(axis)
    return lax.ppermute(array, axis, [(i, i ^ distance) for i in range(count)])


def after(arrays, *earlier):
    tied = lax.optimization_barrier((tuple(arrays), tuple(earlier)))
    return list(tied[0]), list(tied[1])


def kernel_call(kernel, name, outs, scalars, arrays, scratch=(), cost=NO_COST):
    smem = pl.BlockSpec(memory_space=pltpu.SMEM)
    vmem = pl.BlockSpec(memory_space=pltpu.VMEM)
    single = not isinstance(outs, tuple)
    return pl.pallas_call(
        kernel,
        out_shape=outs,
        in_specs=[smem] * len(scalars) + [vmem] * len(arrays),
        out_specs=vmem if single else (vmem,) * len(outs),
        scratch_shapes=list(scratch),
        compiler_params=pltpu.CompilerParams(vmem_limit_bytes=VMEM_LIMIT),
        cost_estimate=cost,
        name=name,
    )(*scalars, *arrays)


def bytes_cost(amount):
    return pl.CostEstimate(flops=0, bytes_accessed=amount, transcendentals=0)


def first_key(order, me, half, plan):
    block = order[2 * me + half]
    first = jnp.maximum(block - plan.stretch_count // 2, 0) * plan.stretch_rows
    return block, pl.multiple_of(first, plan.stretch_rows)


def sort_rows(plan, me, order, block_refs, sorted_ref):
    rows = plan.stretch_rows
    for index, block in enumerate(block_refs):
        for half in range(2):
            to = pl.multiple_of(order[2 * (me ^ index) + half] * rows, rows)
            sorted_ref[pl.ds(to, rows), :] = block[half * rows : (half + 1) * rows, :]


def unsort_rows(plan, me, order, total, keep_ref, send_ref):
    rows = plan.stretch_rows
    for index in range(plan.ctx_count):
        for half in range(2):
            origin = pl.multiple_of(order[2 * (me ^ index) + half] * rows, rows)
            start = (index // 2) * 2 * rows + half * rows
            to_ref = send_ref if index % 2 else keep_ref
            to_ref[start : start + rows, :] = total[pl.ds(origin, rows), :].astype(to_ref.dtype)


def stack_heads(plan, array_ref, stacked_ref):
    rows, width = plan.stretch_rows, plan.head_dim
    for half in range(2):
        for head in range(plan.head_count):
            start = (half * plan.head_count + head) * rows
            stacked_ref[start : start + rows, :] = array_ref[
                half * rows : (half + 1) * rows, head * width : (head + 1) * width
            ]


def unstack_heads(plan, stacked_ref, array_ref):
    rows, width = plan.stretch_rows, plan.head_dim
    for half in range(2):
        for head in range(plan.head_count):
            start = (half * plan.head_count + head) * rows
            array_ref[half * rows : (half + 1) * rows, head * width : (head + 1) * width] = (
                stacked_ref[start : start + rows, :]
            )


NT = (((1,), (1,)), ((), ()))
TN = (((0,), (0,)), ((), ()))


def probs_kernel(plan, ids, order, lengths, q_ref, g_ref, *refs):
    key_refs = refs[: plan.ctx_count]
    probs_ref, keys, qs, gs, keep_ref, send_ref, total = refs[plan.ctx_count :]
    me = ids[0]
    sort_rows(plan, me, order, key_refs, keys)
    stack_heads(plan, q_ref, qs)
    stack_heads(plan, g_ref, gs)
    total[...] = jnp.zeros_like(total)
    ends = []
    running = 0
    for at in range(lengths.shape[0]):
        running = running + lengths[at]
        ends.append(running)

    def step(at, carry):
        half = at // plan.steps
        block, first = first_key(order, me, half, plan)
        part = pl.ds(pl.multiple_of(at * plan.chunk, plan.chunk), plan.chunk)
        inside = (at - half * plan.steps) * plan.chunk
        inside = inside + lax.broadcasted_iota(jnp.int32, (1, plan.chunk), 1)
        at_query = block * plan.stretch_rows + lax.rem(inside, plan.stretch_rows)
        begin = jnp.zeros_like(at_query)
        for end in ends:
            begin = jnp.where(at_query >= end, end, begin)
        at_key = first + lax.broadcasted_iota(jnp.int32, (plan.window, plan.chunk), 0)
        allowed = (at_key >= begin) & (at_key <= at_query)
        k = keys[pl.ds(first, plan.window), :]
        scores = lax.dot_general(k, qs[part, :], NT, preferred_element_type=jnp.float32)
        masked = jnp.where(allowed, scores * plan.score_scale, -jnp.inf)
        expsum = jnp.exp(masked - jnp.max(masked, axis=0, keepdims=True))
        probs = expsum * (1.0 / jnp.sum(expsum, axis=0, keepdims=True))
        probs_low = probs.astype(jnp.bfloat16)
        probs_ref[at] = probs_low
        dv = jnp.dot(probs_low, gs[part, :], preferred_element_type=jnp.float32)
        total[pl.ds(first, plan.window), :] += dv
        return carry

    lax.fori_loop(0, 2 * plan.steps, step, 0)
    unsort_rows(plan, me, order, total, keep_ref, send_ref)


def scores_kernel(plan, ids, order, probs_ref, keys, qs, gs, *refs):
    value_refs = refs[: plan.ctx_count]
    qgrad_ref, keep_ref, send_ref, values, total, dqs = refs[plan.ctx_count :]
    me = ids[0]
    sort_rows(plan, me, order, value_refs, values)
    total[...] = jnp.zeros_like(total)

    def step(at, carry):
        half = at // plan.steps
        block, first = first_key(order, me, half, plan)
        part = pl.ds(pl.multiple_of(at * plan.chunk, plan.chunk), plan.chunk)
        k = keys[pl.ds(first, plan.window), :]
        v = values[pl.ds(first, plan.window), :]
        probs = probs_ref[at].astype(jnp.float32)
        dprob = lax.dot_general(v, gs[part, :], NT, preferred_element_type=jnp.float32)
        delta = jnp.sum(probs * dprob, axis=0, keepdims=True)
        dscore = (probs * (dprob - delta)).astype(jnp.bfloat16)
        dq = lax.dot_general(k, dscore, TN, preferred_element_type=jnp.float32)
        dqs[part, :] = (jnp.transpose(dq) * plan.score_scale).astype(jnp.bfloat16)
        dk = jnp.dot(dscore, qs[part, :], preferred_element_type=jnp.float32) * plan.score_scale
        total[pl.ds(first, plan.window), :] += dk
        return carry

    lax.fori_loop(0, 2 * plan.steps, step, 0)
    unsort_rows(plan, me, order, total, keep_ref, send_ref)
    unstack_heads(plan, dqs, qgrad_ref)


def attention_plan(queries, head_dim, ctx_count):
    row_count, width = queries.shape
    stretch_rows = row_count // 2
    head_count = width // head_dim
    stacked = head_count * stretch_rows
    chunk = 256 if stacked % 256 == 0 else 128
    return Plan(
        ctx_count=ctx_count,
        stretch_rows=stretch_rows,
        stretch_count=2 * ctx_count,
        head_count=head_count,
        head_dim=head_dim,
        chunk=chunk,
        steps=stacked // chunk,
        stacked=2 * stacked,
        seq_rows=row_count * ctx_count,
        window=row_count * ctx_count // 2 + stretch_rows,
        score_scale=1.0 / math.sqrt(head_dim),
    )


def shape_of(rows, width, kind=jnp.bfloat16):
    return jax.ShapeDtypeStruct((rows, width), kind)


def probs_and_value_grad(plan, me, order, lengths, queries, cotangent, key_blocks):
    width = plan.head_dim
    outs = (
        jax.ShapeDtypeStruct((2 * plan.steps, plan.window, plan.chunk), jnp.bfloat16),
        shape_of(plan.seq_rows, width),
        shape_of(plan.stacked, width),
        shape_of(plan.stacked, width),
        shape_of(plan.seq_rows // 2, width, jnp.float32),
        shape_of(plan.seq_rows // 2, width),
    )
    return kernel_call(
        functools.partial(probs_kernel, plan),
        "probs",
        outs,
        (me, order, lengths),
        (queries, cotangent, *key_blocks),
        [pltpu.VMEM((plan.seq_rows, width), jnp.float32)],
        cost=bytes_cost(18 * plan.window * plan.stacked),
    )


def query_and_key_grad(plan, me, order, saved, value_blocks):
    width = plan.head_dim
    outs = (
        shape_of(2 * plan.stretch_rows, plan.head_count * width),
        shape_of(plan.seq_rows // 2, width, jnp.float32),
        shape_of(plan.seq_rows // 2, width),
    )
    return kernel_call(
        functools.partial(scores_kernel, plan),
        "scores",
        outs,
        (me, order),
        (*saved, *value_blocks),
        [
            pltpu.VMEM((plan.seq_rows, width), jnp.bfloat16),
            pltpu.VMEM((plan.seq_rows, width), jnp.float32),
            pltpu.VMEM((plan.stacked, width), jnp.bfloat16),
        ],
        cost=bytes_cost(14 * plan.window * plan.stacked),
    )


def project_kernel(plan, ids, hidden, *refs):
    out_ref = refs[-1]
    dp, core = ids[2], ids[1]
    total = refs[0][...] if plan.start else None
    for (block, side, offset), weight in zip(plan.terms, refs[plan.start : -1]):
        from_column = (dp ^ block) * plan.block_rows + (core ^ side) * plan.side_rows + offset
        columns = pl.ds(pl.multiple_of(from_column, 128), weight.shape[0])
        term = jnp.dot(hidden[:, columns], weight[...], preferred_element_type=jnp.float32)
        total = term if total is None else total + term
    out_ref[...] = total.astype(out_ref.dtype)


def project(ids, start, inputs, block_rows, pieces, kind):
    names = sorted(pieces)
    weights = [pieces[name] for name in names]
    started = [] if start is None else [start]
    plan = Plan(terms=names, start=len(started), block_rows=block_rows, side_rows=block_rows // 2)
    rows = inputs.shape[0]
    amount = sum(2 * weight.size + 2 * rows * weight.shape[0] for weight in weights)
    return kernel_call(
        functools.partial(project_kernel, plan),
        "project",
        shape_of(rows, weights[0].shape[1], kind),
        (ids,),
        (inputs, *started, *weights),
        cost=bytes_cost(amount),
    )


def weight_kernel(plan, ids, *refs):
    hidden = refs[: plan.hidden]
    grads = refs[plan.hidden : -2]
    z, core, dp = ids[0] % plan.sub_count, ids[1], ids[2]
    rows = plan.rows
    share = rows // plan.sub_count
    tile = next(size for size in (512, 256, 128) if rows % size == 0)
    step = math.gcd(share, tile)
    for side, out_ref in ((1, refs[-2]), (0, refs[-1])):
        for at, group in enumerate(plan.groups):
            for start in range(0, rows, tile):
                product = None
                for array, block, grad in group:
                    origin = plan.origin + (core ^ side) * rows + start
                    if block is not None:
                        origin = origin + (dp ^ block) * plan.block_rows
                    columns = pl.ds(pl.multiple_of(origin, 128), tile)
                    term = lax.dot_general(
                        hidden[array][:, columns],
                        grads[grad][...],
                        TN,
                        preferred_element_type=jnp.float32,
                    )
                    product = term if product is None else product + term
                for inner in range(0, tile, step):
                    part, offset = divmod(start + inner, share)
                    to = pl.multiple_of(at * rows + (z ^ part) * share + offset, step)
                    piece = product[inner : inner + step, :]
                    out_ref[pl.ds(to, step), :] = piece.astype(out_ref.dtype)


def weight_rows(ids, hidden, grads, groups, origin, rows, block_rows, sub_count):
    plan = Plan(
        hidden=len(hidden),
        groups=groups,
        origin=origin,
        rows=rows,
        block_rows=block_rows,
        sub_count=sub_count,
    )
    out = shape_of(rows * len(groups), grads[0].shape[1])
    amount = 2 * sum(len(group) for group in groups) * rows * 2 * hidden[0].shape[0] + 4 * out.size
    theirs, ours = kernel_call(
        functools.partial(weight_kernel, plan),
        "weight_rows",
        (out, out),
        (ids,),
        (*hidden, *grads),
        cost=bytes_cost(amount),
    )
    return ours.astype(jnp.float32) + swap(theirs, "ctx", 1).astype(jnp.float32)


def sum_over_dp(array):
    count = lax.axis_size("dp")
    rows = array.shape[0] // count
    total = array[:rows]
    for j in range(1, count):
        leaving = array[j * rows : (j + 1) * rows].astype(jnp.bfloat16)
        total = total + swap(leaving, "dp", j).astype(jnp.float32)
    return total


def sum_along_z(full, sub_count):
    share = full.shape[0] // sub_count
    parts = {m: full[m * share : (m + 1) * share] for m in range(sub_count)}
    bits = [1 << at for at in range(sub_count.bit_length() - 1)]
    for bit in bits:
        for m in list(parts):
            if m & bit:
                came = swap(parts.pop(m).astype(jnp.bfloat16), "ctx", 2 * bit)
                parts[m ^ bit] = parts[m ^ bit] + came.astype(jnp.float32)
    low = parts[0].astype(jnp.bfloat16)
    final = (parts[0] + swap(low, "ctx", 2 * sub_count).astype(jnp.float32)).astype(jnp.bfloat16)
    rows = {0: final}
    for bit in bits[::-1]:
        rows.update({m | bit: swap(one, "ctx", 2 * bit) for m, one in list(rows.items())})
    own = [rows[m] for m in range(sub_count)]
    return own + [swap(one, "ctx", 1) for one in own]


def assemble_kernel(sub_count, regions, ids, *refs):
    out_ref = refs[-1]
    blocks = iter(refs[:-1])
    z, core = ids[0] % sub_count, ids[1]
    for origin, rows in regions:
        share = rows // sub_count
        for side in range(2):
            for m in range(sub_count):
                to = origin + (core ^ side) * rows + (z ^ m) * share
                to = pl.multiple_of(to, share)
                out_ref[pl.ds(to, share), :] = next(blocks)[...].astype(jnp.float32)


def assemble(ids, blocks, sub_count, regions):
    rows = sum(block.shape[0] for block in blocks)
    return kernel_call(
        functools.partial(assemble_kernel, sub_count, regions),
        "assemble",
        shape_of(rows, blocks[0].shape[1], jnp.float32),
        (ids,),
        blocks,
    )


def on_device(hidden_in, queries, grad_out, w_key, w_value, stretch_order, doc_lengths):
    inputs = hidden_in[0]
    head_dim = w_key.shape[1]
    dp_count = lax.axis_size("dp")
    ctx_count = lax.axis_size("ctx")
    z_count = ctx_count // 2
    sub_count = z_count // 2
    dp, ctx = lax.axis_index("dp"), lax.axis_index("ctx")
    z, core = ctx // 2, ctx % 2
    ids = jnp.stack([z, core, dp]).astype(jnp.int32)
    me = jnp.reshape(ctx, (1,)).astype(jnp.int32)
    block_rows = w_key.shape[0]
    half_rows = block_rows // 2
    quarter = half_rows // 2
    bits = [1 << at for at in range(dp_count.bit_length() - 1)]

    def own_pieces(weight):
        return {
            (0, side, offset): lax.dynamic_slice_in_dim(
                weight, (core ^ side) * half_rows + offset, quarter, 0
            )
            for side in range(2)
            for offset in (0, quarter)
        }

    def gather(pieces, steps):
        for step in steps:
            for offset, order in ((0, bits), (quarter, bits[::-1])):
                bit = order[step]
                have = [name for name in pieces if name[1] == 0 and name[2] == offset]
                for j, _, _ in have:
                    pieces[j | bit, 0, offset] = swap(pieces[j, 0, offset], "dp", bit)

    def from_other_core(pieces, names):
        pieces.update({(j, 1, offset): swap(pieces[j, 0, offset], "ctx", 1) for j, _, offset in names})

    def last_step(name):
        return name[0] not in [0] + bits

    key_pieces = own_pieces(w_key)
    gather(key_pieces, range(len(bits)))
    landing = [(j, 0, offset) for j in range(1, dp_count) for offset in (0, quarter)]
    from_other_core(key_pieces, landing)
    first = [(bits[0], 0, 0), (bits[-1], 0, quarter)]
    leaving = [(0, 0, 0), (0, 0, quarter)]
    value_pieces = own_pieces(w_value)
    tied, ended = after(
        [value_pieces[name] for name in leaving], *[key_pieces[name] for name in first]
    )
    value_pieces.update(zip(leaving, tied))
    gather(value_pieces, range(1))

    def project_all(pieces):
        early = {name: one for name, one in pieces.items() if not last_step(name)}
        late = {name: one for name, one in pieces.items() if last_step(name)}
        partial = project(ids, None, inputs, block_rows, early, jnp.float32)
        return project(ids, partial, inputs, block_rows, late, jnp.bfloat16)

    def gather_along_z(own):
        return [swap(own, "ctx", 2 * m) if m else own for m in range(z_count)]

    def both_cores(along):
        return [block for one in along for block in (one, swap(one, "ctx", 1))]

    def over_cores(keep, send):
        return keep + swap(send, "ctx", 1).astype(jnp.float32)

    def to_owner(chip):
        rows = chip.shape[0] // z_count
        total = chip[:rows]
        for m in range(1, z_count):
            leaving = chip[m * rows : (m + 1) * rows].astype(jnp.bfloat16)
            total = total + swap(leaving, "ctx", 2 * m).astype(jnp.float32)
        return total.astype(jnp.bfloat16)

    first_rows = moved_rows(block_rows)
    first_half, last_half = first_rows // 2, (block_rows - first_rows) // 2
    regions = ((0, first_half), (first_rows, last_half))
    moving = [
        lax.dynamic_slice_in_dim(inputs, (dp ^ j) * block_rows, first_rows, 1)
        for j in range(dp_count)
    ]
    def hold(arrays, names):
        tied, ended = after(arrays, *[value_pieces[name] for name in names])
        value_pieces.update(zip(names, ended))
        return tied

    plan = attention_plan(queries[0], head_dim, ctx_count)
    own, *moving[1:] = hold([project_all(key_pieces), *moving[1:]], first)
    gather(value_pieces, range(1, len(bits)))
    from_other_core(value_pieces, first)
    along = gather_along_z(own)
    second = [name for name in landing if name not in first and not last_step(name)]
    along = hold(along, second)
    from_other_core(value_pieces, [name for name in landing if name not in first])
    key_blocks = both_cores(along)
    moving[1:] = hold(moving[1:], landing)
    near = [j for j in range(1, dp_count) if j in bits]
    far = [j for j in range(1, dp_count) if j not in bits]
    moved = {0: moving[0]}
    moved.update({j: swap(moving[j], "dp", j) for j in near})
    key_blocks, (own,) = after(key_blocks, project_all(value_pieces))
    along = gather_along_z(own)
    *saved, keep_v, send_v = probs_and_value_grad(
        plan, me, stretch_order, doc_lengths[0], queries[0], grad_out[0], key_blocks
    )
    along, (send_v,) = after(along, send_v)
    value_blocks = both_cores(along)
    (send_v,), ended = after([send_v], *value_blocks, *[moved[j] for j in near])
    value_blocks = ended[:ctx_count]
    moved.update(zip(near, ended[ctx_count:]))

    ready, ended = after([moving[j] for j in far], *[moved[j] for j in near])
    moved.update(zip(near, ended))
    moved.update({j: swap(one, "dp", j) for j, one in zip(far, ready)})
    query_grad, keep_k, send_k = query_and_key_grad(plan, me, stretch_order, saved, value_blocks)
    chip_v = over_cores(keep_v, send_v)
    chip_k = over_cores(keep_k, send_k)
    value_grad = to_owner(chip_v)
    (value_grad,), (chip_k,) = after([value_grad], chip_k)
    key_grad = to_owner(chip_k)
    (key_grad,), ended = after([key_grad], *[moved[j] for j in far])
    moved.update(zip(far, ended))

    def weight_grad(grad):
        grads = [grad] + [swap(grad, "dp", j) for j in range(1, dp_count)]
        groups = [[(0, j, 0)] for j in range(dp_count)]
        last = weight_rows(
            ids, [inputs], [grad], groups, first_rows, last_half, block_rows, sub_count
        )
        last = sum_along_z(sum_over_dp(last), sub_count)
        groups = [[(j, None, j) for j in range(dp_count)]]
        arrays = [moved[j] for j in range(dp_count)]
        first = weight_rows(ids, arrays, grads, groups, 0, first_half, block_rows, sub_count)
        first = sum_along_z(first, sub_count)
        return assemble(ids, first + last, sub_count, regions)

    value_rows = weight_grad(value_grad)
    key_rows = weight_grad(key_grad)
    return query_grad[None], key_rows, value_rows


def solution(mesh):
    return jax.shard_map(
        on_device,
        mesh=mesh,
        in_specs=(
            P("dp", "ctx", None),
            P("dp", "ctx", None),
            P("dp", "ctx", None),
            P("dp", None),
            P("dp", None),
            P(),
            P("dp", None),
        ),
        out_specs=(P("dp", "ctx", None), P("dp", None), P("dp", None)),
        check_vma=False,
    )
```

```python
import functools
import math

import jax
import jax.numpy as jnp
from jax import lax
from jax.experimental import pallas as pl
from jax.experimental.pallas import tpu as pltpu
from jax.sharding import PartitionSpec as P

VMEM_LIMIT = 28 * 1024 * 1024
NO_COST = pl.CostEstimate(flops=0, bytes_accessed=0, transcendentals=0)


def moved_rows(block_rows):
    return block_rows * 10 // 16 // 256 * 256


class Plan:
    def __init__(self, **fields):
        self.__dict__.update(fields)


def swap(array, axis, distance):
    count = lax.axis_size(axis)
    return lax.ppermute(array, axis, [(i, i ^ distance) for i in range(count)])


def after(arrays, *earlier):
    tied = lax.optimization_barrier((tuple(arrays), tuple(earlier)))
    return list(tied[0]), list(tied[1])


def shape_of(rows, width, kind=jnp.bfloat16):
    return jax.ShapeDtypeStruct((rows, width), kind)


def kernel_call(kernel, name, outs, scalars, arrays, scratch=(), cost=NO_COST):
    smem = pl.BlockSpec(memory_space=pltpu.SMEM)
    vmem = pl.BlockSpec(memory_space=pltpu.VMEM)
    single = not isinstance(outs, tuple)
    return pl.pallas_call(
        kernel,
        out_shape=outs,
        in_specs=[smem] * len(scalars) + [vmem] * len(arrays),
        out_specs=vmem if single else (vmem,) * len(outs),
        scratch_shapes=list(scratch),
        compiler_params=pltpu.CompilerParams(vmem_limit_bytes=VMEM_LIMIT),
        cost_estimate=cost,
        name=name,
    )(*scalars, *arrays)


def bytes_cost(amount):
    return pl.CostEstimate(flops=0, bytes_accessed=amount, transcendentals=0)


TN = (((0,), (0,)), ((), ()))


def attention_kernel(
    shape, ids, order, lengths, q_ref, g_ref, *refs
):
    ctx_count, stretch_rows, head_count, head_dim, window, chunk = shape
    kv_refs = refs[:ctx_count]
    qgrad_ref, keep_ref, send_ref, keys, values, total, qs, gs, dqs = refs[ctx_count:]
    me = ids[0]
    row_count = 2 * stretch_rows
    stretch_count = 2 * ctx_count
    score_scale = 1.0 / math.sqrt(head_dim)

    def place(device, half):
        return pl.multiple_of(order[2 * device + half] * stretch_rows, stretch_rows)

    for index in range(ctx_count):
        for half in range(2):
            rows = pl.ds(place(me ^ index, half), stretch_rows)
            block = kv_refs[index][half * stretch_rows : (half + 1) * stretch_rows, :]
            keys[rows, :] = block[:, :head_dim]
            values[rows, :] = block[:, head_dim:]
    total[...] = jnp.zeros_like(total)
    for half in range(2):
        for head in range(head_count):
            to = slice((half * head_count + head) * stretch_rows, (half * head_count + head + 1) * stretch_rows)
            rows = slice(half * stretch_rows, (half + 1) * stretch_rows)
            columns = slice(head * head_dim, (head + 1) * head_dim)
            qs[to, :] = q_ref[rows, columns]
            gs[to, :] = g_ref[rows, columns]
    ends = []
    running = 0
    for at in range(lengths.shape[0]):
        running = running + lengths[at]
        ends.append(running)
    chunks_half = head_count * stretch_rows // chunk

    def step(at, carry):
        half = at // chunks_half
        block = order[2 * me + half]
        first = jnp.maximum(block - stretch_count // 2, 0) * stretch_rows
        first = pl.multiple_of(first, stretch_rows)
        part = pl.ds(pl.multiple_of(at * chunk, chunk), chunk)
        inside = (at - half * chunks_half) * chunk + lax.broadcasted_iota(jnp.int32, (1, chunk), 1)
        at_query = block * stretch_rows + lax.rem(inside, stretch_rows)
        begin = jnp.zeros_like(at_query)
        for end in ends:
            begin = jnp.where(at_query >= end, end, begin)
        at_key = first + lax.broadcasted_iota(jnp.int32, (window, chunk), 0)
        allowed = (at_key >= begin) & (at_key <= at_query)
        k = keys[pl.ds(first, window), :]
        v = values[pl.ds(first, window), :]
        q = qs[part, :]
        g = gs[part, :]
        last = (((1,), (1,)), ((), ()))
        scores = lax.dot_general(k, q, last, preferred_element_type=jnp.float32) * score_scale
        masked = jnp.where(allowed, scores, -jnp.inf)
        expsum = jnp.exp(masked - jnp.max(masked, axis=0, keepdims=True))
        probs = expsum * (1.0 / jnp.sum(expsum, axis=0, keepdims=True))
        probs_low = probs.astype(jnp.bfloat16)
        dprob = lax.dot_general(v, g, last, preferred_element_type=jnp.float32)
        delta = jnp.sum(probs_low.astype(jnp.float32) * dprob, axis=0, keepdims=True)
        dscore = (probs * (dprob - delta)).astype(jnp.bfloat16)
        dq = lax.dot_general(
            k, dscore, (((0,), (0,)), ((), ())), preferred_element_type=jnp.float32
        )
        dqs[part, :] = (jnp.transpose(dq) * score_scale).astype(jnp.bfloat16)
        dk = jnp.dot(dscore, q, preferred_element_type=jnp.float32) * score_scale
        dv = jnp.dot(probs_low, g, preferred_element_type=jnp.float32)
        total[pl.ds(first, window), :head_dim] += dk
        total[pl.ds(first, window), head_dim:] += dv
        return carry

    lax.fori_loop(0, 2 * chunks_half, step, 0)
    for half in range(2):
        for head in range(head_count):
            origin = slice((half * head_count + head) * stretch_rows, (half * head_count + head + 1) * stretch_rows)
            rows = slice(half * stretch_rows, (half + 1) * stretch_rows)
            columns = slice(head * head_dim, (head + 1) * head_dim)
            qgrad_ref[rows, columns] = dqs[origin, :]
    for index in range(ctx_count):
        for half in range(2):
            rows = pl.ds(place(me ^ index, half), stretch_rows)
            start = (index // 2) * row_count + half * stretch_rows
            if index % 2:
                send_ref[start : start + stretch_rows, :] = total[rows, :].astype(jnp.bfloat16)
            else:
                keep_ref[start : start + stretch_rows, :] = total[rows, :]


def attention(me, order, lengths, queries, cotangent, kv_blocks, head_dim):
    row_count, width = queries.shape
    ctx_count = len(kv_blocks)
    stretch_rows = row_count // 2
    head_count = width // head_dim
    seq_rows = row_count * ctx_count
    window = seq_rows // 2 + stretch_rows
    stacked = head_count * stretch_rows
    chunk = 256 if stacked % 256 == 0 else 128
    shape = (ctx_count, stretch_rows, head_count, head_dim, window, chunk)
    smem = pl.BlockSpec(memory_space=pltpu.SMEM)
    vmem = pl.BlockSpec(memory_space=pltpu.VMEM)
    half_rows = seq_rows // 2
    return pl.pallas_call(
        functools.partial(attention_kernel, shape),
        out_shape=(
            jax.ShapeDtypeStruct((row_count, width), jnp.bfloat16),
            jax.ShapeDtypeStruct((half_rows, 2 * head_dim), jnp.float32),
            jax.ShapeDtypeStruct((half_rows, 2 * head_dim), jnp.bfloat16),
        ),
        in_specs=[smem] * 3 + [vmem] * (2 + ctx_count),
        out_specs=(vmem,) * 3,
        scratch_shapes=[
            pltpu.VMEM((seq_rows, head_dim), jnp.bfloat16),
            pltpu.VMEM((seq_rows, head_dim), jnp.bfloat16),
            pltpu.VMEM((seq_rows, 2 * head_dim), jnp.float32),
            pltpu.VMEM((2 * stacked, head_dim), jnp.bfloat16),
            pltpu.VMEM((2 * stacked, head_dim), jnp.bfloat16),
            pltpu.VMEM((2 * stacked, head_dim), jnp.bfloat16),
        ],
        compiler_params=pltpu.CompilerParams(vmem_limit_bytes=VMEM_LIMIT),
        cost_estimate=NO_COST,
        name="attention",
    )(me, order, lengths, queries, cotangent, *kv_blocks)


def project_kernel(plan, ids, hidden, *refs):
    out_ref = refs[-1]
    dp, core = ids[2], ids[1]
    if plan.start:
        total = refs[0][...]
    else:
        columns = pl.ds(pl.multiple_of(dp * plan.block_rows, plan.block_rows), plan.block_rows)
        total = jnp.concatenate(
            [
                jnp.dot(hidden[:, columns], own[...], preferred_element_type=jnp.float32)
                for own in refs[:2]
            ],
            axis=1,
        )
    for (block, side, offset), weight in zip(plan.terms, refs[1 if plan.start else 2 : -1]):
        from_column = (dp ^ block) * plan.block_rows + (core ^ side) * plan.side_rows + offset
        columns = pl.ds(pl.multiple_of(from_column, 128), weight.shape[0])
        total += jnp.dot(hidden[:, columns], weight[...], preferred_element_type=jnp.float32)
    out_ref[...] = total.astype(out_ref.dtype)


def project(ids, begin, inputs, block_rows, pieces, kind, cost=NO_COST):
    names = sorted(pieces)
    weights = [pieces[name] for name in names]
    plan = Plan(
        terms=names, start=len(begin) == 1, block_rows=block_rows, side_rows=block_rows // 2
    )
    return kernel_call(
        functools.partial(project_kernel, plan),
        "project",
        shape_of(inputs.shape[0], weights[0].shape[1], kind),
        (ids,),
        (inputs, *begin, *weights),
        cost=cost,
    )


def weight_kernel(plan, ids, *refs):
    hidden = refs[: plan.hidden]
    grads = refs[plan.hidden : -2]
    z, core, dp = ids[0] % plan.sub_count, ids[1], ids[2]
    rows = plan.rows
    share = rows // plan.sub_count
    tile = next(size for size in (512, 256, 128) if rows % size == 0)
    step = math.gcd(share, tile)
    for side, out_ref in ((1, refs[-2]), (0, refs[-1])):
        for at, group in enumerate(plan.groups):
            for start in range(0, rows, tile):
                product = None
                for array, block, grad in group:
                    origin = plan.origin + (core ^ side) * rows + start
                    if block is not None:
                        origin = origin + (dp ^ block) * plan.block_rows
                    columns = pl.ds(pl.multiple_of(origin, 128), tile)
                    term = lax.dot_general(
                        hidden[array][:, columns],
                        grads[grad][...],
                        TN,
                        preferred_element_type=jnp.float32,
                    )
                    product = term if product is None else product + term
                for inner in range(0, tile, step):
                    part, offset = divmod(start + inner, share)
                    to = pl.multiple_of(at * rows + (z ^ part) * share + offset, step)
                    piece = product[inner : inner + step, :]
                    out_ref[pl.ds(to, step), :] = piece.astype(out_ref.dtype)


def weight_rows(ids, hidden, grads, groups, origin, rows, block_rows, sub_count):
    plan = Plan(
        hidden=len(hidden),
        groups=groups,
        origin=origin,
        rows=rows,
        block_rows=block_rows,
        sub_count=sub_count,
    )
    out = shape_of(rows * len(groups), grads[0].shape[1])
    theirs, ours = kernel_call(
        functools.partial(weight_kernel, plan),
        "weight_rows",
        (out, out),
        (ids,),
        (*hidden, *grads),
        cost=bytes_cost(1 << 23),
    )
    return ours.astype(jnp.float32) + swap(theirs, "ctx", 1).astype(jnp.float32)


def send_over_dp(array):
    count = lax.axis_size("dp")
    rows = array.shape[0] // count
    leaving = [array[j * rows : (j + 1) * rows] for j in range(count)]
    return leaving[:1] + [
        swap(one.astype(jnp.bfloat16), "dp", j) for j, one in enumerate(leaving) if j
    ]


def sum_of(arrays):
    total = arrays[0]
    for one in arrays[1:]:
        total = total + one.astype(jnp.float32)
    return total


def z_bits(sub_count):
    return [1 << at for at in range(sub_count.bit_length() - 1)]


def scatter_along_z(full, sub_count):
    share = full.shape[0] // sub_count
    parts = {m: full[m * share : (m + 1) * share] for m in range(sub_count)}
    for bit in z_bits(sub_count):
        for m in list(parts):
            if m & bit:
                came = swap(parts.pop(m).astype(jnp.bfloat16), "ctx", 2 * bit)
                parts[m ^ bit] = parts[m ^ bit] + came.astype(jnp.float32)
    return parts[0]


def sum_of_halves(part, sub_count):
    low = swap(part.astype(jnp.bfloat16), "ctx", 2 * sub_count)
    return (part + low.astype(jnp.float32)).astype(jnp.bfloat16)


def gather_parts(part, sub_count):
    rows = {0: part}
    for bit in z_bits(sub_count)[::-1]:
        rows.update({m | bit: swap(one, "ctx", 2 * bit) for m, one in list(rows.items())})
    own = [rows[m] for m in range(sub_count)]
    return own + [swap(one, "ctx", 1) for one in own]


def assemble_kernel(sub_count, regions, ids, *refs):
    key_ref, value_ref = refs[-2:]
    blocks = iter(refs[:-2])
    z, core = ids[0] % sub_count, ids[1]
    for origin, rows in regions:
        share = rows // sub_count
        for side in range(2):
            for m in range(sub_count):
                to = origin + (core ^ side) * rows + (z ^ m) * share
                to = pl.multiple_of(to, share)
                block_ref = next(blocks)
                width = block_ref.shape[1] // 2
                key_ref[pl.ds(to, share), :] = block_ref[:, :width].astype(jnp.float32)
                value_ref[pl.ds(to, share), :] = block_ref[:, width:].astype(jnp.float32)


def assemble(ids, blocks, sub_count, regions):
    rows = sum(block.shape[0] for block in blocks)
    out = shape_of(rows, blocks[0].shape[1] // 2, jnp.float32)
    return kernel_call(
        functools.partial(assemble_kernel, sub_count, regions),
        "assemble",
        (out, out),
        (ids,),
        blocks,
    )


def on_device(hidden_in, queries, grad_out, w_key, w_value, stretch_order, doc_lengths):
    inputs = hidden_in[0]
    head_dim = w_key.shape[1]
    dp_count = lax.axis_size("dp")
    ctx_count = lax.axis_size("ctx")
    z_count = ctx_count // 2
    sub_count = z_count // 2
    dp, ctx = lax.axis_index("dp"), lax.axis_index("ctx")
    z, core = ctx // 2, ctx % 2
    ids = jnp.stack([z, core, dp]).astype(jnp.int32)
    me = jnp.reshape(ctx, (1,)).astype(jnp.int32)
    block_rows = w_key.shape[0]
    half_rows = block_rows // 2
    quarter = half_rows // 2
    bits = [1 << at for at in range(dp_count.bit_length() - 1)]
    near = [j for j in range(1, dp_count) if j in bits]
    far = [j for j in range(1, dp_count) if j not in bits]

    def gather_near(*weights):
        halves = [
            lax.dynamic_slice_in_dim(weight, core * half_rows, half_rows, 0) for weight in weights
        ]
        mine = jnp.concatenate(halves, axis=1)
        return {(j, 0, 0): swap(mine, "dp", j) for j in near}

    def gather_far(landed):
        pieces = {}
        for j in far:
            for offset, bit in ((0, 1 << (j.bit_length() - 1)), (quarter, j & -j)):
                if (j ^ bit) in near:
                    origin = landed[j ^ bit, 0, 0][offset : offset + quarter]
                else:
                    origin = pieces[j ^ bit, 0, offset]
                pieces[j, 0, offset] = swap(origin, "dp", bit)
        return pieces

    def from_other_core(pieces):
        return {(j, 1, offset): swap(one, "ctx", 1) for (j, _, offset), one in pieces.items()}

    def hold(arrays, pieces):
        names = list(pieces)
        tied, ended = after(arrays, *[pieces[name] for name in names])
        pieces.update(zip(names, ended))
        return tied

    def gather_along_z(own):
        return [swap(own, "ctx", 2 * m) if m else own for m in range(z_count)]

    def both_cores(along):
        return [block for one in along for block in (one, swap(one, "ctx", 1))]

    first_rows = moved_rows(block_rows)
    first_half, last_half = first_rows // 2, (block_rows - first_rows) // 2
    regions = ((0, first_half), (first_rows, last_half))
    moving = {
        j: lax.dynamic_slice_in_dim(inputs, (dp ^ j) * block_rows, first_rows, 1)
        for j in range(dp_count)
    }

    near_pieces = gather_near(w_key, w_value)
    far_pieces = gather_far(near_pieces)
    near_pieces.update(from_other_core(near_pieces))
    early = project(
        ids, (w_key, w_value), inputs, block_rows, near_pieces, jnp.float32, bytes_cost(1 << 24)
    )
    others = near + far
    early, *tied = hold([early] + [moving[j] for j in others], far_pieces)
    moving.update(zip(others, tied))
    far_pieces.update(from_other_core(far_pieces))
    own = project(ids, (early,), inputs, block_rows, far_pieces, jnp.bfloat16)
    moved = {0: moving[0]}
    moved.update({j: swap(moving[j], "dp", j) for j in near})
    along = gather_along_z(own)
    along, _ = after(along)
    kv_blocks = both_cores(along)

    query_grad, keep, send = attention(
        me, stretch_order, doc_lengths[0], queries[0], grad_out[0], kv_blocks, head_dim
    )
    ready, ended = after([send] + [moving[j] for j in far], *[moved[j] for j in near])
    send = ready[0]
    moved.update(zip(near, ended))
    moved.update({j: swap(one, "dp", j) for j, one in zip(far, ready[1:])})

    chip = keep + swap(send, "ctx", 1).astype(jnp.float32)
    rows = chip.shape[0] // z_count
    grad = chip[:rows]
    for m in range(1, z_count):
        leaving = chip[m * rows : (m + 1) * rows].astype(jnp.bfloat16)
        grad = grad + swap(leaving, "ctx", 2 * m).astype(jnp.float32)
    grad = grad.astype(jnp.bfloat16)
    grads = [grad] + [swap(grad, "dp", j) for j in range(1, dp_count)]

    (grad,), ended = after([grad], *grads[1:], *[moved[j] for j in far])
    grads[1:] = ended[: dp_count - 1]
    moved.update(zip(far, ended[dp_count - 1 :]))
    groups = [[(0, j, 0)] for j in range(dp_count)]
    last = weight_rows(
        ids, [inputs], [grad], groups, first_rows, last_half, block_rows, sub_count
    )
    last = send_over_dp(last)
    groups = [[(j, None, j) for j in range(dp_count)]]
    arrays = [moved[j] for j in range(dp_count)]
    first = weight_rows(ids, arrays, grads, groups, 0, first_half, block_rows, sub_count)
    first = scatter_along_z(first, sub_count)
    first = sum_of_halves(first, sub_count)
    last, _ = after(last, first)
    last = sum_of_halves(scatter_along_z(sum_of(last), sub_count), sub_count)
    blocks = gather_parts(first, sub_count) + gather_parts(last, sub_count)
    key_rows, value_rows = assemble(ids, blocks, sub_count, regions)
    return query_grad[None], key_rows, value_rows


def solution(mesh):
    return jax.shard_map(
        on_device,
        mesh=mesh,
        in_specs=(
            P("dp", "ctx", None),
            P("dp", "ctx", None),
            P("dp", "ctx", None),
            P("dp", None),
            P("dp", None),
            P(),
            P("dp", None),
        ),
        out_specs=(P("dp", "ctx", None), P("dp", None), P("dp", None)),
        check_vma=False,
    )
```

```python
import functools
import math

import jax
import jax.numpy as jnp
from jax import lax
from jax.experimental import pallas as pl
from jax.experimental.pallas import tpu as pltpu
from jax.sharding import PartitionSpec as P

VMEM_LIMIT = 28 * 1024 * 1024
NO_COST = pl.CostEstimate(flops=0, bytes_accessed=0, transcendentals=0)


def moved_rows(block_rows):
    return block_rows * 10 // 16 // 256 * 256


class Plan:
    def __init__(self, **fields):
        self.__dict__.update(fields)


def swap(array, axis, distance):
    count = lax.axis_size(axis)
    return lax.ppermute(array, axis, [(i, i ^ distance) for i in range(count)])


def after(arrays, *earlier):
    tied = lax.optimization_barrier((tuple(arrays), tuple(earlier)))
    return list(tied[0]), list(tied[1])


def shape_of(rows, width, kind=jnp.bfloat16):
    return jax.ShapeDtypeStruct((rows, width), kind)


def kernel_call(kernel, name, outs, scalars, arrays, scratch=(), cost=NO_COST):
    smem = pl.BlockSpec(memory_space=pltpu.SMEM)
    vmem = pl.BlockSpec(memory_space=pltpu.VMEM)
    single = not isinstance(outs, tuple)
    return pl.pallas_call(
        kernel,
        out_shape=outs,
        in_specs=[smem] * len(scalars) + [vmem] * len(arrays),
        out_specs=vmem if single else (vmem,) * len(outs),
        scratch_shapes=list(scratch),
        compiler_params=pltpu.CompilerParams(vmem_limit_bytes=VMEM_LIMIT),
        cost_estimate=cost,
        name=name,
    )(*scalars, *arrays)


def bytes_cost(amount):
    return pl.CostEstimate(flops=0, bytes_accessed=amount, transcendentals=0)


TN = (((0,), (0,)), ((), ()))


def attention_kernel(
    shape, ids, order, lengths, q_ref, g_ref, *refs
):
    ctx_count, stretch_rows, head_count, head_dim, window, chunk = shape
    kv_refs = refs[:ctx_count]
    qgrad_ref, keep_ref, send_ref, keys, values, total, qs, gs, dqs = refs[ctx_count:]
    me = ids[0]
    row_count = 2 * stretch_rows
    stretch_count = 2 * ctx_count
    score_scale = 1.0 / math.sqrt(head_dim)

    def place(device, half):
        return pl.multiple_of(order[2 * device + half] * stretch_rows, stretch_rows)

    for index in range(ctx_count):
        for half in range(2):
            rows = pl.ds(place(me ^ index, half), stretch_rows)
            block = kv_refs[index][half * stretch_rows : (half + 1) * stretch_rows, :]
            keys[rows, :] = block[:, :head_dim]
            values[rows, :] = block[:, head_dim:]
    total[...] = jnp.zeros_like(total)
    for half in range(2):
        for head in range(head_count):
            to = slice((half * head_count + head) * stretch_rows, (half * head_count + head + 1) * stretch_rows)
            rows = slice(half * stretch_rows, (half + 1) * stretch_rows)
            columns = slice(head * head_dim, (head + 1) * head_dim)
            qs[to, :] = q_ref[rows, columns]
            gs[to, :] = g_ref[rows, columns]
    ends = []
    running = 0
    for at in range(lengths.shape[0]):
        running = running + lengths[at]
        ends.append(running)
    chunks_half = head_count * stretch_rows // chunk

    def step(at, carry):
        half = at // chunks_half
        block = order[2 * me + half]
        first = jnp.maximum(block - stretch_count // 2, 0) * stretch_rows
        first = pl.multiple_of(first, stretch_rows)
        part = pl.ds(pl.multiple_of(at * chunk, chunk), chunk)
        inside = (at - half * chunks_half) * chunk + lax.broadcasted_iota(jnp.int32, (1, chunk), 1)
        at_query = block * stretch_rows + lax.rem(inside, stretch_rows)
        begin = jnp.zeros_like(at_query)
        for end in ends:
            begin = jnp.where(at_query >= end, end, begin)
        at_key = first + lax.broadcasted_iota(jnp.int32, (window, chunk), 0)
        allowed = (at_key >= begin) & (at_key <= at_query)
        k = keys[pl.ds(first, window), :]
        v = values[pl.ds(first, window), :]
        q = qs[part, :]
        g = gs[part, :]
        last = (((1,), (1,)), ((), ()))
        scores = lax.dot_general(k, q, last, preferred_element_type=jnp.float32) * score_scale
        masked = jnp.where(allowed, scores, -jnp.inf)
        expsum = jnp.exp(masked - jnp.max(masked, axis=0, keepdims=True))
        probs = expsum * (1.0 / jnp.sum(expsum, axis=0, keepdims=True))
        probs_low = probs.astype(jnp.bfloat16)
        dprob = lax.dot_general(v, g, last, preferred_element_type=jnp.float32)
        delta = jnp.sum(probs_low.astype(jnp.float32) * dprob, axis=0, keepdims=True)
        dscore = (probs * (dprob - delta)).astype(jnp.bfloat16)
        dq = lax.dot_general(
            k, dscore, (((0,), (0,)), ((), ())), preferred_element_type=jnp.float32
        )
        dqs[part, :] = (jnp.transpose(dq) * score_scale).astype(jnp.bfloat16)
        dk = jnp.dot(dscore, q, preferred_element_type=jnp.float32) * score_scale
        dv = jnp.dot(probs_low, g, preferred_element_type=jnp.float32)
        total[pl.ds(first, window), :head_dim] += dk
        total[pl.ds(first, window), head_dim:] += dv
        return carry

    lax.fori_loop(0, 2 * chunks_half, step, 0)
    for half in range(2):
        for head in range(head_count):
            origin = slice((half * head_count + head) * stretch_rows, (half * head_count + head + 1) * stretch_rows)
            rows = slice(half * stretch_rows, (half + 1) * stretch_rows)
            columns = slice(head * head_dim, (head + 1) * head_dim)
            qgrad_ref[rows, columns] = dqs[origin, :]
    for index in range(ctx_count):
        for half in range(2):
            rows = pl.ds(place(me ^ index, half), stretch_rows)
            start = (index // 2) * row_count + half * stretch_rows
            if index % 2:
                send_ref[start : start + stretch_rows, :] = total[rows, :].astype(jnp.bfloat16)
            else:
                keep_ref[start : start + stretch_rows, :] = total[rows, :]


def attention(me, order, lengths, queries, cotangent, kv_blocks, head_dim):
    row_count, width = queries.shape
    ctx_count = len(kv_blocks)
    stretch_rows = row_count // 2
    head_count = width // head_dim
    seq_rows = row_count * ctx_count
    window = seq_rows // 2 + stretch_rows
    stacked = head_count * stretch_rows
    chunk = 256 if stacked % 256 == 0 else 128
    shape = (ctx_count, stretch_rows, head_count, head_dim, window, chunk)
    smem = pl.BlockSpec(memory_space=pltpu.SMEM)
    vmem = pl.BlockSpec(memory_space=pltpu.VMEM)
    half_rows = seq_rows // 2
    return pl.pallas_call(
        functools.partial(attention_kernel, shape),
        out_shape=(
            jax.ShapeDtypeStruct((row_count, width), jnp.bfloat16),
            jax.ShapeDtypeStruct((half_rows, 2 * head_dim), jnp.float32),
            jax.ShapeDtypeStruct((half_rows, 2 * head_dim), jnp.bfloat16),
        ),
        in_specs=[smem] * 3 + [vmem] * (2 + ctx_count),
        out_specs=(vmem,) * 3,
        scratch_shapes=[
            pltpu.VMEM((seq_rows, head_dim), jnp.bfloat16),
            pltpu.VMEM((seq_rows, head_dim), jnp.bfloat16),
            pltpu.VMEM((seq_rows, 2 * head_dim), jnp.float32),
            pltpu.VMEM((2 * stacked, head_dim), jnp.bfloat16),
            pltpu.VMEM((2 * stacked, head_dim), jnp.bfloat16),
            pltpu.VMEM((2 * stacked, head_dim), jnp.bfloat16),
        ],
        compiler_params=pltpu.CompilerParams(vmem_limit_bytes=VMEM_LIMIT),
        cost_estimate=NO_COST,
        name="attention",
    )(me, order, lengths, queries, cotangent, *kv_blocks)


def project_kernel(plan, ids, hidden, *refs):
    out_ref = refs[-1]
    dp, core = ids[2], ids[1]
    if plan.start:
        total = refs[0][...]
    else:
        columns = pl.ds(pl.multiple_of(dp * plan.block_rows, plan.block_rows), plan.block_rows)
        total = jnp.concatenate(
            [
                jnp.dot(hidden[:, columns], own[...], preferred_element_type=jnp.float32)
                for own in refs[:2]
            ],
            axis=1,
        )
    for (block, side, offset), weight in zip(plan.terms, refs[1 if plan.start else 2 : -1]):
        from_column = (dp ^ block) * plan.block_rows + (core ^ side) * plan.side_rows + offset
        columns = pl.ds(pl.multiple_of(from_column, 128), weight.shape[0])
        total += jnp.dot(hidden[:, columns], weight[...], preferred_element_type=jnp.float32)
    out_ref[...] = total.astype(out_ref.dtype)


def project(ids, begin, inputs, block_rows, pieces, kind, cost=NO_COST):
    names = sorted(pieces)
    weights = [pieces[name] for name in names]
    plan = Plan(
        terms=names, start=len(begin) == 1, block_rows=block_rows, side_rows=block_rows // 2
    )
    return kernel_call(
        functools.partial(project_kernel, plan),
        "project",
        shape_of(inputs.shape[0], weights[0].shape[1], kind),
        (ids,),
        (inputs, *begin, *weights),
        cost=cost,
    )


def split_kernel(rows, keep, came, own_ref, *leaving_refs):
    own_ref[...] = keep[:rows, :] + came[:rows, :].astype(jnp.float32)
    for m, leaving in enumerate(leaving_refs, 1):
        block = slice(m * rows, (m + 1) * rows)
        leaving[...] = (keep[block, :] + came[block, :].astype(jnp.float32)).astype(leaving.dtype)


def add_and_split(keep, came, count):
    rows, width = keep.shape[0] // count, keep.shape[1]
    outs = (shape_of(rows, width, jnp.float32),) + (shape_of(rows, width),) * (count - 1)
    return kernel_call(functools.partial(split_kernel, rows), "split", outs, (), (keep, came))


def total_kernel(*refs):
    total = refs[0][...]
    for one in refs[1:-1]:
        total = total + one[...].astype(jnp.float32)
    refs[-1][...] = total.astype(refs[-1].dtype)


def add_all(arrays):
    out = jax.ShapeDtypeStruct(arrays[0].shape, jnp.bfloat16)
    return kernel_call(total_kernel, "total", out, (), arrays)


def weight_kernel(plan, ids, *refs):
    hidden = refs[: plan.hidden]
    grads = refs[plan.hidden : -2]
    z, core, dp = ids[0] % plan.sub_count, ids[1], ids[2]
    rows = plan.rows
    share = rows // plan.sub_count
    tile = next(size for size in (512, 256, 128) if rows % size == 0)
    step = math.gcd(share, tile)
    for side, out_ref in ((1, refs[-2]), (0, refs[-1])):
        for at, group in enumerate(plan.groups):
            for start in range(0, rows, tile):
                product = None
                for array, block, grad in group:
                    origin = plan.origin + (core ^ side) * rows + start
                    if block is not None:
                        origin = origin + (dp ^ block) * plan.block_rows
                    columns = pl.ds(pl.multiple_of(origin, 128), tile)
                    term = lax.dot_general(
                        hidden[array][:, columns],
                        grads[grad][...],
                        TN,
                        preferred_element_type=jnp.float32,
                    )
                    product = term if product is None else product + term
                for inner in range(0, tile, step):
                    part, offset = divmod(start + inner, share)
                    to = pl.multiple_of(at * rows + (z ^ part) * share + offset, step)
                    piece = product[inner : inner + step, :]
                    out_ref[pl.ds(to, step), :] = piece.astype(out_ref.dtype)


def weight_rows(ids, hidden, grads, groups, origin, rows, block_rows, sub_count):
    plan = Plan(
        hidden=len(hidden),
        groups=groups,
        origin=origin,
        rows=rows,
        block_rows=block_rows,
        sub_count=sub_count,
    )
    out = shape_of(rows * len(groups), grads[0].shape[1])
    theirs, ours = kernel_call(
        functools.partial(weight_kernel, plan),
        "weight_rows",
        (out, out),
        (ids,),
        (*hidden, *grads),
        cost=bytes_cost(1 << 23),
    )
    return ours.astype(jnp.float32) + swap(theirs, "ctx", 1).astype(jnp.float32)


def send_over_dp(array):
    count = lax.axis_size("dp")
    rows = array.shape[0] // count
    leaving = [array[j * rows : (j + 1) * rows] for j in range(count)]
    return leaving[:1] + [
        swap(one.astype(jnp.bfloat16), "dp", j) for j, one in enumerate(leaving) if j
    ]


def sum_of(arrays):
    total = arrays[0]
    for one in arrays[1:]:
        total = total + one.astype(jnp.float32)
    return total


def z_bits(sub_count):
    return [1 << at for at in range(sub_count.bit_length() - 1)]


def scatter_along_z(full, sub_count, earlier=()):
    share = full.shape[0] // sub_count
    parts = {m: full[m * share : (m + 1) * share] for m in range(sub_count)}
    for bit in z_bits(sub_count):
        for m in list(parts):
            if m & bit:
                came = swap(parts.pop(m).astype(jnp.bfloat16), "ctx", 2 * bit)
                (came,), _ = after([came], *earlier)
                parts[m ^ bit] = parts[m ^ bit] + came.astype(jnp.float32)
    return parts[0]


def sum_of_halves(part, sub_count):
    low = swap(part.astype(jnp.bfloat16), "ctx", 2 * sub_count)
    return (part + low.astype(jnp.float32)).astype(jnp.bfloat16)


def gather_parts(part, sub_count):
    rows = {0: part}
    for bit in z_bits(sub_count)[::-1]:
        rows.update({m | bit: swap(one, "ctx", 2 * bit) for m, one in list(rows.items())})
    own = [rows[m] for m in range(sub_count)]
    return own + [swap(one, "ctx", 1) for one in own]


def assemble_kernel(sub_count, regions, ids, *refs):
    key_ref, value_ref = refs[-2:]
    blocks = iter(refs[:-2])
    z, core = ids[0] % sub_count, ids[1]
    for origin, rows in regions:
        share = rows // sub_count
        for side in range(2):
            for m in range(sub_count):
                to = origin + (core ^ side) * rows + (z ^ m) * share
                to = pl.multiple_of(to, share)
                block_ref = next(blocks)
                width = block_ref.shape[1] // 2
                key_ref[pl.ds(to, share), :] = block_ref[:, :width].astype(jnp.float32)
                value_ref[pl.ds(to, share), :] = block_ref[:, width:].astype(jnp.float32)


def assemble(ids, blocks, sub_count, regions):
    rows = sum(block.shape[0] for block in blocks)
    out = shape_of(rows, blocks[0].shape[1] // 2, jnp.float32)
    return kernel_call(
        functools.partial(assemble_kernel, sub_count, regions),
        "assemble",
        (out, out),
        (ids,),
        blocks,
    )


def on_device(hidden_in, queries, grad_out, w_key, w_value, stretch_order, doc_lengths):
    inputs = hidden_in[0]
    head_dim = w_key.shape[1]
    dp_count = lax.axis_size("dp")
    ctx_count = lax.axis_size("ctx")
    z_count = ctx_count // 2
    sub_count = z_count // 2
    dp, ctx = lax.axis_index("dp"), lax.axis_index("ctx")
    z, core = ctx // 2, ctx % 2
    ids = jnp.stack([z, core, dp]).astype(jnp.int32)
    me = jnp.reshape(ctx, (1,)).astype(jnp.int32)
    block_rows = w_key.shape[0]
    half_rows = block_rows // 2
    quarter = half_rows // 2
    bits = [1 << at for at in range(dp_count.bit_length() - 1)]
    near = [j for j in range(1, dp_count) if j in bits]
    far = [j for j in range(1, dp_count) if j not in bits]

    def gather_near(*weights):
        pieces = {}
        for turn in range(2):
            for at, j in enumerate(near):
                offset = ((at + turn) % 2) * quarter
                start = core * half_rows + offset
                rows = [lax.dynamic_slice_in_dim(weight, start, quarter, 0) for weight in weights]
                pieces[j, 0, offset] = swap(jnp.concatenate(rows, axis=1), "dp", j)
        return pieces

    def gather_far(landed):
        pieces = {}
        for j in far:
            for offset, bit in ((0, 1 << (j.bit_length() - 1)), (quarter, j & -j)):
                origin = landed.get((j ^ bit, 0, offset), pieces.get((j ^ bit, 0, offset)))
                pieces[j, 0, offset] = swap(origin, "dp", bit)
        return pieces

    def from_other_core(pieces):
        return {(j, 1, offset): swap(one, "ctx", 1) for (j, _, offset), one in pieces.items()}

    def hold(arrays, pieces):
        names = list(pieces)
        tied, ended = after(arrays, *[pieces[name] for name in names])
        pieces.update(zip(names, ended))
        return tied

    def gather_along_z(own):
        return [swap(own, "ctx", 2 * m) if m else own for m in range(z_count)]

    def both_cores(along):
        return [block for one in along for block in (one, swap(one, "ctx", 1))]

    first_rows = moved_rows(block_rows)
    first_half, last_half = first_rows // 2, (block_rows - first_rows) // 2
    regions = ((0, first_half), (first_rows, last_half))
    moving = {
        j: lax.dynamic_slice_in_dim(inputs, (dp ^ j) * block_rows, first_rows, 1)
        for j in range(dp_count)
    }

    near_pieces = gather_near(w_key, w_value)
    far_pieces = gather_far(near_pieces)
    near_pieces.update(from_other_core(near_pieces))
    early = project(
        ids, (w_key, w_value), inputs, block_rows, near_pieces, jnp.float32, bytes_cost(1 << 24)
    )
    others = near + far
    early, *tied = hold([early] + [moving[j] for j in others], far_pieces)
    moving.update(zip(others, tied))
    far_pieces.update(from_other_core(far_pieces))
    own = project(ids, (early,), inputs, block_rows, far_pieces, jnp.bfloat16)
    moved = {0: moving[0]}
    moved.update({j: swap(moving[j], "dp", j) for j in near})
    along = gather_along_z(own)
    along, tied = after(along, *[moving[j] for j in far])
    moving.update(zip(far, tied))
    kv_blocks = both_cores(along)

    query_grad, keep, send = attention(
        me, stretch_order, doc_lengths[0], queries[0], grad_out[0], kv_blocks, head_dim
    )
    (send,), ended = after([send], *[moved[j] for j in near])
    moved.update(zip(near, ended))
    moved.update({j: swap(moving[j], "dp", j) for j in far})

    own, *leaving = add_and_split(keep, swap(send, "ctx", 1), z_count)
    grad = add_all([own] + [swap(one, "ctx", 2 * m) for m, one in enumerate(leaving, 1)])
    grads = [grad] + [swap(grad, "dp", j) for j in range(1, dp_count)]

    (grad,), ended = after([grad], *grads[1:], *[moved[j] for j in far])
    grads[1:] = ended[: dp_count - 1]
    moved.update(zip(far, ended[dp_count - 1 :]))
    groups = [[(0, j, 0)] for j in range(dp_count)]
    last = weight_rows(
        ids, [inputs], [grad], groups, first_rows, last_half, block_rows, sub_count
    )
    last = send_over_dp(last)
    groups = [[(j, None, j) for j in range(dp_count)]]
    arrays = [moved[j] for j in range(dp_count)]
    first = weight_rows(ids, arrays, grads, groups, 0, first_half, block_rows, sub_count)
    first = scatter_along_z(first, sub_count)
    first = sum_of_halves(first, sub_count)
    last = sum_of_halves(scatter_along_z(sum_of(last), sub_count, [first]), sub_count)
    blocks = gather_parts(first, sub_count) + gather_parts(last, sub_count)
    key_rows, value_rows = assemble(ids, blocks, sub_count, regions)
    return query_grad[None], key_rows, value_rows


def solution(mesh):
    return jax.shard_map(
        on_device,
        mesh=mesh,
        in_specs=(
            P("dp", "ctx", None),
            P("dp", "ctx", None),
            P("dp", "ctx", None),
            P("dp", None),
            P("dp", None),
            P(),
            P("dp", None),
        ),
        out_specs=(P("dp", "ctx", None), P("dp", None), P("dp", None)),
        check_vma=False,
    )
```

```python
import functools
import math

import jax
import jax.numpy as jnp
from jax import lax
from jax.experimental import pallas as pl
from jax.experimental.pallas import tpu as pltpu
from jax.sharding import PartitionSpec as P

VMEM_LIMIT = 28 * 1024 * 1024
NO_COST = pl.CostEstimate(flops=0, bytes_accessed=0, transcendentals=0)


MOVED = (6, 5)
TIED = 1


def region_sizes(block_rows):
    units = block_rows // 256
    sizes = [256 * (units * share // 16) for share in MOVED]
    return sizes + [block_rows - sum(sizes)]


class Plan:
    def __init__(self, **fields):
        self.__dict__.update(fields)


def swap(array, axis, distance):
    count = lax.axis_size(axis)
    return lax.ppermute(array, axis, [(i, i ^ distance) for i in range(count)])


def after(arrays, *earlier):
    tied = lax.optimization_barrier((tuple(arrays), tuple(earlier)))
    return list(tied[0]), list(tied[1])


def shape_of(rows, width, kind=jnp.bfloat16):
    return jax.ShapeDtypeStruct((rows, width), kind)


def kernel_call(kernel, name, outs, scalars, arrays, scratch=(), cost=NO_COST):
    smem = pl.BlockSpec(memory_space=pltpu.SMEM)
    vmem = pl.BlockSpec(memory_space=pltpu.VMEM)
    single = not isinstance(outs, tuple)
    return pl.pallas_call(
        kernel,
        out_shape=outs,
        in_specs=[smem] * len(scalars) + [vmem] * len(arrays),
        out_specs=vmem if single else (vmem,) * len(outs),
        scratch_shapes=list(scratch),
        compiler_params=pltpu.CompilerParams(vmem_limit_bytes=VMEM_LIMIT),
        cost_estimate=cost,
        name=name,
    )(*scalars, *arrays)


def bytes_cost(amount):
    return pl.CostEstimate(flops=0, bytes_accessed=amount, transcendentals=0)


TN = (((0,), (0,)), ((), ()))


def attention_kernel(
    shape, ids, order, lengths, q_ref, g_ref, *refs
):
    ctx_count, stretch_rows, head_count, head_dim, window, chunk = shape
    kv_refs = refs[:ctx_count]
    qgrad_ref, keep_ref, send_ref, keys, values, total, qs, gs, dqs = refs[ctx_count:]
    me = ids[0]
    row_count = 2 * stretch_rows
    stretch_count = 2 * ctx_count
    score_scale = 1.0 / math.sqrt(head_dim)

    def place(device, half):
        return pl.multiple_of(order[2 * device + half] * stretch_rows, stretch_rows)

    for index in range(ctx_count):
        for half in range(2):
            rows = pl.ds(place(me ^ index, half), stretch_rows)
            block = kv_refs[index][half * stretch_rows : (half + 1) * stretch_rows, :]
            keys[rows, :] = block[:, :head_dim]
            values[rows, :] = block[:, head_dim:]
    total[...] = jnp.zeros_like(total)
    for half in range(2):
        for head in range(head_count):
            to = slice((half * head_count + head) * stretch_rows, (half * head_count + head + 1) * stretch_rows)
            rows = slice(half * stretch_rows, (half + 1) * stretch_rows)
            columns = slice(head * head_dim, (head + 1) * head_dim)
            qs[to, :] = q_ref[rows, columns]
            gs[to, :] = g_ref[rows, columns]
    ends = []
    running = 0
    for at in range(lengths.shape[0]):
        running = running + lengths[at]
        ends.append(running)
    chunks_half = head_count * stretch_rows // chunk

    def step(at, carry):
        half = at // chunks_half
        block = order[2 * me + half]
        first = jnp.maximum(block - stretch_count // 2, 0) * stretch_rows
        first = pl.multiple_of(first, stretch_rows)
        part = pl.ds(pl.multiple_of(at * chunk, chunk), chunk)
        inside = (at - half * chunks_half) * chunk + lax.broadcasted_iota(jnp.int32, (1, chunk), 1)
        at_query = block * stretch_rows + lax.rem(inside, stretch_rows)
        begin = jnp.zeros_like(at_query)
        for end in ends:
            begin = jnp.where(at_query >= end, end, begin)
        at_key = first + lax.broadcasted_iota(jnp.int32, (window, chunk), 0)
        allowed = (at_key >= begin) & (at_key <= at_query)
        k = keys[pl.ds(first, window), :]
        v = values[pl.ds(first, window), :]
        q = qs[part, :]
        g = gs[part, :]
        last = (((1,), (1,)), ((), ()))
        scores = lax.dot_general(k, q, last, preferred_element_type=jnp.float32) * score_scale
        masked = jnp.where(allowed, scores, -jnp.inf)
        expsum = jnp.exp(masked - jnp.max(masked, axis=0, keepdims=True))
        probs = expsum * (1.0 / jnp.sum(expsum, axis=0, keepdims=True))
        probs_low = probs.astype(jnp.bfloat16)
        dprob = lax.dot_general(v, g, last, preferred_element_type=jnp.float32)
        delta = jnp.sum(probs_low.astype(jnp.float32) * dprob, axis=0, keepdims=True)
        dscore = (probs * (dprob - delta)).astype(jnp.bfloat16)
        dq = lax.dot_general(
            k, dscore, (((0,), (0,)), ((), ())), preferred_element_type=jnp.float32
        )
        dqs[part, :] = (jnp.transpose(dq) * score_scale).astype(jnp.bfloat16)
        dk = jnp.dot(dscore, q, preferred_element_type=jnp.float32) * score_scale
        dv = jnp.dot(probs_low, g, preferred_element_type=jnp.float32)
        total[pl.ds(first, window), :head_dim] += dk
        total[pl.ds(first, window), head_dim:] += dv
        return carry

    lax.fori_loop(0, 2 * chunks_half, step, 0)
    for half in range(2):
        for head in range(head_count):
            origin = slice((half * head_count + head) * stretch_rows, (half * head_count + head + 1) * stretch_rows)
            rows = slice(half * stretch_rows, (half + 1) * stretch_rows)
            columns = slice(head * head_dim, (head + 1) * head_dim)
            qgrad_ref[rows, columns] = dqs[origin, :]
    for index in range(ctx_count):
        for half in range(2):
            rows = pl.ds(place(me ^ index, half), stretch_rows)
            start = (index // 2) * row_count + half * stretch_rows
            if index % 2:
                send_ref[start : start + stretch_rows, :] = total[rows, :].astype(jnp.bfloat16)
            else:
                keep_ref[start : start + stretch_rows, :] = total[rows, :]


def attention(me, order, lengths, queries, cotangent, kv_blocks, head_dim):
    row_count, width = queries.shape
    ctx_count = len(kv_blocks)
    stretch_rows = row_count // 2
    head_count = width // head_dim
    seq_rows = row_count * ctx_count
    window = seq_rows // 2 + stretch_rows
    stacked = head_count * stretch_rows
    chunk = 256 if stacked % 256 == 0 else 128
    shape = (ctx_count, stretch_rows, head_count, head_dim, window, chunk)
    smem = pl.BlockSpec(memory_space=pltpu.SMEM)
    vmem = pl.BlockSpec(memory_space=pltpu.VMEM)
    half_rows = seq_rows // 2
    return pl.pallas_call(
        functools.partial(attention_kernel, shape),
        out_shape=(
            jax.ShapeDtypeStruct((row_count, width), jnp.bfloat16),
            jax.ShapeDtypeStruct((half_rows, 2 * head_dim), jnp.float32),
            jax.ShapeDtypeStruct((half_rows, 2 * head_dim), jnp.bfloat16),
        ),
        in_specs=[smem] * 3 + [vmem] * (2 + ctx_count),
        out_specs=(vmem,) * 3,
        scratch_shapes=[
            pltpu.VMEM((seq_rows, head_dim), jnp.bfloat16),
            pltpu.VMEM((seq_rows, head_dim), jnp.bfloat16),
            pltpu.VMEM((seq_rows, 2 * head_dim), jnp.float32),
            pltpu.VMEM((2 * stacked, head_dim), jnp.bfloat16),
            pltpu.VMEM((2 * stacked, head_dim), jnp.bfloat16),
            pltpu.VMEM((2 * stacked, head_dim), jnp.bfloat16),
        ],
        compiler_params=pltpu.CompilerParams(vmem_limit_bytes=VMEM_LIMIT),
        cost_estimate=NO_COST,
        name="attention",
    )(me, order, lengths, queries, cotangent, *kv_blocks)


def project_kernel(plan, ids, hidden, *refs):
    out_ref = refs[-1]
    dp, core = ids[2], ids[1]
    if plan.start:
        total = refs[0][...]
    else:
        columns = pl.ds(pl.multiple_of(dp * plan.block_rows, plan.block_rows), plan.block_rows)
        total = jnp.concatenate(
            [
                jnp.dot(hidden[:, columns], own[...], preferred_element_type=jnp.float32)
                for own in refs[:2]
            ],
            axis=1,
        )
    for (block, side, offset), weight in zip(plan.terms, refs[1 if plan.start else 2 : -1]):
        from_column = (dp ^ block) * plan.block_rows + (core ^ side) * plan.side_rows + offset
        columns = pl.ds(pl.multiple_of(from_column, 128), weight.shape[0])
        total += jnp.dot(hidden[:, columns], weight[...], preferred_element_type=jnp.float32)
    out_ref[...] = total.astype(out_ref.dtype)


def project(ids, begin, inputs, block_rows, pieces, kind, cost=NO_COST):
    names = sorted(pieces)
    weights = [pieces[name] for name in names]
    plan = Plan(
        terms=names, start=len(begin) == 1, block_rows=block_rows, side_rows=block_rows // 2
    )
    return kernel_call(
        functools.partial(project_kernel, plan),
        "project",
        shape_of(inputs.shape[0], weights[0].shape[1], kind),
        (ids,),
        (inputs, *begin, *weights),
        cost=cost,
    )


def split_kernel(rows, keep, came, own_ref, *leaving_refs):
    own_ref[...] = keep[:rows, :] + came[:rows, :].astype(jnp.float32)
    for m, leaving in enumerate(leaving_refs, 1):
        block = slice(m * rows, (m + 1) * rows)
        leaving[...] = (keep[block, :] + came[block, :].astype(jnp.float32)).astype(leaving.dtype)


def add_and_split(keep, came, count):
    rows, width = keep.shape[0] // count, keep.shape[1]
    outs = (shape_of(rows, width, jnp.float32),) + (shape_of(rows, width),) * (count - 1)
    return kernel_call(functools.partial(split_kernel, rows), "split", outs, (), (keep, came))


def total_kernel(*refs):
    total = refs[0][...]
    for one in refs[1:-1]:
        total = total + one[...].astype(jnp.float32)
    refs[-1][...] = total.astype(refs[-1].dtype)


def add_all(arrays):
    out = jax.ShapeDtypeStruct(arrays[0].shape, jnp.bfloat16)
    return kernel_call(total_kernel, "total", out, (), arrays)


def weight_kernel(plan, ids, *refs):
    hidden = refs[: plan.hidden]
    grads = refs[plan.hidden : -2]
    z, core, dp = ids[0] % plan.sub_count, ids[1], ids[2]
    rows = plan.rows
    share = rows // plan.sub_count
    tile = next(size for size in (512, 256, 128) if rows % size == 0)
    step = math.gcd(share, tile)
    for side, out_ref in ((1, refs[-2]), (0, refs[-1])):
        for at, group in enumerate(plan.groups):
            for start in range(0, rows, tile):
                product = None
                for array, block, grad in group:
                    origin = plan.origin + (core ^ side) * rows + start
                    if block is not None:
                        origin = origin + (dp ^ block) * plan.block_rows
                    columns = pl.ds(pl.multiple_of(origin, 128), tile)
                    term = lax.dot_general(
                        hidden[array][:, columns],
                        grads[grad][...],
                        TN,
                        preferred_element_type=jnp.float32,
                    )
                    product = term if product is None else product + term
                for inner in range(0, tile, step):
                    part, offset = divmod(start + inner, share)
                    to = pl.multiple_of(at * rows + (z ^ part) * share + offset, step)
                    piece = product[inner : inner + step, :]
                    out_ref[pl.ds(to, step), :] = piece.astype(out_ref.dtype)


def weight_rows(ids, hidden, grads, groups, origin, rows, block_rows, sub_count):
    plan = Plan(
        hidden=len(hidden),
        groups=groups,
        origin=origin,
        rows=rows,
        block_rows=block_rows,
        sub_count=sub_count,
    )
    out = shape_of(rows * len(groups), grads[0].shape[1])
    theirs, ours = kernel_call(
        functools.partial(weight_kernel, plan),
        "weight_rows",
        (out, out),
        (ids,),
        (*hidden, *grads),
        cost=bytes_cost(1 << 23),
    )
    return ours.astype(jnp.float32) + swap(theirs, "ctx", 1).astype(jnp.float32)


def send_over_dp(array):
    count = lax.axis_size("dp")
    rows = array.shape[0] // count
    leaving = [array[j * rows : (j + 1) * rows] for j in range(count)]
    return leaving[:1] + [
        swap(one.astype(jnp.bfloat16), "dp", j) for j, one in enumerate(leaving) if j
    ]


def sum_of(arrays):
    total = arrays[0]
    for one in arrays[1:]:
        total = total + one.astype(jnp.float32)
    return total


def z_bits(sub_count):
    return [1 << at for at in range(sub_count.bit_length() - 1)]


def scatter_along_z(full, sub_count, earlier=()):
    share = full.shape[0] // sub_count
    parts = {m: full[m * share : (m + 1) * share] for m in range(sub_count)}
    for bit in z_bits(sub_count):
        for m in list(parts):
            if m & bit:
                came = swap(parts.pop(m).astype(jnp.bfloat16), "ctx", 2 * bit)
                (came,), _ = after([came], *earlier)
                parts[m ^ bit] = parts[m ^ bit] + came.astype(jnp.float32)
    return parts[0]


def sum_of_halves(part, sub_count):
    low = swap(part.astype(jnp.bfloat16), "ctx", 2 * sub_count)
    return (part + low.astype(jnp.float32)).astype(jnp.bfloat16)


def gather_parts(part, sub_count):
    rows = {0: part}
    for bit in z_bits(sub_count)[::-1]:
        rows.update({m | bit: swap(one, "ctx", 2 * bit) for m, one in list(rows.items())})
    own = [rows[m] for m in range(sub_count)]
    return own + [swap(one, "ctx", 1) for one in own]


def assemble_kernel(sub_count, regions, ids, *refs):
    key_ref, value_ref = refs[-2:]
    blocks = iter(refs[:-2])
    z, core = ids[0] % sub_count, ids[1]
    for origin, rows in regions:
        share = rows // sub_count
        for side in range(2):
            for m in range(sub_count):
                to = origin + (core ^ side) * rows + (z ^ m) * share
                to = pl.multiple_of(to, share)
                block_ref = next(blocks)
                width = block_ref.shape[1] // 2
                key_ref[pl.ds(to, share), :] = block_ref[:, :width].astype(jnp.float32)
                value_ref[pl.ds(to, share), :] = block_ref[:, width:].astype(jnp.float32)


def assemble(ids, blocks, sub_count, regions):
    rows = sum(block.shape[0] for block in blocks)
    out = shape_of(rows, blocks[0].shape[1] // 2, jnp.float32)
    return kernel_call(
        functools.partial(assemble_kernel, sub_count, regions),
        "assemble",
        (out, out),
        (ids,),
        blocks,
    )


def on_device(hidden_in, queries, grad_out, w_key, w_value, stretch_order, doc_lengths):
    inputs = hidden_in[0]
    head_dim = w_key.shape[1]
    dp_count = lax.axis_size("dp")
    ctx_count = lax.axis_size("ctx")
    z_count = ctx_count // 2
    sub_count = z_count // 2
    dp, ctx = lax.axis_index("dp"), lax.axis_index("ctx")
    z, core = ctx // 2, ctx % 2
    ids = jnp.stack([z, core, dp]).astype(jnp.int32)
    me = jnp.reshape(ctx, (1,)).astype(jnp.int32)
    block_rows = w_key.shape[0]
    half_rows = block_rows // 2
    quarter = half_rows // 2
    bits = [1 << at for at in range(dp_count.bit_length() - 1)]
    near = [j for j in range(1, dp_count) if j in bits]
    far = [j for j in range(1, dp_count) if j not in bits]

    def gather_near(*weights):
        pieces = {}
        for turn in range(2):
            for at, j in enumerate(near):
                offset = ((at + turn) % 2) * quarter
                start = core * half_rows + offset
                rows = [lax.dynamic_slice_in_dim(weight, start, quarter, 0) for weight in weights]
                pieces[j, 0, offset] = swap(jnp.concatenate(rows, axis=1), "dp", j)
        return pieces

    def gather_far(landed):
        pieces = {}
        for j in far:
            for offset, bit in ((0, 1 << (j.bit_length() - 1)), (quarter, j & -j)):
                origin = landed.get((j ^ bit, 0, offset), pieces.get((j ^ bit, 0, offset)))
                pieces[j, 0, offset] = swap(origin, "dp", bit)
        return pieces

    def from_other_core(pieces):
        return {(j, 1, offset): swap(one, "ctx", 1) for (j, _, offset), one in pieces.items()}

    def hold(arrays, pieces):
        names = list(pieces)
        tied, ended = after(arrays, *[pieces[name] for name in names])
        pieces.update(zip(names, ended))
        return tied

    def gather_along_z(own):
        return [swap(own, "ctx", 2 * m) if m else own for m in range(z_count)]

    def both_cores(along):
        return [block for one in along for block in (one, swap(one, "ctx", 1))]

    sizes = region_sizes(block_rows)
    regions = [(sum(sizes[:at]), size // 2) for at, size in enumerate(sizes)]
    first_rows = sum(sizes[:-1])
    moving = {
        j: lax.dynamic_slice_in_dim(inputs, (dp ^ j) * block_rows, first_rows, 1)
        for j in range(dp_count)
    }

    near_pieces = gather_near(w_key, w_value)
    far_pieces = gather_far(near_pieces)
    near_pieces.update(from_other_core(near_pieces))
    early = project(
        ids, (w_key, w_value), inputs, block_rows, near_pieces, jnp.float32, bytes_cost(1 << 24)
    )
    others = near + far
    early, *tied = hold([early] + [moving[j] for j in others], far_pieces)
    moving.update(zip(others, tied))
    far_pieces.update(from_other_core(far_pieces))
    own = project(ids, (early,), inputs, block_rows, far_pieces, jnp.bfloat16)
    moved = {0: moving[0]}
    moved.update({j: swap(moving[j], "dp", j) for j in near})
    along = gather_along_z(own)
    along, tied = after(along, *[moving[j] for j in far])
    moving.update(zip(far, tied))
    kv_blocks = both_cores(along)

    query_grad, keep, send = attention(
        me, stretch_order, doc_lengths[0], queries[0], grad_out[0], kv_blocks, head_dim
    )
    moved.update({j: swap(moving[j], "dp", j) for j in far})

    own, *leaving = add_and_split(keep, swap(send, "ctx", 1), z_count)
    grad = add_all([own] + [swap(one, "ctx", 2 * m) for m, one in enumerate(leaving, 1)])
    grads = [grad] + [swap(grad, "dp", j) for j in range(1, dp_count)]

    (grad,), ended = after([grad], *grads[1:], *[moved[j] for j in others])
    grads[1:] = ended[: dp_count - 1]
    moved.update(zip(others, ended[dp_count - 1 :]))
    groups = [[(0, j, 0)] for j in range(dp_count)]
    own = weight_rows(ids, [inputs], [grad], groups, *regions[-1], block_rows, sub_count)
    own = send_over_dp(own)
    groups = [[(j, None, j) for j in range(dp_count)]]
    arrays = [moved[j] for j in range(dp_count)]
    finals = []
    for region in regions[:-1]:
        part = weight_rows(ids, arrays, grads, groups, *region, block_rows, sub_count)
        part = scatter_along_z(part, sub_count)
        finals.append(sum_of_halves(part, sub_count))
    part = scatter_along_z(sum_of(own), sub_count, finals[:TIED])
    finals.append(sum_of_halves(part, sub_count))
    blocks = [one for final in finals for one in gather_parts(final, sub_count)]
    key_rows, value_rows = assemble(ids, blocks, sub_count, regions)
    return query_grad[None], key_rows, value_rows


def solution(mesh):
    return jax.shard_map(
        on_device,
        mesh=mesh,
        in_specs=(
            P("dp", "ctx", None),
            P("dp", "ctx", None),
            P("dp", "ctx", None),
            P("dp", None),
            P("dp", None),
            P(),
            P("dp", None),
        ),
        out_specs=(P("dp", "ctx", None), P("dp", None), P("dp", None)),
        check_vma=False,
    )
```

```python
import functools
import math

import jax
import jax.numpy as jnp
from jax import lax
from jax.experimental import pallas as pl
from jax.experimental.pallas import tpu as pltpu
from jax.sharding import PartitionSpec as P

VMEM_LIMIT = 28 * 1024 * 1024
NO_COST = pl.CostEstimate(flops=0, bytes_accessed=0, transcendentals=0)


MOVED = (4, 6)
TIED = 2


def region_sizes(block_rows):
    units = block_rows // 256
    sizes = [256 * (units * share // 16) for share in MOVED]
    return sizes + [block_rows - sum(sizes)]


class Plan:
    def __init__(self, **fields):
        self.__dict__.update(fields)


def swap(array, axis, distance):
    count = lax.axis_size(axis)
    return lax.ppermute(array, axis, [(i, i ^ distance) for i in range(count)])


def after(arrays, *earlier):
    tied = lax.optimization_barrier((tuple(arrays), tuple(earlier)))
    return list(tied[0]), list(tied[1])


def shape_of(rows, width, kind=jnp.bfloat16):
    return jax.ShapeDtypeStruct((rows, width), kind)


def kernel_call(kernel, name, outs, scalars, arrays, scratch=(), cost=NO_COST):
    smem = pl.BlockSpec(memory_space=pltpu.SMEM)
    vmem = pl.BlockSpec(memory_space=pltpu.VMEM)
    single = not isinstance(outs, tuple)
    return pl.pallas_call(
        kernel,
        out_shape=outs,
        in_specs=[smem] * len(scalars) + [vmem] * len(arrays),
        out_specs=vmem if single else (vmem,) * len(outs),
        scratch_shapes=list(scratch),
        compiler_params=pltpu.CompilerParams(vmem_limit_bytes=VMEM_LIMIT),
        cost_estimate=cost,
        name=name,
    )(*scalars, *arrays)


def bytes_cost(amount):
    return pl.CostEstimate(flops=0, bytes_accessed=amount, transcendentals=0)


TN = (((0,), (0,)), ((), ()))


def attention_kernel(
    shape, ids, order, lengths, q_ref, g_ref, *refs
):
    ctx_count, stretch_rows, head_count, head_dim, window, chunk = shape
    kv_refs = refs[:ctx_count]
    qgrad_ref, keep_ref, send_ref, keys, values, total, qs, gs, dqs = refs[ctx_count:]
    me = ids[0]
    row_count = 2 * stretch_rows
    stretch_count = 2 * ctx_count
    score_scale = 1.0 / math.sqrt(head_dim)

    def place(device, half):
        return pl.multiple_of(order[2 * device + half] * stretch_rows, stretch_rows)

    for index in range(ctx_count):
        for half in range(2):
            rows = pl.ds(place(me ^ index, half), stretch_rows)
            block = kv_refs[index][half * stretch_rows : (half + 1) * stretch_rows, :]
            keys[rows, :] = block[:, :head_dim]
            values[rows, :] = block[:, head_dim:]
    total[...] = jnp.zeros_like(total)
    for half in range(2):
        for head in range(head_count):
            to = slice((half * head_count + head) * stretch_rows, (half * head_count + head + 1) * stretch_rows)
            rows = slice(half * stretch_rows, (half + 1) * stretch_rows)
            columns = slice(head * head_dim, (head + 1) * head_dim)
            qs[to, :] = q_ref[rows, columns]
            gs[to, :] = g_ref[rows, columns]
    ends = []
    running = 0
    for at in range(lengths.shape[0]):
        running = running + lengths[at]
        ends.append(running)
    chunks_half = head_count * stretch_rows // chunk

    def step(at, carry):
        half = at // chunks_half
        block = order[2 * me + half]
        first = jnp.maximum(block - stretch_count // 2, 0) * stretch_rows
        first = pl.multiple_of(first, stretch_rows)
        part = pl.ds(pl.multiple_of(at * chunk, chunk), chunk)
        inside = (at - half * chunks_half) * chunk + lax.broadcasted_iota(jnp.int32, (1, chunk), 1)
        at_query = block * stretch_rows + lax.rem(inside, stretch_rows)
        begin = jnp.zeros_like(at_query)
        for end in ends:
            begin = jnp.where(at_query >= end, end, begin)
        at_key = first + lax.broadcasted_iota(jnp.int32, (window, chunk), 0)
        allowed = (at_key >= begin) & (at_key <= at_query)
        k = keys[pl.ds(first, window), :]
        v = values[pl.ds(first, window), :]
        q = qs[part, :]
        g = gs[part, :]
        last = (((1,), (1,)), ((), ()))
        scores = lax.dot_general(k, q, last, preferred_element_type=jnp.float32) * score_scale
        masked = jnp.where(allowed, scores, -jnp.inf)
        expsum = jnp.exp(masked - jnp.max(masked, axis=0, keepdims=True))
        probs = expsum * (1.0 / jnp.sum(expsum, axis=0, keepdims=True))
        probs_low = probs.astype(jnp.bfloat16)
        dprob = lax.dot_general(v, g, last, preferred_element_type=jnp.float32)
        delta = jnp.sum(probs_low.astype(jnp.float32) * dprob, axis=0, keepdims=True)
        dscore = (probs * (dprob - delta)).astype(jnp.bfloat16)
        dq = lax.dot_general(
            k, dscore, (((0,), (0,)), ((), ())), preferred_element_type=jnp.float32
        )
        dqs[part, :] = (jnp.transpose(dq) * score_scale).astype(jnp.bfloat16)
        dk = jnp.dot(dscore, q, preferred_element_type=jnp.float32) * score_scale
        dv = jnp.dot(probs_low, g, preferred_element_type=jnp.float32)
        total[pl.ds(first, window), :head_dim] += dk
        total[pl.ds(first, window), head_dim:] += dv
        return carry

    lax.fori_loop(0, 2 * chunks_half, step, 0)
    for half in range(2):
        for head in range(head_count):
            origin = slice((half * head_count + head) * stretch_rows, (half * head_count + head + 1) * stretch_rows)
            rows = slice(half * stretch_rows, (half + 1) * stretch_rows)
            columns = slice(head * head_dim, (head + 1) * head_dim)
            qgrad_ref[rows, columns] = dqs[origin, :]
    for index in range(ctx_count):
        for half in range(2):
            rows = pl.ds(place(me ^ index, half), stretch_rows)
            start = (index // 2) * row_count + half * stretch_rows
            if index % 2:
                send_ref[start : start + stretch_rows, :] = total[rows, :].astype(jnp.bfloat16)
            else:
                keep_ref[start : start + stretch_rows, :] = total[rows, :]


def attention(me, order, lengths, queries, cotangent, kv_blocks, head_dim):
    row_count, width = queries.shape
    ctx_count = len(kv_blocks)
    stretch_rows = row_count // 2
    head_count = width // head_dim
    seq_rows = row_count * ctx_count
    window = seq_rows // 2 + stretch_rows
    stacked = head_count * stretch_rows
    chunk = 256 if stacked % 256 == 0 else 128
    shape = (ctx_count, stretch_rows, head_count, head_dim, window, chunk)
    smem = pl.BlockSpec(memory_space=pltpu.SMEM)
    vmem = pl.BlockSpec(memory_space=pltpu.VMEM)
    half_rows = seq_rows // 2
    return pl.pallas_call(
        functools.partial(attention_kernel, shape),
        out_shape=(
            jax.ShapeDtypeStruct((row_count, width), jnp.bfloat16),
            jax.ShapeDtypeStruct((half_rows, 2 * head_dim), jnp.float32),
            jax.ShapeDtypeStruct((half_rows, 2 * head_dim), jnp.bfloat16),
        ),
        in_specs=[smem] * 3 + [vmem] * (2 + ctx_count),
        out_specs=(vmem,) * 3,
        scratch_shapes=[
            pltpu.VMEM((seq_rows, head_dim), jnp.bfloat16),
            pltpu.VMEM((seq_rows, head_dim), jnp.bfloat16),
            pltpu.VMEM((seq_rows, 2 * head_dim), jnp.float32),
            pltpu.VMEM((2 * stacked, head_dim), jnp.bfloat16),
            pltpu.VMEM((2 * stacked, head_dim), jnp.bfloat16),
            pltpu.VMEM((2 * stacked, head_dim), jnp.bfloat16),
        ],
        compiler_params=pltpu.CompilerParams(vmem_limit_bytes=VMEM_LIMIT),
        cost_estimate=NO_COST,
        name="attention",
    )(me, order, lengths, queries, cotangent, *kv_blocks)


def project_kernel(plan, ids, hidden, *refs):
    out_ref = refs[-1]
    dp, core = ids[2], ids[1]
    if plan.start:
        total = refs[0][...]
    else:
        columns = pl.ds(pl.multiple_of(dp * plan.block_rows, plan.block_rows), plan.block_rows)
        total = jnp.concatenate(
            [
                jnp.dot(hidden[:, columns], own[...], preferred_element_type=jnp.float32)
                for own in refs[:2]
            ],
            axis=1,
        )
    for (block, side, offset), weight in zip(plan.terms, refs[1 if plan.start else 2 : -1]):
        from_column = (dp ^ block) * plan.block_rows + (core ^ side) * plan.side_rows + offset
        columns = pl.ds(pl.multiple_of(from_column, 128), weight.shape[0])
        total += jnp.dot(hidden[:, columns], weight[...], preferred_element_type=jnp.float32)
    out_ref[...] = total.astype(out_ref.dtype)


def project(ids, begin, inputs, block_rows, pieces, kind, cost=NO_COST):
    names = sorted(pieces)
    weights = [pieces[name] for name in names]
    plan = Plan(
        terms=names, start=len(begin) == 1, block_rows=block_rows, side_rows=block_rows // 2
    )
    return kernel_call(
        functools.partial(project_kernel, plan),
        "project",
        shape_of(inputs.shape[0], weights[0].shape[1], kind),
        (ids,),
        (inputs, *begin, *weights),
        cost=cost,
    )


def split_kernel(rows, keep, came, own_ref, *leaving_refs):
    own_ref[...] = keep[:rows, :] + came[:rows, :].astype(jnp.float32)
    for m, leaving in enumerate(leaving_refs, 1):
        block = slice(m * rows, (m + 1) * rows)
        leaving[...] = (keep[block, :] + came[block, :].astype(jnp.float32)).astype(leaving.dtype)


def add_and_split(keep, came, count):
    rows, width = keep.shape[0] // count, keep.shape[1]
    outs = (shape_of(rows, width, jnp.float32),) + (shape_of(rows, width),) * (count - 1)
    return kernel_call(functools.partial(split_kernel, rows), "split", outs, (), (keep, came))


def total_kernel(*refs):
    total = refs[0][...]
    for one in refs[1:-1]:
        total = total + one[...].astype(jnp.float32)
    refs[-1][...] = total.astype(refs[-1].dtype)


def add_all(arrays):
    out = jax.ShapeDtypeStruct(arrays[0].shape, jnp.bfloat16)
    return kernel_call(total_kernel, "total", out, (), arrays)


def weight_kernel(plan, ids, *refs):
    hidden = refs[: plan.hidden]
    grads = refs[plan.hidden : -2]
    z, core, dp = ids[0] % plan.sub_count, ids[1], ids[2]
    rows = plan.rows
    share = rows // plan.sub_count
    tile = next(size for size in (512, 256, 128) if rows % size == 0)
    step = math.gcd(share, tile)
    for side, out_ref in ((1, refs[-2]), (0, refs[-1])):
        for at, group in enumerate(plan.groups):
            for start in range(0, rows, tile):
                product = None
                for array, block, grad in group:
                    origin = plan.origin + (core ^ side) * rows + start
                    if block is not None:
                        origin = origin + (dp ^ block) * plan.block_rows
                    columns = pl.ds(pl.multiple_of(origin, 128), tile)
                    term = lax.dot_general(
                        hidden[array][:, columns],
                        grads[grad][...],
                        TN,
                        preferred_element_type=jnp.float32,
                    )
                    product = term if product is None else product + term
                for inner in range(0, tile, step):
                    part, offset = divmod(start + inner, share)
                    to = pl.multiple_of(at * rows + (z ^ part) * share + offset, step)
                    piece = product[inner : inner + step, :]
                    out_ref[pl.ds(to, step), :] = piece.astype(out_ref.dtype)


def weight_rows(ids, hidden, grads, groups, origin, rows, block_rows, sub_count):
    plan = Plan(
        hidden=len(hidden),
        groups=groups,
        origin=origin,
        rows=rows,
        block_rows=block_rows,
        sub_count=sub_count,
    )
    out = shape_of(rows * len(groups), grads[0].shape[1])
    theirs, ours = kernel_call(
        functools.partial(weight_kernel, plan),
        "weight_rows",
        (out, out),
        (ids,),
        (*hidden, *grads),
    )
    return ours.astype(jnp.float32) + swap(theirs, "ctx", 1).astype(jnp.float32)


def parts_over_dp(array):
    count = lax.axis_size("dp")
    rows = array.shape[0] // count
    parts = [array[j * rows : (j + 1) * rows] for j in range(count)]
    return parts[:1] + [part.astype(jnp.bfloat16) for part in parts[1:]]


def sum_of(arrays):
    total = arrays[0]
    for one in arrays[1:]:
        total = total + one.astype(jnp.float32)
    return total


def z_bits(sub_count):
    return [1 << at for at in range(sub_count.bit_length() - 1)]


def scatter_along_z(full, sub_count, earlier=()):
    share = full.shape[0] // sub_count
    parts = {m: full[m * share : (m + 1) * share] for m in range(sub_count)}
    for bit in z_bits(sub_count):
        for m in list(parts):
            if m & bit:
                came = swap(parts.pop(m).astype(jnp.bfloat16), "ctx", 2 * bit)
                (came,), _ = after([came], *earlier)
                parts[m ^ bit] = parts[m ^ bit] + came.astype(jnp.float32)
    return parts[0]


def sum_of_halves(part, sub_count):
    low = swap(part.astype(jnp.bfloat16), "ctx", 2 * sub_count)
    return (part + low.astype(jnp.float32)).astype(jnp.bfloat16)


def gather_parts(part, sub_count):
    rows = {0: part}
    for bit in z_bits(sub_count)[::-1]:
        rows.update({m | bit: swap(one, "ctx", 2 * bit) for m, one in list(rows.items())})
    own = [rows[m] for m in range(sub_count)]
    return own + [swap(one, "ctx", 1) for one in own]


def assemble_kernel(sub_count, regions, ids, *refs):
    key_ref, value_ref = refs[-2:]
    blocks = iter(refs[:-2])
    z, core = ids[0] % sub_count, ids[1]
    for origin, rows in regions:
        share = rows // sub_count
        for side in range(2):
            for m in range(sub_count):
                to = origin + (core ^ side) * rows + (z ^ m) * share
                to = pl.multiple_of(to, share)
                block_ref = next(blocks)
                width = block_ref.shape[1] // 2
                key_ref[pl.ds(to, share), :] = block_ref[:, :width].astype(jnp.float32)
                value_ref[pl.ds(to, share), :] = block_ref[:, width:].astype(jnp.float32)


def assemble(ids, blocks, sub_count, regions):
    rows = sum(block.shape[0] for block in blocks)
    out = shape_of(rows, blocks[0].shape[1] // 2, jnp.float32)
    return kernel_call(
        functools.partial(assemble_kernel, sub_count, regions),
        "assemble",
        (out, out),
        (ids,),
        blocks,
    )


def on_device(hidden_in, queries, grad_out, w_key, w_value, stretch_order, doc_lengths):
    inputs = hidden_in[0]
    head_dim = w_key.shape[1]
    dp_count = lax.axis_size("dp")
    ctx_count = lax.axis_size("ctx")
    z_count = ctx_count // 2
    sub_count = z_count // 2
    dp, ctx = lax.axis_index("dp"), lax.axis_index("ctx")
    z, core = ctx // 2, ctx % 2
    ids = jnp.stack([z, core, dp]).astype(jnp.int32)
    me = jnp.reshape(ctx, (1,)).astype(jnp.int32)
    block_rows = w_key.shape[0]
    half_rows = block_rows // 2
    quarter = half_rows // 2
    bits = [1 << at for at in range(dp_count.bit_length() - 1)]
    near = [j for j in range(1, dp_count) if j in bits]
    far = [j for j in range(1, dp_count) if j not in bits]

    def gather_near(*weights):
        pieces = {}
        for turn in range(2):
            for at, j in enumerate(near):
                offset = ((at + turn) % 2) * quarter
                start = core * half_rows + offset
                rows = [lax.dynamic_slice_in_dim(weight, start, quarter, 0) for weight in weights]
                pieces[j, 0, offset] = swap(jnp.concatenate(rows, axis=1), "dp", j)
        return pieces

    def gather_far(landed):
        pieces = {}
        for j in far:
            for offset, bit in ((0, 1 << (j.bit_length() - 1)), (quarter, j & -j)):
                origin = landed.get((j ^ bit, 0, offset), pieces.get((j ^ bit, 0, offset)))
                pieces[j, 0, offset] = swap(origin, "dp", bit)
        return pieces

    def from_other_core(pieces):
        return {(j, 1, offset): swap(one, "ctx", 1) for (j, _, offset), one in pieces.items()}

    def hold(arrays, pieces):
        names = list(pieces)
        tied, ended = after(arrays, *[pieces[name] for name in names])
        pieces.update(zip(names, ended))
        return tied

    def gather_along_z(own):
        return [swap(own, "ctx", 2 * m) if m else own for m in range(z_count)]

    def both_cores(along):
        return [block for one in along for block in (one, swap(one, "ctx", 1))]

    sizes = region_sizes(block_rows)
    regions = [(sum(sizes[:at]), size // 2) for at, size in enumerate(sizes)]
    first_rows = sum(sizes[:-1])
    moving = {
        j: lax.dynamic_slice_in_dim(inputs, (dp ^ j) * block_rows, first_rows, 1)
        for j in range(dp_count)
    }

    near_pieces = gather_near(w_key, w_value)
    far_pieces = gather_far(near_pieces)
    near_pieces.update(from_other_core(near_pieces))
    early = project(
        ids, (w_key, w_value), inputs, block_rows, near_pieces, jnp.float32, bytes_cost(1 << 24)
    )
    others = near + far
    early, *tied = hold([early] + [moving[j] for j in others], far_pieces)
    moving.update(zip(others, tied))
    far_pieces.update(from_other_core(far_pieces))
    own = project(ids, (early,), inputs, block_rows, far_pieces, jnp.bfloat16)
    moved = {0: moving[0]}
    moved.update({j: swap(moving[j], "dp", j) for j in near})
    along = gather_along_z(own)
    along, tied = after(along, *[moving[j] for j in far])
    moving.update(zip(far, tied))
    kv_blocks = both_cores(along)

    kv_blocks, ended = after(kv_blocks, *[moved[j] for j in near])
    moved.update(zip(near, ended))
    tied, _ = after([moving[j] for j in far], *ended)
    moved.update({j: swap(one, "dp", j) for j, one in zip(far, tied)})
    query_grad, keep, send = attention(
        me, stretch_order, doc_lengths[0], queries[0], grad_out[0], kv_blocks, head_dim
    )
    own, *leaving = add_and_split(keep, swap(send, "ctx", 1), z_count)
    grad = add_all([own] + [swap(one, "ctx", 2 * m) for m, one in enumerate(leaving, 1)])
    grads = [grad] + [swap(grad, "dp", j) for j in range(1, dp_count)]

    (grad,), ended = after([grad], *grads[1:], *[moved[j] for j in far])
    grads[1:] = ended[: dp_count - 1]
    moved.update(zip(far, ended[dp_count - 1 :]))
    groups = [[(0, j, 0)] for j in range(dp_count)]
    own = weight_rows(ids, [inputs], [grad], groups, *regions[-1], block_rows, sub_count)
    own = parts_over_dp(own)
    groups = [[(j, None, j) for j in range(dp_count)]]
    arrays = [moved[j] for j in range(dp_count)]
    moved_parts = [
        weight_rows(ids, arrays, grads, groups, *region, block_rows, sub_count)
        for region in regions[:-1]
    ]
    moved_parts, own = after(moved_parts, *own)
    own = [swap(one, "dp", j) if j else one for j, one in enumerate(own)]
    finals = []
    for part in moved_parts:
        part = scatter_along_z(part, sub_count)
        finals.append(sum_of_halves(part, sub_count))
    part = scatter_along_z(sum_of(own), sub_count, finals[:TIED])
    finals.append(sum_of_halves(part, sub_count))
    blocks = [one for final in finals for one in gather_parts(final, sub_count)]
    key_rows, value_rows = assemble(ids, blocks, sub_count, regions)
    return query_grad[None], key_rows, value_rows


def solution(mesh):
    return jax.shard_map(
        on_device,
        mesh=mesh,
        in_specs=(
            P("dp", "ctx", None),
            P("dp", "ctx", None),
            P("dp", "ctx", None),
            P("dp", None),
            P("dp", None),
            P(),
            P("dp", None),
        ),
        out_specs=(P("dp", "ctx", None), P("dp", None), P("dp", None)),
        check_vma=False,
    )
```

```python
import functools
import math

import jax
import jax.numpy as jnp
from jax import lax
from jax.experimental import pallas as pl
from jax.experimental.pallas import tpu as pltpu
from jax.sharding import PartitionSpec as P

VMEM_LIMIT = 28 * 1024 * 1024
NO_COST = pl.CostEstimate(flops=0, bytes_accessed=0, transcendentals=0)


MOVED = (4, 6)
TIED = 2


def region_sizes(block_rows):
    units = block_rows // 256
    sizes = [256 * (units * share // 16) for share in MOVED]
    return sizes + [block_rows - sum(sizes)]


class Plan:
    def __init__(self, **fields):
        self.__dict__.update(fields)


def swap(array, axis, distance):
    count = lax.axis_size(axis)
    return lax.ppermute(array, axis, [(i, i ^ distance) for i in range(count)])


def after(arrays, *earlier):
    tied = lax.optimization_barrier((tuple(arrays), tuple(earlier)))
    return list(tied[0]), list(tied[1])


def shape_of(rows, width, kind=jnp.bfloat16):
    return jax.ShapeDtypeStruct((rows, width), kind)


def kernel_call(kernel, name, outs, scalars, arrays, scratch=(), cost=NO_COST):
    smem = pl.BlockSpec(memory_space=pltpu.SMEM)
    vmem = pl.BlockSpec(memory_space=pltpu.VMEM)
    single = not isinstance(outs, tuple)
    return pl.pallas_call(
        kernel,
        out_shape=outs,
        in_specs=[smem] * len(scalars) + [vmem] * len(arrays),
        out_specs=vmem if single else (vmem,) * len(outs),
        scratch_shapes=list(scratch),
        compiler_params=pltpu.CompilerParams(vmem_limit_bytes=VMEM_LIMIT),
        cost_estimate=cost,
        name=name,
    )(*scalars, *arrays)


def bytes_cost(amount):
    return pl.CostEstimate(flops=0, bytes_accessed=amount, transcendentals=0)


TN = (((0,), (0,)), ((), ()))


def attention_kernel(
    shape, ids, order, lengths, q_ref, g_ref, *refs
):
    ctx_count, stretch_rows, head_count, head_dim, window, chunk = shape
    kv_refs = refs[:ctx_count]
    qgrad_ref, keep_ref, send_ref, keys, values, total, qs, gs, dqs = refs[ctx_count:]
    me = ids[0]
    row_count = 2 * stretch_rows
    stretch_count = 2 * ctx_count
    score_scale = 1.0 / math.sqrt(head_dim)

    def place(device, half):
        return pl.multiple_of(order[2 * device + half] * stretch_rows, stretch_rows)

    for index in range(ctx_count):
        for half in range(2):
            rows = pl.ds(place(me ^ index, half), stretch_rows)
            block = kv_refs[index][half * stretch_rows : (half + 1) * stretch_rows, :]
            keys[rows, :] = block[:, :head_dim]
            values[rows, :] = block[:, head_dim:]
    total[...] = jnp.zeros_like(total)
    for half in range(2):
        for head in range(head_count):
            to = slice((half * head_count + head) * stretch_rows, (half * head_count + head + 1) * stretch_rows)
            rows = slice(half * stretch_rows, (half + 1) * stretch_rows)
            columns = slice(head * head_dim, (head + 1) * head_dim)
            qs[to, :] = q_ref[rows, columns]
            gs[to, :] = g_ref[rows, columns]
    ends = []
    running = 0
    for at in range(lengths.shape[0]):
        running = running + lengths[at]
        ends.append(running)
    chunks_half = head_count * stretch_rows // chunk

    def step(at, carry):
        half = at // chunks_half
        block = order[2 * me + half]
        first = jnp.maximum(block - stretch_count // 2, 0) * stretch_rows
        first = pl.multiple_of(first, stretch_rows)
        part = pl.ds(pl.multiple_of(at * chunk, chunk), chunk)
        inside = (at - half * chunks_half) * chunk + lax.broadcasted_iota(jnp.int32, (1, chunk), 1)
        at_query = block * stretch_rows + lax.rem(inside, stretch_rows)
        begin = jnp.zeros_like(at_query)
        for end in ends:
            begin = jnp.where(at_query >= end, end, begin)
        at_key = first + lax.broadcasted_iota(jnp.int32, (window, chunk), 0)
        allowed = (at_key >= begin) & (at_key <= at_query)
        k = keys[pl.ds(first, window), :]
        v = values[pl.ds(first, window), :]
        q = qs[part, :]
        g = gs[part, :]
        last = (((1,), (1,)), ((), ()))
        scores = lax.dot_general(k, q, last, preferred_element_type=jnp.float32)
        masked = jnp.where(allowed, scores, -jnp.inf)
        largest = jnp.max(masked, axis=0, keepdims=True)
        expsum = jnp.exp2((masked - largest) * (score_scale * math.log2(math.e)))
        probs = expsum * (1.0 / jnp.sum(expsum, axis=0, keepdims=True))
        probs_low = probs.astype(jnp.bfloat16)
        dprob = lax.dot_general(v, g, last, preferred_element_type=jnp.float32)
        delta = jnp.sum(probs_low.astype(jnp.float32) * dprob, axis=0, keepdims=True)
        dscore = (probs * (dprob - delta)).astype(jnp.bfloat16)
        dq = lax.dot_general(
            k, dscore, (((0,), (0,)), ((), ())), preferred_element_type=jnp.float32
        )
        dqs[part, :] = (jnp.transpose(dq) * score_scale).astype(jnp.bfloat16)
        dk = jnp.dot(dscore, q, preferred_element_type=jnp.float32) * score_scale
        dv = jnp.dot(probs_low, g, preferred_element_type=jnp.float32)
        total[pl.ds(first, window), :head_dim] += dk
        total[pl.ds(first, window), head_dim:] += dv
        return carry

    lax.fori_loop(0, 2 * chunks_half, step, 0, unroll=2)
    for half in range(2):
        for head in range(head_count):
            origin = slice((half * head_count + head) * stretch_rows, (half * head_count + head + 1) * stretch_rows)
            rows = slice(half * stretch_rows, (half + 1) * stretch_rows)
            columns = slice(head * head_dim, (head + 1) * head_dim)
            qgrad_ref[rows, columns] = dqs[origin, :]
    for index in range(ctx_count):
        for half in range(2):
            rows = pl.ds(place(me ^ index, half), stretch_rows)
            start = (index // 2) * row_count + half * stretch_rows
            if index % 2:
                send_ref[start : start + stretch_rows, :] = total[rows, :].astype(jnp.bfloat16)
            else:
                keep_ref[start : start + stretch_rows, :] = total[rows, :]


def attention(me, order, lengths, queries, cotangent, kv_blocks, head_dim):
    row_count, width = queries.shape
    ctx_count = len(kv_blocks)
    stretch_rows = row_count // 2
    head_count = width // head_dim
    seq_rows = row_count * ctx_count
    window = seq_rows // 2 + stretch_rows
    stacked = head_count * stretch_rows
    chunk = 256 if stacked % 256 == 0 else 128
    shape = (ctx_count, stretch_rows, head_count, head_dim, window, chunk)
    smem = pl.BlockSpec(memory_space=pltpu.SMEM)
    vmem = pl.BlockSpec(memory_space=pltpu.VMEM)
    half_rows = seq_rows // 2
    return pl.pallas_call(
        functools.partial(attention_kernel, shape),
        out_shape=(
            jax.ShapeDtypeStruct((row_count, width), jnp.bfloat16),
            jax.ShapeDtypeStruct((half_rows, 2 * head_dim), jnp.float32),
            jax.ShapeDtypeStruct((half_rows, 2 * head_dim), jnp.bfloat16),
        ),
        in_specs=[smem] * 3 + [vmem] * (2 + ctx_count),
        out_specs=(vmem,) * 3,
        scratch_shapes=[
            pltpu.VMEM((seq_rows, head_dim), jnp.bfloat16),
            pltpu.VMEM((seq_rows, head_dim), jnp.bfloat16),
            pltpu.VMEM((seq_rows, 2 * head_dim), jnp.float32),
            pltpu.VMEM((2 * stacked, head_dim), jnp.bfloat16),
            pltpu.VMEM((2 * stacked, head_dim), jnp.bfloat16),
            pltpu.VMEM((2 * stacked, head_dim), jnp.bfloat16),
        ],
        compiler_params=pltpu.CompilerParams(vmem_limit_bytes=VMEM_LIMIT),
        cost_estimate=NO_COST,
        name="attention",
    )(me, order, lengths, queries, cotangent, *kv_blocks)


def project_kernel(plan, ids, hidden, *refs):
    out_ref = refs[-1]
    dp, core = ids[2], ids[1]
    if plan.start:
        total = refs[0][...]
    else:
        columns = pl.ds(pl.multiple_of(dp * plan.block_rows, plan.block_rows), plan.block_rows)
        total = jnp.concatenate(
            [
                jnp.dot(hidden[:, columns], own[...], preferred_element_type=jnp.float32)
                for own in refs[:2]
            ],
            axis=1,
        )
    for (block, side, offset), weight in zip(plan.terms, refs[1 if plan.start else 2 : -1]):
        from_column = (dp ^ block) * plan.block_rows + (core ^ side) * plan.side_rows + offset
        columns = pl.ds(pl.multiple_of(from_column, 128), weight.shape[0])
        total += jnp.dot(hidden[:, columns], weight[...], preferred_element_type=jnp.float32)
    out_ref[...] = total.astype(out_ref.dtype)


def project(ids, begin, inputs, block_rows, pieces, kind, cost=NO_COST):
    names = sorted(pieces)
    weights = [pieces[name] for name in names]
    plan = Plan(
        terms=names, start=len(begin) == 1, block_rows=block_rows, side_rows=block_rows // 2
    )
    return kernel_call(
        functools.partial(project_kernel, plan),
        "project",
        shape_of(inputs.shape[0], weights[0].shape[1], kind),
        (ids,),
        (inputs, *begin, *weights),
        cost=cost,
    )


def split_kernel(rows, keep, came, own_ref, *leaving_refs):
    own_ref[...] = keep[:rows, :] + came[:rows, :].astype(jnp.float32)
    for m, leaving in enumerate(leaving_refs, 1):
        block = slice(m * rows, (m + 1) * rows)
        leaving[...] = (keep[block, :] + came[block, :].astype(jnp.float32)).astype(leaving.dtype)


def add_and_split(keep, came, count):
    rows, width = keep.shape[0] // count, keep.shape[1]
    outs = (shape_of(rows, width, jnp.float32),) + (shape_of(rows, width),) * (count - 1)
    return kernel_call(functools.partial(split_kernel, rows), "split", outs, (), (keep, came))


def total_kernel(*refs):
    total = refs[0][...]
    for one in refs[1:-1]:
        total = total + one[...].astype(jnp.float32)
    refs[-1][...] = total.astype(refs[-1].dtype)


def add_all(arrays):
    out = jax.ShapeDtypeStruct(arrays[0].shape, jnp.bfloat16)
    return kernel_call(total_kernel, "total", out, (), arrays)


def weight_kernel(plan, ids, *refs):
    hidden = refs[: plan.hidden]
    grads = refs[plan.hidden : -2]
    z, core, dp = ids[0] % plan.sub_count, ids[1], ids[2]
    rows = plan.rows
    share = rows // plan.sub_count
    tile = next(size for size in (512, 256, 128) if rows % size == 0)
    step = math.gcd(share, tile)
    for side, out_ref in ((1, refs[-2]), (0, refs[-1])):
        for at, group in enumerate(plan.groups):
            for start in range(0, rows, tile):
                product = None
                for array, block, grad in group:
                    origin = plan.origin + (core ^ side) * rows + start
                    if block is not None:
                        origin = origin + (dp ^ block) * plan.block_rows
                    columns = pl.ds(pl.multiple_of(origin, 128), tile)
                    term = lax.dot_general(
                        hidden[array][:, columns],
                        grads[grad][...],
                        TN,
                        preferred_element_type=jnp.float32,
                    )
                    product = term if product is None else product + term
                for inner in range(0, tile, step):
                    part, offset = divmod(start + inner, share)
                    to = pl.multiple_of(at * rows + (z ^ part) * share + offset, step)
                    piece = product[inner : inner + step, :]
                    out_ref[pl.ds(to, step), :] = piece.astype(out_ref.dtype)


def weight_rows(ids, hidden, grads, groups, origin, rows, block_rows, sub_count):
    plan = Plan(
        hidden=len(hidden),
        groups=groups,
        origin=origin,
        rows=rows,
        block_rows=block_rows,
        sub_count=sub_count,
    )
    out = shape_of(rows * len(groups), grads[0].shape[1])
    theirs, ours = kernel_call(
        functools.partial(weight_kernel, plan),
        "weight_rows",
        (out, out),
        (ids,),
        (*hidden, *grads),
    )
    return ours.astype(jnp.float32) + swap(theirs, "ctx", 1).astype(jnp.float32)


def parts_over_dp(array):
    count = lax.axis_size("dp")
    rows = array.shape[0] // count
    parts = [array[j * rows : (j + 1) * rows] for j in range(count)]
    return parts[:1] + [part.astype(jnp.bfloat16) for part in parts[1:]]


def sum_of(arrays):
    total = arrays[0]
    for one in arrays[1:]:
        total = total + one.astype(jnp.float32)
    return total


def z_bits(sub_count):
    return [1 << at for at in range(sub_count.bit_length() - 1)]


def scatter_along_z(full, sub_count, earlier=()):
    share = full.shape[0] // sub_count
    parts = {m: full[m * share : (m + 1) * share] for m in range(sub_count)}
    for bit in z_bits(sub_count):
        for m in list(parts):
            if m & bit:
                came = swap(parts.pop(m).astype(jnp.bfloat16), "ctx", 2 * bit)
                (came,), _ = after([came], *earlier)
                parts[m ^ bit] = parts[m ^ bit] + came.astype(jnp.float32)
    return parts[0]


def sum_of_halves(part, sub_count):
    low = swap(part.astype(jnp.bfloat16), "ctx", 2 * sub_count)
    return (part + low.astype(jnp.float32)).astype(jnp.bfloat16)


def gather_parts(part, sub_count):
    rows = {0: part}
    for bit in z_bits(sub_count)[::-1]:
        rows.update({m | bit: swap(one, "ctx", 2 * bit) for m, one in list(rows.items())})
    own = [rows[m] for m in range(sub_count)]
    return own + [swap(one, "ctx", 1) for one in own]


def assemble_kernel(sub_count, regions, ids, *refs):
    key_ref, value_ref = refs[-2:]
    blocks = iter(refs[:-2])
    z, core = ids[0] % sub_count, ids[1]
    for origin, rows in regions:
        share = rows // sub_count
        for side in range(2):
            for m in range(sub_count):
                to = origin + (core ^ side) * rows + (z ^ m) * share
                to = pl.multiple_of(to, share)
                block_ref = next(blocks)
                width = block_ref.shape[1] // 2
                key_ref[pl.ds(to, share), :] = block_ref[:, :width].astype(jnp.float32)
                value_ref[pl.ds(to, share), :] = block_ref[:, width:].astype(jnp.float32)


def assemble(ids, blocks, sub_count, regions):
    rows = sum(block.shape[0] for block in blocks)
    out = shape_of(rows, blocks[0].shape[1] // 2, jnp.float32)
    return kernel_call(
        functools.partial(assemble_kernel, sub_count, regions),
        "assemble",
        (out, out),
        (ids,),
        blocks,
    )


def on_device(hidden_in, queries, grad_out, w_key, w_value, stretch_order, doc_lengths):
    inputs = hidden_in[0]
    head_dim = w_key.shape[1]
    dp_count = lax.axis_size("dp")
    ctx_count = lax.axis_size("ctx")
    z_count = ctx_count // 2
    sub_count = z_count // 2
    dp, ctx = lax.axis_index("dp"), lax.axis_index("ctx")
    z, core = ctx // 2, ctx % 2
    ids = jnp.stack([z, core, dp]).astype(jnp.int32)
    me = jnp.reshape(ctx, (1,)).astype(jnp.int32)
    block_rows = w_key.shape[0]
    half_rows = block_rows // 2
    quarter = half_rows // 2
    bits = [1 << at for at in range(dp_count.bit_length() - 1)]
    near = [j for j in range(1, dp_count) if j in bits]
    far = [j for j in range(1, dp_count) if j not in bits]

    def gather_near(*weights):
        pieces = {}
        for turn in range(2):
            for at, j in enumerate(near):
                offset = ((at + turn) % 2) * quarter
                start = core * half_rows + offset
                rows = [lax.dynamic_slice_in_dim(weight, start, quarter, 0) for weight in weights]
                pieces[j, 0, offset] = swap(jnp.concatenate(rows, axis=1), "dp", j)
        return pieces

    def gather_far(landed):
        pieces = {}
        for j in far:
            for offset, bit in ((0, 1 << (j.bit_length() - 1)), (quarter, j & -j)):
                origin = landed.get((j ^ bit, 0, offset), pieces.get((j ^ bit, 0, offset)))
                pieces[j, 0, offset] = swap(origin, "dp", bit)
        return pieces

    def from_other_core(pieces):
        return {(j, 1, offset): swap(one, "ctx", 1) for (j, _, offset), one in pieces.items()}

    def hold(arrays, pieces):
        names = list(pieces)
        tied, ended = after(arrays, *[pieces[name] for name in names])
        pieces.update(zip(names, ended))
        return tied

    def gather_along_z(own):
        return [swap(own, "ctx", 2 * m) if m else own for m in range(z_count)]

    def both_cores(along):
        return [block for one in along for block in (one, swap(one, "ctx", 1))]

    sizes = region_sizes(block_rows)
    regions = [(sum(sizes[:at]), size // 2) for at, size in enumerate(sizes)]
    first_rows = sum(sizes[:-1])
    moving = {
        j: lax.dynamic_slice_in_dim(inputs, (dp ^ j) * block_rows, first_rows, 1)
        for j in range(dp_count)
    }

    near_pieces = gather_near(w_key, w_value)
    far_pieces = gather_far(near_pieces)
    near_pieces.update(from_other_core(near_pieces))
    early = project(
        ids, (w_key, w_value), inputs, block_rows, near_pieces, jnp.float32, bytes_cost(1 << 24)
    )
    others = near + far
    early, *tied = hold([early] + [moving[j] for j in others], far_pieces)
    moving.update(zip(others, tied))
    far_pieces.update(from_other_core(far_pieces))
    own = project(ids, (early,), inputs, block_rows, far_pieces, jnp.bfloat16)
    moved = {0: moving[0]}
    moved.update({j: swap(moving[j], "dp", j) for j in near})
    along = gather_along_z(own)
    tied, _ = after([moving[j] for j in far], *along)
    moving.update(zip(far, tied))
    along, _ = after(along)
    kv_blocks = both_cores(along)

    moved.update({j: swap(moving[j], "dp", j) for j in far})

    query_grad, keep, send = attention(
        me, stretch_order, doc_lengths[0], queries[0], grad_out[0], kv_blocks, head_dim
    )
    (send,), ended = after([send], moved[near[0]])
    moved.update(zip(near, ended))
    own, *leaving = add_and_split(keep, swap(send, "ctx", 1), z_count)
    grad = add_all([own] + [swap(one, "ctx", 2 * m) for m, one in enumerate(leaving, 1)])
    grads = [grad] + [swap(grad, "dp", j) for j in range(1, dp_count)]

    (grad,), ended = after([grad], *grads[1:], *[moved[j] for j in others])
    grads[1:] = ended[: dp_count - 1]
    moved.update(zip(others, ended[dp_count - 1 :]))
    groups = [[(0, j, 0)] for j in range(dp_count)]
    own = weight_rows(ids, [inputs], [grad], groups, *regions[-1], block_rows, sub_count)
    own = parts_over_dp(own)
    groups = [[(j, None, j) for j in range(dp_count)]]
    arrays = [moved[j] for j in range(dp_count)]
    moved_parts = [
        weight_rows(ids, arrays, grads, groups, *region, block_rows, sub_count)
        for region in regions[:-1]
    ]
    moved_parts, own = after(moved_parts, *own)
    own = [swap(one, "dp", j) if j else one for j, one in enumerate(own)]
    finals = []
    for part in moved_parts:
        part = scatter_along_z(part, sub_count)
        finals.append(sum_of_halves(part, sub_count))
    part = scatter_along_z(sum_of(own), sub_count, finals[:TIED])
    finals.append(sum_of_halves(part, sub_count))
    blocks = [one for final in finals for one in gather_parts(final, sub_count)]
    key_rows, value_rows = assemble(ids, blocks, sub_count, regions)
    return query_grad[None], key_rows, value_rows


def solution(mesh):
    return jax.shard_map(
        on_device,
        mesh=mesh,
        in_specs=(
            P("dp", "ctx", None),
            P("dp", "ctx", None),
            P("dp", "ctx", None),
            P("dp", None),
            P("dp", None),
            P(),
            P("dp", None),
        ),
        out_specs=(P("dp", "ctx", None), P("dp", None), P("dp", None)),
        check_vma=False,
    )
```

```python
import functools
import math

import jax
import jax.numpy as jnp
from jax import lax
from jax.experimental import pallas as pl
from jax.experimental.pallas import tpu as pltpu
from jax.sharding import PartitionSpec as P

VMEM_LIMIT = 28 * 1024 * 1024
NO_COST = pl.CostEstimate(flops=0, bytes_accessed=0, transcendentals=0)


MOVED = (4, 6)
TIED = 2


def region_sizes(block_rows):
    units = block_rows // 256
    sizes = [256 * (units * share // 16) for share in MOVED]
    return sizes + [block_rows - sum(sizes)]


class Plan:
    def __init__(self, **fields):
        self.__dict__.update(fields)


def swap(array, axis, distance):
    count = lax.axis_size(axis)
    return lax.ppermute(array, axis, [(i, i ^ distance) for i in range(count)])


def after(arrays, *earlier):
    tied = lax.optimization_barrier((tuple(arrays), tuple(earlier)))
    return list(tied[0]), list(tied[1])


def shape_of(rows, width, kind=jnp.bfloat16):
    return jax.ShapeDtypeStruct((rows, width), kind)


def kernel_call(kernel, name, outs, scalars, arrays, scratch=(), cost=NO_COST):
    smem = pl.BlockSpec(memory_space=pltpu.SMEM)
    vmem = pl.BlockSpec(memory_space=pltpu.VMEM)
    single = not isinstance(outs, tuple)
    return pl.pallas_call(
        kernel,
        out_shape=outs,
        in_specs=[smem] * len(scalars) + [vmem] * len(arrays),
        out_specs=vmem if single else (vmem,) * len(outs),
        scratch_shapes=list(scratch),
        compiler_params=pltpu.CompilerParams(vmem_limit_bytes=VMEM_LIMIT),
        cost_estimate=cost,
        name=name,
    )(*scalars, *arrays)


def bytes_cost(amount):
    return pl.CostEstimate(flops=0, bytes_accessed=amount, transcendentals=0)


TN = (((0,), (0,)), ((), ()))


def attention_kernel(
    shape, ids, order, lengths, q_ref, g_ref, *refs
):
    ctx_count, stretch_rows, head_count, head_dim, window, chunk = shape
    kv_refs = refs[:ctx_count]
    qgrad_ref, keep_ref, send_ref, keys, values, total, qs, gs, dqs = refs[ctx_count:]
    me = ids[0]
    row_count = 2 * stretch_rows
    stretch_count = 2 * ctx_count
    score_scale = 1.0 / math.sqrt(head_dim)

    def place(device, half):
        return pl.multiple_of(order[2 * device + half] * stretch_rows, stretch_rows)

    for index in range(ctx_count):
        for half in range(2):
            rows = pl.ds(place(me ^ index, half), stretch_rows)
            block = kv_refs[index][half * stretch_rows : (half + 1) * stretch_rows, :]
            keys[rows, :] = block[:, :head_dim]
            values[rows, :] = block[:, head_dim:]
    total[...] = jnp.zeros_like(total)
    for half in range(2):
        for head in range(head_count):
            to = slice((half * head_count + head) * stretch_rows, (half * head_count + head + 1) * stretch_rows)
            rows = slice(half * stretch_rows, (half + 1) * stretch_rows)
            columns = slice(head * head_dim, (head + 1) * head_dim)
            qs[to, :] = q_ref[rows, columns]
            gs[to, :] = g_ref[rows, columns]
    ends = []
    running = 0
    for at in range(lengths.shape[0]):
        running = running + lengths[at]
        ends.append(running)
    chunks_half = head_count * stretch_rows // chunk

    def step(at, carry):
        half = at // chunks_half
        block = order[2 * me + half]
        first = jnp.maximum(block - stretch_count // 2, 0) * stretch_rows
        first = pl.multiple_of(first, stretch_rows)
        part = pl.ds(pl.multiple_of(at * chunk, chunk), chunk)
        inside = (at - half * chunks_half) * chunk + lax.broadcasted_iota(jnp.int32, (1, chunk), 1)
        at_query = block * stretch_rows + lax.rem(inside, stretch_rows)
        begin = jnp.zeros_like(at_query)
        for end in ends:
            begin = jnp.where(at_query >= end, end, begin)
        at_key = first + lax.broadcasted_iota(jnp.int32, (window, chunk), 0)
        allowed = (at_key >= begin) & (at_key <= at_query)
        k = keys[pl.ds(first, window), :]
        v = values[pl.ds(first, window), :]
        q = qs[part, :]
        g = gs[part, :]
        last = (((1,), (1,)), ((), ()))
        scores = lax.dot_general(k, q, last, preferred_element_type=jnp.float32)
        masked = jnp.where(allowed, scores, -jnp.inf)
        largest = jnp.max(masked, axis=0, keepdims=True)
        expsum = jnp.exp2((masked - largest) * (score_scale * math.log2(math.e)))
        probs = expsum * (1.0 / jnp.sum(expsum, axis=0, keepdims=True))
        probs_low = probs.astype(jnp.bfloat16)
        dprob = lax.dot_general(v, g, last, preferred_element_type=jnp.float32)
        delta = jnp.sum(probs_low.astype(jnp.float32) * dprob, axis=0, keepdims=True)
        dscore = (probs * (dprob - delta)).astype(jnp.bfloat16)
        dq = lax.dot_general(
            k, dscore, (((0,), (0,)), ((), ())), preferred_element_type=jnp.float32
        )
        dqs[part, :] = (jnp.transpose(dq) * score_scale).astype(jnp.bfloat16)
        dk = jnp.dot(dscore, q, preferred_element_type=jnp.float32) * score_scale
        dv = jnp.dot(probs_low, g, preferred_element_type=jnp.float32)
        total[pl.ds(first, window), :head_dim] += dk
        total[pl.ds(first, window), head_dim:] += dv
        return carry

    lax.fori_loop(0, 2 * chunks_half, step, 0, unroll=2)
    for half in range(2):
        for head in range(head_count):
            origin = slice((half * head_count + head) * stretch_rows, (half * head_count + head + 1) * stretch_rows)
            rows = slice(half * stretch_rows, (half + 1) * stretch_rows)
            columns = slice(head * head_dim, (head + 1) * head_dim)
            qgrad_ref[rows, columns] = dqs[origin, :]
    for index in range(ctx_count):
        for half in range(2):
            rows = pl.ds(place(me ^ index, half), stretch_rows)
            start = (index // 2) * row_count + half * stretch_rows
            if index % 2:
                send_ref[start : start + stretch_rows, :] = total[rows, :].astype(jnp.bfloat16)
            else:
                keep_ref[start : start + stretch_rows, :] = total[rows, :]


def attention(me, order, lengths, queries, cotangent, kv_blocks, head_dim):
    row_count, width = queries.shape
    ctx_count = len(kv_blocks)
    stretch_rows = row_count // 2
    head_count = width // head_dim
    seq_rows = row_count * ctx_count
    window = seq_rows // 2 + stretch_rows
    stacked = head_count * stretch_rows
    chunk = 256 if stacked % 256 == 0 else 128
    shape = (ctx_count, stretch_rows, head_count, head_dim, window, chunk)
    smem = pl.BlockSpec(memory_space=pltpu.SMEM)
    vmem = pl.BlockSpec(memory_space=pltpu.VMEM)
    half_rows = seq_rows // 2
    return pl.pallas_call(
        functools.partial(attention_kernel, shape),
        out_shape=(
            jax.ShapeDtypeStruct((row_count, width), jnp.bfloat16),
            jax.ShapeDtypeStruct((half_rows, 2 * head_dim), jnp.float32),
            jax.ShapeDtypeStruct((half_rows, 2 * head_dim), jnp.bfloat16),
        ),
        in_specs=[smem] * 3 + [vmem] * (2 + ctx_count),
        out_specs=(vmem,) * 3,
        scratch_shapes=[
            pltpu.VMEM((seq_rows, head_dim), jnp.bfloat16),
            pltpu.VMEM((seq_rows, head_dim), jnp.bfloat16),
            pltpu.VMEM((seq_rows, 2 * head_dim), jnp.float32),
            pltpu.VMEM((2 * stacked, head_dim), jnp.bfloat16),
            pltpu.VMEM((2 * stacked, head_dim), jnp.bfloat16),
            pltpu.VMEM((2 * stacked, head_dim), jnp.bfloat16),
        ],
        compiler_params=pltpu.CompilerParams(vmem_limit_bytes=VMEM_LIMIT),
        cost_estimate=NO_COST,
        name="attention",
    )(me, order, lengths, queries, cotangent, *kv_blocks)


def project_kernel(plan, ids, hidden, *refs):
    out_ref = refs[-1]
    dp, core = ids[2], ids[1]
    if plan.start:
        total = refs[0][...]
    else:
        columns = pl.ds(pl.multiple_of(dp * plan.block_rows, plan.block_rows), plan.block_rows)
        total = jnp.concatenate(
            [
                jnp.dot(hidden[:, columns], own[...], preferred_element_type=jnp.float32)
                for own in refs[:2]
            ],
            axis=1,
        )
    for (block, side, offset), weight in zip(plan.terms, refs[1 if plan.start else 2 : -1]):
        from_column = (dp ^ block) * plan.block_rows + (core ^ side) * plan.side_rows + offset
        columns = pl.ds(pl.multiple_of(from_column, 128), weight.shape[0])
        total += jnp.dot(hidden[:, columns], weight[...], preferred_element_type=jnp.float32)
    out_ref[...] = total.astype(out_ref.dtype)


def project(ids, begin, inputs, block_rows, pieces, kind, cost=NO_COST):
    names = sorted(pieces)
    weights = [pieces[name] for name in names]
    plan = Plan(
        terms=names, start=len(begin) == 1, block_rows=block_rows, side_rows=block_rows // 2
    )
    return kernel_call(
        functools.partial(project_kernel, plan),
        "project",
        shape_of(inputs.shape[0], weights[0].shape[1], kind),
        (ids,),
        (inputs, *begin, *weights),
        cost=cost,
    )


def split_kernel(rows, keep, came, own_ref, *leaving_refs):
    own_ref[...] = keep[:rows, :] + came[:rows, :].astype(jnp.float32)
    for m, leaving in enumerate(leaving_refs, 1):
        block = slice(m * rows, (m + 1) * rows)
        leaving[...] = (keep[block, :] + came[block, :].astype(jnp.float32)).astype(leaving.dtype)


def add_and_split(keep, came, count):
    rows, width = keep.shape[0] // count, keep.shape[1]
    outs = (shape_of(rows, width, jnp.float32),) + (shape_of(rows, width),) * (count - 1)
    return kernel_call(functools.partial(split_kernel, rows), "split", outs, (), (keep, came))


def total_kernel(*refs):
    total = refs[0][...]
    for one in refs[1:-1]:
        total = total + one[...].astype(jnp.float32)
    refs[-1][...] = total.astype(refs[-1].dtype)


def add_all(arrays):
    out = jax.ShapeDtypeStruct(arrays[0].shape, jnp.bfloat16)
    return kernel_call(total_kernel, "total", out, (), arrays)


def weight_kernel(plan, ids, *refs):
    hidden = refs[: plan.hidden]
    grads = refs[plan.hidden : -2]
    z, core, dp = ids[0] % plan.sub_count, ids[1], ids[2]
    rows = plan.rows
    share = rows // plan.sub_count
    tile = next(size for size in (512, 256, 128) if rows % size == 0)
    step = math.gcd(share, tile)
    for side, out_ref in ((1, refs[-2]), (0, refs[-1])):
        for at, group in enumerate(plan.groups):
            for start in range(0, rows, tile):
                product = None
                for array, block, grad, shift in group:
                    origin = plan.origin - shift + (core ^ side) * rows + start
                    if block is not None:
                        origin = origin + (dp ^ block) * plan.block_rows
                    columns = pl.ds(pl.multiple_of(origin, 128), tile)
                    term = lax.dot_general(
                        hidden[array][:, columns],
                        grads[grad][...],
                        TN,
                        preferred_element_type=jnp.float32,
                    )
                    product = term if product is None else product + term
                for inner in range(0, tile, step):
                    part, offset = divmod(start + inner, share)
                    to = pl.multiple_of(at * rows + (z ^ part) * share + offset, step)
                    piece = product[inner : inner + step, :]
                    out_ref[pl.ds(to, step), :] = piece.astype(out_ref.dtype)


def weight_rows(ids, hidden, grads, groups, origin, rows, block_rows, sub_count):
    plan = Plan(
        hidden=len(hidden),
        groups=groups,
        origin=origin,
        rows=rows,
        block_rows=block_rows,
        sub_count=sub_count,
    )
    out = shape_of(rows * len(groups), grads[0].shape[1])
    theirs, ours = kernel_call(
        functools.partial(weight_kernel, plan),
        "weight_rows",
        (out, out),
        (ids,),
        (*hidden, *grads),
    )
    return ours, swap(theirs, "ctx", 1)


def add_cores(ours, came):
    return ours.astype(jnp.float32) + came.astype(jnp.float32)


def parts_over_dp(array):
    count = lax.axis_size("dp")
    rows = array.shape[0] // count
    parts = [array[j * rows : (j + 1) * rows] for j in range(count)]
    return parts[:1] + [part.astype(jnp.bfloat16) for part in parts[1:]]


def sum_of(arrays):
    total = arrays[0]
    for one in arrays[1:]:
        total = total + one.astype(jnp.float32)
    return total


def z_bits(sub_count):
    return [1 << at for at in range(sub_count.bit_length() - 1)]


def scatter_along_z(full, sub_count, earlier=()):
    share = full.shape[0] // sub_count
    parts = {m: full[m * share : (m + 1) * share] for m in range(sub_count)}
    for bit in z_bits(sub_count):
        for m in list(parts):
            if m & bit:
                came = swap(parts.pop(m).astype(jnp.bfloat16), "ctx", 2 * bit)
                (came,), _ = after([came], *earlier)
                parts[m ^ bit] = parts[m ^ bit] + came.astype(jnp.float32)
    return parts[0]


def sum_of_halves(part, sub_count):
    low = swap(part.astype(jnp.bfloat16), "ctx", 2 * sub_count)
    return (part + low.astype(jnp.float32)).astype(jnp.bfloat16)


def gather_parts(part, sub_count):
    rows = {0: part}
    for bit in z_bits(sub_count)[::-1]:
        rows.update({m | bit: swap(one, "ctx", 2 * bit) for m, one in list(rows.items())})
    own = [rows[m] for m in range(sub_count)]
    return own + [swap(one, "ctx", 1) for one in own]


def assemble_kernel(sub_count, regions, ids, *refs):
    key_ref, value_ref = refs[-2:]
    blocks = iter(refs[:-2])
    z, core = ids[0] % sub_count, ids[1]
    for origin, rows in regions:
        share = rows // sub_count
        for side in range(2):
            for m in range(sub_count):
                to = origin + (core ^ side) * rows + (z ^ m) * share
                to = pl.multiple_of(to, share)
                block_ref = next(blocks)
                width = block_ref.shape[1] // 2
                key_ref[pl.ds(to, share), :] = block_ref[:, :width].astype(jnp.float32)
                value_ref[pl.ds(to, share), :] = block_ref[:, width:].astype(jnp.float32)


def assemble(ids, blocks, sub_count, regions):
    rows = sum(block.shape[0] for block in blocks)
    out = shape_of(rows, blocks[0].shape[1] // 2, jnp.float32)
    return kernel_call(
        functools.partial(assemble_kernel, sub_count, regions),
        "assemble",
        (out, out),
        (ids,),
        blocks,
    )


def on_device(hidden_in, queries, grad_out, w_key, w_value, stretch_order, doc_lengths):
    inputs = hidden_in[0]
    head_dim = w_key.shape[1]
    dp_count = lax.axis_size("dp")
    ctx_count = lax.axis_size("ctx")
    z_count = ctx_count // 2
    sub_count = z_count // 2
    dp, ctx = lax.axis_index("dp"), lax.axis_index("ctx")
    z, core = ctx // 2, ctx % 2
    ids = jnp.stack([z, core, dp]).astype(jnp.int32)
    me = jnp.reshape(ctx, (1,)).astype(jnp.int32)
    block_rows = w_key.shape[0]
    half_rows = block_rows // 2
    quarter = half_rows // 2
    bits = [1 << at for at in range(dp_count.bit_length() - 1)]
    near = [j for j in range(1, dp_count) if j in bits]
    far = [j for j in range(1, dp_count) if j not in bits]

    def gather_near(*weights):
        pieces = {}
        for turn in range(2):
            for at, j in enumerate(near):
                offset = ((at + turn) % 2) * quarter
                start = core * half_rows + offset
                rows = [lax.dynamic_slice_in_dim(weight, start, quarter, 0) for weight in weights]
                pieces[j, 0, offset] = swap(jnp.concatenate(rows, axis=1), "dp", j)
        return pieces

    def gather_far(landed):
        pieces = {}
        for j in far:
            for offset, bit in ((0, 1 << (j.bit_length() - 1)), (quarter, j & -j)):
                origin = landed.get((j ^ bit, 0, offset), pieces.get((j ^ bit, 0, offset)))
                pieces[j, 0, offset] = swap(origin, "dp", bit)
        return pieces

    def from_other_core(pieces):
        return {(j, 1, offset): swap(one, "ctx", 1) for (j, _, offset), one in pieces.items()}

    def hold(arrays, pieces):
        names = list(pieces)
        tied, ended = after(arrays, *[pieces[name] for name in names])
        pieces.update(zip(names, ended))
        return tied

    def gather_along_z(own):
        return [swap(own, "ctx", 2 * m) if m else own for m in range(z_count)]

    def both_cores(along):
        return [block for one in along for block in (one, swap(one, "ctx", 1))]

    sizes = region_sizes(block_rows)
    regions = [(sum(sizes[:at]), size // 2) for at, size in enumerate(sizes)]
    first_rows = sum(sizes[:-1])
    def columns(j, start, count):
        return lax.dynamic_slice_in_dim(inputs, (dp ^ j) * block_rows + start, count, 1)

    moving = {j: columns(j, 0, first_rows) for j in range(dp_count) if j != near[-1]}
    cuts = {"early": (near[-1], sizes[0], sizes[1]), "late": (near[-1], 0, sizes[0])}
    moving.update({name: columns(*cut) for name, cut in cuts.items()})

    near_pieces = gather_near(w_key, w_value)
    far_pieces = gather_far(near_pieces)
    near_pieces.update(from_other_core(near_pieces))
    early = project(
        ids, (w_key, w_value), inputs, block_rows, near_pieces, jnp.float32, bytes_cost(1 << 24)
    )
    others = [j for j in near if j in moving] + far + list(cuts)
    early, *tied = hold([early] + [moving[j] for j in others], far_pieces)
    moving.update(zip(others, tied))
    far_pieces.update(from_other_core(far_pieces))
    own = project(ids, (early,), inputs, block_rows, far_pieces, jnp.bfloat16)
    moved = {0: moving[0]}
    moved.update({j: swap(moving[j], "dp", j) for j in near if j in moving})
    moved["early"] = swap(moving["early"], "dp", near[-1])
    along = gather_along_z(own)
    rest = ["late"] + far
    tied, _ = after([moving[j] for j in rest], *along)
    moving.update(zip(rest, tied))
    along, _ = after(along)
    kv_blocks = both_cores(along)

    moved["late"] = swap(moving["late"], "dp", near[-1])
    moved.update({j: swap(moving[j], "dp", j) for j in far})

    query_grad, keep, send = attention(
        me, stretch_order, doc_lengths[0], queries[0], grad_out[0], kv_blocks, head_dim
    )
    soon = [j for j in moved if j and j not in rest]
    (send,), ended = after([send], *[moved[j] for j in soon])
    moved.update(zip(soon, ended))
    own, *leaving = add_and_split(keep, swap(send, "ctx", 1), z_count)
    grad = add_all([own] + [swap(one, "ctx", 2 * m) for m, one in enumerate(leaving, 1)])
    grads = [grad] + [swap(grad, "dp", j) for j in range(1, dp_count)]

    (grad,), ended = after([grad], *grads[1:], *[moved[j] for j in rest])
    grads[1:] = ended[: dp_count - 1]
    moved.update(zip(rest, ended[dp_count - 1 :]))
    groups = [[(0, j, 0, 0)] for j in range(dp_count)]
    ours, came = weight_rows(
        ids, [inputs], [grad], groups, *regions[-1], block_rows, sub_count
    )
    own = parts_over_dp(add_cores(ours, came))
    moved_parts = []
    for region, name in zip(regions[:-1], ("late", "early")):
        arrays = [moved[name if j == near[-1] else j] for j in range(dp_count)]
        shifts = [cuts[name][1] if j == near[-1] else 0 for j in range(dp_count)]
        groups = [[(j, None, j, shifts[j]) for j in range(dp_count)]]
        pair = weight_rows(ids, arrays, grads, groups, *region, block_rows, sub_count)
        moved_parts.append(add_cores(*pair))
    moved_parts, own = after(moved_parts, *own)
    own = [swap(one, "dp", j) if j else one for j, one in enumerate(own)]
    finals = []
    for part in moved_parts:
        part = scatter_along_z(part, sub_count)
        finals.append(sum_of_halves(part, sub_count))
    part = scatter_along_z(sum_of(own), sub_count, finals[:TIED])
    finals.append(sum_of_halves(part, sub_count))
    blocks = [one for final in finals for one in gather_parts(final, sub_count)]
    key_rows, value_rows = assemble(ids, blocks, sub_count, regions)
    return query_grad[None], key_rows, value_rows


def solution(mesh):
    return jax.shard_map(
        on_device,
        mesh=mesh,
        in_specs=(
            P("dp", "ctx", None),
            P("dp", "ctx", None),
            P("dp", "ctx", None),
            P("dp", None),
            P("dp", None),
            P(),
            P("dp", None),
        ),
        out_specs=(P("dp", "ctx", None), P("dp", None), P("dp", None)),
        check_vma=False,
    )
```

```python
import functools
import math

import jax
import jax.numpy as jnp
from jax import lax
from jax.experimental import pallas as pl
from jax.experimental.pallas import tpu as pltpu
from jax.sharding import PartitionSpec as P

VMEM_LIMIT = 28 * 1024 * 1024
NO_COST = pl.CostEstimate(flops=0, bytes_accessed=0, transcendentals=0)


MOVED = (4, 6)
TIED = 2


def region_sizes(block_rows):
    units = block_rows // 256
    sizes = [256 * (units * share // 16) for share in MOVED]
    return sizes + [block_rows - sum(sizes)]


class Plan:
    def __init__(self, **fields):
        self.__dict__.update(fields)


def swap(array, axis, distance):
    count = lax.axis_size(axis)
    return lax.ppermute(array, axis, [(i, i ^ distance) for i in range(count)])


def after(arrays, *earlier):
    tied = lax.optimization_barrier((tuple(arrays), tuple(earlier)))
    return list(tied[0]), list(tied[1])


def shape_of(rows, width, kind=jnp.bfloat16):
    return jax.ShapeDtypeStruct((rows, width), kind)


def kernel_call(kernel, name, outs, scalars, arrays, scratch=(), cost=NO_COST):
    smem = pl.BlockSpec(memory_space=pltpu.SMEM)
    vmem = pl.BlockSpec(memory_space=pltpu.VMEM)
    single = not isinstance(outs, tuple)
    return pl.pallas_call(
        kernel,
        out_shape=outs,
        in_specs=[smem] * len(scalars) + [vmem] * len(arrays),
        out_specs=vmem if single else (vmem,) * len(outs),
        scratch_shapes=list(scratch),
        compiler_params=pltpu.CompilerParams(vmem_limit_bytes=VMEM_LIMIT),
        cost_estimate=cost,
        name=name,
    )(*scalars, *arrays)


def bytes_cost(amount):
    return pl.CostEstimate(flops=0, bytes_accessed=amount, transcendentals=0)


TN = (((0,), (0,)), ((), ()))


def attention_kernel(
    shape, ids, order, lengths, q_ref, g_ref, *refs
):
    ctx_count, stretch_rows, head_count, head_dim, window, chunk = shape
    kv_refs = refs[:ctx_count]
    qgrad_ref, keep_ref, send_ref, keys, values, total, qs, gs, dqs = refs[ctx_count:]
    me = ids[0]
    row_count = 2 * stretch_rows
    stretch_count = 2 * ctx_count
    score_scale = 1.0 / math.sqrt(head_dim)

    def place(device, half):
        return pl.multiple_of(order[2 * device + half] * stretch_rows, stretch_rows)

    for index in range(ctx_count):
        for half in range(2):
            rows = pl.ds(place(me ^ index, half), stretch_rows)
            block = kv_refs[index][half * stretch_rows : (half + 1) * stretch_rows, :]
            keys[rows, :] = block[:, :head_dim]
            values[rows, :] = block[:, head_dim:]
    total[...] = jnp.zeros_like(total)
    for half in range(2):
        for head in range(head_count):
            to = slice((half * head_count + head) * stretch_rows, (half * head_count + head + 1) * stretch_rows)
            rows = slice(half * stretch_rows, (half + 1) * stretch_rows)
            columns = slice(head * head_dim, (head + 1) * head_dim)
            qs[to, :] = q_ref[rows, columns]
            gs[to, :] = g_ref[rows, columns]
    ends = []
    running = 0
    for at in range(lengths.shape[0]):
        running = running + lengths[at]
        ends.append(running)
    chunks_half = head_count * stretch_rows // chunk

    def step(at, carry):
        half = at // chunks_half
        block = order[2 * me + half]
        first = jnp.maximum(block - stretch_count // 2, 0) * stretch_rows
        first = pl.multiple_of(first, stretch_rows)
        part = pl.ds(pl.multiple_of(at * chunk, chunk), chunk)
        inside = (at - half * chunks_half) * chunk + lax.broadcasted_iota(jnp.int32, (1, chunk), 1)
        at_query = block * stretch_rows + lax.rem(inside, stretch_rows)
        begin = jnp.zeros_like(at_query)
        for end in ends:
            begin = jnp.where(at_query >= end, end, begin)
        at_key = first + lax.broadcasted_iota(jnp.int32, (window, chunk), 0)
        allowed = (at_key >= begin) & (at_key <= at_query)
        k = keys[pl.ds(first, window), :]
        v = values[pl.ds(first, window), :]
        q = qs[part, :]
        g = gs[part, :]
        last = (((1,), (1,)), ((), ()))
        scores = lax.dot_general(k, q, last, preferred_element_type=jnp.float32)
        masked = jnp.where(allowed, scores, -jnp.inf)
        largest = jnp.max(masked, axis=0, keepdims=True)
        expsum = jnp.exp2((masked - largest) * (score_scale * math.log2(math.e)))
        probs = expsum * (1.0 / jnp.sum(expsum, axis=0, keepdims=True))
        probs_low = probs.astype(jnp.bfloat16)
        dprob = lax.dot_general(v, g, last, preferred_element_type=jnp.float32)
        delta = jnp.sum(probs_low.astype(jnp.float32) * dprob, axis=0, keepdims=True)
        dscore = (probs * (dprob - delta)).astype(jnp.bfloat16)
        dq = lax.dot_general(
            k, dscore, (((0,), (0,)), ((), ())), preferred_element_type=jnp.float32
        )
        dqs[part, :] = (jnp.transpose(dq) * score_scale).astype(jnp.bfloat16)
        dk = jnp.dot(dscore, q, preferred_element_type=jnp.float32) * score_scale
        dv = jnp.dot(probs_low, g, preferred_element_type=jnp.float32)
        total[pl.ds(first, window), :head_dim] += dk
        total[pl.ds(first, window), head_dim:] += dv
        return carry

    lax.fori_loop(0, 2 * chunks_half, step, 0, unroll=2)
    for half in range(2):
        for head in range(head_count):
            origin = slice((half * head_count + head) * stretch_rows, (half * head_count + head + 1) * stretch_rows)
            rows = slice(half * stretch_rows, (half + 1) * stretch_rows)
            columns = slice(head * head_dim, (head + 1) * head_dim)
            qgrad_ref[rows, columns] = dqs[origin, :]
    for index in range(ctx_count):
        for half in range(2):
            rows = pl.ds(place(me ^ index, half), stretch_rows)
            start = (index // 2) * row_count + half * stretch_rows
            if index % 2:
                send_ref[start : start + stretch_rows, :] = total[rows, :].astype(jnp.bfloat16)
            else:
                keep_ref[start : start + stretch_rows, :] = total[rows, :]


def attention(me, order, lengths, queries, cotangent, kv_blocks, head_dim):
    row_count, width = queries.shape
    ctx_count = len(kv_blocks)
    stretch_rows = row_count // 2
    head_count = width // head_dim
    seq_rows = row_count * ctx_count
    window = seq_rows // 2 + stretch_rows
    stacked = head_count * stretch_rows
    chunk = 256 if stacked % 256 == 0 else 128
    shape = (ctx_count, stretch_rows, head_count, head_dim, window, chunk)
    smem = pl.BlockSpec(memory_space=pltpu.SMEM)
    vmem = pl.BlockSpec(memory_space=pltpu.VMEM)
    half_rows = seq_rows // 2
    return pl.pallas_call(
        functools.partial(attention_kernel, shape),
        out_shape=(
            jax.ShapeDtypeStruct((row_count, width), jnp.bfloat16),
            jax.ShapeDtypeStruct((half_rows, 2 * head_dim), jnp.float32),
            jax.ShapeDtypeStruct((half_rows, 2 * head_dim), jnp.bfloat16),
        ),
        in_specs=[smem] * 3 + [vmem] * (2 + ctx_count),
        out_specs=(vmem,) * 3,
        scratch_shapes=[
            pltpu.VMEM((seq_rows, head_dim), jnp.bfloat16),
            pltpu.VMEM((seq_rows, head_dim), jnp.bfloat16),
            pltpu.VMEM((seq_rows, 2 * head_dim), jnp.float32),
            pltpu.VMEM((2 * stacked, head_dim), jnp.bfloat16),
            pltpu.VMEM((2 * stacked, head_dim), jnp.bfloat16),
            pltpu.VMEM((2 * stacked, head_dim), jnp.bfloat16),
        ],
        compiler_params=pltpu.CompilerParams(vmem_limit_bytes=VMEM_LIMIT),
        cost_estimate=NO_COST,
        name="attention",
    )(me, order, lengths, queries, cotangent, *kv_blocks)


def project_kernel(plan, ids, hidden, *refs):
    out_ref = refs[-1]
    dp, core = ids[2], ids[1]
    if plan.start:
        total = refs[0][...]
    else:
        columns = pl.ds(pl.multiple_of(dp * plan.block_rows, plan.block_rows), plan.block_rows)
        total = jnp.concatenate(
            [
                jnp.dot(hidden[:, columns], own[...], preferred_element_type=jnp.float32)
                for own in refs[:2]
            ],
            axis=1,
        )
    for (block, side, offset), weight in zip(plan.terms, refs[1 if plan.start else 2 : -1]):
        from_column = (dp ^ block) * plan.block_rows + (core ^ side) * plan.side_rows + offset
        columns = pl.ds(pl.multiple_of(from_column, 128), weight.shape[0])
        total += jnp.dot(hidden[:, columns], weight[...], preferred_element_type=jnp.float32)
    out_ref[...] = total.astype(out_ref.dtype)


def project(ids, begin, inputs, block_rows, pieces, kind, cost=NO_COST):
    names = sorted(pieces)
    weights = [pieces[name] for name in names]
    plan = Plan(
        terms=names, start=len(begin) == 1, block_rows=block_rows, side_rows=block_rows // 2
    )
    return kernel_call(
        functools.partial(project_kernel, plan),
        "project",
        shape_of(inputs.shape[0], weights[0].shape[1], kind),
        (ids,),
        (inputs, *begin, *weights),
        cost=cost,
    )


def split_kernel(rows, keep, came, own_ref, *leaving_refs):
    own_ref[...] = keep[:rows, :] + came[:rows, :].astype(jnp.float32)
    for m, leaving in enumerate(leaving_refs, 1):
        block = slice(m * rows, (m + 1) * rows)
        leaving[...] = (keep[block, :] + came[block, :].astype(jnp.float32)).astype(leaving.dtype)


def add_and_split(keep, came, count):
    rows, width = keep.shape[0] // count, keep.shape[1]
    outs = (shape_of(rows, width, jnp.float32),) + (shape_of(rows, width),) * (count - 1)
    return kernel_call(functools.partial(split_kernel, rows), "split", outs, (), (keep, came))


def total_kernel(*refs):
    total = refs[0][...]
    for one in refs[1:-1]:
        total = total + one[...].astype(jnp.float32)
    refs[-1][...] = total.astype(refs[-1].dtype)


def add_all(arrays):
    out = jax.ShapeDtypeStruct(arrays[0].shape, jnp.bfloat16)
    return kernel_call(total_kernel, "total", out, (), arrays)


def weight_kernel(plan, ids, *refs):
    hidden = refs[: plan.hidden]
    grads = refs[plan.hidden : -2]
    z, core, dp = ids[0] % plan.sub_count, ids[1], ids[2]
    rows = plan.rows
    share = rows // plan.sub_count
    tile = next(size for size in (512, 256, 128) if rows % size == 0)
    step = math.gcd(share, tile)
    for side, out_ref in ((1, refs[-2]), (0, refs[-1])):
        for at, group in enumerate(plan.groups):
            for start in range(0, rows, tile):
                product = None
                for array, block, grad, shift in group:
                    origin = plan.origin - shift + (core ^ side) * rows + start
                    if block is not None:
                        origin = origin + (dp ^ block) * plan.block_rows
                    columns = pl.ds(pl.multiple_of(origin, 128), tile)
                    term = lax.dot_general(
                        hidden[array][:, columns],
                        grads[grad][...],
                        TN,
                        preferred_element_type=jnp.float32,
                    )
                    product = term if product is None else product + term
                for inner in range(0, tile, step):
                    part, offset = divmod(start + inner, share)
                    to = pl.multiple_of(at * rows + (z ^ part) * share + offset, step)
                    piece = product[inner : inner + step, :]
                    out_ref[pl.ds(to, step), :] = piece.astype(out_ref.dtype)


def weight_rows(ids, hidden, grads, groups, origin, rows, block_rows, sub_count):
    plan = Plan(
        hidden=len(hidden),
        groups=groups,
        origin=origin,
        rows=rows,
        block_rows=block_rows,
        sub_count=sub_count,
    )
    out = shape_of(rows * len(groups), grads[0].shape[1])
    theirs, ours = kernel_call(
        functools.partial(weight_kernel, plan),
        "weight_rows",
        (out, out),
        (ids,),
        (*hidden, *grads),
    )
    return ours, swap(theirs, "ctx", 1)


def add_cores(ours, came):
    return ours.astype(jnp.float32) + came.astype(jnp.float32)


def parts_over_dp(array):
    count = lax.axis_size("dp")
    rows = array.shape[0] // count
    parts = [array[j * rows : (j + 1) * rows] for j in range(count)]
    return parts[:1] + [part.astype(jnp.bfloat16) for part in parts[1:]]


def sum_of(arrays):
    total = arrays[0]
    for one in arrays[1:]:
        total = total + one.astype(jnp.float32)
    return total


def z_bits(sub_count):
    return [1 << at for at in range(sub_count.bit_length() - 1)]


def scatter_along_z(full, sub_count, earlier=()):
    share = full.shape[0] // sub_count
    parts = {m: full[m * share : (m + 1) * share] for m in range(sub_count)}
    for bit in z_bits(sub_count):
        for m in list(parts):
            if m & bit:
                came = swap(parts.pop(m).astype(jnp.bfloat16), "ctx", 2 * bit)
                (came,), _ = after([came], *earlier)
                parts[m ^ bit] = parts[m ^ bit] + came.astype(jnp.float32)
    return parts[0]


def sum_of_halves(part, sub_count, earlier=()):
    low = swap(part.astype(jnp.bfloat16), "ctx", 2 * sub_count)
    (low,), _ = after([low], *earlier)
    return (part + low.astype(jnp.float32)).astype(jnp.bfloat16)


def gather_parts(part, sub_count):
    rows = {0: part}
    for bit in z_bits(sub_count)[::-1]:
        rows.update({m | bit: swap(one, "ctx", 2 * bit) for m, one in list(rows.items())})
    own = [rows[m] for m in range(sub_count)]
    return own + [swap(one, "ctx", 1) for one in own]


def assemble_kernel(sub_count, regions, ids, *refs):
    key_ref, value_ref = refs[-2:]
    blocks = iter(refs[:-2])
    z, core = ids[0] % sub_count, ids[1]
    for origin, rows in regions:
        share = rows // sub_count
        for side in range(2):
            for m in range(sub_count):
                to = origin + (core ^ side) * rows + (z ^ m) * share
                to = pl.multiple_of(to, share)
                block_ref = next(blocks)
                width = block_ref.shape[1] // 2
                key_ref[pl.ds(to, share), :] = block_ref[:, :width].astype(jnp.float32)
                value_ref[pl.ds(to, share), :] = block_ref[:, width:].astype(jnp.float32)


def assemble(ids, blocks, sub_count, regions):
    rows = sum(block.shape[0] for block in blocks)
    out = shape_of(rows, blocks[0].shape[1] // 2, jnp.float32)
    return kernel_call(
        functools.partial(assemble_kernel, sub_count, regions),
        "assemble",
        (out, out),
        (ids,),
        blocks,
    )


def on_device(hidden_in, queries, grad_out, w_key, w_value, stretch_order, doc_lengths):
    inputs = hidden_in[0]
    head_dim = w_key.shape[1]
    dp_count = lax.axis_size("dp")
    ctx_count = lax.axis_size("ctx")
    z_count = ctx_count // 2
    sub_count = z_count // 2
    dp, ctx = lax.axis_index("dp"), lax.axis_index("ctx")
    z, core = ctx // 2, ctx % 2
    ids = jnp.stack([z, core, dp]).astype(jnp.int32)
    me = jnp.reshape(ctx, (1,)).astype(jnp.int32)
    block_rows = w_key.shape[0]
    half_rows = block_rows // 2
    quarter = half_rows // 2
    bits = [1 << at for at in range(dp_count.bit_length() - 1)]
    near = [j for j in range(1, dp_count) if j in bits]
    far = [j for j in range(1, dp_count) if j not in bits]

    def gather_near(*weights):
        pieces = {}
        for turn in range(2):
            for at, j in enumerate(near):
                offset = ((at + turn) % 2) * quarter
                start = core * half_rows + offset
                rows = [lax.dynamic_slice_in_dim(weight, start, quarter, 0) for weight in weights]
                pieces[j, 0, offset] = swap(jnp.concatenate(rows, axis=1), "dp", j)
        return pieces

    def gather_far(landed):
        pieces = {}
        for j in far:
            for offset, bit in ((0, 1 << (j.bit_length() - 1)), (quarter, j & -j)):
                origin = landed.get((j ^ bit, 0, offset), pieces.get((j ^ bit, 0, offset)))
                pieces[j, 0, offset] = swap(origin, "dp", bit)
        return pieces

    def from_other_core(pieces):
        return {(j, 1, offset): swap(one, "ctx", 1) for (j, _, offset), one in pieces.items()}

    def hold(arrays, pieces):
        names = list(pieces)
        tied, ended = after(arrays, *[pieces[name] for name in names])
        pieces.update(zip(names, ended))
        return tied

    def gather_along_z(own):
        return [swap(own, "ctx", 2 * m) if m else own for m in range(z_count)]

    def both_cores(along):
        return [block for one in along for block in (one, swap(one, "ctx", 1))]

    sizes = region_sizes(block_rows)
    regions = [(sum(sizes[:at]), size // 2) for at, size in enumerate(sizes)]
    first_rows = sum(sizes[:-1])
    moving = {
        j: lax.dynamic_slice_in_dim(inputs, (dp ^ j) * block_rows, first_rows, 1)
        for j in range(dp_count)
    }

    near_pieces = gather_near(w_key, w_value)
    far_pieces = gather_far(near_pieces)
    near_pieces.update(from_other_core(near_pieces))
    early = project(
        ids, (w_key, w_value), inputs, block_rows, near_pieces, jnp.float32, bytes_cost(1 << 24)
    )
    others = near + far
    early, *tied = hold([early] + [moving[j] for j in others], far_pieces)
    moving.update(zip(others, tied))
    far_pieces.update(from_other_core(far_pieces))
    tied = hold([moving[j] for j in near[:-1]], far_pieces)
    moving.update(zip(near[:-1], tied))
    own = project(ids, (early,), inputs, block_rows, far_pieces, jnp.bfloat16)
    moved = {0: moving[0]}
    moved[near[-1]] = swap(moving[near[-1]], "dp", near[-1])
    moved.update({j: swap(moving[j], "dp", j) for j in near[:-1]})
    along = gather_along_z(own)
    tied, _ = after([moving[j] for j in far], *along)
    moving.update(zip(far, tied))
    along, _ = after(along)
    kv_blocks = both_cores(along)

    moved.update({j: swap(moving[j], "dp", j) for j in far})

    query_grad, keep, send = attention(
        me, stretch_order, doc_lengths[0], queries[0], grad_out[0], kv_blocks, head_dim
    )
    (send,), ended = after([send], *[moved[j] for j in near])
    moved.update(zip(near, ended))
    own, *leaving = add_and_split(keep, swap(send, "ctx", 1), z_count)
    grad = add_all([own] + [swap(one, "ctx", 2 * m) for m, one in enumerate(leaving, 1)])
    grads = [grad] + [swap(grad, "dp", j) for j in range(1, dp_count)]

    (grad,), ended = after([grad], *grads[1:], *[moved[j] for j in far])
    grads[1:] = ended[: dp_count - 1]
    moved.update(zip(far, ended[dp_count - 1 :]))
    groups = [[(0, j, 0, 0)] for j in range(dp_count)]
    ours, came = weight_rows(
        ids, [inputs], [grad], groups, *regions[-1], block_rows, sub_count
    )
    own = parts_over_dp(add_cores(ours, came))
    groups = [[(j, None, j, 0) for j in range(dp_count)]]
    arrays = [moved[j] for j in range(dp_count)]
    moved_parts = [
        add_cores(*weight_rows(ids, arrays, grads, groups, *region, block_rows, sub_count))
        for region in regions[:-1]
    ]
    moved_parts, own = after(moved_parts, *own)
    own = [swap(one, "dp", j) if j else one for j, one in enumerate(own)]
    finals = []
    for part in moved_parts:
        part = scatter_along_z(part, sub_count)
        finals.append(sum_of_halves(part, sub_count))
    part = scatter_along_z(sum_of(own), sub_count, finals[:TIED])
    blocks = gather_parts(finals[0], sub_count)
    finals.append(sum_of_halves(part, sub_count, blocks))
    blocks += [one for final in finals[1:] for one in gather_parts(final, sub_count)]
    key_rows, value_rows = assemble(ids, blocks, sub_count, regions)
    return query_grad[None], key_rows, value_rows


def solution(mesh):
    return jax.shard_map(
        on_device,
        mesh=mesh,
        in_specs=(
            P("dp", "ctx", None),
            P("dp", "ctx", None),
            P("dp", "ctx", None),
            P("dp", None),
            P("dp", None),
            P(),
            P("dp", None),
        ),
        out_specs=(P("dp", "ctx", None), P("dp", None), P("dp", None)),
        check_vma=False,
    )
```

```python
import functools
import math

import jax
import jax.numpy as jnp
from jax import lax
from jax.experimental import pallas as pl
from jax.experimental.pallas import tpu as pltpu
from jax.sharding import PartitionSpec as P

VMEM_LIMIT = 28 * 1024 * 1024
NO_COST = pl.CostEstimate(flops=0, bytes_accessed=0, transcendentals=0)


MOVED = (4, 6)
TIED = 2


def region_sizes(block_rows):
    units = block_rows // 256
    sizes = [256 * (units * share // 16) for share in MOVED]
    return sizes + [block_rows - sum(sizes)]


class Plan:
    def __init__(self, **fields):
        self.__dict__.update(fields)


def swap(array, axis, distance):
    count = lax.axis_size(axis)
    return lax.ppermute(array, axis, [(i, i ^ distance) for i in range(count)])


def after(arrays, *earlier):
    tied = lax.optimization_barrier((tuple(arrays), tuple(earlier)))
    return list(tied[0]), list(tied[1])


def shape_of(rows, width, kind=jnp.bfloat16):
    return jax.ShapeDtypeStruct((rows, width), kind)


def kernel_call(kernel, name, outs, scalars, arrays, scratch=(), cost=NO_COST):
    smem = pl.BlockSpec(memory_space=pltpu.SMEM)
    vmem = pl.BlockSpec(memory_space=pltpu.VMEM)
    single = not isinstance(outs, tuple)
    return pl.pallas_call(
        kernel,
        out_shape=outs,
        in_specs=[smem] * len(scalars) + [vmem] * len(arrays),
        out_specs=vmem if single else (vmem,) * len(outs),
        scratch_shapes=list(scratch),
        compiler_params=pltpu.CompilerParams(vmem_limit_bytes=VMEM_LIMIT),
        cost_estimate=cost,
        name=name,
    )(*scalars, *arrays)


def bytes_cost(amount):
    return pl.CostEstimate(flops=0, bytes_accessed=amount, transcendentals=0)


TN = (((0,), (0,)), ((), ()))


def attention_kernel(
    shape, ids, order, lengths, q_ref, g_ref, *refs
):
    ctx_count, stretch_rows, head_count, head_dim, window, chunk = shape
    kv_refs = refs[:ctx_count]
    qgrad_ref, keep_ref, send_ref, keys, values, total, qs, gs, dqs = refs[ctx_count:]
    me = ids[0]
    row_count = 2 * stretch_rows
    stretch_count = 2 * ctx_count
    score_scale = 1.0 / math.sqrt(head_dim)

    def place(device, half):
        return pl.multiple_of(order[2 * device + half] * stretch_rows, stretch_rows)

    for index in range(ctx_count):
        for half in range(2):
            rows = pl.ds(place(me ^ index, half), stretch_rows)
            block = kv_refs[index][half * stretch_rows : (half + 1) * stretch_rows, :]
            keys[rows, :] = block[:, :head_dim]
            values[rows, :] = block[:, head_dim:]
    total[...] = jnp.zeros_like(total)
    for half in range(2):
        for head in range(head_count):
            to = slice((half * head_count + head) * stretch_rows, (half * head_count + head + 1) * stretch_rows)
            rows = slice(half * stretch_rows, (half + 1) * stretch_rows)
            columns = slice(head * head_dim, (head + 1) * head_dim)
            qs[to, :] = q_ref[rows, columns]
            gs[to, :] = g_ref[rows, columns]
    ends = []
    running = 0
    for at in range(lengths.shape[0]):
        running = running + lengths[at]
        ends.append(running)
    chunks_half = head_count * stretch_rows // chunk

    def step(at, carry):
        half = at // chunks_half
        block = order[2 * me + half]
        first = jnp.maximum(block - stretch_count // 2, 0) * stretch_rows
        first = pl.multiple_of(first, stretch_rows)
        part = pl.ds(pl.multiple_of(at * chunk, chunk), chunk)
        inside = (at - half * chunks_half) * chunk + lax.broadcasted_iota(jnp.int32, (1, chunk), 1)
        at_query = block * stretch_rows + lax.rem(inside, stretch_rows)
        begin = jnp.zeros_like(at_query)
        for end in ends:
            begin = jnp.where(at_query >= end, end, begin)
        at_key = first + lax.broadcasted_iota(jnp.int32, (window, chunk), 0)
        allowed = (at_key >= begin) & (at_key <= at_query)
        k = keys[pl.ds(first, window), :]
        v = values[pl.ds(first, window), :]
        q = qs[part, :]
        g = gs[part, :]
        last = (((1,), (1,)), ((), ()))
        scores = lax.dot_general(k, q, last, preferred_element_type=jnp.float32)
        masked = jnp.where(allowed, scores, -jnp.inf)
        largest = jnp.max(masked, axis=0, keepdims=True)
        expsum = jnp.exp2((masked - largest) * (score_scale * math.log2(math.e)))
        probs = expsum * (1.0 / jnp.sum(expsum, axis=0, keepdims=True))
        probs_low = probs.astype(jnp.bfloat16)
        dprob = lax.dot_general(v, g, last, preferred_element_type=jnp.float32)
        delta = jnp.sum(probs_low.astype(jnp.float32) * dprob, axis=0, keepdims=True)
        dscore = (probs * (dprob - delta)).astype(jnp.bfloat16)
        dq = lax.dot_general(
            k, dscore, (((0,), (0,)), ((), ())), preferred_element_type=jnp.float32
        )
        dqs[part, :] = (jnp.transpose(dq) * score_scale).astype(jnp.bfloat16)
        dk = jnp.dot(dscore, q, preferred_element_type=jnp.float32) * score_scale
        dv = jnp.dot(probs_low, g, preferred_element_type=jnp.float32)
        total[pl.ds(first, window), :head_dim] += dk
        total[pl.ds(first, window), head_dim:] += dv
        return carry

    lax.fori_loop(0, 2 * chunks_half, step, 0, unroll=2)
    for half in range(2):
        for head in range(head_count):
            origin = slice((half * head_count + head) * stretch_rows, (half * head_count + head + 1) * stretch_rows)
            rows = slice(half * stretch_rows, (half + 1) * stretch_rows)
            columns = slice(head * head_dim, (head + 1) * head_dim)
            qgrad_ref[rows, columns] = dqs[origin, :]
    for index in range(ctx_count):
        for half in range(2):
            rows = pl.ds(place(me ^ index, half), stretch_rows)
            start = (index // 2) * row_count + half * stretch_rows
            if index % 2:
                send_ref[start : start + stretch_rows, :] = total[rows, :].astype(jnp.bfloat16)
            else:
                keep_ref[start : start + stretch_rows, :] = total[rows, :]


def attention(me, order, lengths, queries, cotangent, kv_blocks, head_dim):
    row_count, width = queries.shape
    ctx_count = len(kv_blocks)
    stretch_rows = row_count // 2
    head_count = width // head_dim
    seq_rows = row_count * ctx_count
    window = seq_rows // 2 + stretch_rows
    stacked = head_count * stretch_rows
    chunk = 256 if stacked % 256 == 0 else 128
    shape = (ctx_count, stretch_rows, head_count, head_dim, window, chunk)
    smem = pl.BlockSpec(memory_space=pltpu.SMEM)
    vmem = pl.BlockSpec(memory_space=pltpu.VMEM)
    half_rows = seq_rows // 2
    return pl.pallas_call(
        functools.partial(attention_kernel, shape),
        out_shape=(
            jax.ShapeDtypeStruct((row_count, width), jnp.bfloat16),
            jax.ShapeDtypeStruct((half_rows, 2 * head_dim), jnp.float32),
            jax.ShapeDtypeStruct((half_rows, 2 * head_dim), jnp.bfloat16),
        ),
        in_specs=[smem] * 3 + [vmem] * (2 + ctx_count),
        out_specs=(vmem,) * 3,
        scratch_shapes=[
            pltpu.VMEM((seq_rows, head_dim), jnp.bfloat16),
            pltpu.VMEM((seq_rows, head_dim), jnp.bfloat16),
            pltpu.VMEM((seq_rows, 2 * head_dim), jnp.float32),
            pltpu.VMEM((2 * stacked, head_dim), jnp.bfloat16),
            pltpu.VMEM((2 * stacked, head_dim), jnp.bfloat16),
            pltpu.VMEM((2 * stacked, head_dim), jnp.bfloat16),
        ],
        compiler_params=pltpu.CompilerParams(vmem_limit_bytes=VMEM_LIMIT),
        cost_estimate=NO_COST,
        name="attention",
    )(me, order, lengths, queries, cotangent, *kv_blocks)


def project_kernel(plan, ids, hidden, *refs):
    out_ref = refs[-1]
    dp, core = ids[2], ids[1]
    if plan.start:
        total = refs[0][...]
    else:
        columns = pl.ds(pl.multiple_of(dp * plan.block_rows, plan.block_rows), plan.block_rows)
        total = jnp.concatenate(
            [
                jnp.dot(hidden[:, columns], own[...], preferred_element_type=jnp.float32)
                for own in refs[:2]
            ],
            axis=1,
        )
    for (block, side, offset), weight in zip(plan.terms, refs[1 if plan.start else 2 : -1]):
        from_column = (dp ^ block) * plan.block_rows + (core ^ side) * plan.side_rows + offset
        columns = pl.ds(pl.multiple_of(from_column, 128), weight.shape[0])
        total += jnp.dot(hidden[:, columns], weight[...], preferred_element_type=jnp.float32)
    out_ref[...] = total.astype(out_ref.dtype)


def project(ids, begin, inputs, block_rows, pieces, kind, cost=NO_COST):
    names = sorted(pieces)
    weights = [pieces[name] for name in names]
    plan = Plan(
        terms=names, start=len(begin) == 1, block_rows=block_rows, side_rows=block_rows // 2
    )
    return kernel_call(
        functools.partial(project_kernel, plan),
        "project",
        shape_of(inputs.shape[0], weights[0].shape[1], kind),
        (ids,),
        (inputs, *begin, *weights),
        cost=cost,
    )


def split_kernel(rows, keep, came, own_ref, *leaving_refs):
    own_ref[...] = keep[:rows, :] + came[:rows, :].astype(jnp.float32)
    for m, leaving in enumerate(leaving_refs, 1):
        block = slice(m * rows, (m + 1) * rows)
        leaving[...] = (keep[block, :] + came[block, :].astype(jnp.float32)).astype(leaving.dtype)


def add_and_split(keep, came, count):
    rows, width = keep.shape[0] // count, keep.shape[1]
    outs = (shape_of(rows, width, jnp.float32),) + (shape_of(rows, width),) * (count - 1)
    return kernel_call(functools.partial(split_kernel, rows), "split", outs, (), (keep, came))


def total_kernel(*refs):
    total = refs[0][...]
    for one in refs[1:-1]:
        total = total + one[...].astype(jnp.float32)
    refs[-1][...] = total.astype(refs[-1].dtype)


def add_all(arrays):
    out = jax.ShapeDtypeStruct(arrays[0].shape, jnp.bfloat16)
    return kernel_call(total_kernel, "total", out, (), arrays)


def weight_kernel(plan, ids, *refs):
    hidden = refs[: plan.hidden]
    grads = refs[plan.hidden : -2]
    z, core, dp = ids[0] % plan.sub_count, ids[1], ids[2]
    rows = plan.rows
    share = rows // plan.sub_count
    tile = next(size for size in (512, 256, 128) if rows % size == 0)
    step = math.gcd(share, tile)
    for side, out_ref in ((1, refs[-2]), (0, refs[-1])):
        for at, group in enumerate(plan.groups):
            for start in range(0, rows, tile):
                product = None
                for array, block, grad, shift in group:
                    origin = plan.origin - shift + (core ^ side) * rows + start
                    if block is not None:
                        origin = origin + (dp ^ block) * plan.block_rows
                    columns = pl.ds(pl.multiple_of(origin, 128), tile)
                    term = lax.dot_general(
                        hidden[array][:, columns],
                        grads[grad][...],
                        TN,
                        preferred_element_type=jnp.float32,
                    )
                    product = term if product is None else product + term
                for inner in range(0, tile, step):
                    part, offset = divmod(start + inner, share)
                    to = pl.multiple_of(at * rows + (z ^ part) * share + offset, step)
                    piece = product[inner : inner + step, :]
                    out_ref[pl.ds(to, step), :] = piece.astype(out_ref.dtype)


def weight_rows(ids, hidden, grads, groups, origin, rows, block_rows, sub_count):
    plan = Plan(
        hidden=len(hidden),
        groups=groups,
        origin=origin,
        rows=rows,
        block_rows=block_rows,
        sub_count=sub_count,
    )
    out = shape_of(rows * len(groups), grads[0].shape[1])
    theirs, ours = kernel_call(
        functools.partial(weight_kernel, plan),
        "weight_rows",
        (out, out),
        (ids,),
        (*hidden, *grads),
    )
    return ours, swap(theirs, "ctx", 1)


def add_cores(ours, came):
    return ours.astype(jnp.float32) + came.astype(jnp.float32)


def parts_over_dp(array):
    count = lax.axis_size("dp")
    rows = array.shape[0] // count
    parts = [array[j * rows : (j + 1) * rows] for j in range(count)]
    return parts[:1] + [part.astype(jnp.bfloat16) for part in parts[1:]]


def sum_of(arrays):
    total = arrays[0]
    for one in arrays[1:]:
        total = total + one.astype(jnp.float32)
    return total


def z_bits(sub_count):
    return [1 << at for at in range(sub_count.bit_length() - 1)]


def scatter_along_z(full, sub_count, earlier=()):
    share = full.shape[0] // sub_count
    parts = {m: full[m * share : (m + 1) * share] for m in range(sub_count)}
    for bit in z_bits(sub_count):
        for m in list(parts):
            if m & bit:
                came = swap(parts.pop(m).astype(jnp.bfloat16), "ctx", 2 * bit)
                (came,), _ = after([came], *earlier)
                parts[m ^ bit] = parts[m ^ bit] + came.astype(jnp.float32)
    return parts[0]


def sum_of_halves(part, sub_count, earlier=()):
    low = swap(part.astype(jnp.bfloat16), "ctx", 2 * sub_count)
    (low,), _ = after([low], *earlier)
    return (part + low.astype(jnp.float32)).astype(jnp.bfloat16)


def gather_parts(part, sub_count, earlier=()):
    rows = {0: part}
    for bit in z_bits(sub_count)[::-1]:
        for m, one in list(rows.items()):
            (rows[m | bit],), _ = after([swap(one, "ctx", 2 * bit)], *earlier)
    own = [rows[m] for m in range(sub_count)]
    return own + [swap(one, "ctx", 1) for one in own]


def assemble_kernel(sub_count, regions, first, ids, *refs):
    count = 2 * sub_count * len(regions)
    blocks = iter(refs[2 * (not first) :][:count])
    *outs, buffer, sems = refs[2 * (not first) + count :]
    z, core = ids[0] % sub_count, ids[1]
    copies = []
    filled = 0
    for origin, rows in regions:
        share = rows // sub_count
        for side in range(2):
            for m in range(sub_count):
                to = origin + (core ^ side) * rows + (z ^ m) * share
                to = pl.multiple_of(to, share)
                block_ref = next(blocks)
                width = block_ref.shape[1] // 2
                for which, out_ref in enumerate(outs):
                    piece = buffer.at[which, pl.ds(filled, share), :]
                    piece[...] = block_ref[:, which * width : (which + 1) * width].astype(
                        jnp.float32
                    )
                    copy = pltpu.make_async_copy(
                        piece, out_ref.at[pl.ds(to, share), :], sems.at[len(copies)]
                    )
                    copy.start()
                    copies.append(copy)
                filled += share
    for copy in copies:
        copy.wait()


def assemble(ids, before, blocks, sub_count, regions, block_rows):
    rows = sum(block.shape[0] for block in blocks)
    width = blocks[0].shape[1] // 2
    out = shape_of(block_rows, width, jnp.float32)
    smem = pl.BlockSpec(memory_space=pltpu.SMEM)
    vmem = pl.BlockSpec(memory_space=pltpu.VMEM)
    anywhere = pl.BlockSpec(memory_space=pl.ANY)
    return pl.pallas_call(
        functools.partial(assemble_kernel, sub_count, regions, not before),
        out_shape=(out, out),
        in_specs=[smem] + [anywhere] * len(before) + [vmem] * len(blocks),
        out_specs=(anywhere, anywhere),
        scratch_shapes=[
            pltpu.VMEM((2, rows, width), jnp.float32),
            pltpu.SemaphoreType.DMA((2 * len(blocks),)),
        ],
        input_output_aliases={1: 0, 2: 1} if before else {},
        compiler_params=pltpu.CompilerParams(vmem_limit_bytes=VMEM_LIMIT),
        cost_estimate=NO_COST,
        name="assemble",
    )(ids, *before, *blocks)


def on_device(hidden_in, queries, grad_out, w_key, w_value, stretch_order, doc_lengths):
    inputs = hidden_in[0]
    head_dim = w_key.shape[1]
    dp_count = lax.axis_size("dp")
    ctx_count = lax.axis_size("ctx")
    z_count = ctx_count // 2
    sub_count = z_count // 2
    dp, ctx = lax.axis_index("dp"), lax.axis_index("ctx")
    z, core = ctx // 2, ctx % 2
    ids = jnp.stack([z, core, dp]).astype(jnp.int32)
    me = jnp.reshape(ctx, (1,)).astype(jnp.int32)
    block_rows = w_key.shape[0]
    half_rows = block_rows // 2
    quarter = half_rows // 2
    bits = [1 << at for at in range(dp_count.bit_length() - 1)]
    near = [j for j in range(1, dp_count) if j in bits]
    far = [j for j in range(1, dp_count) if j not in bits]

    def gather_near(*weights):
        pieces = {}
        for turn in range(2):
            for at, j in enumerate(near):
                offset = ((at + turn) % 2) * quarter
                start = core * half_rows + offset
                rows = [lax.dynamic_slice_in_dim(weight, start, quarter, 0) for weight in weights]
                pieces[j, 0, offset] = swap(jnp.concatenate(rows, axis=1), "dp", j)
        return pieces

    def gather_far(landed):
        pieces = {}
        for j in far:
            for offset, bit in ((0, 1 << (j.bit_length() - 1)), (quarter, j & -j)):
                origin = landed.get((j ^ bit, 0, offset), pieces.get((j ^ bit, 0, offset)))
                pieces[j, 0, offset] = swap(origin, "dp", bit)
        return pieces

    def from_other_core(pieces):
        return {(j, 1, offset): swap(one, "ctx", 1) for (j, _, offset), one in pieces.items()}

    def hold(arrays, pieces):
        names = list(pieces)
        tied, ended = after(arrays, *[pieces[name] for name in names])
        pieces.update(zip(names, ended))
        return tied

    def gather_along_z(own):
        return [swap(own, "ctx", 2 * m) if m else own for m in range(z_count)]

    def both_cores(along):
        return [block for one in along for block in (one, swap(one, "ctx", 1))]

    sizes = region_sizes(block_rows)
    regions = [(sum(sizes[:at]), size // 2) for at, size in enumerate(sizes)]
    first_rows = sum(sizes[:-1])
    moving = {
        j: lax.dynamic_slice_in_dim(inputs, (dp ^ j) * block_rows, first_rows, 1)
        for j in range(dp_count)
    }

    near_pieces = gather_near(w_key, w_value)
    far_pieces = gather_far(near_pieces)
    names = list(near_pieces)
    waiting, _ = after([near_pieces[name] for name in names[: len(near)]])
    others = {}
    for name, one in zip(names, waiting):
        (one,), _ = after([one], *others.values())
        others.update(from_other_core({name: one}))
    others.update(from_other_core({name: near_pieces[name] for name in names[len(near) :]}))
    near_pieces.update(others)
    early = project(
        ids, (w_key, w_value), inputs, block_rows, near_pieces, jnp.float32, bytes_cost(1 << 24)
    )
    others = near + far
    early, *tied = hold([early] + [moving[j] for j in others], far_pieces)
    moving.update(zip(others, tied))
    far_pieces.update(from_other_core(far_pieces))
    tied = hold([moving[j] for j in near[:-1]], far_pieces)
    moving.update(zip(near[:-1], tied))
    own = project(ids, (early,), inputs, block_rows, far_pieces, jnp.bfloat16)
    moved = {0: moving[0]}
    moved[near[-1]] = swap(moving[near[-1]], "dp", near[-1])
    moved.update({j: swap(moving[j], "dp", j) for j in near[:-1]})
    along = gather_along_z(own)
    tied, _ = after([moving[j] for j in far], *along)
    moving.update(zip(far, tied))
    along, _ = after(along)
    kv_blocks = both_cores(along)

    moved.update({j: swap(moving[j], "dp", j) for j in far})

    query_grad, keep, send = attention(
        me, stretch_order, doc_lengths[0], queries[0], grad_out[0], kv_blocks, head_dim
    )
    (send,), ended = after([send], *[moved[j] for j in near])
    moved.update(zip(near, ended))
    own, *leaving = add_and_split(keep, swap(send, "ctx", 1), z_count)
    grad = add_all([own] + [swap(one, "ctx", 2 * m) for m, one in enumerate(leaving, 1)])
    grads = [grad] + [swap(grad, "dp", j) for j in range(1, dp_count)]

    (grad,), ended = after([grad], *grads[1:], *[moved[j] for j in far])
    grads[1:] = ended[: dp_count - 1]
    moved.update(zip(far, ended[dp_count - 1 :]))
    groups = [[(0, j, 0, 0)] for j in range(dp_count)]
    ours, came = weight_rows(
        ids, [inputs], [grad], groups, *regions[-1], block_rows, sub_count
    )
    own = parts_over_dp(add_cores(ours, came))
    groups = [[(j, None, j, 0) for j in range(dp_count)]]
    arrays = [moved[j] for j in range(dp_count)]
    moved_parts = [
        add_cores(*weight_rows(ids, arrays, grads, groups, *region, block_rows, sub_count))
        for region in regions[:-1]
    ]
    moved_parts, own = after(moved_parts, *own)
    own = [swap(one, "dp", j) if j else one for j, one in enumerate(own)]
    finals = []
    for part in moved_parts:
        part = scatter_along_z(part, sub_count)
        finals.append(sum_of_halves(part, sub_count))
    part = scatter_along_z(sum_of(own), sub_count, finals[:TIED])
    blocks = gather_parts(finals[0], sub_count)
    last = sum_of_halves(part, sub_count, blocks)
    blocks += [one for final in finals[1:] for one in gather_parts(final, sub_count)]
    outs = assemble(ids, (), blocks, sub_count, regions[:-1], block_rows)
    last = gather_parts(last, sub_count, outs)
    key_rows, value_rows = assemble(ids, outs, last, sub_count, regions[-1:], block_rows)
    return query_grad[None], key_rows, value_rows


def solution(mesh):
    return jax.shard_map(
        on_device,
        mesh=mesh,
        in_specs=(
            P("dp", "ctx", None),
            P("dp", "ctx", None),
            P("dp", "ctx", None),
            P("dp", None),
            P("dp", None),
            P(),
            P("dp", None),
        ),
        out_specs=(P("dp", "ctx", None), P("dp", None), P("dp", None)),
        check_vma=False,
    )
```

```python
import functools
import math

import jax
import jax.numpy as jnp
from jax import lax
from jax.experimental import pallas as pl
from jax.experimental.pallas import tpu as pltpu
from jax.sharding import PartitionSpec as P

VMEM_LIMIT = 28 * 1024 * 1024
NO_COST = pl.CostEstimate(flops=0, bytes_accessed=0, transcendentals=0)


MOVED = (2, 8)


def region_sizes(block_rows):
    units = block_rows // 256
    sizes = [256 * max(1, units * share // 16) for share in MOVED]
    return sizes + [block_rows - sum(sizes)]


class Plan:
    def __init__(self, **fields):
        self.__dict__.update(fields)


def swap(array, axis, distance):
    count = lax.axis_size(axis)
    return lax.ppermute(array, axis, [(i, i ^ distance) for i in range(count)])


def after(arrays, *earlier):
    tied = lax.optimization_barrier((tuple(arrays), tuple(earlier)))
    return list(tied[0]), list(tied[1])


def shape_of(rows, width, kind=jnp.bfloat16):
    return jax.ShapeDtypeStruct((rows, width), kind)


def kernel_call(kernel, name, outs, scalars, arrays, scratch=(), cost=NO_COST):
    smem = pl.BlockSpec(memory_space=pltpu.SMEM)
    vmem = pl.BlockSpec(memory_space=pltpu.VMEM)
    single = not isinstance(outs, tuple)
    return pl.pallas_call(
        kernel,
        out_shape=outs,
        in_specs=[smem] * len(scalars) + [vmem] * len(arrays),
        out_specs=vmem if single else (vmem,) * len(outs),
        scratch_shapes=list(scratch),
        compiler_params=pltpu.CompilerParams(vmem_limit_bytes=VMEM_LIMIT),
        cost_estimate=cost,
        name=name,
    )(*scalars, *arrays)


def bytes_cost(amount):
    return pl.CostEstimate(flops=0, bytes_accessed=amount, transcendentals=0)


TN = (((0,), (0,)), ((), ()))


def attention_kernel(
    shape, ids, order, lengths, q_ref, g_ref, *refs
):
    ctx_count, stretch_rows, head_count, head_dim, window, chunk = shape
    kv_refs = refs[:ctx_count]
    qgrad_ref, keep_ref, send_ref, keys, values, total, qs, gs, dqs = refs[ctx_count:]
    me = ids[0]
    row_count = 2 * stretch_rows
    stretch_count = 2 * ctx_count
    score_scale = 1.0 / math.sqrt(head_dim)

    def place(device, half):
        return pl.multiple_of(order[2 * device + half] * stretch_rows, stretch_rows)

    for index in range(ctx_count):
        for half in range(2):
            rows = pl.ds(place(me ^ index, half), stretch_rows)
            block = kv_refs[index][half * stretch_rows : (half + 1) * stretch_rows, :]
            keys[rows, :] = block[:, :head_dim]
            values[rows, :] = block[:, head_dim:]
    total[...] = jnp.zeros_like(total)
    for half in range(2):
        for head in range(head_count):
            to = slice((half * head_count + head) * stretch_rows, (half * head_count + head + 1) * stretch_rows)
            rows = slice(half * stretch_rows, (half + 1) * stretch_rows)
            columns = slice(head * head_dim, (head + 1) * head_dim)
            qs[to, :] = q_ref[rows, columns]
            gs[to, :] = g_ref[rows, columns]
    ends = []
    running = 0
    for at in range(lengths.shape[0]):
        running = running + lengths[at]
        ends.append(running)
    chunks_half = head_count * stretch_rows // chunk

    def step(at, carry):
        half = at // chunks_half
        block = order[2 * me + half]
        first = jnp.maximum(block - stretch_count // 2, 0) * stretch_rows
        first = pl.multiple_of(first, stretch_rows)
        part = pl.ds(pl.multiple_of(at * chunk, chunk), chunk)
        inside = (at - half * chunks_half) * chunk + lax.broadcasted_iota(jnp.int32, (1, chunk), 1)
        at_query = block * stretch_rows + lax.rem(inside, stretch_rows)
        begin = jnp.zeros_like(at_query)
        for end in ends:
            begin = jnp.where(at_query >= end, end, begin)
        at_key = first + lax.broadcasted_iota(jnp.int32, (window, chunk), 0)
        allowed = (at_key >= begin) & (at_key <= at_query)
        k = keys[pl.ds(first, window), :]
        v = values[pl.ds(first, window), :]
        q = qs[part, :]
        g = gs[part, :]
        last = (((1,), (1,)), ((), ()))
        scores = lax.dot_general(k, q, last, preferred_element_type=jnp.float32)
        masked = jnp.where(allowed, scores, -jnp.inf)
        largest = jnp.max(masked, axis=0, keepdims=True)
        expsum = jnp.exp2((masked - largest) * (score_scale * math.log2(math.e)))
        probs = expsum * (1.0 / jnp.sum(expsum, axis=0, keepdims=True))
        probs_low = probs.astype(jnp.bfloat16)
        dprob = lax.dot_general(v, g, last, preferred_element_type=jnp.float32)
        delta = jnp.sum(probs_low.astype(jnp.float32) * dprob, axis=0, keepdims=True)
        dscore = (probs * (dprob - delta)).astype(jnp.bfloat16)
        dq = lax.dot_general(
            k, dscore, (((0,), (0,)), ((), ())), preferred_element_type=jnp.float32
        )
        dqs[part, :] = (jnp.transpose(dq) * score_scale).astype(jnp.bfloat16)
        dk = jnp.dot(dscore, q, preferred_element_type=jnp.float32) * score_scale
        dv = jnp.dot(probs_low, g, preferred_element_type=jnp.float32)
        total[pl.ds(first, window), :head_dim] += dk
        total[pl.ds(first, window), head_dim:] += dv
        return carry

    lax.fori_loop(0, 2 * chunks_half, step, 0, unroll=2)
    for half in range(2):
        for head in range(head_count):
            origin = slice((half * head_count + head) * stretch_rows, (half * head_count + head + 1) * stretch_rows)
            rows = slice(half * stretch_rows, (half + 1) * stretch_rows)
            columns = slice(head * head_dim, (head + 1) * head_dim)
            qgrad_ref[rows, columns] = dqs[origin, :]
    for index in range(ctx_count):
        for half in range(2):
            rows = pl.ds(place(me ^ index, half), stretch_rows)
            start = (index // 2) * row_count + half * stretch_rows
            if index % 2:
                send_ref[start : start + stretch_rows, :] = total[rows, :].astype(jnp.bfloat16)
            else:
                keep_ref[start : start + stretch_rows, :] = total[rows, :]


def attention(me, order, lengths, queries, cotangent, kv_blocks, head_dim):
    row_count, width = queries.shape
    ctx_count = len(kv_blocks)
    stretch_rows = row_count // 2
    head_count = width // head_dim
    seq_rows = row_count * ctx_count
    window = seq_rows // 2 + stretch_rows
    stacked = head_count * stretch_rows
    chunk = 256 if stacked % 256 == 0 else 128
    shape = (ctx_count, stretch_rows, head_count, head_dim, window, chunk)
    smem = pl.BlockSpec(memory_space=pltpu.SMEM)
    vmem = pl.BlockSpec(memory_space=pltpu.VMEM)
    half_rows = seq_rows // 2
    return pl.pallas_call(
        functools.partial(attention_kernel, shape),
        out_shape=(
            jax.ShapeDtypeStruct((row_count, width), jnp.bfloat16),
            jax.ShapeDtypeStruct((half_rows, 2 * head_dim), jnp.float32),
            jax.ShapeDtypeStruct((half_rows, 2 * head_dim), jnp.bfloat16),
        ),
        in_specs=[smem] * 3 + [vmem] * (2 + ctx_count),
        out_specs=(vmem,) * 3,
        scratch_shapes=[
            pltpu.VMEM((seq_rows, head_dim), jnp.bfloat16),
            pltpu.VMEM((seq_rows, head_dim), jnp.bfloat16),
            pltpu.VMEM((seq_rows, 2 * head_dim), jnp.float32),
            pltpu.VMEM((2 * stacked, head_dim), jnp.bfloat16),
            pltpu.VMEM((2 * stacked, head_dim), jnp.bfloat16),
            pltpu.VMEM((2 * stacked, head_dim), jnp.bfloat16),
        ],
        compiler_params=pltpu.CompilerParams(vmem_limit_bytes=VMEM_LIMIT),
        cost_estimate=NO_COST,
        name="attention",
    )(me, order, lengths, queries, cotangent, *kv_blocks)


def project_kernel(plan, ids, hidden, *refs):
    out_ref = refs[-1]
    dp, core = ids[2], ids[1]
    if plan.start:
        total = refs[0][...]
    else:
        columns = pl.ds(pl.multiple_of(dp * plan.block_rows, plan.block_rows), plan.block_rows)
        total = jnp.concatenate(
            [
                jnp.dot(hidden[:, columns], own[...], preferred_element_type=jnp.float32)
                for own in refs[:2]
            ],
            axis=1,
        )
    for (block, side, offset), weight in zip(plan.terms, refs[1 if plan.start else 2 : -1]):
        from_column = (dp ^ block) * plan.block_rows + (core ^ side) * plan.side_rows + offset
        columns = pl.ds(pl.multiple_of(from_column, 128), weight.shape[0])
        total += jnp.dot(hidden[:, columns], weight[...], preferred_element_type=jnp.float32)
    out_ref[...] = total.astype(out_ref.dtype)


def project(ids, begin, inputs, block_rows, pieces, kind, cost=NO_COST):
    names = sorted(pieces)
    weights = [pieces[name] for name in names]
    plan = Plan(
        terms=names, start=len(begin) == 1, block_rows=block_rows, side_rows=block_rows // 2
    )
    return kernel_call(
        functools.partial(project_kernel, plan),
        "project",
        shape_of(inputs.shape[0], weights[0].shape[1], kind),
        (ids,),
        (inputs, *begin, *weights),
        cost=cost,
    )


def split_kernel(rows, keep, came, own_ref, *leaving_refs):
    own_ref[...] = keep[:rows, :] + came[:rows, :].astype(jnp.float32)
    for m, leaving in enumerate(leaving_refs, 1):
        block = slice(m * rows, (m + 1) * rows)
        leaving[...] = (keep[block, :] + came[block, :].astype(jnp.float32)).astype(leaving.dtype)


def add_and_split(keep, came, count):
    rows, width = keep.shape[0] // count, keep.shape[1]
    outs = (shape_of(rows, width, jnp.float32),) + (shape_of(rows, width),) * (count - 1)
    return kernel_call(functools.partial(split_kernel, rows), "split", outs, (), (keep, came))


def total_kernel(*refs):
    total = refs[0][...]
    for one in refs[1:-1]:
        total = total + one[...].astype(jnp.float32)
    refs[-1][...] = total.astype(refs[-1].dtype)


def add_all(arrays):
    out = jax.ShapeDtypeStruct(arrays[0].shape, jnp.bfloat16)
    return kernel_call(total_kernel, "total", out, (), arrays)


def weight_kernel(plan, ids, *refs):
    hidden = refs[: plan.hidden]
    grads = refs[plan.hidden : -2]
    z, core, dp = ids[0] % plan.sub_count, ids[1], ids[2]
    rows = plan.rows
    share = rows // plan.sub_count
    tile = next(size for size in (512, 256, 128) if rows % size == 0)
    step = math.gcd(share, tile)
    for side, out_ref in ((1, refs[-2]), (0, refs[-1])):
        for at, group in enumerate(plan.groups):
            for start in range(0, rows, tile):
                product = None
                for array, block, grad, shift in group:
                    origin = plan.origin - shift + (core ^ side) * rows + start
                    if block is not None:
                        origin = origin + (dp ^ block) * plan.block_rows
                    columns = pl.ds(pl.multiple_of(origin, 128), tile)
                    term = lax.dot_general(
                        hidden[array][:, columns],
                        grads[grad][...],
                        TN,
                        preferred_element_type=jnp.float32,
                    )
                    product = term if product is None else product + term
                for inner in range(0, tile, step):
                    part, offset = divmod(start + inner, share)
                    to = pl.multiple_of(at * rows + (z ^ part) * share + offset, step)
                    piece = product[inner : inner + step, :]
                    out_ref[pl.ds(to, step), :] = piece.astype(out_ref.dtype)


def weight_rows(ids, hidden, grads, groups, origin, rows, block_rows, sub_count):
    plan = Plan(
        hidden=len(hidden),
        groups=groups,
        origin=origin,
        rows=rows,
        block_rows=block_rows,
        sub_count=sub_count,
    )
    out = shape_of(rows * len(groups), grads[0].shape[1])
    theirs, ours = kernel_call(
        functools.partial(weight_kernel, plan),
        "weight_rows",
        (out, out),
        (ids,),
        (*hidden, *grads),
    )
    return ours, swap(theirs, "ctx", 1)


def add_cores(ours, came):
    return ours.astype(jnp.float32) + came.astype(jnp.float32)


def parts_over_dp(array):
    count = lax.axis_size("dp")
    rows = array.shape[0] // count
    parts = [array[j * rows : (j + 1) * rows] for j in range(count)]
    return parts[:1] + [part.astype(jnp.bfloat16) for part in parts[1:]]


def sum_of(arrays):
    total = arrays[0]
    for one in arrays[1:]:
        total = total + one.astype(jnp.float32)
    return total


def z_bits(sub_count):
    return [1 << at for at in range(sub_count.bit_length() - 1)]


def scatter_along_z(full, sub_count, earlier=()):
    share = full.shape[0] // sub_count
    parts = {m: full[m * share : (m + 1) * share] for m in range(sub_count)}
    for bit in z_bits(sub_count):
        for m in list(parts):
            if m & bit:
                came = swap(parts.pop(m).astype(jnp.bfloat16), "ctx", 2 * bit)
                (came,), _ = after([came], *earlier)
                parts[m ^ bit] = parts[m ^ bit] + came.astype(jnp.float32)
    return parts[0]


def sum_of_halves(part, sub_count, earlier=()):
    low = swap(part.astype(jnp.bfloat16), "ctx", 2 * sub_count)
    (low,), _ = after([low], *earlier)
    return (part + low.astype(jnp.float32)).astype(jnp.bfloat16)


def gather_parts(part, sub_count, earlier=()):
    rows = {0: part}
    for bit in z_bits(sub_count)[::-1]:
        for m, one in list(rows.items()):
            (rows[m | bit],), _ = after([swap(one, "ctx", 2 * bit)], *earlier)
    own = [rows[m] for m in range(sub_count)]
    return own + [swap(one, "ctx", 1) for one in own]


def assemble_kernel(sub_count, regions, first, ids, *refs):
    count = 2 * sub_count * len(regions)
    blocks = iter(refs[2 * (not first) :][:count])
    *outs, buffer, sems = refs[2 * (not first) + count :]
    z, core = ids[0] % sub_count, ids[1]
    copies = []
    filled = 0
    for origin, rows in regions:
        share = rows // sub_count
        for side in range(2):
            for m in range(sub_count):
                to = origin + (core ^ side) * rows + (z ^ m) * share
                to = pl.multiple_of(to, share)
                block_ref = next(blocks)
                width = block_ref.shape[1] // 2
                for which, out_ref in enumerate(outs):
                    piece = buffer.at[which, pl.ds(filled, share), :]
                    piece[...] = block_ref[:, which * width : (which + 1) * width].astype(
                        jnp.float32
                    )
                    copy = pltpu.make_async_copy(
                        piece, out_ref.at[pl.ds(to, share), :], sems.at[len(copies)]
                    )
                    copy.start()
                    copies.append(copy)
                filled += share
    for copy in copies:
        copy.wait()


def assemble(ids, before, blocks, sub_count, regions, block_rows):
    rows = sum(block.shape[0] for block in blocks)
    width = blocks[0].shape[1] // 2
    out = shape_of(block_rows, width, jnp.float32)
    smem = pl.BlockSpec(memory_space=pltpu.SMEM)
    vmem = pl.BlockSpec(memory_space=pltpu.VMEM)
    anywhere = pl.BlockSpec(memory_space=pl.ANY)
    return pl.pallas_call(
        functools.partial(assemble_kernel, sub_count, regions, not before),
        out_shape=(out, out),
        in_specs=[smem] + [anywhere] * len(before) + [vmem] * len(blocks),
        out_specs=(anywhere, anywhere),
        scratch_shapes=[
            pltpu.VMEM((2, rows, width), jnp.float32),
            pltpu.SemaphoreType.DMA((2 * len(blocks),)),
        ],
        input_output_aliases={1: 0, 2: 1} if before else {},
        compiler_params=pltpu.CompilerParams(vmem_limit_bytes=VMEM_LIMIT),
        cost_estimate=NO_COST,
        name="assemble",
    )(ids, *before, *blocks)


def on_device(hidden_in, queries, grad_out, w_key, w_value, stretch_order, doc_lengths):
    inputs = hidden_in[0]
    head_dim = w_key.shape[1]
    dp_count = lax.axis_size("dp")
    ctx_count = lax.axis_size("ctx")
    z_count = ctx_count // 2
    sub_count = z_count // 2
    dp, ctx = lax.axis_index("dp"), lax.axis_index("ctx")
    z, core = ctx // 2, ctx % 2
    ids = jnp.stack([z, core, dp]).astype(jnp.int32)
    me = jnp.reshape(ctx, (1,)).astype(jnp.int32)
    block_rows = w_key.shape[0]
    half_rows = block_rows // 2
    quarter = half_rows // 2
    bits = [1 << at for at in range(dp_count.bit_length() - 1)]
    near = [j for j in range(1, dp_count) if j in bits]
    far = [j for j in range(1, dp_count) if j not in bits]

    def gather_near(*weights):
        pieces = {}
        for turn in range(2):
            for at, j in enumerate(near):
                offset = ((at + turn) % 2) * quarter
                start = core * half_rows + offset
                rows = [lax.dynamic_slice_in_dim(weight, start, quarter, 0) for weight in weights]
                pieces[j, 0, offset] = swap(jnp.concatenate(rows, axis=1), "dp", j)
        return pieces

    def gather_far(landed):
        pieces = {}
        for j in far:
            for offset, bit in ((0, 1 << (j.bit_length() - 1)), (quarter, j & -j)):
                origin = landed.get((j ^ bit, 0, offset), pieces.get((j ^ bit, 0, offset)))
                pieces[j, 0, offset] = swap(origin, "dp", bit)
        return pieces

    def from_other_core(pieces):
        return {(j, 1, offset): swap(one, "ctx", 1) for (j, _, offset), one in pieces.items()}

    def hold(arrays, pieces):
        names = list(pieces)
        tied, ended = after(arrays, *[pieces[name] for name in names])
        pieces.update(zip(names, ended))
        return tied

    def gather_along_z(own):
        return [swap(own, "ctx", 2 * m) if m else own for m in range(z_count)]

    def both_cores(along):
        return [block for one in along for block in (one, swap(one, "ctx", 1))]

    sizes = region_sizes(block_rows)
    regions = [(sum(sizes[:at]), size // 2) for at, size in enumerate(sizes)]
    first_rows = sum(sizes[:-1])
    moving = {
        j: lax.dynamic_slice_in_dim(inputs, (dp ^ j) * block_rows, first_rows, 1)
        for j in range(dp_count)
    }

    near_pieces = gather_near(w_key, w_value)
    far_pieces = gather_far(near_pieces)
    names = list(near_pieces)
    waiting, _ = after([near_pieces[name] for name in names[: len(near)]])
    others = {}
    for name, one in zip(names, waiting):
        (one,), _ = after([one], *others.values())
        others.update(from_other_core({name: one}))
    others.update(from_other_core({name: near_pieces[name] for name in names[len(near) :]}))
    near_pieces.update(others)
    early = project(
        ids, (w_key, w_value), inputs, block_rows, near_pieces, jnp.float32, bytes_cost(1 << 24)
    )
    others = near + far
    early, *tied = hold([early] + [moving[j] for j in others], far_pieces)
    moving.update(zip(others, tied))
    far_pieces.update(from_other_core(far_pieces))
    tied = hold([moving[j] for j in near[:-1]], far_pieces)
    moving.update(zip(near[:-1], tied))
    own = project(ids, (early,), inputs, block_rows, far_pieces, jnp.bfloat16)
    moved = {0: moving[0]}
    moved[near[-1]] = swap(moving[near[-1]], "dp", near[-1])
    moved.update({j: swap(moving[j], "dp", j) for j in near[:-1]})
    along = gather_along_z(own)
    tied, _ = after([moving[j] for j in far], *along)
    moving.update(zip(far, tied))
    along, _ = after(along)
    kv_blocks = both_cores(along)

    far_second = [swap(moving[j][:, sizes[0] :], "dp", j) for j in far]

    query_grad, keep, send = attention(
        me, stretch_order, doc_lengths[0], queries[0], grad_out[0], kv_blocks, head_dim
    )
    (send,), ended = after([send], *[moved[j] for j in near])
    moved.update(zip(near, ended))
    own, *leaving = add_and_split(keep, swap(send, "ctx", 1), z_count)
    grad = add_all([own] + [swap(one, "ctx", 2 * m) for m, one in enumerate(leaving, 1)])
    (grad,), far_second = after([grad], *far_second)
    grads = [grad] + [swap(grad, "dp", j) for j in range(1, dp_count)]

    groups = [[(0, j, 0, 0)] for j in range(dp_count)]
    ours, came = weight_rows(
        ids, [inputs], [grad], groups, *regions[-1], block_rows, sub_count
    )
    own = parts_over_dp(add_cores(ours, came))
    tied, _ = after([moving[j][:, : sizes[0]] for j in far], grad)
    far_first = [swap(one, "dp", j) for one, j in zip(tied, far)]
    grads, ended = after(grads, *own, *far_first)
    own, far_first = ended[: len(own)], ended[len(own) :]
    moved_parts = []
    for region, pieces, shift in zip(regions, (far_first, far_second), (0, sizes[0])):
        groups = [[(j, None, j, shift if j in far else 0) for j in range(dp_count)]]
        arrays = [pieces[far.index(j)] if j in far else moved[j] for j in range(dp_count)]
        pair = weight_rows(ids, arrays, grads, groups, *region, block_rows, sub_count)
        moved_parts.append(add_cores(*pair))
    own = [swap(one, "dp", j) if j else one for j, one in enumerate(own)]
    second = scatter_along_z(moved_parts[1], sub_count)
    (first,), _ = after(moved_parts[:1], second)
    first = scatter_along_z(first, sub_count)
    finals = [sum_of_halves(first, sub_count), sum_of_halves(second, sub_count)]
    part = scatter_along_z(sum_of(own), sub_count, finals[1:])
    finals, _ = after(finals, part)
    blocks = gather_parts(finals[0], sub_count)
    last = sum_of_halves(part, sub_count, blocks)
    blocks += [one for final in finals[1:] for one in gather_parts(final, sub_count)]
    outs = assemble(ids, (), blocks, sub_count, regions[:-1], block_rows)
    last = gather_parts(last, sub_count, outs)
    key_rows, value_rows = assemble(ids, outs, last, sub_count, regions[-1:], block_rows)
    return query_grad[None], key_rows, value_rows


def solution(mesh):
    return jax.shard_map(
        on_device,
        mesh=mesh,
        in_specs=(
            P("dp", "ctx", None),
            P("dp", "ctx", None),
            P("dp", "ctx", None),
            P("dp", None),
            P("dp", None),
            P(),
            P("dp", None),
        ),
        out_specs=(P("dp", "ctx", None), P("dp", None), P("dp", None)),
        check_vma=False,
    )
```

```python
import functools
import math

import jax
import jax.numpy as jnp
from jax import lax
from jax.experimental import pallas as pl
from jax.experimental.pallas import tpu as pltpu
from jax.sharding import PartitionSpec as P

VMEM_LIMIT = 28 * 1024 * 1024
NO_COST = pl.CostEstimate(flops=0, bytes_accessed=0, transcendentals=0)


MOVED = (5, 6)
TIED = 2


def region_sizes(block_rows):
    units = block_rows // 256
    sizes = [256 * (units * share // 16) for share in MOVED]
    return sizes + [block_rows - sum(sizes)]


class Plan:
    def __init__(self, **fields):
        self.__dict__.update(fields)


def swap(array, axis, distance):
    count = lax.axis_size(axis)
    return lax.ppermute(array, axis, [(i, i ^ distance) for i in range(count)])


def after(arrays, *earlier):
    tied = lax.optimization_barrier((tuple(arrays), tuple(earlier)))
    return list(tied[0]), list(tied[1])


def shape_of(rows, width, kind=jnp.bfloat16):
    return jax.ShapeDtypeStruct((rows, width), kind)


def kernel_call(kernel, name, outs, scalars, arrays, scratch=(), cost=NO_COST):
    smem = pl.BlockSpec(memory_space=pltpu.SMEM)
    vmem = pl.BlockSpec(memory_space=pltpu.VMEM)
    single = not isinstance(outs, tuple)
    return pl.pallas_call(
        kernel,
        out_shape=outs,
        in_specs=[smem] * len(scalars) + [vmem] * len(arrays),
        out_specs=vmem if single else (vmem,) * len(outs),
        scratch_shapes=list(scratch),
        compiler_params=pltpu.CompilerParams(vmem_limit_bytes=VMEM_LIMIT),
        cost_estimate=cost,
        name=name,
    )(*scalars, *arrays)


def bytes_cost(amount):
    return pl.CostEstimate(flops=0, bytes_accessed=amount, transcendentals=0)


TN = (((0,), (0,)), ((), ()))


def attention_kernel(
    shape, ids, order, lengths, q_ref, g_ref, *refs
):
    ctx_count, stretch_rows, head_count, head_dim, window, chunk = shape
    kv_refs = refs[:ctx_count]
    qgrad_ref, keep_ref, send_ref, keys, values, total, qs, gs, dqs = refs[ctx_count:]
    me = ids[0]
    row_count = 2 * stretch_rows
    stretch_count = 2 * ctx_count
    score_scale = 1.0 / math.sqrt(head_dim)

    def place(device, half):
        return pl.multiple_of(order[2 * device + half] * stretch_rows, stretch_rows)

    for index in range(ctx_count):
        for half in range(2):
            rows = pl.ds(place(me ^ index, half), stretch_rows)
            block = kv_refs[index][half * stretch_rows : (half + 1) * stretch_rows, :]
            keys[rows, :] = block[:, :head_dim]
            values[rows, :] = block[:, head_dim:]
    total[...] = jnp.zeros_like(total)
    for half in range(2):
        for head in range(head_count):
            to = slice((half * head_count + head) * stretch_rows, (half * head_count + head + 1) * stretch_rows)
            rows = slice(half * stretch_rows, (half + 1) * stretch_rows)
            columns = slice(head * head_dim, (head + 1) * head_dim)
            qs[to, :] = q_ref[rows, columns]
            gs[to, :] = g_ref[rows, columns]
    ends = []
    running = 0
    for at in range(lengths.shape[0]):
        running = running + lengths[at]
        ends.append(running)
    chunks_half = head_count * stretch_rows // chunk

    def step(at, carry):
        half = at // chunks_half
        block = order[2 * me + half]
        first = jnp.maximum(block - stretch_count // 2, 0) * stretch_rows
        first = pl.multiple_of(first, stretch_rows)
        part = pl.ds(pl.multiple_of(at * chunk, chunk), chunk)
        inside = (at - half * chunks_half) * chunk + lax.broadcasted_iota(jnp.int32, (1, chunk), 1)
        at_query = block * stretch_rows + lax.rem(inside, stretch_rows)
        begin = jnp.zeros_like(at_query)
        for end in ends:
            begin = jnp.where(at_query >= end, end, begin)
        at_key = first + lax.broadcasted_iota(jnp.int32, (window, chunk), 0)
        allowed = (at_key >= begin) & (at_key <= at_query)
        k = keys[pl.ds(first, window), :]
        v = values[pl.ds(first, window), :]
        q = qs[part, :]
        g = gs[part, :]
        last = (((1,), (1,)), ((), ()))
        scores = lax.dot_general(k, q, last, preferred_element_type=jnp.float32)
        masked = jnp.where(allowed, scores, -jnp.inf)
        largest = jnp.max(masked, axis=0, keepdims=True)
        expsum = jnp.exp2((masked - largest) * (score_scale * math.log2(math.e)))
        probs = expsum * (1.0 / jnp.sum(expsum, axis=0, keepdims=True))
        probs_low = probs.astype(jnp.bfloat16)
        dprob = lax.dot_general(v, g, last, preferred_element_type=jnp.float32)
        delta = jnp.sum(probs_low.astype(jnp.float32) * dprob, axis=0, keepdims=True)
        dscore = (probs * (dprob - delta)).astype(jnp.bfloat16)
        dq = lax.dot_general(
            k, dscore, (((0,), (0,)), ((), ())), preferred_element_type=jnp.float32
        )
        dqs[part, :] = (jnp.transpose(dq) * score_scale).astype(jnp.bfloat16)
        dk = jnp.dot(dscore, q, preferred_element_type=jnp.float32) * score_scale
        dv = jnp.dot(probs_low, g, preferred_element_type=jnp.float32)
        total[pl.ds(first, window), :head_dim] += dk
        total[pl.ds(first, window), head_dim:] += dv
        return carry

    lax.fori_loop(0, 2 * chunks_half, step, 0, unroll=2)
    for half in range(2):
        for head in range(head_count):
            origin = slice((half * head_count + head) * stretch_rows, (half * head_count + head + 1) * stretch_rows)
            rows = slice(half * stretch_rows, (half + 1) * stretch_rows)
            columns = slice(head * head_dim, (head + 1) * head_dim)
            qgrad_ref[rows, columns] = dqs[origin, :]
    for index in range(ctx_count):
        for half in range(2):
            rows = pl.ds(place(me ^ index, half), stretch_rows)
            start = (index // 2) * row_count + half * stretch_rows
            if index % 2:
                send_ref[start : start + stretch_rows, :] = total[rows, :].astype(jnp.bfloat16)
            else:
                keep_ref[start : start + stretch_rows, :] = total[rows, :]


def attention(me, order, lengths, queries, cotangent, kv_blocks, head_dim):
    row_count, width = queries.shape
    ctx_count = len(kv_blocks)
    stretch_rows = row_count // 2
    head_count = width // head_dim
    seq_rows = row_count * ctx_count
    window = seq_rows // 2 + stretch_rows
    stacked = head_count * stretch_rows
    chunk = 256 if stacked % 256 == 0 else 128
    shape = (ctx_count, stretch_rows, head_count, head_dim, window, chunk)
    smem = pl.BlockSpec(memory_space=pltpu.SMEM)
    vmem = pl.BlockSpec(memory_space=pltpu.VMEM)
    half_rows = seq_rows // 2
    return pl.pallas_call(
        functools.partial(attention_kernel, shape),
        out_shape=(
            jax.ShapeDtypeStruct((row_count, width), jnp.bfloat16),
            jax.ShapeDtypeStruct((half_rows, 2 * head_dim), jnp.float32),
            jax.ShapeDtypeStruct((half_rows, 2 * head_dim), jnp.bfloat16),
        ),
        in_specs=[smem] * 3 + [vmem] * (2 + ctx_count),
        out_specs=(vmem,) * 3,
        scratch_shapes=[
            pltpu.VMEM((seq_rows, head_dim), jnp.bfloat16),
            pltpu.VMEM((seq_rows, head_dim), jnp.bfloat16),
            pltpu.VMEM((seq_rows, 2 * head_dim), jnp.float32),
            pltpu.VMEM((2 * stacked, head_dim), jnp.bfloat16),
            pltpu.VMEM((2 * stacked, head_dim), jnp.bfloat16),
            pltpu.VMEM((2 * stacked, head_dim), jnp.bfloat16),
        ],
        compiler_params=pltpu.CompilerParams(vmem_limit_bytes=VMEM_LIMIT),
        cost_estimate=NO_COST,
        name="attention",
    )(me, order, lengths, queries, cotangent, *kv_blocks)


def project_kernel(plan, ids, hidden, *refs):
    out_ref = refs[-1]
    dp, core = ids[2], ids[1]
    if plan.start:
        total = refs[0][...]
    else:
        columns = pl.ds(pl.multiple_of(dp * plan.block_rows, plan.block_rows), plan.block_rows)
        total = jnp.concatenate(
            [
                jnp.dot(hidden[:, columns], own[...], preferred_element_type=jnp.float32)
                for own in refs[:2]
            ],
            axis=1,
        )
    for (block, side, offset), weight in zip(plan.terms, refs[1 if plan.start else 2 : -1]):
        from_column = (dp ^ block) * plan.block_rows + (core ^ side) * plan.side_rows + offset
        columns = pl.ds(pl.multiple_of(from_column, 128), weight.shape[0])
        total += jnp.dot(hidden[:, columns], weight[...], preferred_element_type=jnp.float32)
    out_ref[...] = total.astype(out_ref.dtype)


def project(ids, begin, inputs, block_rows, pieces, kind, cost=NO_COST):
    names = sorted(pieces)
    weights = [pieces[name] for name in names]
    plan = Plan(
        terms=names, start=len(begin) == 1, block_rows=block_rows, side_rows=block_rows // 2
    )
    return kernel_call(
        functools.partial(project_kernel, plan),
        "project",
        shape_of(inputs.shape[0], weights[0].shape[1], kind),
        (ids,),
        (inputs, *begin, *weights),
        cost=cost,
    )


def split_kernel(rows, keep, came, own_ref, *leaving_refs):
    own_ref[...] = keep[:rows, :] + came[:rows, :].astype(jnp.float32)
    for m, leaving in enumerate(leaving_refs, 1):
        block = slice(m * rows, (m + 1) * rows)
        leaving[...] = (keep[block, :] + came[block, :].astype(jnp.float32)).astype(leaving.dtype)


def add_and_split(keep, came, count):
    rows, width = keep.shape[0] // count, keep.shape[1]
    outs = (shape_of(rows, width, jnp.float32),) + (shape_of(rows, width),) * (count - 1)
    return kernel_call(functools.partial(split_kernel, rows), "split", outs, (), (keep, came))


def total_kernel(*refs):
    total = refs[0][...]
    for one in refs[1:-1]:
        total = total + one[...].astype(jnp.float32)
    refs[-1][...] = total.astype(refs[-1].dtype)


def add_all(arrays):
    out = jax.ShapeDtypeStruct(arrays[0].shape, jnp.bfloat16)
    return kernel_call(total_kernel, "total", out, (), arrays)


def weight_kernel(plan, ids, *refs):
    hidden = refs[: plan.hidden]
    grads = refs[plan.hidden : -2]
    z, core, dp = ids[0] % plan.sub_count, ids[1], ids[2]
    rows = plan.rows
    share = rows // plan.sub_count
    tile = next(size for size in (768, 640, 512, 384, 256, 128) if rows % size == 0)
    step = math.gcd(share, tile)
    for side, out_ref in ((1, refs[-2]), (0, refs[-1])):
        for at, group in enumerate(plan.groups):
            for start in range(0, rows, tile):
                product = None
                for array, block, grad, shift in group:
                    origin = plan.origin - shift + (core ^ side) * rows + start
                    if block is not None:
                        origin = origin + (dp ^ block) * plan.block_rows
                    columns = pl.ds(pl.multiple_of(origin, 128), tile)
                    term = lax.dot_general(
                        hidden[array][:, columns],
                        grads[grad][...],
                        TN,
                        preferred_element_type=jnp.float32,
                    )
                    product = term if product is None else product + term
                for inner in range(0, tile, step):
                    part, offset = divmod(start + inner, share)
                    to = pl.multiple_of(at * rows + (z ^ part) * share + offset, step)
                    piece = product[inner : inner + step, :]
                    out_ref[pl.ds(to, step), :] = piece.astype(out_ref.dtype)


def weight_rows(ids, hidden, grads, groups, origin, rows, block_rows, sub_count):
    plan = Plan(
        hidden=len(hidden),
        groups=groups,
        origin=origin,
        rows=rows,
        block_rows=block_rows,
        sub_count=sub_count,
    )
    out = shape_of(rows * len(groups), grads[0].shape[1])
    theirs, ours = kernel_call(
        functools.partial(weight_kernel, plan),
        "weight_rows",
        (out, out),
        (ids,),
        (*hidden, *grads),
    )
    return ours, swap(theirs, "ctx", 1)


def add_cores(ours, came):
    return ours.astype(jnp.float32) + came.astype(jnp.float32)


def parts_over_dp(array):
    count = lax.axis_size("dp")
    rows = array.shape[0] // count
    parts = [array[j * rows : (j + 1) * rows] for j in range(count)]
    return parts[:1] + [part.astype(jnp.bfloat16) for part in parts[1:]]


def sum_of(arrays):
    total = arrays[0]
    for one in arrays[1:]:
        total = total + one.astype(jnp.float32)
    return total


def z_bits(sub_count):
    return [1 << at for at in range(sub_count.bit_length() - 1)]


def scatter_along_z(full, sub_count, earlier=()):
    share = full.shape[0] // sub_count
    parts = {m: full[m * share : (m + 1) * share] for m in range(sub_count)}
    for bit in z_bits(sub_count):
        for m in list(parts):
            if m & bit:
                came = swap(parts.pop(m).astype(jnp.bfloat16), "ctx", 2 * bit)
                (came,), _ = after([came], *earlier)
                parts[m ^ bit] = parts[m ^ bit] + came.astype(jnp.float32)
    return parts[0]


def sum_of_halves(part, sub_count, earlier=()):
    low = swap(part.astype(jnp.bfloat16), "ctx", 2 * sub_count)
    (low,), _ = after([low], *earlier)
    return (part + low.astype(jnp.float32)).astype(jnp.bfloat16)


def gather_parts(part, sub_count, earlier=()):
    rows = {0: part}
    for bit in z_bits(sub_count)[::-1]:
        for m, one in list(rows.items()):
            (rows[m | bit],), _ = after([swap(one, "ctx", 2 * bit)], *earlier)
    own = [rows[m] for m in range(sub_count)]
    return own + [swap(one, "ctx", 1) for one in own]


def assemble_kernel(sub_count, regions, first, ids, *refs):
    count = 2 * sub_count * len(regions)
    blocks = iter(refs[2 * (not first) :][:count])
    *outs, buffer, sems = refs[2 * (not first) + count :]
    z, core = ids[0] % sub_count, ids[1]
    copies = []
    filled = 0
    for origin, rows in regions:
        share = rows // sub_count
        for side in range(2):
            for m in range(sub_count):
                to = origin + (core ^ side) * rows + (z ^ m) * share
                to = pl.multiple_of(to, share)
                block_ref = next(blocks)
                width = block_ref.shape[1] // 2
                for which, out_ref in enumerate(outs):
                    piece = buffer.at[which, pl.ds(filled, share), :]
                    piece[...] = block_ref[:, which * width : (which + 1) * width].astype(
                        jnp.float32
                    )
                    copy = pltpu.make_async_copy(
                        piece, out_ref.at[pl.ds(to, share), :], sems.at[len(copies)]
                    )
                    copy.start()
                    copies.append(copy)
                filled += share
    for copy in copies:
        copy.wait()


def assemble(ids, before, blocks, sub_count, regions, block_rows):
    rows = sum(block.shape[0] for block in blocks)
    width = blocks[0].shape[1] // 2
    out = shape_of(block_rows, width, jnp.float32)
    smem = pl.BlockSpec(memory_space=pltpu.SMEM)
    vmem = pl.BlockSpec(memory_space=pltpu.VMEM)
    anywhere = pl.BlockSpec(memory_space=pl.ANY)
    return pl.pallas_call(
        functools.partial(assemble_kernel, sub_count, regions, not before),
        out_shape=(out, out),
        in_specs=[smem] + [anywhere] * len(before) + [vmem] * len(blocks),
        out_specs=(anywhere, anywhere),
        scratch_shapes=[
            pltpu.VMEM((2, rows, width), jnp.float32),
            pltpu.SemaphoreType.DMA((2 * len(blocks),)),
        ],
        input_output_aliases={1: 0, 2: 1} if before else {},
        compiler_params=pltpu.CompilerParams(vmem_limit_bytes=VMEM_LIMIT),
        cost_estimate=NO_COST,
        name="assemble",
    )(ids, *before, *blocks)


def on_device(hidden_in, queries, grad_out, w_key, w_value, stretch_order, doc_lengths):
    inputs = hidden_in[0]
    head_dim = w_key.shape[1]
    dp_count = lax.axis_size("dp")
    ctx_count = lax.axis_size("ctx")
    z_count = ctx_count // 2
    sub_count = z_count // 2
    dp, ctx = lax.axis_index("dp"), lax.axis_index("ctx")
    z, core = ctx // 2, ctx % 2
    ids = jnp.stack([z, core, dp]).astype(jnp.int32)
    me = jnp.reshape(ctx, (1,)).astype(jnp.int32)
    block_rows = w_key.shape[0]
    half_rows = block_rows // 2
    quarter = half_rows // 2
    bits = [1 << at for at in range(dp_count.bit_length() - 1)]
    near = [j for j in range(1, dp_count) if j in bits]
    far = [j for j in range(1, dp_count) if j not in bits]

    def gather_near(*weights):
        pieces = {}
        for turn in range(2):
            for at, j in enumerate(near):
                offset = ((at + turn) % 2) * quarter
                start = core * half_rows + offset
                rows = [lax.dynamic_slice_in_dim(weight, start, quarter, 0) for weight in weights]
                pieces[j, 0, offset] = swap(jnp.concatenate(rows, axis=1), "dp", j)
        return pieces

    def gather_far(landed):
        pieces = {}
        for j in far:
            for offset, bit in ((0, 1 << (j.bit_length() - 1)), (quarter, j & -j)):
                origin = landed.get((j ^ bit, 0, offset), pieces.get((j ^ bit, 0, offset)))
                pieces[j, 0, offset] = swap(origin, "dp", bit)
        return pieces

    def from_other_core(pieces):
        return {(j, 1, offset): swap(one, "ctx", 1) for (j, _, offset), one in pieces.items()}

    def hold(arrays, pieces):
        names = list(pieces)
        tied, ended = after(arrays, *[pieces[name] for name in names])
        pieces.update(zip(names, ended))
        return tied

    def gather_along_z(own):
        return [swap(own, "ctx", 2 * m) if m else own for m in range(z_count)]

    def both_cores(along):
        return [block for one in along for block in (one, swap(one, "ctx", 1))]

    sizes = region_sizes(block_rows)
    regions = [(sum(sizes[:at]), size // 2) for at, size in enumerate(sizes)]
    first_rows = sum(sizes[:-1])
    moving = {
        j: lax.dynamic_slice_in_dim(inputs, (dp ^ j) * block_rows, first_rows, 1)
        for j in range(dp_count)
    }

    near_pieces = gather_near(w_key, w_value)
    far_pieces = gather_far(near_pieces)
    names = list(near_pieces)
    waiting, _ = after([near_pieces[name] for name in names[: len(near)]])
    others = {}
    for name, one in zip(names, waiting):
        (one,), _ = after([one], *others.values())
        others.update(from_other_core({name: one}))
    others.update(from_other_core({name: near_pieces[name] for name in names[len(near) :]}))
    near_pieces.update(others)
    early = project(
        ids, (w_key, w_value), inputs, block_rows, near_pieces, jnp.float32, bytes_cost(1 << 24)
    )
    others = near + far
    early, *tied = hold([early] + [moving[j] for j in others], far_pieces)
    moving.update(zip(others, tied))
    far_pieces.update(from_other_core(far_pieces))
    tied = hold([moving[j] for j in near[:-1]], far_pieces)
    moving.update(zip(near[:-1], tied))
    own = project(ids, (early,), inputs, block_rows, far_pieces, jnp.bfloat16)
    moved = {0: moving[0]}
    moved[near[-1]] = swap(moving[near[-1]], "dp", near[-1])
    moved.update({j: swap(moving[j], "dp", j) for j in near[:-1]})
    along = gather_along_z(own)
    tied, _ = after([moving[j] for j in far], *along)
    moving.update(zip(far, tied))
    along, _ = after(along)
    kv_blocks = both_cores(along)

    moved.update({j: swap(moving[j], "dp", j) for j in far})

    query_grad, keep, send = attention(
        me, stretch_order, doc_lengths[0], queries[0], grad_out[0], kv_blocks, head_dim
    )
    (send,), ended = after([send], *[moved[j] for j in near])
    moved.update(zip(near, ended))
    own, *leaving = add_and_split(keep, swap(send, "ctx", 1), z_count)
    grad = add_all([own] + [swap(one, "ctx", 2 * m) for m, one in enumerate(leaving, 1)])
    grads = [grad] + [swap(grad, "dp", j) for j in range(1, dp_count)]

    (grad,), ended = after([grad], *grads[1:], *[moved[j] for j in far])
    grads[1:] = ended[: dp_count - 1]
    moved.update(zip(far, ended[dp_count - 1 :]))
    groups = [[(0, j, 0, 0)] for j in range(dp_count)]
    ours, came = weight_rows(
        ids, [inputs], [grad], groups, *regions[-1], block_rows, sub_count
    )
    own = parts_over_dp(add_cores(ours, came))
    groups = [[(j, None, j, 0) for j in range(dp_count)]]
    arrays = [moved[j] for j in range(dp_count)]
    moved_parts = [
        add_cores(*weight_rows(ids, arrays, grads, groups, *region, block_rows, sub_count))
        for region in regions[:-1]
    ]
    moved_parts, own = after(moved_parts, *own)
    own = [swap(one, "dp", j) if j else one for j, one in enumerate(own)]
    finals = []
    for part in moved_parts:
        part = scatter_along_z(part, sub_count)
        finals.append(sum_of_halves(part, sub_count))
    part = scatter_along_z(sum_of(own), sub_count, finals[:TIED])
    blocks = gather_parts(finals[0], sub_count)
    last = sum_of_halves(part, sub_count, blocks)
    blocks += [one for final in finals[1:] for one in gather_parts(final, sub_count)]
    outs = assemble(ids, (), blocks, sub_count, regions[:-1], block_rows)
    last = gather_parts(last, sub_count)
    key_rows, value_rows = assemble(ids, outs, last, sub_count, regions[-1:], block_rows)
    return query_grad[None], key_rows, value_rows


def solution(mesh):
    return jax.shard_map(
        on_device,
        mesh=mesh,
        in_specs=(
            P("dp", "ctx", None),
            P("dp", "ctx", None),
            P("dp", "ctx", None),
            P("dp", None),
            P("dp", None),
            P(),
            P("dp", None),
        ),
        out_specs=(P("dp", "ctx", None), P("dp", None), P("dp", None)),
        check_vma=False,
    )
```

```python
import functools
import math

import jax
import jax.numpy as jnp
from jax import lax
from jax.experimental import pallas as pl
from jax.experimental.pallas import tpu as pltpu
from jax.sharding import PartitionSpec as P

VMEM_LIMIT = 28 * 1024 * 1024
NO_COST = pl.CostEstimate(flops=0, bytes_accessed=0, transcendentals=0)


MOVED = (4, 6)
TIED = 2


def region_sizes(block_rows):
    units = block_rows // 256
    sizes = [256 * (units * share // 16) for share in MOVED]
    return sizes + [block_rows - sum(sizes)]


class Plan:
    def __init__(self, **fields):
        self.__dict__.update(fields)


def swap(array, axis, distance):
    count = lax.axis_size(axis)
    return lax.ppermute(array, axis, [(i, i ^ distance) for i in range(count)])


def after(arrays, *earlier):
    tied = lax.optimization_barrier((tuple(arrays), tuple(earlier)))
    return list(tied[0]), list(tied[1])


def shape_of(rows, width, kind=jnp.bfloat16):
    return jax.ShapeDtypeStruct((rows, width), kind)


def kernel_call(kernel, name, outs, scalars, arrays, scratch=(), cost=NO_COST):
    smem = pl.BlockSpec(memory_space=pltpu.SMEM)
    vmem = pl.BlockSpec(memory_space=pltpu.VMEM)
    single = not isinstance(outs, tuple)
    return pl.pallas_call(
        kernel,
        out_shape=outs,
        in_specs=[smem] * len(scalars) + [vmem] * len(arrays),
        out_specs=vmem if single else (vmem,) * len(outs),
        scratch_shapes=list(scratch),
        compiler_params=pltpu.CompilerParams(vmem_limit_bytes=VMEM_LIMIT),
        cost_estimate=cost,
        name=name,
    )(*scalars, *arrays)


def bytes_cost(amount):
    return pl.CostEstimate(flops=0, bytes_accessed=amount, transcendentals=0)


TN = (((0,), (0,)), ((), ()))


def attention_kernel(
    shape, ids, order, lengths, q_ref, g_ref, *refs
):
    ctx_count, stretch_rows, head_count, head_dim, window, chunk = shape
    kv_refs = refs[:ctx_count]
    qgrad_ref, keep_ref, send_ref, keys, values, total, qs, gs, dqs = refs[ctx_count:]
    me = ids[0]
    row_count = 2 * stretch_rows
    stretch_count = 2 * ctx_count
    score_scale = 1.0 / math.sqrt(head_dim)

    def place(device, half):
        return pl.multiple_of(order[2 * device + half] * stretch_rows, stretch_rows)

    for index in range(ctx_count):
        for half in range(2):
            rows = pl.ds(place(me ^ index, half), stretch_rows)
            block = kv_refs[index][half * stretch_rows : (half + 1) * stretch_rows, :]
            keys[rows, :] = block[:, :head_dim]
            values[rows, :] = block[:, head_dim:]
    total[...] = jnp.zeros_like(total)
    for half in range(2):
        for head in range(head_count):
            to = slice((half * head_count + head) * stretch_rows, (half * head_count + head + 1) * stretch_rows)
            rows = slice(half * stretch_rows, (half + 1) * stretch_rows)
            columns = slice(head * head_dim, (head + 1) * head_dim)
            qs[to, :] = q_ref[rows, columns]
            gs[to, :] = g_ref[rows, columns]
    ends = []
    running = 0
    for at in range(lengths.shape[0]):
        running = running + lengths[at]
        ends.append(running)
    chunks_half = head_count * stretch_rows // chunk

    def step(at, carry):
        half = at // chunks_half
        block = order[2 * me + half]
        first = jnp.maximum(block - stretch_count // 2, 0) * stretch_rows
        first = pl.multiple_of(first, stretch_rows)
        part = pl.ds(pl.multiple_of(at * chunk, chunk), chunk)
        inside = (at - half * chunks_half) * chunk + lax.broadcasted_iota(jnp.int32, (1, chunk), 1)
        at_query = block * stretch_rows + lax.rem(inside, stretch_rows)
        begin = jnp.zeros_like(at_query)
        for end in ends:
            begin = jnp.where(at_query >= end, end, begin)
        at_key = lax.broadcasted_iota(jnp.int32, (window, chunk), 0)
        allowed = (at_key + (first - begin)).astype(jnp.uint32) <= (at_query - begin).astype(
            jnp.uint32
        )
        k = keys[pl.ds(first, window), :]
        v = values[pl.ds(first, window), :]
        q = qs[part, :]
        g = gs[part, :]
        last = (((1,), (1,)), ((), ()))
        scores = lax.dot_general(k, q, last, preferred_element_type=jnp.float32)
        masked = jnp.where(allowed, scores, -jnp.inf)
        largest = jnp.max(masked, axis=0, keepdims=True)
        expsum = jnp.exp2((masked - largest) * (score_scale * math.log2(math.e)))
        probs = expsum * (1.0 / jnp.sum(expsum, axis=0, keepdims=True))
        probs_low = probs.astype(jnp.bfloat16)
        dprob = lax.dot_general(v, g, last, preferred_element_type=jnp.float32)
        delta = jnp.sum(probs_low.astype(jnp.float32) * dprob, axis=0, keepdims=True)
        dscore = (probs * (dprob - delta)).astype(jnp.bfloat16)
        dq = lax.dot_general(
            k, dscore, (((0,), (0,)), ((), ())), preferred_element_type=jnp.float32
        )
        dqs[part, :] = (jnp.transpose(dq) * score_scale).astype(jnp.bfloat16)
        dk = jnp.dot(dscore, q, preferred_element_type=jnp.float32) * score_scale
        dv = jnp.dot(probs_low, g, preferred_element_type=jnp.float32)
        total[pl.ds(first, window), :head_dim] += dk
        total[pl.ds(first, window), head_dim:] += dv
        return carry

    lax.fori_loop(0, 2 * chunks_half, step, 0, unroll=3)
    for half in range(2):
        for head in range(head_count):
            origin = slice((half * head_count + head) * stretch_rows, (half * head_count + head + 1) * stretch_rows)
            rows = slice(half * stretch_rows, (half + 1) * stretch_rows)
            columns = slice(head * head_dim, (head + 1) * head_dim)
            qgrad_ref[rows, columns] = dqs[origin, :]
    for index in range(ctx_count):
        for half in range(2):
            rows = pl.ds(place(me ^ index, half), stretch_rows)
            start = (index // 2) * row_count + half * stretch_rows
            if index % 2:
                send_ref[start : start + stretch_rows, :] = total[rows, :].astype(jnp.bfloat16)
            else:
                keep_ref[start : start + stretch_rows, :] = total[rows, :]


def attention(me, order, lengths, queries, cotangent, kv_blocks, head_dim):
    row_count, width = queries.shape
    ctx_count = len(kv_blocks)
    stretch_rows = row_count // 2
    head_count = width // head_dim
    seq_rows = row_count * ctx_count
    window = seq_rows // 2 + stretch_rows
    stacked = head_count * stretch_rows
    chunk = 256 if stacked % 256 == 0 else 128
    shape = (ctx_count, stretch_rows, head_count, head_dim, window, chunk)
    smem = pl.BlockSpec(memory_space=pltpu.SMEM)
    vmem = pl.BlockSpec(memory_space=pltpu.VMEM)
    half_rows = seq_rows // 2
    return pl.pallas_call(
        functools.partial(attention_kernel, shape),
        out_shape=(
            jax.ShapeDtypeStruct((row_count, width), jnp.bfloat16),
            jax.ShapeDtypeStruct((half_rows, 2 * head_dim), jnp.float32),
            jax.ShapeDtypeStruct((half_rows, 2 * head_dim), jnp.bfloat16),
        ),
        in_specs=[smem] * 3 + [vmem] * (2 + ctx_count),
        out_specs=(vmem,) * 3,
        scratch_shapes=[
            pltpu.VMEM((seq_rows, head_dim), jnp.bfloat16),
            pltpu.VMEM((seq_rows, head_dim), jnp.bfloat16),
            pltpu.VMEM((seq_rows, 2 * head_dim), jnp.float32),
            pltpu.VMEM((2 * stacked, head_dim), jnp.bfloat16),
            pltpu.VMEM((2 * stacked, head_dim), jnp.bfloat16),
            pltpu.VMEM((2 * stacked, head_dim), jnp.bfloat16),
        ],
        compiler_params=pltpu.CompilerParams(vmem_limit_bytes=VMEM_LIMIT),
        cost_estimate=NO_COST,
        name="attention",
    )(me, order, lengths, queries, cotangent, *kv_blocks)


def project_kernel(plan, ids, hidden, *refs):
    out_ref = refs[-1]
    dp, core = ids[2], ids[1]
    if plan.start:
        total = refs[0][...]
    else:
        columns = pl.ds(pl.multiple_of(dp * plan.block_rows, plan.block_rows), plan.block_rows)
        total = jnp.concatenate(
            [
                jnp.dot(hidden[:, columns], own[...], preferred_element_type=jnp.float32)
                for own in refs[:2]
            ],
            axis=1,
        )
    for (block, side, offset), weight in zip(plan.terms, refs[1 if plan.start else 2 : -1]):
        from_column = (dp ^ block) * plan.block_rows + (core ^ side) * plan.side_rows + offset
        columns = pl.ds(pl.multiple_of(from_column, 128), weight.shape[0])
        total += jnp.dot(hidden[:, columns], weight[...], preferred_element_type=jnp.float32)
    out_ref[...] = total.astype(out_ref.dtype)


def project(ids, begin, inputs, block_rows, pieces, kind, cost=NO_COST):
    names = sorted(pieces)
    weights = [pieces[name] for name in names]
    plan = Plan(
        terms=names, start=len(begin) == 1, block_rows=block_rows, side_rows=block_rows // 2
    )
    return kernel_call(
        functools.partial(project_kernel, plan),
        "project",
        shape_of(inputs.shape[0], weights[0].shape[1], kind),
        (ids,),
        (inputs, *begin, *weights),
        cost=cost,
    )


def split_kernel(rows, keep, came, own_ref, *leaving_refs):
    own_ref[...] = keep[:rows, :] + came[:rows, :].astype(jnp.float32)
    for m, leaving in enumerate(leaving_refs, 1):
        block = slice(m * rows, (m + 1) * rows)
        leaving[...] = (keep[block, :] + came[block, :].astype(jnp.float32)).astype(leaving.dtype)


def add_and_split(keep, came, count):
    rows, width = keep.shape[0] // count, keep.shape[1]
    outs = (shape_of(rows, width, jnp.float32),) + (shape_of(rows, width),) * (count - 1)
    return kernel_call(functools.partial(split_kernel, rows), "split", outs, (), (keep, came))


def total_kernel(*refs):
    total = refs[0][...]
    for one in refs[1:-1]:
        total = total + one[...].astype(jnp.float32)
    refs[-1][...] = total.astype(refs[-1].dtype)


def add_all(arrays):
    out = jax.ShapeDtypeStruct(arrays[0].shape, jnp.bfloat16)
    return kernel_call(total_kernel, "total", out, (), arrays)


def weight_kernel(plan, ids, *refs):
    hidden = refs[: plan.hidden]
    grads = refs[plan.hidden : -2]
    z, core, dp = ids[0] % plan.sub_count, ids[1], ids[2]
    rows = plan.rows
    share = rows // plan.sub_count
    tile = next(size for size in (512, 256, 128) if rows % size == 0)
    step = math.gcd(share, tile)
    for side, out_ref in ((1, refs[-2]), (0, refs[-1])):
        for at, group in enumerate(plan.groups):
            for start in range(0, rows, tile):
                product = None
                for array, block, grad, shift in group:
                    origin = plan.origin - shift + (core ^ side) * rows + start
                    if block is not None:
                        origin = origin + (dp ^ block) * plan.block_rows
                    columns = pl.ds(pl.multiple_of(origin, 128), tile)
                    term = lax.dot_general(
                        hidden[array][:, columns],
                        grads[grad][...],
                        TN,
                        preferred_element_type=jnp.float32,
                    )
                    product = term if product is None else product + term
                for inner in range(0, tile, step):
                    part, offset = divmod(start + inner, share)
                    to = pl.multiple_of(at * rows + (z ^ part) * share + offset, step)
                    piece = product[inner : inner + step, :]
                    out_ref[pl.ds(to, step), :] = piece.astype(out_ref.dtype)


def weight_rows(ids, hidden, grads, groups, origin, rows, block_rows, sub_count):
    plan = Plan(
        hidden=len(hidden),
        groups=groups,
        origin=origin,
        rows=rows,
        block_rows=block_rows,
        sub_count=sub_count,
    )
    out = shape_of(rows * len(groups), grads[0].shape[1])
    theirs, ours = kernel_call(
        functools.partial(weight_kernel, plan),
        "weight_rows",
        (out, out),
        (ids,),
        (*hidden, *grads),
    )
    return ours, swap(theirs, "ctx", 1)


def add_cores(ours, came):
    return ours.astype(jnp.float32) + came.astype(jnp.float32)


def parts_over_dp(array):
    count = lax.axis_size("dp")
    rows = array.shape[0] // count
    parts = [array[j * rows : (j + 1) * rows] for j in range(count)]
    return parts[:1] + [part.astype(jnp.bfloat16) for part in parts[1:]]


def sum_of(arrays):
    total = arrays[0]
    for one in arrays[1:]:
        total = total + one.astype(jnp.float32)
    return total


def z_bits(sub_count):
    return [1 << at for at in range(sub_count.bit_length() - 1)]


def scatter_along_z(full, sub_count, earlier=()):
    share = full.shape[0] // sub_count
    parts = {m: full[m * share : (m + 1) * share] for m in range(sub_count)}
    for bit in z_bits(sub_count):
        for m in list(parts):
            if m & bit:
                came = swap(parts.pop(m).astype(jnp.bfloat16), "ctx", 2 * bit)
                (came,), _ = after([came], *earlier)
                parts[m ^ bit] = parts[m ^ bit] + came.astype(jnp.float32)
    return parts[0]


def sum_of_halves(part, sub_count, earlier=()):
    low = swap(part.astype(jnp.bfloat16), "ctx", 2 * sub_count)
    (low,), _ = after([low], *earlier)
    return (part + low.astype(jnp.float32)).astype(jnp.bfloat16)


def gather_parts(part, sub_count, earlier=()):
    rows = {0: part}
    for bit in z_bits(sub_count)[::-1]:
        for m, one in list(rows.items()):
            (rows[m | bit],), _ = after([swap(one, "ctx", 2 * bit)], *earlier)
    own = [rows[m] for m in range(sub_count)]
    return own + [swap(one, "ctx", 1) for one in own]


def assemble_kernel(sub_count, regions, first, ids, *refs):
    count = 2 * sub_count * len(regions)
    blocks = iter(refs[2 * (not first) :][:count])
    *outs, buffer, sems = refs[2 * (not first) + count :]
    z, core = ids[0] % sub_count, ids[1]
    copies = []
    filled = 0
    for origin, rows in regions:
        share = rows // sub_count
        for side in range(2):
            for m in range(sub_count):
                to = origin + (core ^ side) * rows + (z ^ m) * share
                to = pl.multiple_of(to, share)
                block_ref = next(blocks)
                width = block_ref.shape[1] // 2
                for which, out_ref in enumerate(outs):
                    piece = buffer.at[which, pl.ds(filled, share), :]
                    piece[...] = block_ref[:, which * width : (which + 1) * width].astype(
                        jnp.float32
                    )
                    copy = pltpu.make_async_copy(
                        piece, out_ref.at[pl.ds(to, share), :], sems.at[len(copies)]
                    )
                    copy.start()
                    copies.append(copy)
                filled += share
    for copy in copies:
        copy.wait()


def assemble(ids, before, blocks, sub_count, regions, block_rows):
    rows = sum(block.shape[0] for block in blocks)
    width = blocks[0].shape[1] // 2
    out = shape_of(block_rows, width, jnp.float32)
    smem = pl.BlockSpec(memory_space=pltpu.SMEM)
    vmem = pl.BlockSpec(memory_space=pltpu.VMEM)
    anywhere = pl.BlockSpec(memory_space=pl.ANY)
    return pl.pallas_call(
        functools.partial(assemble_kernel, sub_count, regions, not before),
        out_shape=(out, out),
        in_specs=[smem] + [anywhere] * len(before) + [vmem] * len(blocks),
        out_specs=(anywhere, anywhere),
        scratch_shapes=[
            pltpu.VMEM((2, rows, width), jnp.float32),
            pltpu.SemaphoreType.DMA((2 * len(blocks),)),
        ],
        input_output_aliases={1: 0, 2: 1} if before else {},
        compiler_params=pltpu.CompilerParams(vmem_limit_bytes=VMEM_LIMIT),
        cost_estimate=NO_COST,
        name="assemble",
    )(ids, *before, *blocks)


def on_device(hidden_in, queries, grad_out, w_key, w_value, stretch_order, doc_lengths):
    inputs = hidden_in[0]
    head_dim = w_key.shape[1]
    dp_count = lax.axis_size("dp")
    ctx_count = lax.axis_size("ctx")
    z_count = ctx_count // 2
    sub_count = z_count // 2
    dp, ctx = lax.axis_index("dp"), lax.axis_index("ctx")
    z, core = ctx // 2, ctx % 2
    ids = jnp.stack([z, core, dp]).astype(jnp.int32)
    me = jnp.reshape(ctx, (1,)).astype(jnp.int32)
    block_rows = w_key.shape[0]
    half_rows = block_rows // 2
    quarter = half_rows // 2
    bits = [1 << at for at in range(dp_count.bit_length() - 1)]
    near = [j for j in range(1, dp_count) if j in bits]
    far = [j for j in range(1, dp_count) if j not in bits]

    def gather_near(*weights):
        pieces = {}
        for turn in range(2):
            for at, j in enumerate(near):
                offset = ((at + turn) % 2) * quarter
                start = core * half_rows + offset
                rows = [lax.dynamic_slice_in_dim(weight, start, quarter, 0) for weight in weights]
                pieces[j, 0, offset] = swap(jnp.concatenate(rows, axis=1), "dp", j)
        return pieces

    def gather_far(landed):
        pieces = {}
        for j in far:
            for offset, bit in ((0, 1 << (j.bit_length() - 1)), (quarter, j & -j)):
                origin = landed.get((j ^ bit, 0, offset), pieces.get((j ^ bit, 0, offset)))
                pieces[j, 0, offset] = swap(origin, "dp", bit)
        return pieces

    def from_other_core(pieces):
        return {(j, 1, offset): swap(one, "ctx", 1) for (j, _, offset), one in pieces.items()}

    def hold(arrays, pieces):
        names = list(pieces)
        tied, ended = after(arrays, *[pieces[name] for name in names])
        pieces.update(zip(names, ended))
        return tied

    def gather_along_z(own):
        return [swap(own, "ctx", 2 * m) if m else own for m in range(z_count)]

    def both_cores(along):
        return [block for one in along for block in (one, swap(one, "ctx", 1))]

    sizes = region_sizes(block_rows)
    regions = [(sum(sizes[:at]), size // 2) for at, size in enumerate(sizes)]
    first_rows = sum(sizes[:-1])
    moving = {
        j: lax.dynamic_slice_in_dim(inputs, (dp ^ j) * block_rows, first_rows, 1)
        for j in range(dp_count)
    }

    near_pieces = gather_near(w_key, w_value)
    far_pieces = gather_far(near_pieces)
    names = list(near_pieces)
    waiting, _ = after([near_pieces[name] for name in names[: len(near)]])
    others = {}
    for name, one in zip(names, waiting):
        (one,), _ = after([one], *others.values())
        others.update(from_other_core({name: one}))
    others.update(from_other_core({name: near_pieces[name] for name in names[len(near) :]}))
    near_pieces.update(others)
    early = project(
        ids, (w_key, w_value), inputs, block_rows, near_pieces, jnp.float32, bytes_cost(1 << 24)
    )
    others = near + far
    early, *tied = hold([early] + [moving[j] for j in others], far_pieces)
    moving.update(zip(others, tied))
    far_pieces.update(from_other_core(far_pieces))
    tied = hold([moving[j] for j in near[:-1]], far_pieces)
    moving.update(zip(near[:-1], tied))
    own = project(ids, (early,), inputs, block_rows, far_pieces, jnp.bfloat16)
    moved = {0: moving[0]}
    moved[near[-1]] = swap(moving[near[-1]], "dp", near[-1])
    moved.update({j: swap(moving[j], "dp", j) for j in near[:-1]})
    along = gather_along_z(own)
    tied, _ = after([moving[j] for j in far], *along)
    moving.update(zip(far, tied))
    along, _ = after(along)
    kv_blocks = both_cores(along)

    moved.update({j: swap(moving[j], "dp", j) for j in far})

    query_grad, keep, send = attention(
        me, stretch_order, doc_lengths[0], queries[0], grad_out[0], kv_blocks, head_dim
    )
    (send,), ended = after([send], *[moved[j] for j in near])
    moved.update(zip(near, ended))
    own, *leaving = add_and_split(keep, swap(send, "ctx", 1), z_count)
    grad = add_all([own] + [swap(one, "ctx", 2 * m) for m, one in enumerate(leaving, 1)])
    grads = [grad] + [swap(grad, "dp", j) for j in range(1, dp_count)]

    (grad,), ended = after([grad], *grads[1:], *[moved[j] for j in far])
    grads[1:] = ended[: dp_count - 1]
    moved.update(zip(far, ended[dp_count - 1 :]))
    groups = [[(0, j, 0, 0)] for j in range(dp_count)]
    ours, came = weight_rows(
        ids, [inputs], [grad], groups, *regions[-1], block_rows, sub_count
    )
    own = parts_over_dp(add_cores(ours, came))
    groups = [[(j, None, j, 0) for j in range(dp_count)]]
    arrays = [moved[j] for j in range(dp_count)]
    moved_parts = [
        add_cores(*weight_rows(ids, arrays, grads, groups, *region, block_rows, sub_count))
        for region in regions[:-1]
    ]
    moved_parts, own = after(moved_parts, *own)
    own = [swap(one, "dp", j) if j else one for j, one in enumerate(own)]
    finals = []
    for part in moved_parts:
        part = scatter_along_z(part, sub_count)
        finals.append(sum_of_halves(part, sub_count))
    part = scatter_along_z(sum_of(own), sub_count, finals[:TIED])
    finals, _ = after(finals, part)
    blocks = gather_parts(finals[0], sub_count)
    last = sum_of_halves(part, sub_count)
    (last,), _ = after([last], *blocks)
    blocks += [one for final in finals[1:] for one in gather_parts(final, sub_count)]
    outs = assemble(ids, (), blocks, sub_count, regions[:-1], block_rows)
    last = gather_parts(last, sub_count)
    key_rows, value_rows = assemble(ids, outs, last, sub_count, regions[-1:], block_rows)
    return query_grad[None], key_rows, value_rows


def solution(mesh):
    return jax.shard_map(
        on_device,
        mesh=mesh,
        in_specs=(
            P("dp", "ctx", None),
            P("dp", "ctx", None),
            P("dp", "ctx", None),
            P("dp", None),
            P("dp", None),
            P(),
            P("dp", None),
        ),
        out_specs=(P("dp", "ctx", None), P("dp", None), P("dp", None)),
        check_vma=False,
    )
```

```python
import functools
import math

import jax
import jax.numpy as jnp
from jax import lax
from jax.experimental import pallas as pl
from jax.experimental.pallas import tpu as pltpu
from jax.sharding import PartitionSpec as P

VMEM_LIMIT = 28 * 1024 * 1024
NO_COST = pl.CostEstimate(flops=0, bytes_accessed=0, transcendentals=0)


MOVED = (4, 6)
TIED = 2


def region_sizes(block_rows):
    units = block_rows // 256
    sizes = [256 * (units * share // 16) for share in MOVED]
    return sizes + [block_rows - sum(sizes)]


class Plan:
    def __init__(self, **fields):
        self.__dict__.update(fields)


def swap(array, axis, distance):
    count = lax.axis_size(axis)
    return lax.ppermute(array, axis, [(i, i ^ distance) for i in range(count)])


def after(arrays, *earlier):
    tied = lax.optimization_barrier((tuple(arrays), tuple(earlier)))
    return list(tied[0]), list(tied[1])


def shape_of(rows, width, kind=jnp.bfloat16):
    return jax.ShapeDtypeStruct((rows, width), kind)


def kernel_call(kernel, name, outs, scalars, arrays, scratch=(), cost=NO_COST):
    smem = pl.BlockSpec(memory_space=pltpu.SMEM)
    vmem = pl.BlockSpec(memory_space=pltpu.VMEM)
    single = not isinstance(outs, tuple)
    return pl.pallas_call(
        kernel,
        out_shape=outs,
        in_specs=[smem] * len(scalars) + [vmem] * len(arrays),
        out_specs=vmem if single else (vmem,) * len(outs),
        scratch_shapes=list(scratch),
        compiler_params=pltpu.CompilerParams(vmem_limit_bytes=VMEM_LIMIT),
        cost_estimate=cost,
        name=name,
    )(*scalars, *arrays)


def bytes_cost(amount):
    return pl.CostEstimate(flops=0, bytes_accessed=amount, transcendentals=0)


TN = (((0,), (0,)), ((), ()))


def attention_kernel(
    shape, ids, order, lengths, q_ref, g_ref, *refs
):
    ctx_count, stretch_rows, head_count, head_dim, window, chunk = shape
    kv_refs = refs[:ctx_count]
    qgrad_ref, keep_ref, send_ref, keys, values, total, qs, gs, dqs = refs[ctx_count:]
    me = ids[0]
    row_count = 2 * stretch_rows
    stretch_count = 2 * ctx_count
    score_scale = 1.0 / math.sqrt(head_dim)

    def place(device, half):
        return pl.multiple_of(order[2 * device + half] * stretch_rows, stretch_rows)

    for index in range(ctx_count):
        for half in range(2):
            rows = pl.ds(place(me ^ index, half), stretch_rows)
            block = kv_refs[index][half * stretch_rows : (half + 1) * stretch_rows, :]
            keys[rows, :] = block[:, :head_dim]
            values[rows, :] = block[:, head_dim:]
    total[...] = jnp.zeros_like(total)
    for half in range(2):
        for head in range(head_count):
            to = slice((half * head_count + head) * stretch_rows, (half * head_count + head + 1) * stretch_rows)
            rows = slice(half * stretch_rows, (half + 1) * stretch_rows)
            columns = slice(head * head_dim, (head + 1) * head_dim)
            qs[to, :] = q_ref[rows, columns]
            gs[to, :] = g_ref[rows, columns]
    ends = []
    running = 0
    for at in range(lengths.shape[0]):
        running = running + lengths[at]
        ends.append(running)
    chunks_half = head_count * stretch_rows // chunk

    def step(at, carry):
        half = at // chunks_half
        block = order[2 * me + half]
        first = jnp.maximum(block - stretch_count // 2, 0) * stretch_rows
        first = pl.multiple_of(first, stretch_rows)
        part = pl.ds(pl.multiple_of(at * chunk, chunk), chunk)
        inside = (at - half * chunks_half) * chunk + lax.broadcasted_iota(jnp.int32, (1, chunk), 1)
        at_query = block * stretch_rows + lax.rem(inside, stretch_rows)
        begin = jnp.zeros_like(at_query)
        for end in ends:
            begin = jnp.where(at_query >= end, end, begin)
        at_key = lax.broadcasted_iota(jnp.int32, (window, chunk), 0)
        allowed = (at_key + (first - begin)).astype(jnp.uint32) <= (at_query - begin).astype(
            jnp.uint32
        )
        k = keys[pl.ds(first, window), :]
        v = values[pl.ds(first, window), :]
        q = qs[part, :]
        g = gs[part, :]
        last = (((1,), (1,)), ((), ()))
        scores = lax.dot_general(k, q, last, preferred_element_type=jnp.float32)
        masked = jnp.where(allowed, scores, -jnp.inf)
        largest = jnp.max(masked, axis=0, keepdims=True)
        expsum = jnp.exp2((masked - largest) * (score_scale * math.log2(math.e)))
        probs = expsum * (1.0 / jnp.sum(expsum, axis=0, keepdims=True))
        probs_low = probs.astype(jnp.bfloat16)
        dprob = lax.dot_general(v, g, last, preferred_element_type=jnp.float32)
        delta = jnp.sum(probs_low.astype(jnp.float32) * dprob, axis=0, keepdims=True)
        dscore = (probs * (dprob - delta)).astype(jnp.bfloat16)
        dq = lax.dot_general(
            k, dscore, (((0,), (0,)), ((), ())), preferred_element_type=jnp.float32
        )
        dqs[part, :] = (jnp.transpose(dq) * score_scale).astype(jnp.bfloat16)
        dk = jnp.dot(dscore, q, preferred_element_type=jnp.float32) * score_scale
        dv = jnp.dot(probs_low, g, preferred_element_type=jnp.float32)
        total[pl.ds(first, window), :head_dim] += dk
        total[pl.ds(first, window), head_dim:] += dv
        return carry

    lax.fori_loop(0, 2 * chunks_half, step, 0, unroll=3)
    for half in range(2):
        for head in range(head_count):
            origin = slice((half * head_count + head) * stretch_rows, (half * head_count + head + 1) * stretch_rows)
            rows = slice(half * stretch_rows, (half + 1) * stretch_rows)
            columns = slice(head * head_dim, (head + 1) * head_dim)
            qgrad_ref[rows, columns] = dqs[origin, :]
    for index in range(ctx_count):
        for half in range(2):
            rows = pl.ds(place(me ^ index, half), stretch_rows)
            start = (index // 2) * row_count + half * stretch_rows
            if index % 2:
                send_ref[start : start + stretch_rows, :] = total[rows, :].astype(jnp.bfloat16)
            else:
                keep_ref[start : start + stretch_rows, :] = total[rows, :]


def attention(me, order, lengths, queries, cotangent, kv_blocks, head_dim):
    row_count, width = queries.shape
    ctx_count = len(kv_blocks)
    stretch_rows = row_count // 2
    head_count = width // head_dim
    seq_rows = row_count * ctx_count
    window = seq_rows // 2 + stretch_rows
    stacked = head_count * stretch_rows
    chunk = 256 if stacked % 256 == 0 else 128
    shape = (ctx_count, stretch_rows, head_count, head_dim, window, chunk)
    smem = pl.BlockSpec(memory_space=pltpu.SMEM)
    vmem = pl.BlockSpec(memory_space=pltpu.VMEM)
    half_rows = seq_rows // 2
    return pl.pallas_call(
        functools.partial(attention_kernel, shape),
        out_shape=(
            jax.ShapeDtypeStruct((row_count, width), jnp.bfloat16),
            jax.ShapeDtypeStruct((half_rows, 2 * head_dim), jnp.float32),
            jax.ShapeDtypeStruct((half_rows, 2 * head_dim), jnp.bfloat16),
        ),
        in_specs=[smem] * 3 + [vmem] * (2 + ctx_count),
        out_specs=(vmem,) * 3,
        scratch_shapes=[
            pltpu.VMEM((seq_rows, head_dim), jnp.bfloat16),
            pltpu.VMEM((seq_rows, head_dim), jnp.bfloat16),
            pltpu.VMEM((seq_rows, 2 * head_dim), jnp.float32),
            pltpu.VMEM((2 * stacked, head_dim), jnp.bfloat16),
            pltpu.VMEM((2 * stacked, head_dim), jnp.bfloat16),
            pltpu.VMEM((2 * stacked, head_dim), jnp.bfloat16),
        ],
        compiler_params=pltpu.CompilerParams(vmem_limit_bytes=VMEM_LIMIT),
        cost_estimate=NO_COST,
        name="attention",
    )(me, order, lengths, queries, cotangent, *kv_blocks)


def project_kernel(plan, ids, hidden, *refs):
    out_ref = refs[-1]
    dp, core = ids[2], ids[1]
    if plan.start:
        total = refs[0][...]
    else:
        columns = pl.ds(pl.multiple_of(dp * plan.block_rows, plan.block_rows), plan.block_rows)
        total = jnp.concatenate(
            [
                jnp.dot(hidden[:, columns], own[...], preferred_element_type=jnp.float32)
                for own in refs[:2]
            ],
            axis=1,
        )
    for (block, side, offset), weight in zip(plan.terms, refs[1 if plan.start else 2 : -1]):
        from_column = (dp ^ block) * plan.block_rows + (core ^ side) * plan.side_rows + offset
        columns = pl.ds(pl.multiple_of(from_column, 128), weight.shape[0])
        total += jnp.dot(hidden[:, columns], weight[...], preferred_element_type=jnp.float32)
    out_ref[...] = total.astype(out_ref.dtype)


def project(ids, begin, inputs, block_rows, pieces, kind, cost=NO_COST):
    names = sorted(pieces)
    weights = [pieces[name] for name in names]
    plan = Plan(
        terms=names, start=len(begin) == 1, block_rows=block_rows, side_rows=block_rows // 2
    )
    return kernel_call(
        functools.partial(project_kernel, plan),
        "project",
        shape_of(inputs.shape[0], weights[0].shape[1], kind),
        (ids,),
        (inputs, *begin, *weights),
        cost=cost,
    )


def split_kernel(rows, keep, came, own_ref, *leaving_refs):
    own_ref[...] = keep[:rows, :] + came[:rows, :].astype(jnp.float32)
    for m, leaving in enumerate(leaving_refs, 1):
        block = slice(m * rows, (m + 1) * rows)
        leaving[...] = (keep[block, :] + came[block, :].astype(jnp.float32)).astype(leaving.dtype)


def add_and_split(keep, came, count):
    rows, width = keep.shape[0] // count, keep.shape[1]
    outs = (shape_of(rows, width, jnp.float32),) + (shape_of(rows, width),) * (count - 1)
    return kernel_call(functools.partial(split_kernel, rows), "split", outs, (), (keep, came))


def total_kernel(*refs):
    total = refs[0][...]
    for one in refs[1:-1]:
        total = total + one[...].astype(jnp.float32)
    refs[-1][...] = total.astype(refs[-1].dtype)


def add_all(arrays):
    out = jax.ShapeDtypeStruct(arrays[0].shape, jnp.bfloat16)
    return kernel_call(total_kernel, "total", out, (), arrays)


def weight_kernel(plan, ids, *refs):
    hidden = refs[: plan.hidden]
    grads = refs[plan.hidden : -2]
    z, core, dp = ids[0] % plan.sub_count, ids[1], ids[2]
    rows = plan.rows
    share = rows // plan.sub_count
    tile = next(size for size in (512, 256, 128) if rows % size == 0)
    step = math.gcd(share, tile)
    for side, out_ref in ((1, refs[-2]), (0, refs[-1])):
        for at, group in enumerate(plan.groups):
            for start in range(0, rows, tile):
                product = None
                for array, block, grad, shift in group:
                    origin = plan.origin - shift + (core ^ side) * rows + start
                    if block is not None:
                        origin = origin + (dp ^ block) * plan.block_rows
                    columns = pl.ds(pl.multiple_of(origin, 128), tile)
                    term = lax.dot_general(
                        hidden[array][:, columns],
                        grads[grad][...],
                        TN,
                        preferred_element_type=jnp.float32,
                    )
                    product = term if product is None else product + term
                for inner in range(0, tile, step):
                    part, offset = divmod(start + inner, share)
                    to = pl.multiple_of(at * rows + (z ^ part) * share + offset, step)
                    piece = product[inner : inner + step, :]
                    out_ref[pl.ds(to, step), :] = piece.astype(out_ref.dtype)


def weight_rows(ids, hidden, grads, groups, origin, rows, block_rows, sub_count):
    plan = Plan(
        hidden=len(hidden),
        groups=groups,
        origin=origin,
        rows=rows,
        block_rows=block_rows,
        sub_count=sub_count,
    )
    out = shape_of(rows * len(groups), grads[0].shape[1])
    theirs, ours = kernel_call(
        functools.partial(weight_kernel, plan),
        "weight_rows",
        (out, out),
        (ids,),
        (*hidden, *grads),
    )
    return ours, swap(theirs, "ctx", 1)


def add_cores(ours, came):
    return ours.astype(jnp.float32) + came.astype(jnp.float32)


def parts_over_dp(array):
    count = lax.axis_size("dp")
    rows = array.shape[0] // count
    parts = [array[j * rows : (j + 1) * rows] for j in range(count)]
    return parts[:1] + [part.astype(jnp.bfloat16) for part in parts[1:]]


def sum_of(arrays):
    total = arrays[0]
    for one in arrays[1:]:
        total = total + one.astype(jnp.float32)
    return total


def z_bits(sub_count):
    return [1 << at for at in range(sub_count.bit_length() - 1)]


def scatter_along_z(full, sub_count, earlier=()):
    share = full.shape[0] // sub_count
    parts = {m: full[m * share : (m + 1) * share] for m in range(sub_count)}
    for bit in z_bits(sub_count):
        for m in list(parts):
            if m & bit:
                came = swap(parts.pop(m).astype(jnp.bfloat16), "ctx", 2 * bit)
                (came,), _ = after([came], *earlier)
                parts[m ^ bit] = parts[m ^ bit] + came.astype(jnp.float32)
    return parts[0]


def sum_of_halves(part, sub_count, earlier=()):
    low = swap(part.astype(jnp.bfloat16), "ctx", 2 * sub_count)
    (low,), _ = after([low], *earlier)
    return (part + low.astype(jnp.float32)).astype(jnp.bfloat16)


def gather_parts(part, sub_count, earlier=()):
    rows = {0: part}
    for bit in z_bits(sub_count)[::-1]:
        for m, one in list(rows.items()):
            (rows[m | bit],), _ = after([swap(one, "ctx", 2 * bit)], *earlier)
    own = [rows[m] for m in range(sub_count)]
    return own + [swap(one, "ctx", 1) for one in own]


def assemble_kernel(sub_count, regions, first, ids, *refs):
    count = 2 * sub_count * len(regions)
    blocks = iter(refs[2 * (not first) :][:count])
    *outs, buffer, sems = refs[2 * (not first) + count :]
    z, core = ids[0] % sub_count, ids[1]
    copies = []
    filled = 0
    for origin, rows in regions:
        share = rows // sub_count
        for side in range(2):
            for m in range(sub_count):
                to = origin + (core ^ side) * rows + (z ^ m) * share
                to = pl.multiple_of(to, share)
                block_ref = next(blocks)
                width = block_ref.shape[1] // 2
                for which, out_ref in enumerate(outs):
                    piece = buffer.at[which, pl.ds(filled, share), :]
                    piece[...] = block_ref[:, which * width : (which + 1) * width].astype(
                        jnp.float32
                    )
                    copy = pltpu.make_async_copy(
                        piece, out_ref.at[pl.ds(to, share), :], sems.at[len(copies)]
                    )
                    copy.start()
                    copies.append(copy)
                filled += share
    for copy in copies:
        copy.wait()


def assemble(ids, before, blocks, sub_count, regions, block_rows):
    rows = sum(block.shape[0] for block in blocks)
    width = blocks[0].shape[1] // 2
    out = shape_of(block_rows, width, jnp.float32)
    smem = pl.BlockSpec(memory_space=pltpu.SMEM)
    vmem = pl.BlockSpec(memory_space=pltpu.VMEM)
    anywhere = pl.BlockSpec(memory_space=pl.ANY)
    return pl.pallas_call(
        functools.partial(assemble_kernel, sub_count, regions, not before),
        out_shape=(out, out),
        in_specs=[smem] + [anywhere] * len(before) + [vmem] * len(blocks),
        out_specs=(anywhere, anywhere),
        scratch_shapes=[
            pltpu.VMEM((2, rows, width), jnp.float32),
            pltpu.SemaphoreType.DMA((2 * len(blocks),)),
        ],
        input_output_aliases={1: 0, 2: 1} if before else {},
        compiler_params=pltpu.CompilerParams(vmem_limit_bytes=VMEM_LIMIT),
        cost_estimate=NO_COST,
        name="assemble",
    )(ids, *before, *blocks)


def on_device(hidden_in, queries, grad_out, w_key, w_value, stretch_order, doc_lengths):
    inputs = hidden_in[0]
    head_dim = w_key.shape[1]
    dp_count = lax.axis_size("dp")
    ctx_count = lax.axis_size("ctx")
    z_count = ctx_count // 2
    sub_count = z_count // 2
    dp, ctx = lax.axis_index("dp"), lax.axis_index("ctx")
    z, core = ctx // 2, ctx % 2
    ids = jnp.stack([z, core, dp]).astype(jnp.int32)
    me = jnp.reshape(ctx, (1,)).astype(jnp.int32)
    block_rows = w_key.shape[0]
    half_rows = block_rows // 2
    quarter = half_rows // 2
    bits = [1 << at for at in range(dp_count.bit_length() - 1)]
    near = [j for j in range(1, dp_count) if j in bits]
    far = [j for j in range(1, dp_count) if j not in bits]

    def gather_near(*weights):
        pieces = {}
        for turn in range(2):
            for at, j in enumerate(near):
                offset = ((at + turn) % 2) * quarter
                start = core * half_rows + offset
                rows = [lax.dynamic_slice_in_dim(weight, start, quarter, 0) for weight in weights]
                pieces[j, 0, offset] = swap(jnp.concatenate(rows, axis=1), "dp", j)
        return pieces

    def gather_far(landed):
        pieces = {}
        for j in far:
            for offset, bit in ((0, 1 << (j.bit_length() - 1)), (quarter, j & -j)):
                origin = landed.get((j ^ bit, 0, offset), pieces.get((j ^ bit, 0, offset)))
                pieces[j, 0, offset] = swap(origin, "dp", bit)
        return pieces

    def from_other_core(pieces):
        return {(j, 1, offset): swap(one, "ctx", 1) for (j, _, offset), one in pieces.items()}

    def hold(arrays, pieces):
        names = list(pieces)
        tied, ended = after(arrays, *[pieces[name] for name in names])
        pieces.update(zip(names, ended))
        return tied

    def gather_along_z(own):
        return [swap(own, "ctx", 2 * m) if m else own for m in range(z_count)]

    def both_cores(along):
        return [block for one in along for block in (one, swap(one, "ctx", 1))]

    sizes = region_sizes(block_rows)
    regions = [(sum(sizes[:at]), size // 2) for at, size in enumerate(sizes)]
    first_rows = sum(sizes[:-1])
    moving = {
        j: lax.dynamic_slice_in_dim(inputs, (dp ^ j) * block_rows, first_rows, 1)
        for j in range(dp_count)
    }

    near_pieces = gather_near(w_key, w_value)
    far_pieces = gather_far(near_pieces)
    names = list(near_pieces)
    waiting, _ = after([near_pieces[name] for name in names[: len(near)]])
    others = {}
    for name, one in zip(names, waiting):
        (one,), _ = after([one], *others.values())
        others.update(from_other_core({name: one}))
    others.update(from_other_core({name: near_pieces[name] for name in names[len(near) :]}))
    near_pieces.update(others)
    early = project(
        ids, (w_key, w_value), inputs, block_rows, near_pieces, jnp.float32, bytes_cost(1 << 24)
    )
    others = near + far
    early, *tied = hold([early] + [moving[j] for j in others], far_pieces)
    moving.update(zip(others, tied))
    far_pieces.update(from_other_core(far_pieces))
    tied = hold([moving[j] for j in near[:-1]], far_pieces)
    moving.update(zip(near[:-1], tied))
    own = project(ids, (early,), inputs, block_rows, far_pieces, jnp.bfloat16)
    moved = {0: moving[0]}
    moved[near[-1]] = swap(moving[near[-1]], "dp", near[-1])
    moved.update({j: swap(moving[j], "dp", j) for j in near[:-1]})
    along = gather_along_z(own)
    tied, _ = after([moving[j] for j in far], *along)
    moving.update(zip(far, tied))
    along, _ = after(along)
    kv_blocks = both_cores(along)

    moved.update({j: swap(moving[j], "dp", j) for j in far})

    query_grad, keep, send = attention(
        me, stretch_order, doc_lengths[0], queries[0], grad_out[0], kv_blocks, head_dim
    )
    (send,), ended = after([send], *[moved[j] for j in near])
    moved.update(zip(near, ended))
    own, *leaving = add_and_split(keep, swap(send, "ctx", 1), z_count)
    grad = add_all([own] + [swap(one, "ctx", 2 * m) for m, one in enumerate(leaving, 1)])
    grads = [grad] + [swap(grad, "dp", j) for j in range(1, dp_count)]

    (grad,), ended = after([grad], *grads[1:], *[moved[j] for j in far])
    grads[1:] = ended[: dp_count - 1]
    moved.update(zip(far, ended[dp_count - 1 :]))
    groups = [[(0, j, 0, 0)] for j in range(dp_count)]
    ours, came = weight_rows(
        ids, [inputs], [grad], groups, *regions[-1], block_rows, sub_count
    )
    own = parts_over_dp(add_cores(ours, came))
    groups = [[(j, None, j, 0) for j in range(dp_count)]]
    arrays = [moved[j] for j in range(dp_count)]
    moved_parts = [
        add_cores(*weight_rows(ids, arrays, grads, groups, *region, block_rows, sub_count))
        for region in regions[:-1]
    ]
    moved_parts, own = after(moved_parts, *own)
    own = [swap(one, "dp", j) if j else one for j, one in enumerate(own)]
    finals = []
    for part in moved_parts:
        part = scatter_along_z(part, sub_count)
        finals.append(sum_of_halves(part, sub_count))
    blocks = gather_parts(finals[0], sub_count)
    part = scatter_along_z(sum_of(own), sub_count, finals + blocks[:sub_count])
    finals[1:], _ = after(finals[1:], part)
    last = sum_of_halves(part, sub_count)
    (last,), _ = after([last], *blocks)
    blocks += [one for final in finals[1:] for one in gather_parts(final, sub_count)]
    outs = assemble(ids, (), blocks, sub_count, regions[:-1], block_rows)
    last = gather_parts(last, sub_count)
    key_rows, value_rows = assemble(ids, outs, last, sub_count, regions[-1:], block_rows)
    return query_grad[None], key_rows, value_rows


def solution(mesh):
    return jax.shard_map(
        on_device,
        mesh=mesh,
        in_specs=(
            P("dp", "ctx", None),
            P("dp", "ctx", None),
            P("dp", "ctx", None),
            P("dp", None),
            P("dp", None),
            P(),
            P("dp", None),
        ),
        out_specs=(P("dp", "ctx", None), P("dp", None), P("dp", None)),
        check_vma=False,
    )
```

```python
import functools
import math

import jax
import jax.numpy as jnp
from jax import lax
from jax.experimental import pallas as pl
from jax.experimental.pallas import tpu as pltpu
from jax.sharding import PartitionSpec as P

VMEM_LIMIT = 28 * 1024 * 1024
NO_COST = pl.CostEstimate(flops=0, bytes_accessed=0, transcendentals=0)


MOVED = (4, 6)
TIED = 2


def region_sizes(block_rows):
    units = block_rows // 256
    sizes = [256 * (units * share // 16) for share in MOVED]
    return sizes + [block_rows - sum(sizes)]


class Plan:
    def __init__(self, **fields):
        self.__dict__.update(fields)


def swap(array, axis, distance):
    count = lax.axis_size(axis)
    return lax.ppermute(array, axis, [(i, i ^ distance) for i in range(count)])


def after(arrays, *earlier):
    tied = lax.optimization_barrier((tuple(arrays), tuple(earlier)))
    return list(tied[0]), list(tied[1])


def shape_of(rows, width, kind=jnp.bfloat16):
    return jax.ShapeDtypeStruct((rows, width), kind)


def kernel_call(kernel, name, outs, scalars, arrays, scratch=(), cost=NO_COST):
    smem = pl.BlockSpec(memory_space=pltpu.SMEM)
    vmem = pl.BlockSpec(memory_space=pltpu.VMEM)
    single = not isinstance(outs, tuple)
    return pl.pallas_call(
        kernel,
        out_shape=outs,
        in_specs=[smem] * len(scalars) + [vmem] * len(arrays),
        out_specs=vmem if single else (vmem,) * len(outs),
        scratch_shapes=list(scratch),
        compiler_params=pltpu.CompilerParams(vmem_limit_bytes=VMEM_LIMIT),
        cost_estimate=cost,
        name=name,
    )(*scalars, *arrays)


def bytes_cost(amount):
    return pl.CostEstimate(flops=0, bytes_accessed=amount, transcendentals=0)


TN = (((0,), (0,)), ((), ()))


def attention_kernel(
    shape, ids, order, lengths, q_ref, g_ref, *refs
):
    ctx_count, stretch_rows, head_count, head_dim, window, chunk = shape
    kv_refs = refs[:ctx_count]
    qgrad_ref, keep_ref, send_ref, keys, values, total, qs, gs, dqs = refs[ctx_count:]
    me = ids[0]
    row_count = 2 * stretch_rows
    stretch_count = 2 * ctx_count
    score_scale = 1.0 / math.sqrt(head_dim)

    def place(device, half):
        return pl.multiple_of(order[2 * device + half] * stretch_rows, stretch_rows)

    for index in range(ctx_count):
        for half in range(2):
            rows = pl.ds(place(me ^ index, half), stretch_rows)
            block = kv_refs[index][half * stretch_rows : (half + 1) * stretch_rows, :]
            keys[rows, :] = block[:, :head_dim]
            values[rows, :] = block[:, head_dim:]
    total[...] = jnp.zeros_like(total)
    for half in range(2):
        for head in range(head_count):
            to = slice((half * head_count + head) * stretch_rows, (half * head_count + head + 1) * stretch_rows)
            rows = slice(half * stretch_rows, (half + 1) * stretch_rows)
            columns = slice(head * head_dim, (head + 1) * head_dim)
            qs[to, :] = q_ref[rows, columns]
            gs[to, :] = g_ref[rows, columns]
    ends = []
    running = 0
    for at in range(lengths.shape[0]):
        running = running + lengths[at]
        ends.append(running)
    chunks_half = head_count * stretch_rows // chunk

    def step(at, carry):
        half = at // chunks_half
        block = order[2 * me + half]
        first = jnp.maximum(block - stretch_count // 2, 0) * stretch_rows
        first = pl.multiple_of(first, stretch_rows)
        part = pl.ds(pl.multiple_of(at * chunk, chunk), chunk)
        inside = (at - half * chunks_half) * chunk + lax.broadcasted_iota(jnp.int32, (1, chunk), 1)
        at_query = block * stretch_rows + lax.rem(inside, stretch_rows)
        begin = jnp.zeros_like(at_query)
        for end in ends:
            begin = jnp.where(at_query >= end, end, begin)
        at_key = lax.broadcasted_iota(jnp.int32, (window, chunk), 0)
        allowed = (at_key + (first - begin)).astype(jnp.uint32) <= (at_query - begin).astype(
            jnp.uint32
        )
        k = keys[pl.ds(first, window), :]
        v = values[pl.ds(first, window), :]
        q = qs[part, :]
        g = gs[part, :]
        last = (((1,), (1,)), ((), ()))
        scores = lax.dot_general(k, q, last, preferred_element_type=jnp.float32)
        masked = jnp.where(allowed, scores, -jnp.inf)
        largest = jnp.max(masked, axis=0, keepdims=True)
        expsum = jnp.exp2((masked - largest) * (score_scale * math.log2(math.e)))
        probs = expsum * (1.0 / jnp.sum(expsum, axis=0, keepdims=True))
        probs_low = probs.astype(jnp.bfloat16)
        dprob = lax.dot_general(v, g, last, preferred_element_type=jnp.float32)
        delta = jnp.sum(probs_low.astype(jnp.float32) * dprob, axis=0, keepdims=True)
        dscore = (probs * (dprob - delta)).astype(jnp.bfloat16)
        dq = lax.dot_general(
            k, dscore, (((0,), (0,)), ((), ())), preferred_element_type=jnp.float32
        )
        dqs[part, :] = (jnp.transpose(dq) * score_scale).astype(jnp.bfloat16)
        dk = jnp.dot(dscore, q, preferred_element_type=jnp.float32) * score_scale
        dv = jnp.dot(probs_low, g, preferred_element_type=jnp.float32)
        total[pl.ds(first, window), :head_dim] += dk
        total[pl.ds(first, window), head_dim:] += dv
        return carry

    lax.fori_loop(0, 2 * chunks_half, step, 0, unroll=3)
    for half in range(2):
        for head in range(head_count):
            origin = slice((half * head_count + head) * stretch_rows, (half * head_count + head + 1) * stretch_rows)
            rows = slice(half * stretch_rows, (half + 1) * stretch_rows)
            columns = slice(head * head_dim, (head + 1) * head_dim)
            qgrad_ref[rows, columns] = dqs[origin, :]
    for index in range(ctx_count):
        for half in range(2):
            rows = pl.ds(place(me ^ index, half), stretch_rows)
            start = (index // 2) * row_count + half * stretch_rows
            if index % 2:
                send_ref[start : start + stretch_rows, :] = total[rows, :].astype(jnp.bfloat16)
            else:
                keep_ref[start : start + stretch_rows, :] = total[rows, :]


def attention(me, order, lengths, queries, cotangent, kv_blocks, head_dim):
    row_count, width = queries.shape
    ctx_count = len(kv_blocks)
    stretch_rows = row_count // 2
    head_count = width // head_dim
    seq_rows = row_count * ctx_count
    window = seq_rows // 2 + stretch_rows
    stacked = head_count * stretch_rows
    chunk = 256 if stacked % 256 == 0 else 128
    shape = (ctx_count, stretch_rows, head_count, head_dim, window, chunk)
    smem = pl.BlockSpec(memory_space=pltpu.SMEM)
    vmem = pl.BlockSpec(memory_space=pltpu.VMEM)
    half_rows = seq_rows // 2
    return pl.pallas_call(
        functools.partial(attention_kernel, shape),
        out_shape=(
            jax.ShapeDtypeStruct((row_count, width), jnp.bfloat16),
            jax.ShapeDtypeStruct((half_rows, 2 * head_dim), jnp.float32),
            jax.ShapeDtypeStruct((half_rows, 2 * head_dim), jnp.bfloat16),
        ),
        in_specs=[smem] * 3 + [vmem] * (2 + ctx_count),
        out_specs=(vmem,) * 3,
        scratch_shapes=[
            pltpu.VMEM((seq_rows, head_dim), jnp.bfloat16),
            pltpu.VMEM((seq_rows, head_dim), jnp.bfloat16),
            pltpu.VMEM((seq_rows, 2 * head_dim), jnp.float32),
            pltpu.VMEM((2 * stacked, head_dim), jnp.bfloat16),
            pltpu.VMEM((2 * stacked, head_dim), jnp.bfloat16),
            pltpu.VMEM((2 * stacked, head_dim), jnp.bfloat16),
        ],
        compiler_params=pltpu.CompilerParams(vmem_limit_bytes=VMEM_LIMIT),
        cost_estimate=NO_COST,
        name="attention",
    )(me, order, lengths, queries, cotangent, *kv_blocks)


def project_kernel(plan, ids, hidden, *refs):
    out_ref = refs[-1]
    dp, core = ids[2], ids[1]
    if plan.start:
        total = refs[0][...]
    else:
        columns = pl.ds(pl.multiple_of(dp * plan.block_rows, plan.block_rows), plan.block_rows)
        total = jnp.concatenate(
            [
                jnp.dot(hidden[:, columns], own[...], preferred_element_type=jnp.float32)
                for own in refs[:2]
            ],
            axis=1,
        )
    for (block, side, offset), weight in zip(plan.terms, refs[1 if plan.start else 2 : -1]):
        from_column = (dp ^ block) * plan.block_rows + (core ^ side) * plan.side_rows + offset
        columns = pl.ds(pl.multiple_of(from_column, 128), weight.shape[0])
        total += jnp.dot(hidden[:, columns], weight[...], preferred_element_type=jnp.float32)
    out_ref[...] = total.astype(out_ref.dtype)


def project(ids, begin, inputs, block_rows, pieces, kind, cost=NO_COST):
    names = sorted(pieces)
    weights = [pieces[name] for name in names]
    plan = Plan(
        terms=names, start=len(begin) == 1, block_rows=block_rows, side_rows=block_rows // 2
    )
    return kernel_call(
        functools.partial(project_kernel, plan),
        "project",
        shape_of(inputs.shape[0], weights[0].shape[1], kind),
        (ids,),
        (inputs, *begin, *weights),
        cost=cost,
    )


def split_kernel(rows, keep, came, own_ref, *leaving_refs):
    own_ref[...] = keep[:rows, :] + came[:rows, :].astype(jnp.float32)
    for m, leaving in enumerate(leaving_refs, 1):
        block = slice(m * rows, (m + 1) * rows)
        leaving[...] = (keep[block, :] + came[block, :].astype(jnp.float32)).astype(leaving.dtype)


def add_and_split(keep, came, count):
    rows, width = keep.shape[0] // count, keep.shape[1]
    outs = (shape_of(rows, width, jnp.float32),) + (shape_of(rows, width),) * (count - 1)
    return kernel_call(functools.partial(split_kernel, rows), "split", outs, (), (keep, came))


def total_kernel(*refs):
    total = refs[0][...]
    for one in refs[1:-1]:
        total = total + one[...].astype(jnp.float32)
    refs[-1][...] = total.astype(refs[-1].dtype)


def add_all(arrays):
    out = jax.ShapeDtypeStruct(arrays[0].shape, jnp.bfloat16)
    return kernel_call(total_kernel, "total", out, (), arrays)


def weight_kernel(plan, ids, *refs):
    hidden = refs[: plan.hidden]
    grads = refs[plan.hidden : -2]
    z, core, dp = ids[0] % plan.sub_count, ids[1], ids[2]
    rows = plan.rows
    share = rows // plan.sub_count
    tile = next(size for size in (512, 256, 128) if rows % size == 0)
    step = math.gcd(share, tile)
    for side, out_ref in ((1, refs[-2]), (0, refs[-1])):
        for at, group in enumerate(plan.groups):
            for start in range(0, rows, tile):
                product = None
                for array, block, grad, shift in group:
                    origin = plan.origin - shift + (core ^ side) * rows + start
                    if block is not None:
                        origin = origin + (dp ^ block) * plan.block_rows
                    columns = pl.ds(pl.multiple_of(origin, 128), tile)
                    term = lax.dot_general(
                        hidden[array][:, columns],
                        grads[grad][...],
                        TN,
                        preferred_element_type=jnp.float32,
                    )
                    product = term if product is None else product + term
                for inner in range(0, tile, step):
                    part, offset = divmod(start + inner, share)
                    to = pl.multiple_of(at * rows + (z ^ part) * share + offset, step)
                    piece = product[inner : inner + step, :]
                    out_ref[pl.ds(to, step), :] = piece.astype(out_ref.dtype)


def weight_rows(ids, hidden, grads, groups, origin, rows, block_rows, sub_count):
    plan = Plan(
        hidden=len(hidden),
        groups=groups,
        origin=origin,
        rows=rows,
        block_rows=block_rows,
        sub_count=sub_count,
    )
    out = shape_of(rows * len(groups), grads[0].shape[1])
    theirs, ours = kernel_call(
        functools.partial(weight_kernel, plan),
        "weight_rows",
        (out, out),
        (ids,),
        (*hidden, *grads),
    )
    return ours, swap(theirs, "ctx", 1)


def add_cores(ours, came):
    return ours.astype(jnp.float32) + came.astype(jnp.float32)


def parts_over_dp(array):
    count = lax.axis_size("dp")
    rows = array.shape[0] // count
    parts = [array[j * rows : (j + 1) * rows] for j in range(count)]
    return parts[:1] + [part.astype(jnp.bfloat16) for part in parts[1:]]


def sum_of(arrays):
    total = arrays[0]
    for one in arrays[1:]:
        total = total + one.astype(jnp.float32)
    return total


def z_bits(sub_count):
    return [1 << at for at in range(sub_count.bit_length() - 1)]


def scatter_along_z(full, sub_count, earlier=()):
    share = full.shape[0] // sub_count
    parts = {m: full[m * share : (m + 1) * share] for m in range(sub_count)}
    for bit in z_bits(sub_count):
        for m in list(parts):
            if m & bit:
                came = swap(parts.pop(m).astype(jnp.bfloat16), "ctx", 2 * bit)
                (came,), _ = after([came], *earlier)
                parts[m ^ bit] = parts[m ^ bit] + came.astype(jnp.float32)
    return parts[0]


def sum_of_halves(part, sub_count, earlier=()):
    low = swap(part.astype(jnp.bfloat16), "ctx", 2 * sub_count)
    (low,), _ = after([low], *earlier)
    return (part + low.astype(jnp.float32)).astype(jnp.bfloat16)


def gather_parts(part, sub_count, earlier=()):
    rows = {0: part}
    for bit in z_bits(sub_count)[::-1]:
        for m, one in list(rows.items()):
            (rows[m | bit],), _ = after([swap(one, "ctx", 2 * bit)], *earlier)
    own = [rows[m] for m in range(sub_count)]
    return own + [swap(one, "ctx", 1) for one in own]


def assemble_kernel(sub_count, regions, first, ids, *refs):
    count = 2 * sub_count * len(regions)
    blocks = iter(refs[2 * (not first) :][:count])
    *outs, buffer, sems = refs[2 * (not first) + count :]
    z, core = ids[0] % sub_count, ids[1]
    copies = []
    filled = 0
    for origin, rows in regions:
        share = rows // sub_count
        for side in range(2):
            for m in range(sub_count):
                to = origin + (core ^ side) * rows + (z ^ m) * share
                to = pl.multiple_of(to, math.gcd(origin, share))
                block_ref = next(blocks)
                width = block_ref.shape[1] // 2
                for which, out_ref in enumerate(outs):
                    piece = buffer.at[which, pl.ds(filled, share), :]
                    piece[...] = block_ref[:, which * width : (which + 1) * width].astype(
                        jnp.float32
                    )
                    copy = pltpu.make_async_copy(
                        piece, out_ref.at[pl.ds(to, share), :], sems.at[len(copies)]
                    )
                    copy.start()
                    copies.append(copy)
                filled += share
    for copy in copies:
        copy.wait()


def assemble(ids, before, blocks, sub_count, regions, block_rows):
    rows = sum(block.shape[0] for block in blocks)
    width = blocks[0].shape[1] // 2
    out = shape_of(block_rows, width, jnp.float32)
    smem = pl.BlockSpec(memory_space=pltpu.SMEM)
    vmem = pl.BlockSpec(memory_space=pltpu.VMEM)
    anywhere = pl.BlockSpec(memory_space=pl.ANY)
    return pl.pallas_call(
        functools.partial(assemble_kernel, sub_count, regions, not before),
        out_shape=(out, out),
        in_specs=[smem] + [anywhere] * len(before) + [vmem] * len(blocks),
        out_specs=(anywhere, anywhere),
        scratch_shapes=[
            pltpu.VMEM((2, rows, width), jnp.float32),
            pltpu.SemaphoreType.DMA((2 * len(blocks),)),
        ],
        input_output_aliases={1: 0, 2: 1} if before else {},
        compiler_params=pltpu.CompilerParams(vmem_limit_bytes=VMEM_LIMIT),
        cost_estimate=NO_COST,
        name="assemble",
    )(ids, *before, *blocks)


def on_device(hidden_in, queries, grad_out, w_key, w_value, stretch_order, doc_lengths):
    inputs = hidden_in[0]
    head_dim = w_key.shape[1]
    dp_count = lax.axis_size("dp")
    ctx_count = lax.axis_size("ctx")
    z_count = ctx_count // 2
    sub_count = z_count // 2
    dp, ctx = lax.axis_index("dp"), lax.axis_index("ctx")
    z, core = ctx // 2, ctx % 2
    ids = jnp.stack([z, core, dp]).astype(jnp.int32)
    me = jnp.reshape(ctx, (1,)).astype(jnp.int32)
    block_rows = w_key.shape[0]
    half_rows = block_rows // 2
    quarter = half_rows // 2
    bits = [1 << at for at in range(dp_count.bit_length() - 1)]
    near = [j for j in range(1, dp_count) if j in bits]
    far = [j for j in range(1, dp_count) if j not in bits]

    def gather_near(*weights):
        pieces = {}
        for turn in range(2):
            for at, j in enumerate(near):
                offset = ((at + turn) % 2) * quarter
                start = core * half_rows + offset
                rows = [lax.dynamic_slice_in_dim(weight, start, quarter, 0) for weight in weights]
                pieces[j, 0, offset] = swap(jnp.concatenate(rows, axis=1), "dp", j)
        return pieces

    def gather_far(landed):
        pieces = {}
        for j in far:
            for offset, bit in ((0, 1 << (j.bit_length() - 1)), (quarter, j & -j)):
                origin = landed.get((j ^ bit, 0, offset), pieces.get((j ^ bit, 0, offset)))
                pieces[j, 0, offset] = swap(origin, "dp", bit)
        return pieces

    def from_other_core(pieces):
        return {(j, 1, offset): swap(one, "ctx", 1) for (j, _, offset), one in pieces.items()}

    def hold(arrays, pieces):
        names = list(pieces)
        tied, ended = after(arrays, *[pieces[name] for name in names])
        pieces.update(zip(names, ended))
        return tied

    def gather_along_z(own):
        return [swap(own, "ctx", 2 * m) if m else own for m in range(z_count)]

    def both_cores(along):
        return [block for one in along for block in (one, swap(one, "ctx", 1))]

    sizes = region_sizes(block_rows)
    regions = [(sum(sizes[:at]), size // 2) for at, size in enumerate(sizes)]
    first_rows = sum(sizes[:-1])
    moving = {
        j: lax.dynamic_slice_in_dim(inputs, (dp ^ j) * block_rows, first_rows, 1)
        for j in range(dp_count)
    }

    near_pieces = gather_near(w_key, w_value)
    far_pieces = gather_far(near_pieces)
    names = list(near_pieces)
    waiting, _ = after([near_pieces[name] for name in names[: len(near)]])
    others = {}
    for name, one in zip(names, waiting):
        (one,), _ = after([one], *others.values())
        others.update(from_other_core({name: one}))
    others.update(from_other_core({name: near_pieces[name] for name in names[len(near) :]}))
    near_pieces.update(others)
    early = project(
        ids, (w_key, w_value), inputs, block_rows, near_pieces, jnp.float32, bytes_cost(1 << 24)
    )
    others = near + far
    early, *tied = hold([early] + [moving[j] for j in others], far_pieces)
    moving.update(zip(others, tied))
    far_pieces.update(from_other_core(far_pieces))
    soonest = list(far_pieces)[len(far_pieces) // 2]
    tied, (far_pieces[soonest],) = after([moving[j] for j in near[:-1]], far_pieces[soonest])
    moving.update(zip(near[:-1], tied))
    own = project(ids, (early,), inputs, block_rows, far_pieces, jnp.bfloat16)
    moved = {0: moving[0]}
    moved[near[-1]] = swap(moving[near[-1]], "dp", near[-1])
    moved.update({j: swap(moving[j], "dp", j) for j in near[:-1]})
    along = gather_along_z(own)
    tied, _ = after([moving[j] for j in far], *along)
    moving.update(zip(far, tied))
    along, _ = after(along)
    kv_blocks = both_cores(along)

    moved.update({j: swap(moving[j], "dp", j) for j in far})

    query_grad, keep, send = attention(
        me, stretch_order, doc_lengths[0], queries[0], grad_out[0], kv_blocks, head_dim
    )
    (send,), ended = after([send], *[moved[j] for j in near])
    moved.update(zip(near, ended))
    own, *leaving = add_and_split(keep, swap(send, "ctx", 1), z_count)
    grad = add_all([own] + [swap(one, "ctx", 2 * m) for m, one in enumerate(leaving, 1)])
    grads = [grad] + [swap(grad, "dp", j) for j in range(1, dp_count)]

    (grad,), ended = after([grad], *grads[1:], *[moved[j] for j in far])
    grads[1:] = ended[: dp_count - 1]
    moved.update(zip(far, ended[dp_count - 1 :]))
    groups = [[(0, j, 0, 0)] for j in range(dp_count)]
    ours, came = weight_rows(
        ids, [inputs], [grad], groups, *regions[-1], block_rows, sub_count
    )
    own = parts_over_dp(add_cores(ours, came))
    groups = [[(j, None, j, 0) for j in range(dp_count)]]
    arrays = [moved[j] for j in range(dp_count)]
    moved_parts = [
        add_cores(*weight_rows(ids, arrays, grads, groups, *region, block_rows, sub_count))
        for region in regions[:-1]
    ]
    moved_parts, own = after(moved_parts, *own)
    own = [swap(one, "dp", j) if j else one for j, one in enumerate(own)]
    finals = []
    for part in moved_parts:
        part = scatter_along_z(part, sub_count)
        finals.append(sum_of_halves(part, sub_count))
    part = scatter_along_z(sum_of(own), sub_count, finals[:TIED])
    blocks = gather_parts(finals[0], sub_count)
    last = sum_of_halves(part, sub_count, blocks)
    blocks += [one for final in finals[1:] for one in gather_parts(final, sub_count)]
    outs = assemble(ids, (), blocks, sub_count, regions[:-1], block_rows)
    last = gather_parts(last, sub_count, outs)
    key_rows, value_rows = assemble(ids, outs, last, sub_count, regions[-1:], block_rows)
    return query_grad[None], key_rows, value_rows


def solution(mesh):
    return jax.shard_map(
        on_device,
        mesh=mesh,
        in_specs=(
            P("dp", "ctx", None),
            P("dp", "ctx", None),
            P("dp", "ctx", None),
            P("dp", None),
            P("dp", None),
            P(),
            P("dp", None),
        ),
        out_specs=(P("dp", "ctx", None), P("dp", None), P("dp", None)),
        check_vma=False,
    )
```

```python
import functools
import math

import jax
import jax.numpy as jnp
from jax import lax
from jax.experimental import pallas as pl
from jax.experimental.pallas import tpu as pltpu
from jax.sharding import PartitionSpec as P

VMEM_LIMIT = 28 * 1024 * 1024
NO_COST = pl.CostEstimate(flops=0, bytes_accessed=0, transcendentals=0)


MOVED = (4, 6)
TIED = 2


def region_sizes(block_rows):
    units = block_rows // 256
    sizes = [256 * (units * share // 16) for share in MOVED]
    return sizes + [block_rows - sum(sizes)]


class Plan:
    def __init__(self, **fields):
        self.__dict__.update(fields)


def swap(array, axis, distance):
    count = lax.axis_size(axis)
    return lax.ppermute(array, axis, [(i, i ^ distance) for i in range(count)])


def after(arrays, *earlier):
    tied = lax.optimization_barrier((tuple(arrays), tuple(earlier)))
    return list(tied[0]), list(tied[1])


def shape_of(rows, width, kind=jnp.bfloat16):
    return jax.ShapeDtypeStruct((rows, width), kind)


def kernel_call(kernel, name, outs, scalars, arrays, scratch=(), cost=NO_COST):
    smem = pl.BlockSpec(memory_space=pltpu.SMEM)
    vmem = pl.BlockSpec(memory_space=pltpu.VMEM)
    single = not isinstance(outs, tuple)
    return pl.pallas_call(
        kernel,
        out_shape=outs,
        in_specs=[smem] * len(scalars) + [vmem] * len(arrays),
        out_specs=vmem if single else (vmem,) * len(outs),
        scratch_shapes=list(scratch),
        compiler_params=pltpu.CompilerParams(vmem_limit_bytes=VMEM_LIMIT),
        cost_estimate=cost,
        name=name,
    )(*scalars, *arrays)


def bytes_cost(amount):
    return pl.CostEstimate(flops=0, bytes_accessed=amount, transcendentals=0)


TN = (((0,), (0,)), ((), ()))


def attention_kernel(
    shape, ids, order, lengths, q_ref, g_ref, *refs
):
    ctx_count, stretch_rows, head_count, head_dim, window, chunk = shape
    kv_refs = refs[:ctx_count]
    qgrad_ref, keep_ref, send_ref, keys, values, total, qs, gs, dqs = refs[ctx_count:]
    me = ids[0]
    row_count = 2 * stretch_rows
    stretch_count = 2 * ctx_count
    score_scale = 1.0 / math.sqrt(head_dim)

    def place(device, half):
        return pl.multiple_of(order[2 * device + half] * stretch_rows, stretch_rows)

    for index in range(ctx_count):
        for half in range(2):
            rows = pl.ds(place(me ^ index, half), stretch_rows)
            block = kv_refs[index][half * stretch_rows : (half + 1) * stretch_rows, :]
            keys[rows, :] = block[:, :head_dim]
            values[rows, :] = block[:, head_dim:]
    total[...] = jnp.zeros_like(total)
    for half in range(2):
        for head in range(head_count):
            to = slice((half * head_count + head) * stretch_rows, (half * head_count + head + 1) * stretch_rows)
            rows = slice(half * stretch_rows, (half + 1) * stretch_rows)
            columns = slice(head * head_dim, (head + 1) * head_dim)
            qs[to, :] = q_ref[rows, columns]
            gs[to, :] = g_ref[rows, columns]
    ends = []
    running = 0
    for at in range(lengths.shape[0]):
        running = running + lengths[at]
        ends.append(running)
    chunks_half = head_count * stretch_rows // chunk

    def step(at, carry):
        half = at // chunks_half
        block = order[2 * me + half]
        first = jnp.maximum(block - stretch_count // 2, 0) * stretch_rows
        first = pl.multiple_of(first, stretch_rows)
        part = pl.ds(pl.multiple_of(at * chunk, chunk), chunk)
        inside = (at - half * chunks_half) * chunk + lax.broadcasted_iota(jnp.int32, (1, chunk), 1)
        at_query = block * stretch_rows + lax.rem(inside, stretch_rows)
        begin = jnp.zeros_like(at_query)
        for end in ends:
            begin = jnp.where(at_query >= end, end, begin)
        at_key = lax.broadcasted_iota(jnp.int32, (window, chunk), 0)
        allowed = (at_key + (first - begin)).astype(jnp.uint32) <= (at_query - begin).astype(
            jnp.uint32
        )
        k = keys[pl.ds(first, window), :]
        v = values[pl.ds(first, window), :]
        q = qs[part, :]
        g = gs[part, :]
        last = (((1,), (1,)), ((), ()))
        scores = lax.dot_general(k, q, last, preferred_element_type=jnp.float32)
        masked = jnp.where(allowed, scores, -jnp.inf)
        largest = jnp.max(masked, axis=0, keepdims=True)
        expsum = jnp.exp2((masked - largest) * (score_scale * math.log2(math.e)))
        probs = expsum * (1.0 / jnp.sum(expsum, axis=0, keepdims=True))
        probs_low = probs.astype(jnp.bfloat16)
        dprob = lax.dot_general(v, g, last, preferred_element_type=jnp.float32)
        delta = jnp.sum(probs_low.astype(jnp.float32) * dprob, axis=0, keepdims=True)
        dscore = (probs * (dprob - delta)).astype(jnp.bfloat16)
        dq = lax.dot_general(
            k, dscore, (((0,), (0,)), ((), ())), preferred_element_type=jnp.float32
        )
        dqs[part, :] = (jnp.transpose(dq) * score_scale).astype(jnp.bfloat16)
        dk = jnp.dot(dscore, q, preferred_element_type=jnp.float32) * score_scale
        dv = jnp.dot(probs_low, g, preferred_element_type=jnp.float32)
        total[pl.ds(first, window), :head_dim] += dk
        total[pl.ds(first, window), head_dim:] += dv
        return carry

    lax.fori_loop(0, 2 * chunks_half, step, 0, unroll=3)
    for half in range(2):
        for head in range(head_count):
            origin = slice((half * head_count + head) * stretch_rows, (half * head_count + head + 1) * stretch_rows)
            rows = slice(half * stretch_rows, (half + 1) * stretch_rows)
            columns = slice(head * head_dim, (head + 1) * head_dim)
            qgrad_ref[rows, columns] = dqs[origin, :]
    for index in range(ctx_count):
        for half in range(2):
            rows = pl.ds(place(me ^ index, half), stretch_rows)
            start = (index // 2) * row_count + half * stretch_rows
            if index % 2:
                send_ref[start : start + stretch_rows, :] = total[rows, :].astype(jnp.bfloat16)
            else:
                keep_ref[start : start + stretch_rows, :] = total[rows, :]


def attention(me, order, lengths, queries, cotangent, kv_blocks, head_dim):
    row_count, width = queries.shape
    ctx_count = len(kv_blocks)
    stretch_rows = row_count // 2
    head_count = width // head_dim
    seq_rows = row_count * ctx_count
    window = seq_rows // 2 + stretch_rows
    stacked = head_count * stretch_rows
    chunk = 256 if stacked % 256 == 0 else 128
    shape = (ctx_count, stretch_rows, head_count, head_dim, window, chunk)
    smem = pl.BlockSpec(memory_space=pltpu.SMEM)
    vmem = pl.BlockSpec(memory_space=pltpu.VMEM)
    half_rows = seq_rows // 2
    return pl.pallas_call(
        functools.partial(attention_kernel, shape),
        out_shape=(
            jax.ShapeDtypeStruct((row_count, width), jnp.bfloat16),
            jax.ShapeDtypeStruct((half_rows, 2 * head_dim), jnp.float32),
            jax.ShapeDtypeStruct((half_rows, 2 * head_dim), jnp.bfloat16),
        ),
        in_specs=[smem] * 3 + [vmem] * (2 + ctx_count),
        out_specs=(vmem,) * 3,
        scratch_shapes=[
            pltpu.VMEM((seq_rows, head_dim), jnp.bfloat16),
            pltpu.VMEM((seq_rows, head_dim), jnp.bfloat16),
            pltpu.VMEM((seq_rows, 2 * head_dim), jnp.float32),
            pltpu.VMEM((2 * stacked, head_dim), jnp.bfloat16),
            pltpu.VMEM((2 * stacked, head_dim), jnp.bfloat16),
            pltpu.VMEM((2 * stacked, head_dim), jnp.bfloat16),
        ],
        compiler_params=pltpu.CompilerParams(vmem_limit_bytes=VMEM_LIMIT),
        cost_estimate=NO_COST,
        name="attention",
    )(me, order, lengths, queries, cotangent, *kv_blocks)


def project_kernel(plan, ids, hidden, *refs):
    out_ref = refs[-1]
    dp, core = ids[2], ids[1]
    if plan.start:
        total = refs[0][...]
    else:
        columns = pl.ds(pl.multiple_of(dp * plan.block_rows, plan.block_rows), plan.block_rows)
        total = jnp.concatenate(
            [
                jnp.dot(hidden[:, columns], own[...], preferred_element_type=jnp.float32)
                for own in refs[:2]
            ],
            axis=1,
        )
    for (block, side, offset), weight in zip(plan.terms, refs[1 if plan.start else 2 : -1]):
        from_column = (dp ^ block) * plan.block_rows + (core ^ side) * plan.side_rows + offset
        columns = pl.ds(pl.multiple_of(from_column, 128), weight.shape[0])
        total += jnp.dot(hidden[:, columns], weight[...], preferred_element_type=jnp.float32)
    out_ref[...] = total.astype(out_ref.dtype)


def project(ids, begin, inputs, block_rows, pieces, kind, cost=NO_COST):
    names = sorted(pieces)
    weights = [pieces[name] for name in names]
    plan = Plan(
        terms=names, start=len(begin) == 1, block_rows=block_rows, side_rows=block_rows // 2
    )
    return kernel_call(
        functools.partial(project_kernel, plan),
        "project",
        shape_of(inputs.shape[0], weights[0].shape[1], kind),
        (ids,),
        (inputs, *begin, *weights),
        cost=cost,
    )


def split_kernel(rows, keep, came, own_ref, *leaving_refs):
    own_ref[...] = keep[:rows, :] + came[:rows, :].astype(jnp.float32)
    for m, leaving in enumerate(leaving_refs, 1):
        block = slice(m * rows, (m + 1) * rows)
        leaving[...] = (keep[block, :] + came[block, :].astype(jnp.float32)).astype(leaving.dtype)


def add_and_split(keep, came, count):
    rows, width = keep.shape[0] // count, keep.shape[1]
    outs = (shape_of(rows, width, jnp.float32),) + (shape_of(rows, width),) * (count - 1)
    return kernel_call(functools.partial(split_kernel, rows), "split", outs, (), (keep, came))


def total_kernel(*refs):
    total = refs[0][...]
    for one in refs[1:-1]:
        total = total + one[...].astype(jnp.float32)
    refs[-1][...] = total.astype(refs[-1].dtype)


def add_all(arrays):
    out = jax.ShapeDtypeStruct(arrays[0].shape, jnp.bfloat16)
    return kernel_call(total_kernel, "total", out, (), arrays)


def weight_kernel(plan, ids, *refs):
    hidden = refs[: plan.hidden]
    grads = refs[plan.hidden : -2]
    z, core, dp = ids[0] % plan.sub_count, ids[1], ids[2]
    rows = plan.rows
    share = rows // plan.sub_count
    tile = next(size for size in (512, 256, 128) if rows % size == 0)
    step = math.gcd(share, tile)
    for side, out_ref in ((1, refs[-2]), (0, refs[-1])):
        for at, group in enumerate(plan.groups):
            for start in range(0, rows, tile):
                product = None
                for array, block, grad, shift in group:
                    origin = plan.origin - shift + (core ^ side) * rows + start
                    if block is not None:
                        origin = origin + (dp ^ block) * plan.block_rows
                    columns = pl.ds(pl.multiple_of(origin, 128), tile)
                    term = lax.dot_general(
                        hidden[array][:, columns],
                        grads[grad][...],
                        TN,
                        preferred_element_type=jnp.float32,
                    )
                    product = term if product is None else product + term
                for inner in range(0, tile, step):
                    part, offset = divmod(start + inner, share)
                    to = pl.multiple_of(at * rows + (z ^ part) * share + offset, step)
                    piece = product[inner : inner + step, :]
                    out_ref[pl.ds(to, step), :] = piece.astype(out_ref.dtype)


def weight_rows(ids, hidden, grads, groups, origin, rows, block_rows, sub_count, earlier=()):
    plan = Plan(
        hidden=len(hidden),
        groups=groups,
        origin=origin,
        rows=rows,
        block_rows=block_rows,
        sub_count=sub_count,
    )
    out = shape_of(rows * len(groups), grads[0].shape[1])
    theirs, ours = kernel_call(
        functools.partial(weight_kernel, plan),
        "weight_rows",
        (out, out),
        (ids,),
        (*hidden, *grads),
    )
    (theirs,), _ = after([theirs], *earlier)
    return ours, swap(theirs, "ctx", 1)


def add_cores(ours, came):
    return ours.astype(jnp.float32) + came.astype(jnp.float32)


def parts_over_dp(array):
    count = lax.axis_size("dp")
    rows = array.shape[0] // count
    parts = [array[j * rows : (j + 1) * rows] for j in range(count)]
    return parts[:1] + [part.astype(jnp.bfloat16) for part in parts[1:]]


def sum_of(arrays):
    total = arrays[0]
    for one in arrays[1:]:
        total = total + one.astype(jnp.float32)
    return total


def z_bits(sub_count):
    return [1 << at for at in range(sub_count.bit_length() - 1)]


def scatter_along_z(full, sub_count, earlier=()):
    share = full.shape[0] // sub_count
    parts = {m: full[m * share : (m + 1) * share] for m in range(sub_count)}
    for bit in z_bits(sub_count):
        for m in list(parts):
            if m & bit:
                came = swap(parts.pop(m).astype(jnp.bfloat16), "ctx", 2 * bit)
                (came,), _ = after([came], *earlier)
                parts[m ^ bit] = parts[m ^ bit] + came.astype(jnp.float32)
    return parts[0]


def sum_of_halves(part, sub_count, earlier=()):
    low = swap(part.astype(jnp.bfloat16), "ctx", 2 * sub_count)
    (low,), _ = after([low], *earlier)
    return (part + low.astype(jnp.float32)).astype(jnp.bfloat16)


def gather_parts(part, sub_count, earlier=()):
    rows = {0: part}
    for bit in z_bits(sub_count)[::-1]:
        for m, one in list(rows.items()):
            (rows[m | bit],), _ = after([swap(one, "ctx", 2 * bit)], *earlier)
    own = [rows[m] for m in range(sub_count)]
    return own + [swap(one, "ctx", 1) for one in own]


def assemble_kernel(sub_count, regions, first, ids, *refs):
    count = 2 * sub_count * len(regions)
    blocks = iter(refs[2 * (not first) :][:count])
    *outs, buffer, sems = refs[2 * (not first) + count :]
    z, core = ids[0] % sub_count, ids[1]
    copies = []
    filled = 0
    for origin, rows in regions:
        share = rows // sub_count
        for side in range(2):
            for m in range(sub_count):
                to = origin + (core ^ side) * rows + (z ^ m) * share
                to = pl.multiple_of(to, math.gcd(origin, share))
                block_ref = next(blocks)
                width = block_ref.shape[1] // 2
                for which, out_ref in enumerate(outs):
                    piece = buffer.at[which, pl.ds(filled, share), :]
                    piece[...] = block_ref[:, which * width : (which + 1) * width].astype(
                        jnp.float32
                    )
                    copy = pltpu.make_async_copy(
                        piece, out_ref.at[pl.ds(to, share), :], sems.at[len(copies)]
                    )
                    copy.start()
                    copies.append(copy)
                filled += share
    for copy in copies:
        copy.wait()


def assemble(ids, before, blocks, sub_count, regions, block_rows):
    rows = sum(block.shape[0] for block in blocks)
    width = blocks[0].shape[1] // 2
    out = shape_of(block_rows, width, jnp.float32)
    smem = pl.BlockSpec(memory_space=pltpu.SMEM)
    vmem = pl.BlockSpec(memory_space=pltpu.VMEM)
    anywhere = pl.BlockSpec(memory_space=pl.ANY)
    return pl.pallas_call(
        functools.partial(assemble_kernel, sub_count, regions, not before),
        out_shape=(out, out),
        in_specs=[smem] + [anywhere] * len(before) + [vmem] * len(blocks),
        out_specs=(anywhere, anywhere),
        scratch_shapes=[
            pltpu.VMEM((2, rows, width), jnp.float32),
            pltpu.SemaphoreType.DMA((2 * len(blocks),)),
        ],
        input_output_aliases={1: 0, 2: 1} if before else {},
        compiler_params=pltpu.CompilerParams(vmem_limit_bytes=VMEM_LIMIT),
        cost_estimate=NO_COST,
        name="assemble",
    )(ids, *before, *blocks)


def on_device(hidden_in, queries, grad_out, w_key, w_value, stretch_order, doc_lengths):
    inputs = hidden_in[0]
    head_dim = w_key.shape[1]
    dp_count = lax.axis_size("dp")
    ctx_count = lax.axis_size("ctx")
    z_count = ctx_count // 2
    sub_count = z_count // 2
    dp, ctx = lax.axis_index("dp"), lax.axis_index("ctx")
    z, core = ctx // 2, ctx % 2
    ids = jnp.stack([z, core, dp]).astype(jnp.int32)
    me = jnp.reshape(ctx, (1,)).astype(jnp.int32)
    block_rows = w_key.shape[0]
    half_rows = block_rows // 2
    quarter = half_rows // 2
    bits = [1 << at for at in range(dp_count.bit_length() - 1)]
    near = [j for j in range(1, dp_count) if j in bits]
    far = [j for j in range(1, dp_count) if j not in bits]

    def gather_near(*weights):
        pieces = {}
        for turn in range(2):
            for at, j in enumerate(near):
                offset = ((at + turn) % 2) * quarter
                start = core * half_rows + offset
                rows = [lax.dynamic_slice_in_dim(weight, start, quarter, 0) for weight in weights]
                pieces[j, 0, offset] = swap(jnp.concatenate(rows, axis=1), "dp", j)
        return pieces

    def gather_far(landed):
        pieces = {}
        for j in far:
            for offset, bit in ((0, 1 << (j.bit_length() - 1)), (quarter, j & -j)):
                origin = landed.get((j ^ bit, 0, offset), pieces.get((j ^ bit, 0, offset)))
                pieces[j, 0, offset] = swap(origin, "dp", bit)
        return pieces

    def from_other_core(pieces):
        return {(j, 1, offset): swap(one, "ctx", 1) for (j, _, offset), one in pieces.items()}

    def hold(arrays, pieces):
        names = list(pieces)
        tied, ended = after(arrays, *[pieces[name] for name in names])
        pieces.update(zip(names, ended))
        return tied

    def gather_along_z(own):
        return [swap(own, "ctx", 2 * m) if m else own for m in range(z_count)]

    def both_cores(along):
        return [block for one in along for block in (one, swap(one, "ctx", 1))]

    sizes = region_sizes(block_rows)
    regions = [(sum(sizes[:at]), size // 2) for at, size in enumerate(sizes)]
    first_rows = sum(sizes[:-1])
    moving = {
        j: lax.dynamic_slice_in_dim(inputs, (dp ^ j) * block_rows, first_rows, 1)
        for j in range(dp_count)
    }

    near_pieces = gather_near(w_key, w_value)
    far_pieces = gather_far(near_pieces)
    names = list(near_pieces)
    waiting, _ = after([near_pieces[name] for name in names[: len(near)]])
    others = {}
    for name, one in zip(names, waiting):
        (one,), _ = after([one], *others.values())
        others.update(from_other_core({name: one}))
    others.update(from_other_core({name: near_pieces[name] for name in names[len(near) :]}))
    near_pieces.update(others)
    early = project(
        ids, (w_key, w_value), inputs, block_rows, near_pieces, jnp.float32, bytes_cost(1 << 24)
    )
    others = near + far
    early, *tied = hold([early] + [moving[j] for j in others], far_pieces)
    moving.update(zip(others, tied))
    far_pieces.update(from_other_core(far_pieces))
    soonest = list(far_pieces)[len(far_pieces) // 2]
    tied, (far_pieces[soonest],) = after([moving[j] for j in near[:-1]], far_pieces[soonest])
    moving.update(zip(near[:-1], tied))
    own = project(ids, (early,), inputs, block_rows, far_pieces, jnp.bfloat16)
    moved = {0: moving[0]}
    moved[near[-1]] = swap(moving[near[-1]], "dp", near[-1])
    moved.update({j: swap(moving[j], "dp", j) for j in near[:-1]})
    along = gather_along_z(own)
    tied, _ = after([moving[j] for j in far], *along)
    moving.update(zip(far, tied))
    along, _ = after(along)
    kv_blocks = both_cores(along)

    moved.update({j: swap(moving[j], "dp", j) for j in far})

    query_grad, keep, send = attention(
        me, stretch_order, doc_lengths[0], queries[0], grad_out[0], kv_blocks, head_dim
    )
    (send,), ended = after([send], *[moved[j] for j in near])
    moved.update(zip(near, ended))
    own, *leaving = add_and_split(keep, swap(send, "ctx", 1), z_count)
    grad = add_all([own] + [swap(one, "ctx", 2 * m) for m, one in enumerate(leaving, 1)])
    grads = [grad] + [swap(grad, "dp", j) for j in range(1, dp_count)]

    (grad,), ended = after([grad], grads[near[0]], *[moved[j] for j in far])
    grads[near[0]] = ended[0]
    moved.update(zip(far, ended[1:]))
    groups = [[(0, j, 0, 0)] for j in range(dp_count)]
    ours, came = weight_rows(
        ids, [inputs], [grad], groups, *regions[-1], block_rows, sub_count, grads[1:]
    )
    own = parts_over_dp(add_cores(ours, came))
    groups = [[(j, None, j, 0) for j in range(dp_count)]]
    arrays = [moved[j] for j in range(dp_count)]
    moved_parts = [
        add_cores(*weight_rows(ids, arrays, grads, groups, *region, block_rows, sub_count))
        for region in regions[:-1]
    ]
    moved_parts, own = after(moved_parts, *own)
    own = [swap(one, "dp", j) if j else one for j, one in enumerate(own)]
    finals = []
    for part in moved_parts:
        part = scatter_along_z(part, sub_count)
        finals.append(sum_of_halves(part, sub_count))
    part = scatter_along_z(sum_of(own), sub_count, finals[:TIED])
    blocks = gather_parts(finals[0], sub_count)
    last = sum_of_halves(part, sub_count, blocks)
    blocks += [one for final in finals[1:] for one in gather_parts(final, sub_count)]
    outs = assemble(ids, (), blocks, sub_count, regions[:-1], block_rows)
    last = gather_parts(last, sub_count, outs)
    key_rows, value_rows = assemble(ids, outs, last, sub_count, regions[-1:], block_rows)
    return query_grad[None], key_rows, value_rows


def solution(mesh):
    return jax.shard_map(
        on_device,
        mesh=mesh,
        in_specs=(
            P("dp", "ctx", None),
            P("dp", "ctx", None),
            P("dp", "ctx", None),
            P("dp", None),
            P("dp", None),
            P(),
            P("dp", None),
        ),
        out_specs=(P("dp", "ctx", None), P("dp", None), P("dp", None)),
        check_vma=False,
    )
```

```python
import functools
import math

import jax
import jax.numpy as jnp
from jax import lax
from jax.experimental import pallas as pl
from jax.experimental.pallas import tpu as pltpu
from jax.sharding import PartitionSpec as P

VMEM_LIMIT = 28 * 1024 * 1024
NO_COST = pl.CostEstimate(flops=0, bytes_accessed=0, transcendentals=0)


MOVED = (4, 6)
TIED = 2


def region_sizes(block_rows):
    units = block_rows // 256
    sizes = [256 * (units * share // 16) for share in MOVED]
    return sizes + [block_rows - sum(sizes)]


class Plan:
    def __init__(self, **fields):
        self.__dict__.update(fields)


def swap(array, axis, distance):
    count = lax.axis_size(axis)
    return lax.ppermute(array, axis, [(i, i ^ distance) for i in range(count)])


def after(arrays, *earlier):
    tied = lax.optimization_barrier((tuple(arrays), tuple(earlier)))
    return list(tied[0]), list(tied[1])


def shape_of(rows, width, kind=jnp.bfloat16):
    return jax.ShapeDtypeStruct((rows, width), kind)


def kernel_call(kernel, name, outs, scalars, arrays, scratch=(), cost=NO_COST):
    smem = pl.BlockSpec(memory_space=pltpu.SMEM)
    vmem = pl.BlockSpec(memory_space=pltpu.VMEM)
    single = not isinstance(outs, tuple)
    return pl.pallas_call(
        kernel,
        out_shape=outs,
        in_specs=[smem] * len(scalars) + [vmem] * len(arrays),
        out_specs=vmem if single else (vmem,) * len(outs),
        scratch_shapes=list(scratch),
        compiler_params=pltpu.CompilerParams(vmem_limit_bytes=VMEM_LIMIT),
        cost_estimate=cost,
        name=name,
    )(*scalars, *arrays)


def bytes_cost(amount):
    return pl.CostEstimate(flops=0, bytes_accessed=amount, transcendentals=0)


TN = (((0,), (0,)), ((), ()))


def attention_kernel(
    shape, ids, order, lengths, q_ref, g_ref, *refs
):
    ctx_count, stretch_rows, head_count, head_dim, window, chunk = shape
    kv_refs = refs[:ctx_count]
    qgrad_ref, keep_ref, send_ref, keys, values, total, qs, gs, dqs = refs[ctx_count:]
    me = ids[0]
    row_count = 2 * stretch_rows
    stretch_count = 2 * ctx_count
    score_scale = 1.0 / math.sqrt(head_dim)

    def place(device, half):
        return pl.multiple_of(order[2 * device + half] * stretch_rows, stretch_rows)

    for index in range(ctx_count):
        for half in range(2):
            rows = pl.ds(place(me ^ index, half), stretch_rows)
            block = kv_refs[index][half * stretch_rows : (half + 1) * stretch_rows, :]
            keys[rows, :] = block[:, :head_dim]
            values[rows, :] = block[:, head_dim:]
    total[...] = jnp.zeros_like(total)
    for half in range(2):
        for head in range(head_count):
            to = slice((half * head_count + head) * stretch_rows, (half * head_count + head + 1) * stretch_rows)
            rows = slice(half * stretch_rows, (half + 1) * stretch_rows)
            columns = slice(head * head_dim, (head + 1) * head_dim)
            qs[to, :] = q_ref[rows, columns]
            gs[to, :] = g_ref[rows, columns]
    ends = []
    running = 0
    for at in range(lengths.shape[0]):
        running = running + lengths[at]
        ends.append(running)
    chunks_half = head_count * stretch_rows // chunk

    def step(at, carry):
        half = at // chunks_half
        block = order[2 * me + half]
        first = jnp.maximum(block - stretch_count // 2, 0) * stretch_rows
        first = pl.multiple_of(first, stretch_rows)
        part = pl.ds(pl.multiple_of(at * chunk, chunk), chunk)
        inside = (at - half * chunks_half) * chunk + lax.broadcasted_iota(jnp.int32, (1, chunk), 1)
        at_query = block * stretch_rows + lax.rem(inside, stretch_rows)
        begin = jnp.zeros_like(at_query)
        for end in ends:
            begin = jnp.where(at_query >= end, end, begin)
        at_key = lax.broadcasted_iota(jnp.int32, (window, chunk), 0)
        allowed = (at_key + (first - begin)).astype(jnp.uint32) <= (at_query - begin).astype(
            jnp.uint32
        )
        k = keys[pl.ds(first, window), :]
        v = values[pl.ds(first, window), :]
        q = qs[part, :]
        g = gs[part, :]
        last = (((1,), (1,)), ((), ()))
        scores = lax.dot_general(k, q, last, preferred_element_type=jnp.float32)
        masked = jnp.where(allowed, scores, -jnp.inf)
        largest = jnp.max(masked, axis=0, keepdims=True)
        expsum = jnp.exp2((masked - largest) * (score_scale * math.log2(math.e)))
        probs = expsum * (1.0 / jnp.sum(expsum, axis=0, keepdims=True))
        probs_low = probs.astype(jnp.bfloat16)
        dprob = lax.dot_general(v, g, last, preferred_element_type=jnp.float32)
        delta = jnp.sum(probs_low.astype(jnp.float32) * dprob, axis=0, keepdims=True)
        dscore = (probs * (dprob - delta)).astype(jnp.bfloat16)
        dq = lax.dot_general(
            k, dscore, (((0,), (0,)), ((), ())), preferred_element_type=jnp.float32
        )
        dqs[part, :] = (jnp.transpose(dq) * score_scale).astype(jnp.bfloat16)
        dk = jnp.dot(dscore, q, preferred_element_type=jnp.float32) * score_scale
        dv = jnp.dot(probs_low, g, preferred_element_type=jnp.float32)
        total[pl.ds(first, window), :head_dim] += dk
        total[pl.ds(first, window), head_dim:] += dv
        return carry

    lax.fori_loop(0, 2 * chunks_half, step, 0, unroll=3)
    for half in range(2):
        for head in range(head_count):
            origin = slice((half * head_count + head) * stretch_rows, (half * head_count + head + 1) * stretch_rows)
            rows = slice(half * stretch_rows, (half + 1) * stretch_rows)
            columns = slice(head * head_dim, (head + 1) * head_dim)
            qgrad_ref[rows, columns] = dqs[origin, :]
    for index in range(ctx_count):
        for half in range(2):
            rows = pl.ds(place(me ^ index, half), stretch_rows)
            start = (index // 2) * row_count + half * stretch_rows
            if index % 2:
                send_ref[start : start + stretch_rows, :] = total[rows, :].astype(jnp.bfloat16)
            else:
                keep_ref[start : start + stretch_rows, :] = total[rows, :]


def attention(me, order, lengths, queries, cotangent, kv_blocks, head_dim):
    row_count, width = queries.shape
    ctx_count = len(kv_blocks)
    stretch_rows = row_count // 2
    head_count = width // head_dim
    seq_rows = row_count * ctx_count
    window = seq_rows // 2 + stretch_rows
    stacked = head_count * stretch_rows
    chunk = 256 if stacked % 256 == 0 else 128
    shape = (ctx_count, stretch_rows, head_count, head_dim, window, chunk)
    smem = pl.BlockSpec(memory_space=pltpu.SMEM)
    vmem = pl.BlockSpec(memory_space=pltpu.VMEM)
    half_rows = seq_rows // 2
    return pl.pallas_call(
        functools.partial(attention_kernel, shape),
        out_shape=(
            jax.ShapeDtypeStruct((row_count, width), jnp.bfloat16),
            jax.ShapeDtypeStruct((half_rows, 2 * head_dim), jnp.float32),
            jax.ShapeDtypeStruct((half_rows, 2 * head_dim), jnp.bfloat16),
        ),
        in_specs=[smem] * 3 + [vmem] * (2 + ctx_count),
        out_specs=(vmem,) * 3,
        scratch_shapes=[
            pltpu.VMEM((seq_rows, head_dim), jnp.bfloat16),
            pltpu.VMEM((seq_rows, head_dim), jnp.bfloat16),
            pltpu.VMEM((seq_rows, 2 * head_dim), jnp.float32),
            pltpu.VMEM((2 * stacked, head_dim), jnp.bfloat16),
            pltpu.VMEM((2 * stacked, head_dim), jnp.bfloat16),
            pltpu.VMEM((2 * stacked, head_dim), jnp.bfloat16),
        ],
        compiler_params=pltpu.CompilerParams(vmem_limit_bytes=VMEM_LIMIT),
        cost_estimate=NO_COST,
        name="attention",
    )(me, order, lengths, queries, cotangent, *kv_blocks)


def project_kernel(plan, ids, hidden, *refs):
    out_ref = refs[-1]
    dp, core = ids[2], ids[1]
    if plan.start:
        total = refs[0][...]
    else:
        columns = pl.ds(pl.multiple_of(dp * plan.block_rows, plan.block_rows), plan.block_rows)
        total = jnp.concatenate(
            [
                jnp.dot(hidden[:, columns], own[...], preferred_element_type=jnp.float32)
                for own in refs[:2]
            ],
            axis=1,
        )
    for (block, side, offset), weight in zip(plan.terms, refs[1 if plan.start else 2 : -1]):
        from_column = (dp ^ block) * plan.block_rows + (core ^ side) * plan.side_rows + offset
        columns = pl.ds(pl.multiple_of(from_column, 128), weight.shape[0])
        total += jnp.dot(hidden[:, columns], weight[...], preferred_element_type=jnp.float32)
    out_ref[...] = total.astype(out_ref.dtype)


def project(ids, begin, inputs, block_rows, pieces, kind, cost=NO_COST):
    names = sorted(pieces)
    weights = [pieces[name] for name in names]
    plan = Plan(
        terms=names, start=len(begin) == 1, block_rows=block_rows, side_rows=block_rows // 2
    )
    return kernel_call(
        functools.partial(project_kernel, plan),
        "project",
        shape_of(inputs.shape[0], weights[0].shape[1], kind),
        (ids,),
        (inputs, *begin, *weights),
        cost=cost,
    )


def split_kernel(rows, keep, came, own_ref, *leaving_refs):
    own_ref[...] = keep[:rows, :] + came[:rows, :].astype(jnp.float32)
    for m, leaving in enumerate(leaving_refs, 1):
        block = slice(m * rows, (m + 1) * rows)
        leaving[...] = (keep[block, :] + came[block, :].astype(jnp.float32)).astype(leaving.dtype)


def add_and_split(keep, came, count):
    rows, width = keep.shape[0] // count, keep.shape[1]
    outs = (shape_of(rows, width, jnp.float32),) + (shape_of(rows, width),) * (count - 1)
    return kernel_call(functools.partial(split_kernel, rows), "split", outs, (), (keep, came))


def total_kernel(*refs):
    total = refs[0][...]
    for one in refs[1:-1]:
        total = total + one[...].astype(jnp.float32)
    refs[-1][...] = total.astype(refs[-1].dtype)


def add_all(arrays):
    out = jax.ShapeDtypeStruct(arrays[0].shape, jnp.bfloat16)
    return kernel_call(total_kernel, "total", out, (), arrays)


def weight_kernel(plan, ids, *refs):
    hidden = refs[: plan.hidden]
    grads = refs[plan.hidden : -2]
    z, core, dp = ids[0] % plan.sub_count, ids[1], ids[2]
    rows = plan.rows
    share = rows // plan.sub_count
    tile = next(size for size in (512, 256, 128) if rows % size == 0)
    step = math.gcd(share, tile)
    for side, out_ref in ((1, refs[-2]), (0, refs[-1])):
        for at, group in enumerate(plan.groups):
            for start in range(0, rows, tile):
                product = None
                for array, block, grad, shift in group:
                    origin = plan.origin - shift + (core ^ side) * rows + start
                    if block is not None:
                        origin = origin + (dp ^ block) * plan.block_rows
                    columns = pl.ds(pl.multiple_of(origin, 128), tile)
                    term = lax.dot_general(
                        hidden[array][:, columns],
                        grads[grad][...],
                        TN,
                        preferred_element_type=jnp.float32,
                    )
                    product = term if product is None else product + term
                for inner in range(0, tile, step):
                    part, offset = divmod(start + inner, share)
                    to = pl.multiple_of(at * rows + (z ^ part) * share + offset, step)
                    piece = product[inner : inner + step, :]
                    out_ref[pl.ds(to, step), :] = piece.astype(out_ref.dtype)


def weight_rows(ids, hidden, grads, groups, origin, rows, block_rows, sub_count, earlier=()):
    plan = Plan(
        hidden=len(hidden),
        groups=groups,
        origin=origin,
        rows=rows,
        block_rows=block_rows,
        sub_count=sub_count,
    )
    out = shape_of(rows * len(groups), grads[0].shape[1])
    theirs, ours = kernel_call(
        functools.partial(weight_kernel, plan),
        "weight_rows",
        (out, out),
        (ids,),
        (*hidden, *grads),
    )
    (theirs,), _ = after([theirs], *earlier)
    return ours, swap(theirs, "ctx", 1)


def add_cores(ours, came):
    return ours.astype(jnp.float32) + came.astype(jnp.float32)


def parts_over_dp(array):
    count = lax.axis_size("dp")
    rows = array.shape[0] // count
    parts = [array[j * rows : (j + 1) * rows] for j in range(count)]
    return parts[:1] + [part.astype(jnp.bfloat16) for part in parts[1:]]


def sum_of(arrays):
    total = arrays[0]
    for one in arrays[1:]:
        total = total + one.astype(jnp.float32)
    return total


def z_bits(sub_count):
    return [1 << at for at in range(sub_count.bit_length() - 1)]


def scatter_along_z(full, sub_count, earlier=()):
    share = full.shape[0] // sub_count
    parts = {m: full[m * share : (m + 1) * share] for m in range(sub_count)}
    for bit in z_bits(sub_count):
        for m in list(parts):
            if m & bit:
                came = swap(parts.pop(m).astype(jnp.bfloat16), "ctx", 2 * bit)
                (came,), _ = after([came], *earlier)
                parts[m ^ bit] = parts[m ^ bit] + came.astype(jnp.float32)
    return parts[0]


def sum_of_halves(part, sub_count, earlier=()):
    low = swap(part.astype(jnp.bfloat16), "ctx", 2 * sub_count)
    (low,), _ = after([low], *earlier)
    return (part + low.astype(jnp.float32)).astype(jnp.bfloat16)


def gather_parts(part, sub_count, earlier=()):
    rows = {0: part}
    for bit in z_bits(sub_count)[::-1]:
        for m, one in list(rows.items()):
            (rows[m | bit],), _ = after([swap(one, "ctx", 2 * bit)], *earlier)
    own = [rows[m] for m in range(sub_count)]
    return own + [swap(one, "ctx", 1) for one in own]


def assemble_kernel(sub_count, regions, first, ids, *refs):
    count = 2 * sub_count * len(regions)
    blocks = iter(refs[2 * (not first) :][:count])
    *outs, buffer, sems = refs[2 * (not first) + count :]
    z, core = ids[0] % sub_count, ids[1]
    copies = []
    filled = 0
    for origin, rows in regions:
        share = rows // sub_count
        for side in range(2):
            for m in range(sub_count):
                to = origin + (core ^ side) * rows + (z ^ m) * share
                to = pl.multiple_of(to, math.gcd(origin, share))
                block_ref = next(blocks)
                width = block_ref.shape[1] // 2
                for which, out_ref in enumerate(outs):
                    piece = buffer.at[which, pl.ds(filled, share), :]
                    piece[...] = block_ref[:, which * width : (which + 1) * width].astype(
                        jnp.float32
                    )
                    copy = pltpu.make_async_copy(
                        piece, out_ref.at[pl.ds(to, share), :], sems.at[len(copies)]
                    )
                    copy.start()
                    copies.append(copy)
                filled += share
    for copy in copies:
        copy.wait()


def assemble(ids, before, blocks, sub_count, regions, block_rows):
    rows = sum(block.shape[0] for block in blocks)
    width = blocks[0].shape[1] // 2
    out = shape_of(block_rows, width, jnp.float32)
    smem = pl.BlockSpec(memory_space=pltpu.SMEM)
    vmem = pl.BlockSpec(memory_space=pltpu.VMEM)
    anywhere = pl.BlockSpec(memory_space=pl.ANY)
    return pl.pallas_call(
        functools.partial(assemble_kernel, sub_count, regions, not before),
        out_shape=(out, out),
        in_specs=[smem] + [anywhere] * len(before) + [vmem] * len(blocks),
        out_specs=(anywhere, anywhere),
        scratch_shapes=[
            pltpu.VMEM((2, rows, width), jnp.float32),
            pltpu.SemaphoreType.DMA((2 * len(blocks),)),
        ],
        input_output_aliases={1: 0, 2: 1} if before else {},
        compiler_params=pltpu.CompilerParams(vmem_limit_bytes=VMEM_LIMIT),
        cost_estimate=NO_COST,
        name="assemble",
    )(ids, *before, *blocks)


def on_device(hidden_in, queries, grad_out, w_key, w_value, stretch_order, doc_lengths):
    inputs = hidden_in[0]
    head_dim = w_key.shape[1]
    dp_count = lax.axis_size("dp")
    ctx_count = lax.axis_size("ctx")
    z_count = ctx_count // 2
    sub_count = z_count // 2
    dp, ctx = lax.axis_index("dp"), lax.axis_index("ctx")
    z, core = ctx // 2, ctx % 2
    ids = jnp.stack([z, core, dp]).astype(jnp.int32)
    me = jnp.reshape(ctx, (1,)).astype(jnp.int32)
    block_rows = w_key.shape[0]
    half_rows = block_rows // 2
    quarter = half_rows // 2
    bits = [1 << at for at in range(dp_count.bit_length() - 1)]
    near = [j for j in range(1, dp_count) if j in bits]
    far = [j for j in range(1, dp_count) if j not in bits]

    def gather_near(*weights):
        pieces = {}
        for turn in range(2):
            for at, j in enumerate(near):
                offset = ((at + turn) % 2) * quarter
                start = core * half_rows + offset
                rows = [lax.dynamic_slice_in_dim(weight, start, quarter, 0) for weight in weights]
                pieces[j, 0, offset] = swap(jnp.concatenate(rows, axis=1), "dp", j)
        return pieces

    def gather_far(landed):
        pieces = {}
        for j in far:
            for offset, bit in ((0, 1 << (j.bit_length() - 1)), (quarter, j & -j)):
                origin = landed.get((j ^ bit, 0, offset), pieces.get((j ^ bit, 0, offset)))
                pieces[j, 0, offset] = swap(origin, "dp", bit)
        return pieces

    def from_other_core(pieces):
        return {(j, 1, offset): swap(one, "ctx", 1) for (j, _, offset), one in pieces.items()}

    def hold(arrays, pieces):
        names = list(pieces)
        tied, ended = after(arrays, *[pieces[name] for name in names])
        pieces.update(zip(names, ended))
        return tied

    def gather_along_z(own):
        return [swap(own, "ctx", 2 * m) if m else own for m in range(z_count)]

    def both_cores(along):
        return [block for one in along for block in (one, swap(one, "ctx", 1))]

    sizes = region_sizes(block_rows)
    regions = [(sum(sizes[:at]), size // 2) for at, size in enumerate(sizes)]
    first_rows = sum(sizes[:-1])
    moving = {
        j: lax.dynamic_slice_in_dim(inputs, (dp ^ j) * block_rows, first_rows, 1)
        for j in range(dp_count)
    }

    near_pieces = gather_near(w_key, w_value)
    far_pieces = gather_far(near_pieces)
    names = list(near_pieces)
    waiting, _ = after([near_pieces[name] for name in names[: len(near)]])
    others = {}
    for name, one in zip(names, waiting):
        (one,), _ = after([one], *others.values())
        others.update(from_other_core({name: one}))
    others.update(from_other_core({name: near_pieces[name] for name in names[len(near) :]}))
    near_pieces.update(others)
    early = project(
        ids, (w_key, w_value), inputs, block_rows, near_pieces, jnp.float32, bytes_cost(1 << 24)
    )
    others = near + far
    early, *tied = hold([early] + [moving[j] for j in others], far_pieces)
    moving.update(zip(others, tied))
    far_pieces.update(from_other_core(far_pieces))
    soonest = list(far_pieces)[len(far_pieces) // 2]
    tied, (far_pieces[soonest],) = after([moving[j] for j in near[:-1]], far_pieces[soonest])
    moving.update(zip(near[:-1], tied))
    own = project(ids, (early,), inputs, block_rows, far_pieces, jnp.bfloat16)
    moved = {0: moving[0]}
    moved[near[-1]] = swap(moving[near[-1]], "dp", near[-1])
    moved.update({j: swap(moving[j], "dp", j) for j in near[:-1]})
    along = gather_along_z(own)
    tied, _ = after([moving[j] for j in far], *along)
    moving.update(zip(far, tied))
    along, _ = after(along)
    kv_blocks = both_cores(along)

    moved.update({j: swap(moving[j], "dp", j) for j in far})

    query_grad, keep, send = attention(
        me, stretch_order, doc_lengths[0], queries[0], grad_out[0], kv_blocks, head_dim
    )
    (send,), ended = after([send], *[moved[j] for j in near])
    moved.update(zip(near, ended))
    own, *leaving = add_and_split(keep, swap(send, "ctx", 1), z_count)
    grad = add_all([own] + [swap(one, "ctx", 2 * m) for m, one in enumerate(leaving, 1)])
    grads = [grad] + [swap(grad, "dp", j) for j in range(1, dp_count)]

    groups = [[(0, j, 0, 0)] for j in range(dp_count)]
    ours, came = weight_rows(
        ids, [inputs], [grad], groups, *regions[-1], block_rows, sub_count, [*grads[1:], *[moved[j] for j in far]]
    )
    own = parts_over_dp(add_cores(ours, came))
    groups = [[(j, None, j, 0) for j in range(dp_count)]]
    arrays = [moved[j] for j in range(dp_count)]
    moved_parts = [
        add_cores(*weight_rows(ids, arrays, grads, groups, *region, block_rows, sub_count))
        for region in regions[:-1]
    ]
    moved_parts, own = after(moved_parts, *own)
    own = [swap(one, "dp", j) if j else one for j, one in enumerate(own)]
    finals = []
    for part in moved_parts:
        part = scatter_along_z(part, sub_count)
        finals.append(sum_of_halves(part, sub_count))
    part = scatter_along_z(sum_of(own), sub_count, finals[:TIED])
    blocks = gather_parts(finals[0], sub_count)
    last = sum_of_halves(part, sub_count, blocks)
    blocks += [one for final in finals[1:] for one in gather_parts(final, sub_count)]
    outs = assemble(ids, (), blocks, sub_count, regions[:-1], block_rows)
    last = gather_parts(last, sub_count, outs)
    key_rows, value_rows = assemble(ids, outs, last, sub_count, regions[-1:], block_rows)
    return query_grad[None], key_rows, value_rows


def solution(mesh):
    return jax.shard_map(
        on_device,
        mesh=mesh,
        in_specs=(
            P("dp", "ctx", None),
            P("dp", "ctx", None),
            P("dp", "ctx", None),
            P("dp", None),
            P("dp", None),
            P(),
            P("dp", None),
        ),
        out_specs=(P("dp", "ctx", None), P("dp", None), P("dp", None)),
        check_vma=False,
    )
```

```python
import functools
import math

import jax
import jax.numpy as jnp
from jax import lax
from jax.experimental import pallas as pl
from jax.experimental.pallas import tpu as pltpu
from jax.sharding import PartitionSpec as P

VMEM_LIMIT = 28 * 1024 * 1024
NO_COST = pl.CostEstimate(flops=0, bytes_accessed=0, transcendentals=0)


MOVED = (4, 6)
TIED = 2


def region_sizes(block_rows):
    units = block_rows // 256
    sizes = [256 * (units * share // 16) for share in MOVED]
    return sizes + [block_rows - sum(sizes)]


class Plan:
    def __init__(self, **fields):
        self.__dict__.update(fields)


def swap(array, axis, distance):
    count = lax.axis_size(axis)
    return lax.ppermute(array, axis, [(i, i ^ distance) for i in range(count)])


def after(arrays, *earlier):
    tied = lax.optimization_barrier((tuple(arrays), tuple(earlier)))
    return list(tied[0]), list(tied[1])


def shape_of(rows, width, kind=jnp.bfloat16):
    return jax.ShapeDtypeStruct((rows, width), kind)


def kernel_call(kernel, name, outs, scalars, arrays, scratch=(), cost=NO_COST):
    smem = pl.BlockSpec(memory_space=pltpu.SMEM)
    vmem = pl.BlockSpec(memory_space=pltpu.VMEM)
    single = not isinstance(outs, tuple)
    return pl.pallas_call(
        kernel,
        out_shape=outs,
        in_specs=[smem] * len(scalars) + [vmem] * len(arrays),
        out_specs=vmem if single else (vmem,) * len(outs),
        scratch_shapes=list(scratch),
        compiler_params=pltpu.CompilerParams(vmem_limit_bytes=VMEM_LIMIT),
        cost_estimate=cost,
        name=name,
    )(*scalars, *arrays)


def bytes_cost(amount):
    return pl.CostEstimate(flops=0, bytes_accessed=amount, transcendentals=0)


TN = (((0,), (0,)), ((), ()))


def attention_kernel(
    shape, ids, order, lengths, q_ref, g_ref, *refs
):
    ctx_count, stretch_rows, head_count, head_dim, window, chunk = shape
    kv_refs = refs[:ctx_count]
    qgrad_ref, keep_ref, send_ref, keys, values, total, qs, gs, dqs = refs[ctx_count:]
    me = ids[0]
    row_count = 2 * stretch_rows
    stretch_count = 2 * ctx_count
    score_scale = 1.0 / math.sqrt(head_dim)

    def place(device, half):
        return pl.multiple_of(order[2 * device + half] * stretch_rows, stretch_rows)

    for index in range(ctx_count):
        for half in range(2):
            rows = pl.ds(place(me ^ index, half), stretch_rows)
            block = kv_refs[index][half * stretch_rows : (half + 1) * stretch_rows, :]
            keys[rows, :] = block[:, :head_dim]
            values[rows, :] = block[:, head_dim:]
    total[...] = jnp.zeros_like(total)
    for half in range(2):
        for head in range(head_count):
            to = slice((half * head_count + head) * stretch_rows, (half * head_count + head + 1) * stretch_rows)
            rows = slice(half * stretch_rows, (half + 1) * stretch_rows)
            columns = slice(head * head_dim, (head + 1) * head_dim)
            qs[to, :] = q_ref[rows, columns]
            gs[to, :] = g_ref[rows, columns]
    ends = []
    running = 0
    for at in range(lengths.shape[0]):
        running = running + lengths[at]
        ends.append(running)
    chunks_half = head_count * stretch_rows // chunk

    def step(at, carry):
        half = at // chunks_half
        block = order[2 * me + half]
        first = jnp.maximum(block - stretch_count // 2, 0) * stretch_rows
        first = pl.multiple_of(first, stretch_rows)
        part = pl.ds(pl.multiple_of(at * chunk, chunk), chunk)
        inside = (at - half * chunks_half) * chunk + lax.broadcasted_iota(jnp.int32, (1, chunk), 1)
        at_query = block * stretch_rows + lax.rem(inside, stretch_rows)
        begin = jnp.zeros_like(at_query)
        for end in ends:
            begin = jnp.where(at_query >= end, end, begin)
        at_key = lax.broadcasted_iota(jnp.int32, (window, chunk), 0)
        allowed = (at_key + (first - begin)).astype(jnp.uint32) <= (at_query - begin).astype(
            jnp.uint32
        )
        k = keys[pl.ds(first, window), :]
        v = values[pl.ds(first, window), :]
        q = qs[part, :]
        g = gs[part, :]
        last = (((1,), (1,)), ((), ()))
        scores = lax.dot_general(k, q, last, preferred_element_type=jnp.float32)
        masked = jnp.where(allowed, scores, -jnp.inf)
        largest = jnp.max(masked, axis=0, keepdims=True)
        expsum = jnp.exp2((masked - largest) * (score_scale * math.log2(math.e)))
        probs = expsum * (1.0 / jnp.sum(expsum, axis=0, keepdims=True))
        probs_low = probs.astype(jnp.bfloat16)
        dprob = lax.dot_general(v, g, last, preferred_element_type=jnp.float32)
        delta = jnp.sum(probs_low.astype(jnp.float32) * dprob, axis=0, keepdims=True)
        dscore = (probs * (dprob - delta)).astype(jnp.bfloat16)
        dq = lax.dot_general(
            k, dscore, (((0,), (0,)), ((), ())), preferred_element_type=jnp.float32
        )
        dqs[part, :] = (jnp.transpose(dq) * score_scale).astype(jnp.bfloat16)
        dk = jnp.dot(dscore, q, preferred_element_type=jnp.float32) * score_scale
        dv = jnp.dot(probs_low, g, preferred_element_type=jnp.float32)
        total[pl.ds(first, window), :head_dim] += dk
        total[pl.ds(first, window), head_dim:] += dv
        return carry

    lax.fori_loop(0, 2 * chunks_half, step, 0, unroll=3)
    for half in range(2):
        for head in range(head_count):
            origin = slice((half * head_count + head) * stretch_rows, (half * head_count + head + 1) * stretch_rows)
            rows = slice(half * stretch_rows, (half + 1) * stretch_rows)
            columns = slice(head * head_dim, (head + 1) * head_dim)
            qgrad_ref[rows, columns] = dqs[origin, :]
    for index in range(ctx_count):
        for half in range(2):
            rows = pl.ds(place(me ^ index, half), stretch_rows)
            start = (index // 2) * row_count + half * stretch_rows
            if index % 2:
                send_ref[start : start + stretch_rows, :] = total[rows, :].astype(jnp.bfloat16)
            else:
                keep_ref[start : start + stretch_rows, :] = total[rows, :]


def attention(me, order, lengths, queries, cotangent, kv_blocks, head_dim):
    row_count, width = queries.shape
    ctx_count = len(kv_blocks)
    stretch_rows = row_count // 2
    head_count = width // head_dim
    seq_rows = row_count * ctx_count
    window = seq_rows // 2 + stretch_rows
    stacked = head_count * stretch_rows
    chunk = 256 if stacked % 256 == 0 else 128
    shape = (ctx_count, stretch_rows, head_count, head_dim, window, chunk)
    smem = pl.BlockSpec(memory_space=pltpu.SMEM)
    vmem = pl.BlockSpec(memory_space=pltpu.VMEM)
    half_rows = seq_rows // 2
    return pl.pallas_call(
        functools.partial(attention_kernel, shape),
        out_shape=(
            jax.ShapeDtypeStruct((row_count, width), jnp.bfloat16),
            jax.ShapeDtypeStruct((half_rows, 2 * head_dim), jnp.float32),
            jax.ShapeDtypeStruct((half_rows, 2 * head_dim), jnp.bfloat16),
        ),
        in_specs=[smem] * 3 + [vmem] * (2 + ctx_count),
        out_specs=(vmem,) * 3,
        scratch_shapes=[
            pltpu.VMEM((seq_rows, head_dim), jnp.bfloat16),
            pltpu.VMEM((seq_rows, head_dim), jnp.bfloat16),
            pltpu.VMEM((seq_rows, 2 * head_dim), jnp.float32),
            pltpu.VMEM((2 * stacked, head_dim), jnp.bfloat16),
            pltpu.VMEM((2 * stacked, head_dim), jnp.bfloat16),
            pltpu.VMEM((2 * stacked, head_dim), jnp.bfloat16),
        ],
        compiler_params=pltpu.CompilerParams(vmem_limit_bytes=VMEM_LIMIT),
        cost_estimate=NO_COST,
        name="attention",
    )(me, order, lengths, queries, cotangent, *kv_blocks)


def project_kernel(plan, ids, hidden, *refs):
    out_ref = refs[-1]
    dp, core = ids[2], ids[1]
    if plan.start:
        total = refs[0][...]
    else:
        columns = pl.ds(pl.multiple_of(dp * plan.block_rows, plan.block_rows), plan.block_rows)
        total = jnp.concatenate(
            [
                jnp.dot(hidden[:, columns], own[...], preferred_element_type=jnp.float32)
                for own in refs[:2]
            ],
            axis=1,
        )
    for (block, side, offset), weight in zip(plan.terms, refs[1 if plan.start else 2 : -1]):
        from_column = (dp ^ block) * plan.block_rows + (core ^ side) * plan.side_rows + offset
        columns = pl.ds(pl.multiple_of(from_column, 128), weight.shape[0])
        total += jnp.dot(hidden[:, columns], weight[...], preferred_element_type=jnp.float32)
    out_ref[...] = total.astype(out_ref.dtype)


def project(ids, begin, inputs, block_rows, pieces, kind, cost=NO_COST):
    names = sorted(pieces)
    weights = [pieces[name] for name in names]
    plan = Plan(
        terms=names, start=len(begin) == 1, block_rows=block_rows, side_rows=block_rows // 2
    )
    return kernel_call(
        functools.partial(project_kernel, plan),
        "project",
        shape_of(inputs.shape[0], weights[0].shape[1], kind),
        (ids,),
        (inputs, *begin, *weights),
        cost=cost,
    )


def split_kernel(rows, keep, came, own_ref, *leaving_refs):
    own_ref[...] = keep[:rows, :] + came[:rows, :].astype(jnp.float32)
    for m, leaving in enumerate(leaving_refs, 1):
        block = slice(m * rows, (m + 1) * rows)
        leaving[...] = (keep[block, :] + came[block, :].astype(jnp.float32)).astype(leaving.dtype)


def add_and_split(keep, came, count):
    rows, width = keep.shape[0] // count, keep.shape[1]
    outs = (shape_of(rows, width, jnp.float32),) + (shape_of(rows, width),) * (count - 1)
    return kernel_call(functools.partial(split_kernel, rows), "split", outs, (), (keep, came))


def total_kernel(*refs):
    total = refs[0][...]
    for one in refs[1:-1]:
        total = total + one[...].astype(jnp.float32)
    refs[-1][...] = total.astype(refs[-1].dtype)


def add_all(arrays):
    out = jax.ShapeDtypeStruct(arrays[0].shape, jnp.bfloat16)
    return kernel_call(total_kernel, "total", out, (), arrays)


def weight_kernel(plan, ids, *refs):
    hidden = refs[: plan.hidden]
    grads = refs[plan.hidden : -2]
    z, core, dp = ids[0] % plan.sub_count, ids[1], ids[2]
    rows = plan.rows
    share = rows // plan.sub_count
    tile = next(size for size in (512, 256, 128) if rows % size == 0)
    step = math.gcd(share, tile)
    for side, out_ref in ((1, refs[-2]), (0, refs[-1])):
        for at, group in enumerate(plan.groups):
            for start in range(0, rows, tile):
                product = None
                for array, block, grad, shift in group:
                    origin = plan.origin - shift + (core ^ side) * rows + start
                    if block is not None:
                        origin = origin + (dp ^ block) * plan.block_rows
                    columns = pl.ds(pl.multiple_of(origin, 128), tile)
                    term = lax.dot_general(
                        hidden[array][:, columns],
                        grads[grad][...],
                        TN,
                        preferred_element_type=jnp.float32,
                    )
                    product = term if product is None else product + term
                for inner in range(0, tile, step):
                    part, offset = divmod(start + inner, share)
                    to = pl.multiple_of(at * rows + (z ^ part) * share + offset, step)
                    piece = product[inner : inner + step, :]
                    out_ref[pl.ds(to, step), :] = piece.astype(out_ref.dtype)


def weight_rows(ids, hidden, grads, groups, origin, rows, block_rows, sub_count, earlier=()):
    plan = Plan(
        hidden=len(hidden),
        groups=groups,
        origin=origin,
        rows=rows,
        block_rows=block_rows,
        sub_count=sub_count,
    )
    out = shape_of(rows * len(groups), grads[0].shape[1])
    theirs, ours = kernel_call(
        functools.partial(weight_kernel, plan),
        "weight_rows",
        (out, out),
        (ids,),
        (*hidden, *grads),
    )
    (theirs,), _ = after([theirs], *earlier)
    return ours, swap(theirs, "ctx", 1)


def add_cores(ours, came):
    return ours.astype(jnp.float32) + came.astype(jnp.float32)


def parts_over_dp(array):
    count = lax.axis_size("dp")
    rows = array.shape[0] // count
    parts = [array[j * rows : (j + 1) * rows] for j in range(count)]
    return parts[:1] + [part.astype(jnp.bfloat16) for part in parts[1:]]


def sum_of(arrays):
    total = arrays[0]
    for one in arrays[1:]:
        total = total + one.astype(jnp.float32)
    return total


def z_bits(sub_count):
    return [1 << at for at in range(sub_count.bit_length() - 1)]


def scatter_along_z(full, sub_count, earlier=()):
    share = full.shape[0] // sub_count
    parts = {m: full[m * share : (m + 1) * share] for m in range(sub_count)}
    for bit in z_bits(sub_count):
        for m in list(parts):
            if m & bit:
                came = swap(parts.pop(m).astype(jnp.bfloat16), "ctx", 2 * bit)
                (came,), _ = after([came], *earlier)
                parts[m ^ bit] = parts[m ^ bit] + came.astype(jnp.float32)
    return parts[0]


def sum_of_halves(part, sub_count, earlier=()):
    low = swap(part.astype(jnp.bfloat16), "ctx", 2 * sub_count)
    (low,), _ = after([low], *earlier)
    return (part + low.astype(jnp.float32)).astype(jnp.bfloat16)


def gather_parts(part, sub_count, earlier=()):
    rows = {0: part}
    for bit in z_bits(sub_count)[::-1]:
        for m, one in list(rows.items()):
            (rows[m | bit],), _ = after([swap(one, "ctx", 2 * bit)], *earlier)
    own = [rows[m] for m in range(sub_count)]
    return own + [swap(one, "ctx", 1) for one in own]


def assemble_kernel(sub_count, regions, first, ids, *refs):
    count = 2 * sub_count * len(regions)
    blocks = iter(refs[2 * (not first) :][:count])
    *outs, buffer, sems = refs[2 * (not first) + count :]
    z, core = ids[0] % sub_count, ids[1]
    copies = []
    filled = 0
    for origin, rows in regions:
        share = rows // sub_count
        for side in range(2):
            for m in range(sub_count):
                to = origin + (core ^ side) * rows + (z ^ m) * share
                to = pl.multiple_of(to, math.gcd(origin, share))
                block_ref = next(blocks)
                width = block_ref.shape[1] // 2
                for which, out_ref in enumerate(outs):
                    piece = buffer.at[which, pl.ds(filled, share), :]
                    piece[...] = block_ref[:, which * width : (which + 1) * width].astype(
                        jnp.float32
                    )
                    copy = pltpu.make_async_copy(
                        piece, out_ref.at[pl.ds(to, share), :], sems.at[len(copies)]
                    )
                    copy.start()
                    copies.append(copy)
                filled += share
    for copy in copies:
        copy.wait()


def assemble(ids, before, blocks, sub_count, regions, block_rows):
    rows = sum(block.shape[0] for block in blocks)
    width = blocks[0].shape[1] // 2
    out = shape_of(block_rows, width, jnp.float32)
    smem = pl.BlockSpec(memory_space=pltpu.SMEM)
    vmem = pl.BlockSpec(memory_space=pltpu.VMEM)
    anywhere = pl.BlockSpec(memory_space=pl.ANY)
    return pl.pallas_call(
        functools.partial(assemble_kernel, sub_count, regions, not before),
        out_shape=(out, out),
        in_specs=[smem] + [anywhere] * len(before) + [vmem] * len(blocks),
        out_specs=(anywhere, anywhere),
        scratch_shapes=[
            pltpu.VMEM((2, rows, width), jnp.float32),
            pltpu.SemaphoreType.DMA((2 * len(blocks),)),
        ],
        input_output_aliases={1: 0, 2: 1} if before else {},
        compiler_params=pltpu.CompilerParams(vmem_limit_bytes=VMEM_LIMIT),
        cost_estimate=NO_COST,
        name="assemble",
    )(ids, *before, *blocks)


def on_device(hidden_in, queries, grad_out, w_key, w_value, stretch_order, doc_lengths):
    inputs = hidden_in[0]
    head_dim = w_key.shape[1]
    dp_count = lax.axis_size("dp")
    ctx_count = lax.axis_size("ctx")
    z_count = ctx_count // 2
    sub_count = z_count // 2
    dp, ctx = lax.axis_index("dp"), lax.axis_index("ctx")
    z, core = ctx // 2, ctx % 2
    ids = jnp.stack([z, core, dp]).astype(jnp.int32)
    me = jnp.reshape(ctx, (1,)).astype(jnp.int32)
    block_rows = w_key.shape[0]
    half_rows = block_rows // 2
    quarter = half_rows // 2
    bits = [1 << at for at in range(dp_count.bit_length() - 1)]
    near = [j for j in range(1, dp_count) if j in bits]
    far = [j for j in range(1, dp_count) if j not in bits]

    def gather_near(*weights):
        pieces = {}
        for turn in range(2):
            for at, j in enumerate(near):
                offset = ((at + turn) % 2) * quarter
                start = core * half_rows + offset
                rows = [lax.dynamic_slice_in_dim(weight, start, quarter, 0) for weight in weights]
                pieces[j, 0, offset] = swap(jnp.concatenate(rows, axis=1), "dp", j)
        return pieces

    def gather_far(landed):
        pieces = {}
        for j in far:
            for offset, bit in ((0, 1 << (j.bit_length() - 1)), (quarter, j & -j)):
                origin = landed.get((j ^ bit, 0, offset), pieces.get((j ^ bit, 0, offset)))
                pieces[j, 0, offset] = swap(origin, "dp", bit)
        return pieces

    def from_other_core(pieces):
        return {(j, 1, offset): swap(one, "ctx", 1) for (j, _, offset), one in pieces.items()}

    def hold(arrays, pieces):
        names = list(pieces)
        tied, ended = after(arrays, *[pieces[name] for name in names])
        pieces.update(zip(names, ended))
        return tied

    def gather_along_z(own):
        return [swap(own, "ctx", 2 * m) if m else own for m in range(z_count)]

    def both_cores(along):
        return [block for one in along for block in (one, swap(one, "ctx", 1))]

    sizes = region_sizes(block_rows)
    regions = [(sum(sizes[:at]), size // 2) for at, size in enumerate(sizes)]
    first_rows = sum(sizes[:-1])
    moving = {
        j: lax.dynamic_slice_in_dim(inputs, (dp ^ j) * block_rows, first_rows, 1)
        for j in range(dp_count)
    }

    near_pieces = gather_near(w_key, w_value)
    far_pieces = gather_far(near_pieces)
    names = list(near_pieces)
    waiting, _ = after([near_pieces[name] for name in names[: len(near)]])
    others = {}
    for name, one in zip(names, waiting):
        (one,), _ = after([one], *others.values())
        others.update(from_other_core({name: one}))
    others.update(from_other_core({name: near_pieces[name] for name in names[len(near) :]}))
    near_pieces.update(others)
    early = project(
        ids, (w_key, w_value), inputs, block_rows, near_pieces, jnp.float32, bytes_cost(1 << 24)
    )
    others = near + far
    early, *tied = hold([early] + [moving[j] for j in others], far_pieces)
    moving.update(zip(others, tied))
    far_pieces.update(from_other_core(far_pieces))
    soonest = list(far_pieces)[len(far_pieces) // 2]
    tied, (far_pieces[soonest],) = after([moving[j] for j in near[:-1]], far_pieces[soonest])
    moving.update(zip(near[:-1], tied))
    own = project(ids, (early,), inputs, block_rows, far_pieces, jnp.bfloat16)
    moved = {0: moving[0]}
    moved[near[-1]] = swap(moving[near[-1]], "dp", near[-1])
    moved.update({j: swap(moving[j], "dp", j) for j in near[:-1]})
    along = gather_along_z(own)
    tied, _ = after([moving[j] for j in far], *along)
    moving.update(zip(far, tied))
    along, _ = after(along)
    kv_blocks = both_cores(along)

    moved.update({j: swap(moving[j], "dp", j) for j in far})

    query_grad, keep, send = attention(
        me, stretch_order, doc_lengths[0], queries[0], grad_out[0], kv_blocks, head_dim
    )
    (send,), ended = after([send], *[moved[j] for j in near])
    moved.update(zip(near, ended))
    own, *leaving = add_and_split(keep, swap(send, "ctx", 1), z_count)
    grad = add_all([own] + [swap(one, "ctx", 2 * m) for m, one in enumerate(leaving, 1)])
    grads = [grad] + [swap(grad, "dp", j) for j in range(1, dp_count)]

    (grad,), ended = after([grad], grads[near[0]], *[moved[j] for j in far])
    grads[near[0]] = ended[0]
    moved.update(zip(far, ended[1:]))
    groups = [[(0, j, 0, 0)] for j in range(dp_count)]
    ours, came = weight_rows(
        ids, [inputs], [grad], groups, *regions[-1], block_rows, sub_count, grads[1:]
    )
    own = parts_over_dp(add_cores(ours, came))
    groups = [[(j, None, j, 0) for j in range(dp_count)]]
    arrays = [moved[j] for j in range(dp_count)]
    moved_parts = [
        add_cores(*weight_rows(ids, arrays, grads, groups, *region, block_rows, sub_count))
        for region in regions[:-1]
    ]
    moved_parts[1:], own = after(moved_parts[1:], *own)
    ready = [own, ()]
    own = [swap(one, "dp", j) if j else one for j, one in enumerate(own)]
    finals = []
    for part, earlier in zip(moved_parts, ready):
        part = scatter_along_z(part, sub_count, earlier)
        finals.append(sum_of_halves(part, sub_count))
    part = scatter_along_z(sum_of(own), sub_count, finals[:TIED])
    blocks = gather_parts(finals[0], sub_count)
    last = sum_of_halves(part, sub_count, blocks)
    blocks += [one for final in finals[1:] for one in gather_parts(final, sub_count)]
    outs = assemble(ids, (), blocks, sub_count, regions[:-1], block_rows)
    last = gather_parts(last, sub_count, outs)
    key_rows, value_rows = assemble(ids, outs, last, sub_count, regions[-1:], block_rows)
    return query_grad[None], key_rows, value_rows


def solution(mesh):
    return jax.shard_map(
        on_device,
        mesh=mesh,
        in_specs=(
            P("dp", "ctx", None),
            P("dp", "ctx", None),
            P("dp", "ctx", None),
            P("dp", None),
            P("dp", None),
            P(),
            P("dp", None),
        ),
        out_specs=(P("dp", "ctx", None), P("dp", None), P("dp", None)),
        check_vma=False,
    )
```
